32 devices in a mesh: groups: 2 (over y), dp: 4 (over z), tensor: 2 (over x), seq: 2 (over core).
Axes of the slice: x: 2, y: 2, z: 4, core: 2. Of those that a mesh axis runs over, the one named last changes fastest.
Arguments:
- acts: bfloat16 [64, 256, 4096], P(('groups', 'dp'), 'seq', 'tensor'), parts along dimension 0, may hold values from -6 to 6
- grads: bfloat16 [64, 256, 14336], P(('groups', 'dp'), 'seq', 'tensor'), parts along dimension 0, may hold values from -0.375 to 0.375
- in_ids: int32 [64], P('tensor'), may hold values from 0 to 31
- in_signs: int32 [64], P('tensor'), may hold values from 0 to 1
- out_ids: int32 [224], P('tensor'), may hold values from 0 to 31
- out_signs: int32 [224], P('tensor'), may hold values from 0 to 1
- in_table: bfloat16 [32, 4096], replicated, may hold values from -0.09375 to 0.09375
- out_table: bfloat16 [32, 4096], replicated, may hold values from -0.046875 to 0.046875
Outputs:
- projected: float32 [64, 4096], P(('groups', 'dp'), ('tensor', 'seq')), parts along dimension 0
- fisher: float32 [8192, 4096], P(('groups', 'tensor', 'seq'), 'dp'), parts along dimension 0
The draws below stay inside these ranges and needn't reach their ends.
There are 2 independent parts, one for each index of `groups`. The reference program is written for one: setup_inputs(seed, part) draws one part's arguments, and reference() takes and returns one part's arrays. A program takes and returns all parts, laid end to end along the dimension named above; an argument that names none is the same for every part. Nothing has to cross between parts.
Inputs may be any that keep to these rules, and one draw needn't show every extreme that they name: `in_signs`: signs are bits: the block's sign is 2 s - 1. `out_signs`: signs are bits: the block's sign is 2 s - 1.
All inputs are finite; a program needn't handle non-finite values.
Results may differ from the reference program's by a relative error of at most 0.0003.
Values sent between devices are 32-bit elements; how exact they have to be, the bound alone decides.
No kernel may reach another device: no remote copies, remote signals or barrier semaphores. Data moves between devices by JAX's collectives and lax.ppermute only.
A program may use at most 64 MiB of HBM per device.

```python
import jax
import jax.numpy as jnp
from jax import lax

D = 4096
FF = 14336
PROJ = 64
BLOCK = 64
NTAB = 32
LEN = 256
EXAMPLES = 32


def set_ends(array, stream_key, smallest, largest):
    shape = array.shape
    place = [jax.random.randint(jax.random.fold_in(stream_key, axis), (), 0, shape[axis]) for axis in range(len(shape))]
    array = array.at[tuple(place)].set(smallest)
    longest = shape.index(max(shape))
    place[longest] = (place[longest] + 1) % shape[longest]
    return array.at[tuple(place)].set(largest)


def steps_of(rng, extent, shards, smallest, high):
    def one(position, shards_of):
        steps = jax.random.uniform(jax.random.fold_in(jax.random.fold_in(rng, 6), position), (shards_of,), jnp.float32, smallest / len(shards), high / len(shards))
        return jnp.repeat(jnp.exp(steps), extent[position] // shards_of).reshape((-1,) + (1,) * (len(extent) - position - 1))

    loudness = one(*shards[0])
    for cut in shards[1:]:
        loudness = loudness * one(*cut)
    return loudness


def scatter_about(key, extent, width, bound, cuts=(), kind=jnp.bfloat16):
    factor_of = steps_of(key, extent, cuts, -0.22, 0.18) if cuts else 1.0
    values = jax.random.normal(key, extent, jnp.float32) * width * factor_of
    return jnp.minimum(jnp.maximum(values, -bound), bound).astype(kind)


def setup_inputs(seed: int = 0, part: int = 0) -> dict:
    key_of = jax.random.split(jax.random.key(seed), 9)
    part_splits = jax.random.split(jax.random.fold_in(key_of[8], part), 9)
    return {
        "acts": scatter_about(part_splits[0], (EXAMPLES, LEN, D), 1.0, 6.0, ((0, 4), (1, 2), (2, 2))),
        "grads": scatter_about(part_splits[1], (EXAMPLES, LEN, FF), 0.0625, 0.375, ((0, 4), (1, 2), (2, 2))),
        "in_ids": set_ends(jax.random.randint(key_of[2], (D // BLOCK,), 0, NTAB), jax.random.fold_in(key_of[2], 1), 0, NTAB - 1).astype(jnp.int32),
        "in_signs": set_ends(jax.random.randint(key_of[3], (D // BLOCK,), 0, 2), jax.random.fold_in(key_of[3], 1), 0, 1).astype(jnp.int32),
        "out_ids": set_ends(jax.random.randint(key_of[4], (FF // BLOCK,), 0, NTAB), jax.random.fold_in(key_of[4], 1), 0, NTAB - 1).astype(jnp.int32),
        "out_signs": set_ends(jax.random.randint(key_of[5], (FF // BLOCK,), 0, 2), jax.random.fold_in(key_of[5], 1), 0, 1).astype(jnp.int32),
        "in_table": scatter_about(key_of[6], (NTAB, BLOCK * PROJ), D ** -0.5, 0.09375),
        "out_table": scatter_about(key_of[7], (NTAB, BLOCK * PROJ), FF ** -0.5, 0.046875),
    }


def build_matrix(ids, signs, table):
    blocks = table[ids].astype(jnp.float32) * (2 * signs - 1).astype(jnp.float32)[:, None]
    return blocks.reshape(-1, PROJ).astype(jnp.bfloat16)


def reference(acts, grads, in_ids, in_signs, out_ids, out_signs, in_table, out_table):
    in_proj = build_matrix(in_ids, in_signs, in_table)
    out_proj = build_matrix(out_ids, out_signs, out_table)
    count = acts.shape[0]
    act_low = jnp.dot(acts.reshape(-1, acts.shape[2]), in_proj, preferred_element_type=jnp.float32)
    grad_low = jnp.dot(grads.reshape(-1, grads.shape[2]), out_proj, preferred_element_type=jnp.float32)
    act_low = act_low.reshape(count, -1, PROJ)
    grad_low = grad_low.reshape(count, -1, PROJ)
    kron = jnp.einsum("etp,etq->epq", grad_low, act_low, precision=lax.Precision.HIGHEST)
    projected = kron.reshape(count, PROJ * PROJ)
    fisher = lax.dot_general(projected, projected, (((0,), (0,)), ((), ())), precision=lax.Precision.HIGHEST) / count
    return projected, fisher
```

```python
import functools

import jax
import jax.numpy as jnp
from jax import lax
from jax.experimental import pallas as pl
from jax.experimental.pallas import tpu as pltpu
from jax.sharding import PartitionSpec as P

PROJ = 64
BLOCK = 64
LANES = 128
VMEM_BYTES = 48 * 1024 * 1024
PLANE = ("tensor", "seq")


def chunk_of(width):
    chunk = 1024
    while width % chunk:
        chunk -= LANES
    return chunk


def split3(x):
    high = x.astype(jnp.bfloat16)
    rest = x - high.astype(jnp.float32)
    mid = rest.astype(jnp.bfloat16)
    low = (rest - mid.astype(jnp.float32)).astype(jnp.bfloat16)
    return high, mid, low


def build_matrix(ids, signs, table, spread, matrix):
    entries = table.shape[0]
    left = lax.broadcasted_iota(jnp.int32, (entries, LANES), 1) < PROJ
    for row in range(BLOCK):
        pair = row // 2 * LANES
        both = table[:, pair : pair + LANES].astype(jnp.float32)
        keep = left if row % 2 == 0 else jnp.logical_not(left)
        spread[pl.ds(row, entries, stride=BLOCK), :] = jnp.where(keep, both, 0.0)
    blocks = ids.shape[0]
    unroll = 4 if blocks % 4 == 0 else 1

    def some(step, carry):
        for part in range(unroll):
            j = step * unroll + part
            start = pl.multiple_of(ids[j] * BLOCK, BLOCK)
            sign = (2 * signs[j] - 1).astype(jnp.float32)
            into = pl.multiple_of(j * BLOCK, BLOCK)
            matrix[pl.ds(into, BLOCK), :] = (spread[pl.ds(start, BLOCK), :] * sign).astype(jnp.bfloat16)
        return carry

    lax.fori_loop(0, blocks // unroll, some, 0)


def project_kernel(transpose, ids, signs, table, rows_ref, out, spread, matrix, held, total, sems):
    chunks, _, chunk = held.shape
    copies = [
        pltpu.make_async_copy(rows_ref.at[:, pl.ds(c * chunk, chunk)], held.at[c], sems.at[c])
        for c in range(chunks)
    ]
    for copy in copies:
        copy.start()
    build_matrix(ids, signs, table, spread, matrix)
    for c, copy in enumerate(copies):
        copy.wait()
        part = jnp.dot(
            held[c], matrix[pl.ds(c * chunk, chunk), :], preferred_element_type=jnp.float32
        )
        if c == 0:
            total[...] = part
        else:
            total[...] += part
    pairs, tokens, _ = out.shape
    left = lax.broadcasted_iota(jnp.int32, (tokens, LANES), 1) < PROJ
    for pair in range(pairs):
        first = total[pl.ds(2 * pair * tokens, tokens), :]
        second = total[pl.ds((2 * pair + 1) * tokens, tokens), :]
        first = first + pltpu.roll(first, PROJ, 1)
        second = second + pltpu.roll(second, PROJ, 1)
        packed = jnp.where(left, first, second)
        out[pair] = packed.T if transpose else packed


def project(values, ids, signs, table, transpose, name):
    count, tokens, width = values.shape
    chunk = chunk_of(width)
    chunks = width // chunk
    rows = count * tokens
    smem = pl.BlockSpec(memory_space=pltpu.SMEM)
    vmem = pl.BlockSpec(memory_space=pltpu.VMEM)
    shape = (count // 2, LANES, tokens) if transpose else (count // 2, tokens, LANES)
    return pl.pallas_call(
        functools.partial(project_kernel, transpose),
        out_shape=jax.ShapeDtypeStruct(shape, jnp.float32),
        in_specs=[smem, smem, vmem, pl.BlockSpec(memory_space=pl.ANY)],
        out_specs=vmem,
        scratch_shapes=[
            pltpu.VMEM((table.shape[0] * BLOCK, LANES), jnp.float32),
            pltpu.VMEM((width, LANES), jnp.bfloat16),
            pltpu.VMEM((chunks, rows, chunk), jnp.bfloat16),
            pltpu.VMEM((rows, LANES), jnp.float32),
            pltpu.SemaphoreType.DMA((chunks,)),
        ],
        compiler_params=pltpu.CompilerParams(vmem_limit_bytes=VMEM_BYTES),
        cost_estimate=pl.CostEstimate(
            flops=2 * rows * width * LANES, bytes_accessed=2 * rows * width, transcendentals=0
        ),
        name=name,
    )(ids, signs, table, values.reshape(rows, width))


def kron_kernel(shards, acts, grads, *refs):
    summands, outs, products = refs[: len(refs) - shards - 1], refs[-shards - 1 : -1], refs[-1]
    pairs, tokens, _ = acts.shape
    for pair in range(pairs):
        act = acts[pair]
        for other in summands:
            act = act + other[pair]
        a1, a2, a3 = split3(act)
        g1, g2, g3 = split3(grads[pair])
        left = jnp.concatenate([g1, g1, g2, g1, g3, g2], axis=1)
        right = jnp.concatenate([a1, a2, a1, a3, a1, a2], axis=0)
        products[pl.ds(pair * LANES, LANES), :] = jnp.dot(left, right, preferred_element_type=jnp.float32)
    count = 2 * pairs
    lower = lax.broadcasted_iota(jnp.int32, (count, LANES), 1) < PROJ
    even = lax.broadcasted_iota(jnp.int32, (count, LANES), 0) % 2 == 0
    here = even == lower
    width = outs[0].shape[1]
    if shards == 1:
        place = 0
    else:
        place = lax.axis_index("tensor") * lax.axis_size("seq") + lax.axis_index("seq")
    for step, out in enumerate(outs):
        piece = lax.rem(place + step, shards) if shards > 1 else 0
        for tile in range(width // LANES):
            row = piece * (width // PROJ) + 2 * tile
            both = []
            for p in (row, row + 1):
                v = products[pl.ds(p, count, stride=PROJ), :]
                both.append(jnp.where(here, v, pltpu.roll(v, PROJ, 1)))
            out[:, pl.ds(tile * LANES, LANES)] = jnp.where(lower, both[0], both[1])


def kron_pieces(act_parts, grads, shards):
    pairs, _, tokens = grads.shape
    vmem = pl.BlockSpec(memory_space=pltpu.VMEM)
    piece = jax.ShapeDtypeStruct((2 * pairs, PROJ * PROJ // shards), jnp.float32)
    return pl.pallas_call(
        functools.partial(kron_kernel, shards),
        out_shape=[piece] * shards,
        in_specs=[vmem] * (1 + len(act_parts)),
        out_specs=[vmem] * shards,
        scratch_shapes=[pltpu.VMEM((pairs * LANES, LANES), jnp.float32)],
        compiler_params=pltpu.CompilerParams(vmem_limit_bytes=VMEM_BYTES),
        name="kron",
    )(act_parts[0], grads, *act_parts[1:])


def fisher_kernel(scale, order, *refs):
    pieces = order.shape[0] // 2
    lefts, rights = refs[:pieces], refs[pieces : 2 * pieces]
    out, left, right, left_parts, right_parts = refs[2 * pieces :]
    rows = lefts[0].shape[0]

    @pl.when(pl.program_id(0) == 0)
    def _():
        for k in range(pieces):
            left[pl.ds(pl.multiple_of(order[k] * rows, 8), rows), :] = lefts[k][...]
            right[pl.ds(pl.multiple_of(order[pieces + k] * rows, 8), rows), :] = rights[k][...]
        l1, l2, l3 = split3(left[...])
        r1, r2, r3 = split3(right[...] * scale)
        left_parts[...] = jnp.concatenate([l1, l1, l2, l1, l3, l2], axis=0)
        right_parts[...] = jnp.concatenate([r1, r2, r1, r3, r1, r2], axis=0)

    height = out.shape[0]
    start = pl.multiple_of(pl.program_id(0) * height, LANES)
    out[...] = lax.dot_general(
        left_parts[:, pl.ds(start, height)],
        right_parts[...],
        (((0,), (0,)), ((), ())),
        preferred_element_type=jnp.float32,
    )


def fisher_block(lefts, rights, order):
    pieces = len(lefts)
    rows, height = lefts[0].shape
    width = rights[0].shape[1]
    total = rows * pieces
    block = height // 4
    whole = pl.BlockSpec((rows, height), lambda i: (0, 0))
    whole_right = pl.BlockSpec((rows, width), lambda i: (0, 0))
    return pl.pallas_call(
        functools.partial(fisher_kernel, 1.0 / total),
        grid=(height // block,),
        out_shape=jax.ShapeDtypeStruct((height, width), jnp.float32),
        in_specs=[pl.BlockSpec(memory_space=pltpu.SMEM)] + [whole] * pieces + [whole_right] * pieces,
        out_specs=pl.BlockSpec((block, width), lambda i: (i, 0)),
        scratch_shapes=[
            pltpu.VMEM((total, height), jnp.float32),
            pltpu.VMEM((total, width), jnp.float32),
            pltpu.VMEM((6 * total, height), jnp.bfloat16),
            pltpu.VMEM((6 * total, width), jnp.bfloat16),
        ],
        compiler_params=pltpu.CompilerParams(vmem_limit_bytes=VMEM_BYTES),
        name="fisher",
    )(order, *lefts, *rights)


def local(acts, grads, in_ids, in_signs, out_ids, out_signs, in_table, out_table):
    tensor, seq, dp = (lax.axis_size(name) for name in ("tensor", "seq", "dp"))
    shards = tensor * seq
    place = lax.axis_index("tensor") * seq + lax.axis_index("seq")
    mine_dp = lax.axis_index("dp")

    act = project(acts, in_ids, in_signs, in_table, False, "project_acts")
    if tensor == 2:
        act_parts = [act, lax.ppermute(act, "tensor", [(0, 1), (1, 0)])]
    else:
        act_parts = [lax.psum(act, "tensor")]
    grad = project(grads, out_ids, out_signs, out_table, True, "project_grads")

    if shards != dp or shards > 4:
        kron = lax.psum(kron_pieces(act_parts, grad, 1)[0], PLANE)
        width = kron.shape[1] // shards
        mine = lax.dynamic_slice_in_dim(kron, place * width, width, 1)
        every = lax.all_gather(kron, "dp", axis=0, tiled=True)
        left = lax.dynamic_slice_in_dim(every, place * width, width, 1)
        columns = kron.shape[1] // dp
        right = lax.dynamic_slice_in_dim(every, mine_dp * columns, columns, 1)
        fisher = lax.dot_general(
            left, right, (((0,), (0,)), ((), ())), precision=lax.Precision.HIGHEST
        ) / left.shape[0]
        return mine, fisher

    pieces = kron_pieces(act_parts, grad, shards)
    mine = pieces[0]
    for k in range(1, shards):
        mine = mine + lax.ppermute(pieces[k], PLANE, [(p, (p + k) % shards) for p in range(shards)])

    lefts, rights = [mine], []
    for k in range(1, dp):
        lefts.append(lax.ppermute(mine, "dp", [(d, (d + k) % dp) for d in range(dp)]))
    for k in range(dp):
        pairs = [
            (d * shards + p, p * shards + (d + k) % shards) for d in range(dp) for p in range(shards)
        ]
        rights.append(lax.ppermute(mine, ("dp",) + PLANE, pairs))
    steps = jnp.arange(dp, dtype=jnp.int32)
    order = jnp.concatenate([(mine_dp - steps) % dp, (place - steps) % dp]).astype(jnp.int32)
    return mine, fisher_block(lefts, rights, order)


def solution(mesh):
    in_specs = (
        P(("groups", "dp"), "seq", "tensor"),
        P(("groups", "dp"), "seq", "tensor"),
        P("tensor"),
        P("tensor"),
        P("tensor"),
        P("tensor"),
        P(),
        P(),
    )
    out_specs = (P(("groups", "dp"), ("tensor", "seq")), P(("groups", "tensor", "seq"), "dp"))
    return jax.shard_map(local, mesh=mesh, in_specs=in_specs, out_specs=out_specs, check_vma=False)
```

```python
import functools

import jax
import jax.numpy as jnp
from jax import lax
from jax.experimental import pallas as pl
from jax.experimental.pallas import tpu as pltpu
from jax.sharding import PartitionSpec as P

PROJ = 64
BLOCK = 64
LANES = 128
VMEM_BYTES = 48 * 1024 * 1024
ALL_VMEM = 48 * 1024 * 1024
PLANE = ("tensor", "seq")


def chunk_of(width, most):
    chunk = most
    while width % chunk:
        chunk -= LANES
    return chunk


def split3(x):
    high = x.astype(jnp.bfloat16)
    rest = x - high.astype(jnp.float32)
    mid = rest.astype(jnp.bfloat16)
    low = (rest - mid.astype(jnp.float32)).astype(jnp.bfloat16)
    return high, mid, low


def spread_table(table, spread, signed):
    entries = table.shape[0]
    left = lax.broadcasted_iota(jnp.int32, (entries, LANES), 1) < PROJ
    for row in range(BLOCK):
        pair = row // 2 * LANES
        both = table[:, pair : pair + LANES].astype(jnp.float32)
        keep = left if row % 2 == 0 else jnp.logical_not(left)
        spread[pl.ds(row, entries, stride=BLOCK), :] = jnp.where(keep, both, 0.0)
    plain = spread[...].astype(jnp.bfloat16)
    signed[pl.ds(entries * BLOCK, entries * BLOCK), :] = plain
    signed[pl.ds(0, entries * BLOCK), :] = -plain


def lay_blocks(ids, signs, entries, signed, matrix, first, last):
    for j in range(first, last):
        start = pl.multiple_of((signs[j] * entries + ids[j]) * BLOCK, BLOCK)
        matrix[pl.ds(j * BLOCK, BLOCK), :] = signed[pl.ds(start, BLOCK), :]


def project_kernel(transpose, fetch, ids, signs, table, rows_ref, out, spread, signed, matrix, held, total, sems, *own):
    chunks, _, chunk = held.shape
    copies = [
        pltpu.make_async_copy(rows_ref.at[:, pl.ds(c * chunk, chunk)], held.at[c], sems.at[c])
        for c in range(chunks)
    ]
    if fetch:
        small = [
            pltpu.make_async_copy(source, kept, sems.at[chunks + k])
            for k, (source, kept) in enumerate(zip((table, ids, signs), own))
        ]
        for copy in small:
            copy.start()
        table, ids, signs = own
    for copy in copies:
        copy.start()
    if fetch:
        small[0].wait()
    spread_table(table, spread, signed)
    if fetch:
        small[1].wait()
        small[2].wait()
    blocks = chunk // BLOCK
    lay = functools.partial(lay_blocks, ids, signs, table.shape[0], signed, matrix)
    lay(0, blocks)
    for c, copy in enumerate(copies):
        copy.wait()
        if c + 1 < chunks:
            lay((c + 1) * blocks, (c + 2) * blocks)
        part = jnp.dot(
            held[c], matrix[pl.ds(c * chunk, chunk), :], preferred_element_type=jnp.float32
        )
        if c == 0:
            total[...] = part
        else:
            total[...] += part
    pairs, tokens, _ = out.shape
    left = lax.broadcasted_iota(jnp.int32, (tokens, LANES), 1) < PROJ
    for pair in range(pairs):
        first = total[pl.ds(2 * pair * tokens, tokens), :]
        second = total[pl.ds((2 * pair + 1) * tokens, tokens), :]
        first = first + pltpu.roll(first, PROJ, 1)
        second = second + pltpu.roll(second, PROJ, 1)
        packed = jnp.where(left, first, second)
        out[pair] = packed.T if transpose else packed


def project(values, ids, signs, table, transpose, fetch, most, name):
    count, tokens, width = values.shape
    chunk = chunk_of(width, most)
    chunks = width // chunk
    rows = count * tokens
    entries = table.shape[0]
    smem = pl.BlockSpec(memory_space=pltpu.SMEM)
    vmem = pl.BlockSpec(memory_space=pltpu.VMEM)
    hbm = pl.BlockSpec(memory_space=pltpu.HBM)
    shape = (count // 2, LANES, tokens) if transpose else (count // 2, tokens, LANES)
    own = [
        pltpu.VMEM(table.shape, table.dtype),
        pltpu.SMEM(ids.shape, ids.dtype),
        pltpu.SMEM(signs.shape, signs.dtype),
    ]
    operands = [ids, signs, table, values.reshape(rows, width)]
    if fetch:
        operands = [pltpu.with_memory_space_constraint(each, pltpu.HBM) for each in operands]
    return pl.pallas_call(
        functools.partial(project_kernel, transpose, fetch),
        out_shape=jax.ShapeDtypeStruct(shape, jnp.float32),
        in_specs=[hbm] * 4 if fetch else [smem, smem, vmem, hbm],
        out_specs=vmem,
        scratch_shapes=[
            pltpu.VMEM((entries * BLOCK, LANES), jnp.float32),
            pltpu.VMEM((2 * entries * BLOCK, LANES), jnp.bfloat16),
            pltpu.VMEM((width, LANES), jnp.bfloat16),
            pltpu.VMEM((chunks, rows, chunk), jnp.bfloat16),
            pltpu.VMEM((rows, LANES), jnp.float32),
            pltpu.SemaphoreType.DMA((chunks + 3,)),
        ]
        + (own if fetch else []),
        compiler_params=pltpu.CompilerParams(vmem_limit_bytes=ALL_VMEM if fetch else VMEM_BYTES),
        cost_estimate=pl.CostEstimate(
            flops=2 * rows * width * LANES, bytes_accessed=2 * rows * width, transcendentals=0
        ),
        name=name,
    )(*operands)


def kron_kernel(acts, grads, *refs):
    summands, out, products = refs[:-2], refs[-2], refs[-1]
    pairs, tokens, _ = acts.shape
    for pair in range(pairs):
        act = acts[pair]
        for other in summands:
            act = act + other[pair]
        a1, a2, a3 = split3(act)
        g1, g2, g3 = split3(grads[pair])
        left = jnp.concatenate([g1, g1, g2, g1, g3, g2], axis=1)
        right = jnp.concatenate([a1, a2, a1, a3, a1, a2], axis=0)
        products[pl.ds(pair * LANES, LANES), :] = jnp.dot(left, right, preferred_element_type=jnp.float32)
    count = 2 * pairs
    lower = lax.broadcasted_iota(jnp.int32, (count, LANES), 1) < PROJ
    even = lax.broadcasted_iota(jnp.int32, (count, LANES), 0) % 2 == 0
    here = even == lower
    for tile in range(out.shape[1] // LANES):
        both = []
        for p in (2 * tile, 2 * tile + 1):
            v = products[pl.ds(p, count, stride=PROJ), :]
            both.append(jnp.where(here, v, pltpu.roll(v, PROJ, 1)))
        out[:, pl.ds(tile * LANES, LANES)] = jnp.where(lower, both[0], both[1])


def kron_of(act_parts, grads):
    pairs = grads.shape[0]
    vmem = pl.BlockSpec(memory_space=pltpu.VMEM)
    return pl.pallas_call(
        kron_kernel,
        out_shape=jax.ShapeDtypeStruct((2 * pairs, PROJ * PROJ), jnp.float32),
        in_specs=[vmem] * (1 + len(act_parts)),
        out_specs=vmem,
        scratch_shapes=[pltpu.VMEM((pairs * LANES, LANES), jnp.float32)],
        compiler_params=pltpu.CompilerParams(vmem_limit_bytes=VMEM_BYTES),
        name="kron",
    )(act_parts[0], grads, *act_parts[1:])


def place_in_plane():
    return lax.axis_index("tensor") * lax.axis_size("seq") + lax.axis_index("seq")


def pieces_kernel(here, there, mine, *parcels):
    count, width = mine.shape
    dp = len(parcels)
    start = pl.multiple_of(place_in_plane() * width, LANES)
    row = here[:, pl.ds(start, width)] + there[:, pl.ds(start, width)]
    mine[...] = row
    for k, parcel in enumerate(parcels):
        parcel[pl.ds(0, count), :] = row
        other = lax.rem(lax.axis_index("dp") + k, dp)
        start = pl.multiple_of(other * width, LANES)
        parcel[pl.ds(count, count), :] = here[:, pl.ds(start, width)] + there[:, pl.ds(start, width)]


def pieces_of(here, there, dp):
    count, width = here.shape
    vmem = pl.BlockSpec(memory_space=pltpu.VMEM)
    shapes = [(count, width // dp)] + [(2 * count, width // dp)] * dp
    return pl.pallas_call(
        pieces_kernel,
        out_shape=[jax.ShapeDtypeStruct(shape, jnp.float32) for shape in shapes],
        in_specs=[vmem] * 2,
        out_specs=[vmem] * len(shapes),
        compiler_params=pltpu.CompilerParams(vmem_limit_bytes=VMEM_BYTES),
        name="pieces",
    )(here, there)


def fisher_kernel(scale, *refs):
    parcels, (out, left_parts, right_parts) = refs[:-3], refs[-3:]
    rows = parcels[0].shape[0] // 2

    @pl.when(pl.program_id(0) == 0)
    def _():
        left = jnp.concatenate([parcel[pl.ds(0, rows), :] for parcel in parcels], axis=0)
        right = jnp.concatenate([parcel[pl.ds(rows, rows), :] for parcel in parcels], axis=0)
        l1, l2, l3 = split3(left)
        r1, r2, r3 = split3(right * scale)
        left_parts[...] = jnp.concatenate([l1, l1, l2, l1, l3, l2], axis=0)
        right_parts[...] = jnp.concatenate([r1, r2, r1, r3, r1, r2], axis=0)

    height = out.shape[0]
    start = pl.multiple_of(pl.program_id(0) * height, LANES)
    out[...] = lax.dot_general(
        left_parts[:, pl.ds(start, height)],
        right_parts[...],
        (((0,), (0,)), ((), ())),
        preferred_element_type=jnp.float32,
    )


def fisher_block(parcels):
    rows, width = parcels[0].shape
    total = rows // 2 * len(parcels)
    block = LANES
    whole = pl.BlockSpec((rows, width), lambda i: (0, 0))
    return pl.pallas_call(
        functools.partial(fisher_kernel, 1.0 / total),
        grid=(width // block,),
        out_shape=jax.ShapeDtypeStruct((width, width), jnp.float32),
        in_specs=[whole] * len(parcels),
        out_specs=pl.BlockSpec((block, width), lambda i: (i, 0)),
        scratch_shapes=[pltpu.VMEM((6 * total, width), jnp.bfloat16)] * 2,
        compiler_params=pltpu.CompilerParams(vmem_limit_bytes=VMEM_BYTES),
        name="fisher",
    )(*parcels)


def local(acts, grads, in_ids, in_signs, out_ids, out_signs, in_table, out_table):
    tensor, seq, dp = (lax.axis_size(name) for name in ("tensor", "seq", "dp"))
    shards = tensor * seq

    act = project(acts, in_ids, in_signs, in_table, False, True, 512, "project_acts")
    if tensor == 2:
        act_parts = [act, lax.ppermute(act, "tensor", [(0, 1), (1, 0)])]
    else:
        act_parts = [lax.psum(act, "tensor")]
    grad = project(grads, out_ids, out_signs, out_table, True, False, 1024, "project_grads")
    kron = kron_of(act_parts, grad)

    if tensor != 2 or seq != 2 or shards != dp:
        kron = lax.psum(kron, PLANE)
        width = kron.shape[1] // shards
        place = place_in_plane()
        mine = lax.dynamic_slice_in_dim(kron, place * width, width, 1)
        every = lax.all_gather(kron, "dp", axis=0, tiled=True)
        left = lax.dynamic_slice_in_dim(every, place * width, width, 1)
        columns = kron.shape[1] // dp
        right = lax.dynamic_slice_in_dim(every, lax.axis_index("dp") * columns, columns, 1)
        fisher = lax.dot_general(
            left, right, (((0,), (0,)), ((), ())), precision=lax.Precision.HIGHEST
        ) / left.shape[0]
        return mine, fisher

    swap = [(0, 1), (1, 0)]
    kron = kron + lax.ppermute(kron, "seq", swap)
    mine, *parcels = pieces_of(kron, lax.ppermute(kron, "tensor", swap), dp)
    for k in range(1, dp):
        parcels[k] = lax.ppermute(parcels[k], "dp", [(d, (d + k) % dp) for d in range(dp)])
    return mine, fisher_block(parcels)


def solution(mesh):
    in_specs = (
        P(("groups", "dp"), "seq", "tensor"),
        P(("groups", "dp"), "seq", "tensor"),
        P("tensor"),
        P("tensor"),
        P("tensor"),
        P("tensor"),
        P(),
        P(),
    )
    out_specs = (P(("groups", "dp"), ("tensor", "seq")), P(("groups", "tensor", "seq"), "dp"))
    return jax.shard_map(local, mesh=mesh, in_specs=in_specs, out_specs=out_specs, check_vma=False)
```

```python
import functools

import jax
import jax.numpy as jnp
from jax import lax
from jax.experimental import pallas as pl
from jax.experimental.pallas import tpu as pltpu
from jax.sharding import PartitionSpec as P

PROJ = 64
BLOCK = 64
LANES = 128
VMEM_BYTES = 48 * 1024 * 1024
ALL_VMEM = 48 * 1024 * 1024
PLANE = ("tensor", "seq")


def chunk_of(width, most):
    chunk = most
    while width % chunk:
        chunk -= LANES
    return chunk


def split3(x):
    high = x.astype(jnp.bfloat16)
    rest = x - high.astype(jnp.float32)
    mid = rest.astype(jnp.bfloat16)
    low = (rest - mid.astype(jnp.float32)).astype(jnp.bfloat16)
    return high, mid, low


def spread_table(table, spread, signed):
    entries = table.shape[0]
    left = lax.broadcasted_iota(jnp.int32, (entries, LANES), 1) < PROJ
    for row in range(BLOCK):
        pair = row // 2 * LANES
        both = table[:, pair : pair + LANES].astype(jnp.float32)
        keep = left if row % 2 == 0 else jnp.logical_not(left)
        spread[pl.ds(row, entries, stride=BLOCK), :] = jnp.where(keep, both, 0.0)
    plain = spread[...].astype(jnp.bfloat16)
    signed[pl.ds(entries * BLOCK, entries * BLOCK), :] = plain
    signed[pl.ds(0, entries * BLOCK), :] = -plain


def lay_blocks(ids, signs, entries, signed, matrix, first, last):
    for j in range(first, last):
        start = pl.multiple_of((signs[j] * entries + ids[j]) * BLOCK, BLOCK)
        matrix[pl.ds(j * BLOCK, BLOCK), :] = signed[pl.ds(start, BLOCK), :]


def project_kernel(fetch, ids, signs, table, rows_ref, out, spread, signed, matrix, held, total, sems, *own):
    chunks, _, chunk = held.shape
    copies = [
        pltpu.make_async_copy(rows_ref.at[:, pl.ds(c * chunk, chunk)], held.at[c], sems.at[c])
        for c in range(chunks)
    ]
    if fetch:
        small = [
            pltpu.make_async_copy(source, kept, sems.at[chunks + k])
            for k, (source, kept) in enumerate(zip((table, ids, signs), own))
        ]
        for copy in small:
            copy.start()
        table, ids, signs = own
    for copy in copies:
        copy.start()
    if fetch:
        small[0].wait()
    spread_table(table, spread, signed)
    if fetch:
        small[1].wait()
        small[2].wait()
    blocks = chunk // BLOCK
    lay = functools.partial(lay_blocks, ids, signs, table.shape[0], signed, matrix)
    lay(0, blocks)
    for c, copy in enumerate(copies):
        copy.wait()
        if c + 1 < chunks:
            lay((c + 1) * blocks, (c + 2) * blocks)
        part = lax.dot_general(
            matrix[pl.ds(c * chunk, chunk), :],
            held[c],
            (((0,), (1,)), ((), ())),
            preferred_element_type=jnp.float32,
        )
        if c == 0:
            total[...] = part
        else:
            total[...] += part
    pairs, _, tokens = out.shape
    for pair in range(pairs):
        for half in range(2):
            lanes = pl.ds((2 * pair + half) * tokens, tokens)
            out[pair, pl.ds(half * PROJ, PROJ), :] = total[pl.ds(0, PROJ), lanes] + total[pl.ds(PROJ, PROJ), lanes]


def project(values, ids, signs, table, fetch, most, name):
    count, tokens, width = values.shape
    chunk = chunk_of(width, most)
    chunks = width // chunk
    rows = count * tokens
    entries = table.shape[0]
    smem = pl.BlockSpec(memory_space=pltpu.SMEM)
    vmem = pl.BlockSpec(memory_space=pltpu.VMEM)
    hbm = pl.BlockSpec(memory_space=pltpu.HBM)
    shape = (count // 2, LANES, tokens)
    own = [
        pltpu.VMEM(table.shape, table.dtype),
        pltpu.SMEM(ids.shape, ids.dtype),
        pltpu.SMEM(signs.shape, signs.dtype),
    ]
    operands = [ids, signs, table, values.reshape(rows, width)]
    if fetch:
        operands = [pltpu.with_memory_space_constraint(each, pltpu.HBM) for each in operands]
    return pl.pallas_call(
        functools.partial(project_kernel, fetch),
        out_shape=jax.ShapeDtypeStruct(shape, jnp.float32),
        in_specs=[hbm] * 4 if fetch else [smem, smem, vmem, hbm],
        out_specs=vmem,
        scratch_shapes=[
            pltpu.VMEM((entries * BLOCK, LANES), jnp.float32),
            pltpu.VMEM((2 * entries * BLOCK, LANES), jnp.bfloat16),
            pltpu.VMEM((width, LANES), jnp.bfloat16),
            pltpu.VMEM((chunks, rows, chunk), jnp.bfloat16),
            pltpu.VMEM((LANES, rows), jnp.float32),
            pltpu.SemaphoreType.DMA((chunks + 3,)),
        ]
        + (own if fetch else []),
        compiler_params=pltpu.CompilerParams(vmem_limit_bytes=ALL_VMEM if fetch else VMEM_BYTES),
        cost_estimate=pl.CostEstimate(
            flops=2 * rows * width * LANES, bytes_accessed=2 * rows * width, transcendentals=0
        ),
        name=name,
    )(*operands)


def kron_kernel(acts, grads, *refs):
    summands, out, products = refs[:-2], refs[-2], refs[-1]
    pairs = acts.shape[0]
    for pair in range(pairs):
        act = acts[pair]
        for other in summands:
            act = act + other[pair]
        a1, a2, a3 = split3(act)
        g1, g2, g3 = split3(grads[pair])
        left = jnp.concatenate([g1, g1, g2, g1, g3, g2], axis=1)
        right = jnp.concatenate([a1, a2, a1, a3, a1, a2], axis=1)
        products[pl.ds(pair * LANES, LANES), :] = lax.dot_general(
            left, right, (((1,), (1,)), ((), ())), preferred_element_type=jnp.float32
        )
    count = 2 * pairs
    lower = lax.broadcasted_iota(jnp.int32, (count, LANES), 1) < PROJ
    even = lax.broadcasted_iota(jnp.int32, (count, LANES), 0) % 2 == 0
    here = even == lower
    for tile in range(out.shape[1] // LANES):
        both = []
        for p in (2 * tile, 2 * tile + 1):
            v = products[pl.ds(p, count, stride=PROJ), :]
            both.append(jnp.where(here, v, pltpu.roll(v, PROJ, 1)))
        out[:, pl.ds(tile * LANES, LANES)] = jnp.where(lower, both[0], both[1])


def kron_of(act_parts, grads):
    pairs = grads.shape[0]
    vmem = pl.BlockSpec(memory_space=pltpu.VMEM)
    return pl.pallas_call(
        kron_kernel,
        out_shape=jax.ShapeDtypeStruct((2 * pairs, PROJ * PROJ), jnp.float32),
        in_specs=[vmem] * (1 + len(act_parts)),
        out_specs=vmem,
        scratch_shapes=[pltpu.VMEM((pairs * LANES, LANES), jnp.float32)],
        compiler_params=pltpu.CompilerParams(vmem_limit_bytes=VMEM_BYTES),
        name="kron",
    )(act_parts[0], grads, *act_parts[1:])


def place_in_plane():
    return lax.axis_index("tensor") * lax.axis_size("seq") + lax.axis_index("seq")


def pieces_kernel(here, there, mine, *parcels):
    count, width = mine.shape
    dp = len(parcels)
    start = pl.multiple_of(place_in_plane() * width, LANES)
    row = here[:, pl.ds(start, width)] + there[:, pl.ds(start, width)]
    mine[...] = row
    for k, parcel in enumerate(parcels):
        parcel[pl.ds(0, count), :] = row
        other = lax.rem(lax.axis_index("dp") + k, dp)
        start = pl.multiple_of(other * width, LANES)
        parcel[pl.ds(count, count), :] = here[:, pl.ds(start, width)] + there[:, pl.ds(start, width)]


def pieces_of(here, there, dp):
    count, width = here.shape
    vmem = pl.BlockSpec(memory_space=pltpu.VMEM)
    shapes = [(count, width // dp)] + [(2 * count, width // dp)] * dp
    return pl.pallas_call(
        pieces_kernel,
        out_shape=[jax.ShapeDtypeStruct(shape, jnp.float32) for shape in shapes],
        in_specs=[vmem] * 2,
        out_specs=[vmem] * len(shapes),
        compiler_params=pltpu.CompilerParams(vmem_limit_bytes=VMEM_BYTES),
        name="pieces",
    )(here, there)


def fisher_kernel(scale, *refs):
    parcels, (out, made, sems) = refs[:-3], refs[-3:]
    rows = parcels[0].shape[0] // 2
    left = jnp.concatenate([parcel[pl.ds(0, rows), :] for parcel in parcels], axis=0)
    right = jnp.concatenate([parcel[pl.ds(rows, rows), :] for parcel in parcels], axis=0)
    l1, l2, l3 = split3(left)
    r1, r2, r3 = split3(right * scale)
    left_parts = jnp.concatenate([l1, l1, l2, l1, l3, l2, l2, l3], axis=0).T
    right_parts = jnp.concatenate([r1, r2, r1, r3, r1, r2, r3, r2], axis=0)
    blocks, _, width = made.shape
    copies = []
    for block in range(blocks):
        columns = slice(block * width, (block + 1) * width)
        made[block] = jnp.dot(left_parts, right_parts[:, columns], preferred_element_type=jnp.float32)
        copies.append(
            pltpu.make_async_copy(made.at[block], out.at[:, pl.ds(block * width, width)], sems.at[block])
        )
        copies[-1].start()
    for copy in copies:
        copy.wait()


def fisher_block(parcels):
    rows, width = parcels[0].shape
    total = rows // 2 * len(parcels)
    blocks = 4
    return pl.pallas_call(
        functools.partial(fisher_kernel, 1.0 / total),
        out_shape=jax.ShapeDtypeStruct((width, width), jnp.float32),
        in_specs=[pl.BlockSpec(memory_space=pltpu.VMEM)] * len(parcels),
        out_specs=pl.BlockSpec(memory_space=pltpu.HBM),
        scratch_shapes=[
            pltpu.VMEM((blocks, width, width // blocks), jnp.float32),
            pltpu.SemaphoreType.DMA((blocks,)),
        ],
        compiler_params=pltpu.CompilerParams(vmem_limit_bytes=VMEM_BYTES),
        name="fisher",
    )(*parcels)


def local(acts, grads, in_ids, in_signs, out_ids, out_signs, in_table, out_table):
    tensor, seq, dp = (lax.axis_size(name) for name in ("tensor", "seq", "dp"))
    shards = tensor * seq

    act = project(acts, in_ids, in_signs, in_table, True, 512, "project_acts")
    if tensor == 2:
        act_parts = [act, lax.ppermute(act, "tensor", [(0, 1), (1, 0)])]
    else:
        act_parts = [lax.psum(act, "tensor")]
    grad = project(grads, out_ids, out_signs, out_table, False, 1024, "project_grads")
    kron = kron_of(act_parts, grad)

    if tensor != 2 or seq != 2 or shards != dp:
        kron = lax.psum(kron, PLANE)
        width = kron.shape[1] // shards
        place = place_in_plane()
        mine = lax.dynamic_slice_in_dim(kron, place * width, width, 1)
        every = lax.all_gather(kron, "dp", axis=0, tiled=True)
        left = lax.dynamic_slice_in_dim(every, place * width, width, 1)
        columns = kron.shape[1] // dp
        right = lax.dynamic_slice_in_dim(every, lax.axis_index("dp") * columns, columns, 1)
        fisher = lax.dot_general(
            left, right, (((0,), (0,)), ((), ())), precision=lax.Precision.HIGHEST
        ) / left.shape[0]
        return mine, fisher

    swap = [(0, 1), (1, 0)]
    kron = kron + lax.ppermute(kron, "seq", swap)
    mine, *parcels = pieces_of(kron, lax.ppermute(kron, "tensor", swap), dp)
    for k in range(1, dp):
        parcels[k] = lax.ppermute(parcels[k], "dp", [(d, (d + k) % dp) for d in range(dp)])
    return mine, fisher_block(parcels)


def solution(mesh):
    in_specs = (
        P(("groups", "dp"), "seq", "tensor"),
        P(("groups", "dp"), "seq", "tensor"),
        P("tensor"),
        P("tensor"),
        P("tensor"),
        P("tensor"),
        P(),
        P(),
    )
    out_specs = (P(("groups", "dp"), ("tensor", "seq")), P(("groups", "tensor", "seq"), "dp"))
    return jax.shard_map(local, mesh=mesh, in_specs=in_specs, out_specs=out_specs, check_vma=False)
```

```python
import functools

import jax
import jax.numpy as jnp
from jax import lax
from jax.experimental import pallas as pl
from jax.experimental.pallas import tpu as pltpu
from jax.sharding import PartitionSpec as P

PROJ = 64
BLOCK = 64
LANES = 128
VMEM_BYTES = 48 * 1024 * 1024
PLANE = ("tensor", "seq")


HALVES = 2


def chunks_of(width, most):
    if width >= 4 * most:
        inner = width - most
        ends = [most // 2] * 2
    else:
        inner, ends = width, []
    chunk = most
    while inner % chunk:
        chunk -= LANES
    return ends[:1] + [chunk] * (inner // chunk) + ends[1:]


def split3(x):
    high = x.astype(jnp.bfloat16)
    rest = x - high.astype(jnp.float32)
    mid = rest.astype(jnp.bfloat16)
    low = (rest - mid.astype(jnp.float32)).astype(jnp.bfloat16)
    return high, mid, low


def spread_table(table, spread, signed):
    entries = table.shape[0]
    stride = spread.shape[0] // entries
    for row in range(0, BLOCK, 2):
        both = table[:, row * PROJ : row * PROJ + LANES].astype(jnp.float32)
        spread[pl.ds(row, entries, stride=stride), :] = both
        spread[pl.ds(row + 1, entries, stride=stride), :] = pltpu.roll(both, PROJ, 1)
    for entry in range(entries):
        block = spread[pl.ds(entry * stride, BLOCK), :].astype(jnp.bfloat16)
        signed[pl.ds((entries + entry) * BLOCK, BLOCK), :] = block
        signed[pl.ds(entry * BLOCK, BLOCK), :] = -block


def lay_blocks(ids, signs, entries, signed, matrix, first, last):
    for j in range(first, last):
        start = pl.multiple_of((signs[j] * entries + ids[j]) * BLOCK, BLOCK)
        matrix[pl.ds(j * BLOCK, BLOCK), :] = signed[pl.ds(start, BLOCK), :]


def project_kernel(widths, fetch, ids, signs, table, rows_ref, *refs):
    outs, (spread, signed, matrix, held, total, sems, *own) = refs[:HALVES], refs[HALVES:]
    copies, starts, start = [], [], 0
    for c, width in enumerate(widths):
        columns = pl.ds(start, width)
        copies.append(pltpu.make_async_copy(rows_ref.at[:, columns], held.at[:, columns], sems.at[c]))
        starts.append(start)
        start += width
    if fetch:
        small = [
            pltpu.make_async_copy(source, kept, sems.at[len(widths) + k])
            for k, (source, kept) in enumerate(zip((table, ids, signs), own))
        ]
        for copy in small:
            copy.start()
        table, ids, signs = own
    for copy in copies:
        copy.start()
    if fetch:
        small[0].wait()
    spread_table(table, spread, signed)
    if fetch:
        small[1].wait()
        small[2].wait()
    lay = functools.partial(lay_blocks, ids, signs, table.shape[0], signed, matrix)
    lay(0, widths[0] // BLOCK)
    for c, copy in enumerate(copies):
        columns = pl.ds(starts[c], widths[c])
        copy.wait()
        if c + 1 < len(widths):
            lay(starts[c + 1] // BLOCK, (starts[c + 1] + widths[c + 1]) // BLOCK)
        part = lax.dot_general(
            matrix[columns, :PROJ],
            held[:, columns],
            (((0,), (1,)), ((), ())),
            preferred_element_type=jnp.float32,
        )
        if c == 0:
            total[...] = part
        else:
            total[...] += part
    pairs, _, tokens = outs[0].shape
    for h, out in enumerate(outs):
        for pair in range(pairs):
            for side in range(2):
                example = 2 * (h * pairs + pair) + side
                out[pair, pl.ds(side * PROJ, PROJ), :] = total[:, pl.ds(example * tokens, tokens)]


def project(values, ids, signs, table, fetch, most, name):
    count, tokens, width = values.shape
    widths = chunks_of(width, most)
    rows = count * tokens
    entries = table.shape[0]
    smem = pl.BlockSpec(memory_space=pltpu.SMEM)
    vmem = pl.BlockSpec(memory_space=pltpu.VMEM)
    hbm = pl.BlockSpec(memory_space=pltpu.HBM)
    own = [
        pltpu.VMEM(table.shape, table.dtype),
        pltpu.SMEM(ids.shape, ids.dtype),
        pltpu.SMEM(signs.shape, signs.dtype),
    ]
    operands = [ids, signs, table, values.reshape(rows, width)]
    if fetch:
        operands = [pltpu.with_memory_space_constraint(each, pltpu.HBM) for each in operands]
    return pl.pallas_call(
        functools.partial(project_kernel, widths, fetch),
        out_shape=[jax.ShapeDtypeStruct((count // 2 // HALVES, LANES, tokens), jnp.float32)] * HALVES,
        in_specs=[hbm] * 4 if fetch else [smem, smem, vmem, hbm],
        out_specs=[vmem] * HALVES,
        scratch_shapes=[
            pltpu.VMEM((entries * (BLOCK + 8), LANES), jnp.float32),
            pltpu.VMEM((2 * entries * BLOCK, LANES), jnp.bfloat16),
            pltpu.VMEM((width, LANES), jnp.bfloat16),
            pltpu.VMEM((rows, width), jnp.bfloat16),
            pltpu.VMEM((PROJ, rows), jnp.float32),
            pltpu.SemaphoreType.DMA((len(widths) + 3,)),
        ]
        + (own if fetch else []),
        compiler_params=pltpu.CompilerParams(vmem_limit_bytes=VMEM_BYTES),
        cost_estimate=pl.CostEstimate(
            flops=2 * rows * width * LANES, bytes_accessed=2 * rows * width, transcendentals=0
        ),
        name=name,
    )(*operands)


def kron_kernel(acts, grads, *refs):
    summands, out, products = refs[:-2], refs[-2], refs[-1]
    pairs = acts.shape[0]
    for pair in range(pairs):
        act = acts[pair]
        for other in summands:
            act = act + other[pair]
        a1, a2, a3 = split3(act)
        g1, g2, g3 = split3(grads[pair])
        left = jnp.concatenate([g1, g1, g2, g1, g3, g2], axis=1)
        right = jnp.concatenate([a1, a2, a1, a3, a1, a2], axis=1)
        products[pl.ds(pair * LANES, LANES), :] = lax.dot_general(
            left, right, (((1,), (1,)), ((), ())), preferred_element_type=jnp.float32
        )
    count = 2 * pairs
    lower = lax.broadcasted_iota(jnp.int32, (count, LANES), 1) < PROJ
    even = lax.broadcasted_iota(jnp.int32, (count, LANES), 0) % 2 == 0
    here = even == lower
    for tile in range(out.shape[1] // LANES):
        both = []
        for p in (2 * tile, 2 * tile + 1):
            v = products[pl.ds(p, count, stride=PROJ), :]
            both.append(jnp.where(here, v, pltpu.roll(v, PROJ, 1)))
        out[:, pl.ds(tile * LANES, LANES)] = jnp.where(lower, both[0], both[1])


def kron_of(act_parts, grads):
    pairs = grads.shape[0]
    vmem = pl.BlockSpec(memory_space=pltpu.VMEM)
    return pl.pallas_call(
        kron_kernel,
        out_shape=jax.ShapeDtypeStruct((2 * pairs, PROJ * PROJ), jnp.float32),
        in_specs=[vmem] * (1 + len(act_parts)),
        out_specs=vmem,
        scratch_shapes=[pltpu.VMEM((pairs * LANES, LANES), jnp.float32)],
        compiler_params=pltpu.CompilerParams(vmem_limit_bytes=VMEM_BYTES),
        name="kron",
    )(act_parts[0], grads, *act_parts[1:])


def place_in_plane():
    return lax.axis_index("tensor") * lax.axis_size("seq") + lax.axis_index("seq")


def pieces_kernel(here, there, *parcels):
    count = here.shape[0]
    dp = len(parcels)
    width = parcels[0].shape[1]
    start = pl.multiple_of(place_in_plane() * width, LANES)
    row = here[:, pl.ds(start, width)] + there[:, pl.ds(start, width)]
    for k, parcel in enumerate(parcels):
        parcel[pl.ds(0, count), :] = row
        other = lax.rem(lax.axis_index("dp") + k, dp)
        start = pl.multiple_of(other * width, LANES)
        parcel[pl.ds(count, count), :] = here[:, pl.ds(start, width)] + there[:, pl.ds(start, width)]


def pieces_of(here, there, dp):
    count, width = here.shape
    vmem = pl.BlockSpec(memory_space=pltpu.VMEM)
    return pl.pallas_call(
        pieces_kernel,
        out_shape=[jax.ShapeDtypeStruct((2 * count, width // dp), jnp.float32)] * dp,
        in_specs=[vmem] * 2,
        out_specs=[vmem] * dp,
        compiler_params=pltpu.CompilerParams(vmem_limit_bytes=VMEM_BYTES),
        name="pieces",
    )(here, there)


def fisher_kernel(scale, *refs):
    parcels, (mine, out, made, kept, left, right, sems) = refs[:-7], refs[-7:]
    rows = parcels[0].shape[0] // 2
    for k, parcel in enumerate(parcels):
        left[pl.ds(k * rows, rows), :] = parcel[pl.ds(0, rows), :]
        right[pl.ds(k * rows, rows), :] = parcel[pl.ds(rows, rows), :]
    blocks, _, width = made.shape
    kept[...] = left[pl.ds(0, kept.shape[0]), :]
    copies = [pltpu.make_async_copy(kept, mine, sems.at[blocks])]
    copies[0].start()
    l1, l2, l3 = split3(left[...])
    r1, r2, r3 = split3(right[...] * scale)
    left_parts = jnp.concatenate([l1, l1, l2, l1, l3, l2, l2, l3], axis=0).T
    right_parts = jnp.concatenate([r1, r2, r1, r3, r1, r2, r3, r2], axis=0)
    for block in range(blocks):
        columns = slice(block * width, (block + 1) * width)
        made[block] = jnp.dot(left_parts, right_parts[:, columns], preferred_element_type=jnp.float32)
        copies.append(
            pltpu.make_async_copy(made.at[block], out.at[:, pl.ds(block * width, width)], sems.at[block])
        )
        copies[-1].start()
    for copy in copies:
        copy.wait()


def fisher_block(parcels):
    rows, width = parcels[0].shape
    rows //= 2
    total = rows * len(parcels)
    blocks = 4
    hbm = pl.BlockSpec(memory_space=pltpu.HBM)
    return pl.pallas_call(
        functools.partial(fisher_kernel, 1.0 / total),
        out_shape=[
            jax.ShapeDtypeStruct((rows * HALVES, width), jnp.float32),
            jax.ShapeDtypeStruct((width, width), jnp.float32),
        ],
        in_specs=[pl.BlockSpec(memory_space=pltpu.VMEM)] * len(parcels),
        out_specs=[hbm] * 2,
        scratch_shapes=[
            pltpu.VMEM((blocks, width, width // blocks), jnp.float32),
            pltpu.VMEM((rows * HALVES, width), jnp.float32),
            pltpu.VMEM((total, width), jnp.float32),
            pltpu.VMEM((total, width), jnp.float32),
            pltpu.SemaphoreType.DMA((blocks + 1,)),
        ],
        compiler_params=pltpu.CompilerParams(vmem_limit_bytes=VMEM_BYTES),
        name="fisher",
    )(*parcels)


def local(acts, grads, in_ids, in_signs, out_ids, out_signs, in_table, out_table):
    tensor, seq, dp = (lax.axis_size(name) for name in ("tensor", "seq", "dp"))
    shards = tensor * seq
    swap = [(0, 1), (1, 0)]

    act_halves = project(acts, in_ids, in_signs, in_table, True, 512, "project_acts")
    if tensor == 2:
        act_halves = [[act, lax.ppermute(act, "tensor", swap)] for act in act_halves]
    else:
        act_halves = [[lax.psum(act, "tensor")] for act in act_halves]
    grad_halves = project(grads, out_ids, out_signs, out_table, False, 1024, "project_grads")
    krons = [kron_of(parts, grad) for parts, grad in zip(act_halves, grad_halves)]

    if tensor != 2 or seq != 2 or shards != dp:
        kron = lax.psum(jnp.concatenate(krons, axis=0), PLANE)
        width = kron.shape[1] // shards
        place = place_in_plane()
        mine = lax.dynamic_slice_in_dim(kron, place * width, width, 1)
        every = lax.all_gather(kron, "dp", axis=0, tiled=True)
        left = lax.dynamic_slice_in_dim(every, place * width, width, 1)
        columns = kron.shape[1] // dp
        right = lax.dynamic_slice_in_dim(every, lax.axis_index("dp") * columns, columns, 1)
        fisher = lax.dot_general(
            left, right, (((0,), (0,)), ((), ())), precision=lax.Precision.HIGHEST
        ) / left.shape[0]
        return mine, fisher

    krons = [kron + lax.ppermute(kron, "seq", swap) for kron in krons]
    there = [lax.ppermute(kron, "tensor", swap) for kron in krons]
    halves = [pieces_of(kron, other, dp) for kron, other in zip(krons, there)]
    parcels = [parcel[0] for parcel in halves]
    for k in range(1, dp):
        for parcel in halves:
            parcels.append(lax.ppermute(parcel[k], "dp", [(d, (d + k) % dp) for d in range(dp)]))
    mine, fisher = fisher_block(parcels)
    return mine, fisher


def solution(mesh):
    in_specs = (
        P(("groups", "dp"), "seq", "tensor"),
        P(("groups", "dp"), "seq", "tensor"),
        P("tensor"),
        P("tensor"),
        P("tensor"),
        P("tensor"),
        P(),
        P(),
    )
    out_specs = (P(("groups", "dp"), ("tensor", "seq")), P(("groups", "tensor", "seq"), "dp"))
    return jax.shard_map(local, mesh=mesh, in_specs=in_specs, out_specs=out_specs, check_vma=False)
```

```python
import functools

import jax
import jax.numpy as jnp
from jax import lax
from jax.experimental import pallas as pl
from jax.experimental.pallas import tpu as pltpu
from jax.sharding import PartitionSpec as P

PROJ = 64
BLOCK = 64
LANES = 128
VMEM_BYTES = 48 * 1024 * 1024


def chunks_of(width, most):
    if width >= 4 * most:
        inner = width - most
        ends = [most // 2] * 2
    else:
        inner, ends = width, []
    chunk = most
    while inner % chunk:
        chunk -= LANES
    return ends[:1] + [chunk] * (inner // chunk) + ends[1:]


def split3(x):
    high = x.astype(jnp.bfloat16)
    rest = x - high.astype(jnp.float32)
    mid = rest.astype(jnp.bfloat16)
    low = (rest - mid.astype(jnp.float32)).astype(jnp.bfloat16)
    return high, mid, low


def spread_table(table, spread, signed):
    entries = table.shape[0]
    stride = spread.shape[0] // entries
    for row in range(0, BLOCK, 2):
        both = table[:, row * PROJ : row * PROJ + LANES].astype(jnp.float32)
        spread[pl.ds(row, entries, stride=stride), :] = both
        spread[pl.ds(row + 1, entries, stride=stride), :] = pltpu.roll(both, PROJ, 1)
    for entry in range(entries):
        block = spread[pl.ds(entry * stride, BLOCK), :].astype(jnp.bfloat16)
        signed[pl.ds((entries + entry) * BLOCK, BLOCK), :] = block
        signed[pl.ds(entry * BLOCK, BLOCK), :] = -block


def lay_blocks(ids, signs, entries, signed, matrix, first, last):
    for j in range(first, last):
        start = pl.multiple_of((signs[j] * entries + ids[j]) * BLOCK, BLOCK)
        matrix[pl.ds(j * BLOCK, BLOCK), :] = signed[pl.ds(start, BLOCK), :]


def project_kernel(widths, fetch, ids, signs, table, rows_ref, *refs):
    out, spread, signed, matrix, held, total, sems, *own = refs
    copies, starts, start = [], [], 0
    for c, width in enumerate(widths):
        columns = pl.ds(start, width)
        copies.append(pltpu.make_async_copy(rows_ref.at[:, columns], held.at[:, columns], sems.at[c]))
        starts.append(start)
        start += width
    if fetch:
        small = [
            pltpu.make_async_copy(source, kept, sems.at[len(widths) + k])
            for k, (source, kept) in enumerate(zip((table, ids, signs), own))
        ]
        for copy in small:
            copy.start()
        table, ids, signs = own
    for copy in copies:
        copy.start()
    if fetch:
        small[0].wait()
    spread_table(table, spread, signed)
    if fetch:
        small[1].wait()
        small[2].wait()
    lay = functools.partial(lay_blocks, ids, signs, table.shape[0], signed, matrix)
    lay(0, widths[0] // BLOCK)
    for c, copy in enumerate(copies):
        columns = pl.ds(starts[c], widths[c])
        copy.wait()
        if c + 1 < len(widths):
            lay(starts[c + 1] // BLOCK, (starts[c + 1] + widths[c + 1]) // BLOCK)
        part = lax.dot_general(
            matrix[columns, :PROJ],
            held[:, columns],
            (((0,), (1,)), ((), ())),
            preferred_element_type=jnp.float32,
        )
        if c == 0:
            total[...] = part
        else:
            total[...] += part
    pairs, _, tokens = out.shape
    for pair in range(pairs):
        for side in range(2):
            out[pair, pl.ds(side * PROJ, PROJ), :] = total[:, pl.ds((2 * pair + side) * tokens, tokens)]


def project(values, ids, signs, table, fetch, most, name):
    count, tokens, width = values.shape
    widths = chunks_of(width, most)
    rows = count * tokens
    entries = table.shape[0]
    smem = pl.BlockSpec(memory_space=pltpu.SMEM)
    vmem = pl.BlockSpec(memory_space=pltpu.VMEM)
    hbm = pl.BlockSpec(memory_space=pltpu.HBM)
    own = [
        pltpu.VMEM(table.shape, table.dtype),
        pltpu.SMEM(ids.shape, ids.dtype),
        pltpu.SMEM(signs.shape, signs.dtype),
    ]
    operands = [ids, signs, table, values.reshape(rows, width)]
    if fetch:
        operands = [pltpu.with_memory_space_constraint(each, pltpu.HBM) for each in operands]
    return pl.pallas_call(
        functools.partial(project_kernel, widths, fetch),
        out_shape=jax.ShapeDtypeStruct((count // 2, LANES, tokens), jnp.float32),
        in_specs=[hbm] * 4 if fetch else [smem, smem, vmem, hbm],
        out_specs=vmem,
        scratch_shapes=[
            pltpu.VMEM((entries * (BLOCK + 8), LANES), jnp.float32),
            pltpu.VMEM((2 * entries * BLOCK, LANES), jnp.bfloat16),
            pltpu.VMEM((width, LANES), jnp.bfloat16),
            pltpu.VMEM((rows, width), jnp.bfloat16),
            pltpu.VMEM((PROJ, rows), jnp.float32),
            pltpu.SemaphoreType.DMA((len(widths) + 3,)),
        ]
        + (own if fetch else []),
        compiler_params=pltpu.CompilerParams(vmem_limit_bytes=VMEM_BYTES),
        cost_estimate=pl.CostEstimate(
            flops=2 * rows * width * LANES, bytes_accessed=2 * rows * width, transcendentals=0
        ),
        name=name,
    )(*operands)


def kron_kernel(cuts, acts, grads, *refs):
    parts = cuts[1]
    summands, outs, rows, products = refs[: -parts - 2], refs[-parts - 2 : -2], refs[-2], refs[-1]
    pairs = acts.shape[0]
    for pair in range(pairs):
        act = acts[pair]
        for other in summands:
            act = act + other[pair]
        a1, a2, a3 = split3(act)
        g1, g2, g3 = split3(grads[pair])
        left = jnp.concatenate([g1, g1, g2, g1, g3, g2], axis=1)
        right = jnp.concatenate([a1, a2, a1, a3, a1, a2], axis=1)
        products[pl.ds(pair * LANES, LANES), :] = lax.dot_general(
            left, right, (((1,), (1,)), ((), ())), preferred_element_type=jnp.float32
        )
    count = 2 * pairs
    lower = lax.broadcasted_iota(jnp.int32, (count, LANES), 1) < PROJ
    even = lax.broadcasted_iota(jnp.int32, (count, LANES), 0) % 2 == 0
    here = even == lower
    tiles = rows.shape[2] // LANES // cuts[0]
    for tile in range(PROJ * PROJ // LANES):
        both = []
        for p in (2 * tile, 2 * tile + 1):
            v = products[pl.ds(p, count, stride=PROJ), :]
            both.append(jnp.where(here, v, pltpu.roll(v, PROJ, 1)))
        block, part, within = tile // tiles // parts, tile // tiles % parts, tile % tiles
        rows[part, :, pl.ds((block * tiles + within) * LANES, LANES)] = jnp.where(lower, both[0], both[1])
    for k, out in enumerate(outs):
        part = lax.rem(lax.axis_index("seq") + k, parts) if parts > 1 else 0
        out[...] = rows[part]


def kron_of(act_parts, grads, cuts):
    pairs = grads.shape[0]
    parts = cuts[1]
    width = PROJ * PROJ // parts
    vmem = pl.BlockSpec(memory_space=pltpu.VMEM)
    return pl.pallas_call(
        functools.partial(kron_kernel, cuts),
        out_shape=[jax.ShapeDtypeStruct((2 * pairs, width), jnp.float32)] * parts,
        in_specs=[vmem] * (1 + len(act_parts)),
        out_specs=[vmem] * parts,
        scratch_shapes=[
            pltpu.VMEM((parts, 2 * pairs, width), jnp.float32),
            pltpu.VMEM((pairs * LANES, LANES), jnp.float32),
        ],
        compiler_params=pltpu.CompilerParams(vmem_limit_bytes=VMEM_BYTES),
        name="kron",
    )(act_parts[0], grads, *act_parts[1:])


def parcels_kernel(here, there, *parcels):
    count = here.shape[0]
    dp = len(parcels)
    width = parcels[0].shape[1]
    core, chip = lax.axis_index("seq"), lax.axis_index("tensor") * 2
    blocks = [chip + core, chip + 1 - core]
    for k, parcel in enumerate(parcels):
        for step, block in enumerate(blocks + [lax.rem(lax.axis_index("dp") + k, dp)]):
            lanes = pl.ds(pl.multiple_of(block * width, LANES), width)
            parcel[pl.ds(step * count, count), :] = here[:, lanes] + there[:, lanes]


def parcels_of(here, there, dp):
    count, width = here.shape
    vmem = pl.BlockSpec(memory_space=pltpu.VMEM)
    return pl.pallas_call(
        parcels_kernel,
        out_shape=[jax.ShapeDtypeStruct((3 * count, width // dp), jnp.float32)] * dp,
        in_specs=[vmem] * 2,
        out_specs=[vmem] * dp,
        compiler_params=pltpu.CompilerParams(vmem_limit_bytes=VMEM_BYTES),
        name="parcels",
    )(here, there)


def bundle_kernel(*refs):
    parcels, out = refs[:-1], refs[-1]
    rows = 2 * parcels[0].shape[0] // 3
    for k, parcel in enumerate(parcels):
        out[pl.ds(k * rows, rows), :] = parcel[pl.ds(rows // 2, rows), :]


def bundle_of(parcels):
    rows, width = parcels[0].shape
    vmem = pl.BlockSpec(memory_space=pltpu.VMEM)
    return pl.pallas_call(
        bundle_kernel,
        out_shape=jax.ShapeDtypeStruct((2 * rows // 3 * len(parcels), width), jnp.float32),
        in_specs=[vmem] * len(parcels),
        out_specs=vmem,
        compiler_params=pltpu.CompilerParams(vmem_limit_bytes=VMEM_BYTES),
        name="bundle",
    )(*parcels)


def fisher_kernel(scale, bundle, *refs):
    parcels, (mine, out, made, kept, left, right, sems) = refs[:-7], refs[-7:]
    rows = parcels[0].shape[0] // 3
    part = parcels[0].shape[1]
    core = lax.axis_index("seq")
    own = pl.ds(pl.multiple_of(core * part, LANES), part)
    others = pl.ds(pl.multiple_of((1 - core) * part, LANES), part)
    for k, parcel in enumerate(parcels):
        into = pl.ds(k * rows, rows)
        left[into, own] = parcel[pl.ds(0, rows), :]
        left[into, others] = bundle[pl.ds(2 * k * rows, rows), :]
        right[into, own] = parcel[pl.ds(2 * rows, rows), :]
        right[into, others] = bundle[pl.ds((2 * k + 1) * rows, rows), :]
    blocks, _, width = made.shape
    kept[...] = left[pl.ds(0, rows), :]
    copies = [pltpu.make_async_copy(kept, mine, sems.at[blocks])]
    copies[0].start()
    l1, l2, l3 = split3(left[...])
    r1, r2, r3 = split3(right[...] * scale)
    left_parts = jnp.concatenate([l1, l1, l2, l1, l3, l2, l2, l3], axis=0).T
    right_parts = jnp.concatenate([r1, r2, r1, r3, r1, r2, r3, r2], axis=0)
    for block in range(blocks):
        columns = slice(block * width, (block + 1) * width)
        made[block] = jnp.dot(left_parts, right_parts[:, columns], preferred_element_type=jnp.float32)
        copies.append(
            pltpu.make_async_copy(made.at[block], out.at[:, pl.ds(block * width, width)], sems.at[block])
        )
        copies[-1].start()
    for copy in copies:
        copy.wait()


def fisher_block(parcels, bundle):
    rows, part = parcels[0].shape
    rows //= 3
    width = 2 * part
    total = rows * len(parcels)
    blocks = 4
    hbm = pl.BlockSpec(memory_space=pltpu.HBM)
    return pl.pallas_call(
        functools.partial(fisher_kernel, 1.0 / total),
        out_shape=[
            jax.ShapeDtypeStruct((rows, width), jnp.float32),
            jax.ShapeDtypeStruct((width, width), jnp.float32),
        ],
        in_specs=[pl.BlockSpec(memory_space=pltpu.VMEM)] * (1 + len(parcels)),
        out_specs=[hbm] * 2,
        scratch_shapes=[
            pltpu.VMEM((blocks, width, width // blocks), jnp.float32),
            pltpu.VMEM((rows, width), jnp.float32),
            pltpu.VMEM((total, width), jnp.float32),
            pltpu.VMEM((total, width), jnp.float32),
            pltpu.SemaphoreType.DMA((blocks + 1,)),
        ],
        compiler_params=pltpu.CompilerParams(vmem_limit_bytes=VMEM_BYTES),
        name="fisher",
    )(bundle, *parcels)


def local(acts, grads, in_ids, in_signs, out_ids, out_signs, in_table, out_table):
    tensor, seq, dp = (lax.axis_size(name) for name in ("tensor", "seq", "dp"))
    shards = tensor * seq
    small = tensor == 2 and seq == 2 and dp == 4
    swap = [(0, 1), (1, 0)]

    act = project(acts, in_ids, in_signs, in_table, True, 512, "project_acts")
    if tensor == 2:
        act_parts = [act, lax.ppermute(act, "tensor", swap)]
    else:
        act_parts = [lax.psum(act, "tensor")]
    grad = project(grads, out_ids, out_signs, out_table, False, 1024, "project_grads")
    krons = kron_of(act_parts, grad, (shards, seq) if small else (1, 1))

    if not small:
        kron = lax.psum(krons[0], ("tensor", "seq"))
        width = kron.shape[1] // shards
        place = lax.axis_index("tensor") * seq + lax.axis_index("seq")
        mine = lax.dynamic_slice_in_dim(kron, place * width, width, 1)
        every = lax.all_gather(kron, "dp", axis=0, tiled=True)
        left = lax.dynamic_slice_in_dim(every, place * width, width, 1)
        columns = kron.shape[1] // dp
        right = lax.dynamic_slice_in_dim(every, lax.axis_index("dp") * columns, columns, 1)
        fisher = lax.dot_general(
            left, right, (((0,), (0,)), ((), ())), precision=lax.Precision.HIGHEST
        ) / left.shape[0]
        return mine, fisher

    part = krons[0] + lax.ppermute(krons[1], "seq", swap)
    parcels = list(parcels_of(part, lax.ppermute(part, "tensor", swap), dp))
    for k in range(1, dp):
        parcels[k] = lax.ppermute(parcels[k], "dp", [(d, (d + k) % dp) for d in range(dp)])
    mine, fisher = fisher_block(parcels, lax.ppermute(bundle_of(parcels), "seq", swap))
    return mine, fisher


def solution(mesh):
    in_specs = (
        P(("groups", "dp"), "seq", "tensor"),
        P(("groups", "dp"), "seq", "tensor"),
        P("tensor"),
        P("tensor"),
        P("tensor"),
        P("tensor"),
        P(),
        P(),
    )
    out_specs = (P(("groups", "dp"), ("tensor", "seq")), P(("groups", "tensor", "seq"), "dp"))
    return jax.shard_map(local, mesh=mesh, in_specs=in_specs, out_specs=out_specs, check_vma=False)
```

```python
import functools

import jax
import jax.numpy as jnp
from jax import lax
from jax.experimental import pallas as pl
from jax.experimental.pallas import tpu as pltpu
from jax.sharding import PartitionSpec as P

PROJ = 64
BLOCK = 64
LANES = 128
VMEM_BYTES = 48 * 1024 * 1024


def chunks_of(width, most):
    if width >= 4 * most:
        inner = width - most
        ends = [most // 2] * 2
    else:
        inner, ends = width, []
    chunk = most
    while inner % chunk:
        chunk -= LANES
    return ends[:1] + [chunk] * (inner // chunk) + ends[1:]


def split3(x):
    high = x.astype(jnp.bfloat16)
    rest = x - high.astype(jnp.float32)
    mid = rest.astype(jnp.bfloat16)
    low = (rest - mid.astype(jnp.float32)).astype(jnp.bfloat16)
    return high, mid, low


def spread_table(table, spread, signed):
    entries = table.shape[0]
    stride = spread.shape[0] // entries
    for row in range(0, BLOCK, 2):
        both = table[:, row * PROJ : row * PROJ + LANES].astype(jnp.float32)
        spread[pl.ds(row, entries, stride=stride), :] = both
        spread[pl.ds(row + 1, entries, stride=stride), :] = pltpu.roll(both, PROJ, 1)
    for entry in range(entries):
        block = spread[pl.ds(entry * stride, BLOCK), :].astype(jnp.bfloat16)
        signed[pl.ds((entries + entry) * BLOCK, BLOCK), :] = block
        signed[pl.ds(entry * BLOCK, BLOCK), :] = -block


def lay_blocks(ids, signs, entries, signed, matrix, first, last):
    for j in range(first, last):
        start = pl.multiple_of((signs[j] * entries + ids[j]) * BLOCK, BLOCK)
        matrix[pl.ds(j * BLOCK, BLOCK), :] = signed[pl.ds(start, BLOCK), :]


def project_kernel(widths, fetch, ids, signs, table, rows_ref, *refs):
    out, spread, signed, matrix, held, total, sems, *own = refs
    copies, starts, start = [], [], 0
    for c, width in enumerate(widths):
        columns = pl.ds(start, width)
        copies.append(pltpu.make_async_copy(rows_ref.at[:, columns], held.at[:, columns], sems.at[c]))
        starts.append(start)
        start += width
    if fetch:
        small = [
            pltpu.make_async_copy(source, kept, sems.at[len(widths) + k])
            for k, (source, kept) in enumerate(zip((table, ids, signs), own))
        ]
        for copy in small:
            copy.start()
        table, ids, signs = own
    for copy in copies:
        copy.start()
    if fetch:
        small[0].wait()
    spread_table(table, spread, signed)
    if fetch:
        small[1].wait()
        small[2].wait()
    lay = functools.partial(lay_blocks, ids, signs, table.shape[0], signed, matrix)
    lay(0, widths[0] // BLOCK)
    for c, copy in enumerate(copies):
        columns = pl.ds(starts[c], widths[c])
        copy.wait()
        if c + 1 < len(widths):
            lay(starts[c + 1] // BLOCK, (starts[c + 1] + widths[c + 1]) // BLOCK)
        part = lax.dot_general(
            matrix[columns, :PROJ],
            held[:, columns],
            (((0,), (1,)), ((), ())),
            preferred_element_type=jnp.float32,
        )
        if c == 0:
            total[...] = part
        else:
            total[...] += part
    pairs, _, tokens = out.shape
    for pair in range(pairs):
        for side in range(2):
            out[pair, pl.ds(side * PROJ, PROJ), :] = total[:, pl.ds((2 * pair + side) * tokens, tokens)]


def project(values, ids, signs, table, fetch, most, name):
    count, tokens, width = values.shape
    widths = chunks_of(width, most)
    rows = count * tokens
    entries = table.shape[0]
    smem = pl.BlockSpec(memory_space=pltpu.SMEM)
    vmem = pl.BlockSpec(memory_space=pltpu.VMEM)
    hbm = pl.BlockSpec(memory_space=pltpu.HBM)
    own = [
        pltpu.VMEM(table.shape, table.dtype),
        pltpu.SMEM(ids.shape, ids.dtype),
        pltpu.SMEM(signs.shape, signs.dtype),
    ]
    operands = [ids, signs, table, values.reshape(rows, width)]
    if fetch:
        operands = [pltpu.with_memory_space_constraint(each, pltpu.HBM) for each in operands]
    return pl.pallas_call(
        functools.partial(project_kernel, widths, fetch),
        out_shape=jax.ShapeDtypeStruct((count // 2, LANES, tokens), jnp.float32),
        in_specs=[hbm] * 4 if fetch else [smem, smem, vmem, hbm],
        out_specs=vmem,
        scratch_shapes=[
            pltpu.VMEM((entries * (BLOCK + 8), LANES), jnp.float32),
            pltpu.VMEM((2 * entries * BLOCK, LANES), jnp.bfloat16),
            pltpu.VMEM((width, LANES), jnp.bfloat16),
            pltpu.VMEM((rows, width), jnp.bfloat16),
            pltpu.VMEM((PROJ, rows), jnp.float32),
            pltpu.SemaphoreType.DMA((len(widths) + 3,)),
        ]
        + (own if fetch else []),
        compiler_params=pltpu.CompilerParams(vmem_limit_bytes=VMEM_BYTES),
        cost_estimate=pl.CostEstimate(
            flops=2 * rows * width * LANES, bytes_accessed=2 * rows * width, transcendentals=0
        ),
        name=name,
    )(*operands)


def kron_kernel(cuts, acts, grads, *refs):
    parts = cuts[1]
    summands, outs, rows, products = refs[: -parts - 2], refs[-parts - 2 : -2], refs[-2], refs[-1]
    pairs = acts.shape[0]
    for pair in range(pairs):
        act = acts[pair]
        for other in summands:
            act = act + other[pair]
        a1, a2, a3 = split3(act)
        g1, g2, g3 = split3(grads[pair])
        left = jnp.concatenate([g1, g1, g2, g1, g3, g2], axis=1)
        right = jnp.concatenate([a1, a2, a1, a3, a1, a2], axis=1)
        products[pl.ds(pair * LANES, LANES), :] = lax.dot_general(
            left, right, (((1,), (1,)), ((), ())), preferred_element_type=jnp.float32
        )
    count = 2 * pairs
    lower = lax.broadcasted_iota(jnp.int32, (count, LANES), 1) < PROJ
    even = lax.broadcasted_iota(jnp.int32, (count, LANES), 0) % 2 == 0
    here = even == lower
    tiles = rows.shape[2] // LANES // cuts[0]
    for tile in range(PROJ * PROJ // LANES):
        both = []
        for p in (2 * tile, 2 * tile + 1):
            v = products[pl.ds(p, count, stride=PROJ), :]
            both.append(jnp.where(here, v, pltpu.roll(v, PROJ, 1)))
        block, part, within = tile // tiles // parts, tile // tiles % parts, tile % tiles
        rows[part, :, pl.ds((block * tiles + within) * LANES, LANES)] = jnp.where(lower, both[0], both[1])
    for k, out in enumerate(outs):
        part = lax.rem(lax.axis_index("seq") + k, parts) if parts > 1 else 0
        out[...] = rows[part]


def kron_of(act_parts, grads, cuts):
    pairs = grads.shape[0]
    parts = cuts[1]
    width = PROJ * PROJ // parts
    vmem = pl.BlockSpec(memory_space=pltpu.VMEM)
    return pl.pallas_call(
        functools.partial(kron_kernel, cuts),
        out_shape=[jax.ShapeDtypeStruct((2 * pairs, width), jnp.float32)] * parts,
        in_specs=[vmem] * (1 + len(act_parts)),
        out_specs=[vmem] * parts,
        scratch_shapes=[
            pltpu.VMEM((parts, 2 * pairs, width), jnp.float32),
            pltpu.VMEM((pairs * LANES, LANES), jnp.float32),
        ],
        compiler_params=pltpu.CompilerParams(vmem_limit_bytes=VMEM_BYTES),
        name="kron",
    )(act_parts[0], grads, *act_parts[1:])


def parcels_kernel(here, there, out):
    count = here.shape[0]
    width = out.shape[1]
    core, chip = lax.axis_index("seq"), lax.axis_index("tensor") * 2
    for d in range(out.shape[0] // (3 * count)):
        for step, block in enumerate((chip + core, chip + 1 - core, d)):
            lanes = pl.ds(pl.multiple_of(block * width, LANES), width)
            out[pl.ds((3 * d + step) * count, count), :] = here[:, lanes] + there[:, lanes]


def parcels_of(here, there, dp):
    count, width = here.shape
    vmem = pl.BlockSpec(memory_space=pltpu.VMEM)
    return pl.pallas_call(
        parcels_kernel,
        out_shape=jax.ShapeDtypeStruct((3 * count * dp, width // dp), jnp.float32),
        in_specs=[vmem] * 2,
        out_specs=vmem,
        compiler_params=pltpu.CompilerParams(vmem_limit_bytes=VMEM_BYTES),
        name="parcels",
    )(here, there)


def bundle_kernel(rows, parcels, out):
    for d in range(parcels.shape[0] // (3 * rows)):
        out[pl.ds(2 * d * rows, 2 * rows), :] = parcels[pl.ds((3 * d + 1) * rows, 2 * rows), :]


def bundle_of(parcels, rows):
    vmem = pl.BlockSpec(memory_space=pltpu.VMEM)
    return pl.pallas_call(
        functools.partial(bundle_kernel, rows),
        out_shape=jax.ShapeDtypeStruct((2 * parcels.shape[0] // 3, parcels.shape[1]), jnp.float32),
        in_specs=[vmem],
        out_specs=vmem,
        compiler_params=pltpu.CompilerParams(vmem_limit_bytes=VMEM_BYTES),
        name="bundle",
    )(parcels)


def fisher_kernel(scale, bundle, parcels, mine, out, made, kept, left, right, sems):
    rows, part = kept.shape[0], parcels.shape[1]
    core = lax.axis_index("seq")
    own = pl.ds(pl.multiple_of(core * part, LANES), part)
    others = pl.ds(pl.multiple_of((1 - core) * part, LANES), part)
    for d in range(left.shape[0] // rows):
        into = pl.ds(d * rows, rows)
        left[into, own] = parcels[pl.ds(3 * d * rows, rows), :]
        left[into, others] = bundle[pl.ds(2 * d * rows, rows), :]
        right[into, own] = parcels[pl.ds((3 * d + 2) * rows, rows), :]
        right[into, others] = bundle[pl.ds((2 * d + 1) * rows, rows), :]
    blocks, _, width = made.shape
    kept[...] = left[pl.ds(pl.multiple_of(lax.axis_index("dp") * rows, rows), rows), :]
    copies = [pltpu.make_async_copy(kept, mine, sems.at[blocks])]
    copies[0].start()
    l1, l2, l3 = split3(left[...])
    r1, r2, r3 = split3(right[...] * scale)
    left_parts = jnp.concatenate([l1, l1, l2, l1, l3, l2, l2, l3], axis=0).T
    right_parts = jnp.concatenate([r1, r2, r1, r3, r1, r2, r3, r2], axis=0)
    for block in range(blocks):
        columns = slice(block * width, (block + 1) * width)
        made[block] = jnp.dot(left_parts, right_parts[:, columns], preferred_element_type=jnp.float32)
        copies.append(
            pltpu.make_async_copy(made.at[block], out.at[:, pl.ds(block * width, width)], sems.at[block])
        )
        copies[-1].start()
    for copy in copies:
        copy.wait()


def fisher_block(parcels, bundle, rows):
    total = parcels.shape[0] // 3
    width = 2 * parcels.shape[1]
    blocks = 4
    hbm = pl.BlockSpec(memory_space=pltpu.HBM)
    return pl.pallas_call(
        functools.partial(fisher_kernel, 1.0 / total),
        out_shape=[
            jax.ShapeDtypeStruct((rows, width), jnp.float32),
            jax.ShapeDtypeStruct((width, width), jnp.float32),
        ],
        in_specs=[pl.BlockSpec(memory_space=pltpu.VMEM)] * 2,
        out_specs=[hbm] * 2,
        scratch_shapes=[
            pltpu.VMEM((blocks, width, width // blocks), jnp.float32),
            pltpu.VMEM((rows, width), jnp.float32),
            pltpu.VMEM((total, width), jnp.float32),
            pltpu.VMEM((total, width), jnp.float32),
            pltpu.SemaphoreType.DMA((blocks + 1,)),
        ],
        compiler_params=pltpu.CompilerParams(vmem_limit_bytes=VMEM_BYTES),
        name="fisher",
    )(bundle, parcels)


def local(acts, grads, in_ids, in_signs, out_ids, out_signs, in_table, out_table):
    tensor, seq, dp = (lax.axis_size(name) for name in ("tensor", "seq", "dp"))
    shards = tensor * seq
    small = tensor == 2 and seq == 2 and dp == 4
    swap = [(0, 1), (1, 0)]

    act = project(acts, in_ids, in_signs, in_table, True, 512, "project_acts")
    if tensor == 2:
        act_parts = [act, lax.ppermute(act, "tensor", swap)]
    else:
        act_parts = [lax.psum(act, "tensor")]
    grad = project(grads, out_ids, out_signs, out_table, False, 1024, "project_grads")
    krons = kron_of(act_parts, grad, (shards, seq) if small else (1, 1))

    if not small:
        kron = lax.psum(krons[0], ("tensor", "seq"))
        width = kron.shape[1] // shards
        place = lax.axis_index("tensor") * seq + lax.axis_index("seq")
        mine = lax.dynamic_slice_in_dim(kron, place * width, width, 1)
        every = lax.all_gather(kron, "dp", axis=0, tiled=True)
        left = lax.dynamic_slice_in_dim(every, place * width, width, 1)
        columns = kron.shape[1] // dp
        right = lax.dynamic_slice_in_dim(every, lax.axis_index("dp") * columns, columns, 1)
        fisher = lax.dot_general(
            left, right, (((0,), (0,)), ((), ())), precision=lax.Precision.HIGHEST
        ) / left.shape[0]
        return mine, fisher

    part = krons[0] + lax.ppermute(krons[1], "seq", swap)
    parcels = parcels_of(part, lax.ppermute(part, "tensor", swap), dp)
    parcels = lax.all_to_all(parcels, "dp", 0, 0, tiled=True)
    rows = part.shape[0]
    mine, fisher = fisher_block(parcels, lax.ppermute(bundle_of(parcels, rows), "seq", swap), rows)
    return mine, fisher


def solution(mesh):
    in_specs = (
        P(("groups", "dp"), "seq", "tensor"),
        P(("groups", "dp"), "seq", "tensor"),
        P("tensor"),
        P("tensor"),
        P("tensor"),
        P("tensor"),
        P(),
        P(),
    )
    out_specs = (P(("groups", "dp"), ("tensor", "seq")), P(("groups", "tensor", "seq"), "dp"))
    return jax.shard_map(local, mesh=mesh, in_specs=in_specs, out_specs=out_specs, check_vma=False)
```

```python
import functools

import jax
import jax.numpy as jnp
from jax import lax
from jax.experimental import pallas as pl
from jax.experimental.pallas import tpu as pltpu
from jax.sharding import PartitionSpec as P

PROJ = 64
BLOCK = 64
LANES = 128
VMEM_BYTES = 48 * 1024 * 1024


def chunks_of(width, most):
    if width < 4 * most:
        most = LANES
    ends = most // 2 // LANES * LANES
    inner = width - 2 * ends
    chunk = most
    while inner % chunk:
        chunk -= LANES
    return [ends] * (ends > 0) + [chunk] * (inner // chunk) + [ends] * (ends > 0)


def split3(x):
    high = x.astype(jnp.bfloat16)
    rest = x - high.astype(jnp.float32)
    mid = rest.astype(jnp.bfloat16)
    low = (rest - mid.astype(jnp.float32)).astype(jnp.bfloat16)
    return high, mid, low


def spread_table(table, spread, signed):
    entries = table.shape[0]
    stride = spread.shape[0] // entries
    for row in range(0, BLOCK, 2):
        both = table[:, row * PROJ : row * PROJ + LANES].astype(jnp.float32)
        spread[pl.ds(row, entries, stride=stride), :] = both
        spread[pl.ds(row + 1, entries, stride=stride), :] = pltpu.roll(both, PROJ, 1)
    for entry in range(entries):
        block = spread[pl.ds(entry * stride, BLOCK), :].astype(jnp.bfloat16)
        signed[pl.ds((entries + entry) * BLOCK, BLOCK), :] = block
        signed[pl.ds(entry * BLOCK, BLOCK), :] = -block


def lay_blocks(ids, signs, entries, signed, matrix, first, last):
    for j in range(first, last):
        start = pl.multiple_of((signs[j] * entries + ids[j]) * BLOCK, BLOCK)
        matrix[pl.ds(j * BLOCK, BLOCK), :] = signed[pl.ds(start, BLOCK), :]


def project_kernel(widths, fetch, ids, signs, table, rows_ref, *refs):
    out, spread, signed, matrix, held, total, sems, *own = refs
    copies, starts, start = [], [], 0
    for c, width in enumerate(widths):
        columns = pl.ds(start, width)
        copies.append(pltpu.make_async_copy(rows_ref.at[:, columns], held.at[:, columns], sems.at[c]))
        starts.append(start)
        start += width
    if fetch:
        small = [
            pltpu.make_async_copy(source, kept, sems.at[len(widths) + k])
            for k, (source, kept) in enumerate(zip((table, ids, signs), own))
        ]
        for copy in small:
            copy.start()
        table, ids, signs = own
    for c, copy in enumerate(copies):
        copy.start(priority=c % 2)
    if fetch:
        small[0].wait()
    spread_table(table, spread, signed)
    if fetch:
        small[1].wait()
        small[2].wait()
    lay = functools.partial(lay_blocks, ids, signs, table.shape[0], signed, matrix)
    lay(0, widths[0] // BLOCK)
    for c, copy in enumerate(copies):
        columns = pl.ds(starts[c], widths[c])
        copy.wait()
        if c + 1 < len(widths):
            lay(starts[c + 1] // BLOCK, (starts[c + 1] + widths[c + 1]) // BLOCK)
        part = lax.dot_general(
            matrix[columns, :PROJ],
            held[:, columns],
            (((0,), (1,)), ((), ())),
            preferred_element_type=jnp.float32,
        )
        if c == 0:
            total[...] = part
        else:
            total[...] += part
    pairs, _, tokens = out.shape
    for pair in range(pairs):
        for side in range(2):
            out[pair, pl.ds(side * PROJ, PROJ), :] = total[:, pl.ds((2 * pair + side) * tokens, tokens)]


def project(values, ids, signs, table, fetch, most, name):
    count, tokens, width = values.shape
    widths = chunks_of(width, most)
    rows = count * tokens
    entries = table.shape[0]
    smem = pl.BlockSpec(memory_space=pltpu.SMEM)
    vmem = pl.BlockSpec(memory_space=pltpu.VMEM)
    hbm = pl.BlockSpec(memory_space=pltpu.HBM)
    own = [
        pltpu.VMEM(table.shape, table.dtype),
        pltpu.SMEM(ids.shape, ids.dtype),
        pltpu.SMEM(signs.shape, signs.dtype),
    ]
    operands = [ids, signs, table, values.reshape(rows, width)]
    if fetch:
        operands = [pltpu.with_memory_space_constraint(each, pltpu.HBM) for each in operands]
    return pl.pallas_call(
        functools.partial(project_kernel, widths, fetch),
        out_shape=jax.ShapeDtypeStruct((count // 2, LANES, tokens), jnp.float32),
        in_specs=[hbm] * 4 if fetch else [smem, smem, vmem, hbm],
        out_specs=vmem,
        scratch_shapes=[
            pltpu.VMEM((entries * (BLOCK + 8), LANES), jnp.float32),
            pltpu.VMEM((2 * entries * BLOCK, LANES), jnp.bfloat16),
            pltpu.VMEM((width, LANES), jnp.bfloat16),
            pltpu.VMEM((rows, width), jnp.bfloat16),
            pltpu.VMEM((PROJ, rows), jnp.float32),
            pltpu.SemaphoreType.DMA((len(widths) + 3,)),
        ]
        + (own if fetch else []),
        compiler_params=pltpu.CompilerParams(vmem_limit_bytes=VMEM_BYTES),
        cost_estimate=pl.CostEstimate(
            flops=2 * rows * width * LANES, bytes_accessed=2 * rows * width, transcendentals=0
        ),
        name=name,
    )(*operands)


def kron_kernel(cuts, acts, grads, *refs):
    parts = cuts[1]
    summands, outs, rows, products = refs[: -parts - 2], refs[-parts - 2 : -2], refs[-2], refs[-1]
    pairs = acts.shape[0]
    for pair in range(pairs):
        act = acts[pair]
        for other in summands:
            act = act + other[pair]
        a1, a2, a3 = split3(act)
        g1, g2, g3 = split3(grads[pair])
        left = jnp.concatenate([g1, g1, g2, g1, g3, g2], axis=1)
        right = jnp.concatenate([a1, a2, a1, a3, a1, a2], axis=1)
        products[pl.ds(pair * LANES, LANES), :] = lax.dot_general(
            left, right, (((1,), (1,)), ((), ())), preferred_element_type=jnp.float32
        )
    count = 2 * pairs
    lower = lax.broadcasted_iota(jnp.int32, (count, LANES), 1) < PROJ
    even = lax.broadcasted_iota(jnp.int32, (count, LANES), 0) % 2 == 0
    here = even == lower
    tiles = rows.shape[2] // LANES // cuts[0]
    for tile in range(PROJ * PROJ // LANES):
        both = []
        for p in (2 * tile, 2 * tile + 1):
            v = products[pl.ds(p, count, stride=PROJ), :]
            both.append(jnp.where(here, v, pltpu.roll(v, PROJ, 1)))
        block, part, within = tile // tiles // parts, tile // tiles % parts, tile % tiles
        rows[part, :, pl.ds((block * tiles + within) * LANES, LANES)] = jnp.where(lower, both[0], both[1])
    for k, out in enumerate(outs):
        part = lax.rem(lax.axis_index("seq") + k, parts) if parts > 1 else 0
        out[...] = rows[part]


def kron_of(act_parts, grads, cuts):
    pairs = grads.shape[0]
    parts = cuts[1]
    width = PROJ * PROJ // parts
    vmem = pl.BlockSpec(memory_space=pltpu.VMEM)
    return pl.pallas_call(
        functools.partial(kron_kernel, cuts),
        out_shape=[jax.ShapeDtypeStruct((2 * pairs, width), jnp.float32)] * parts,
        in_specs=[vmem] * (1 + len(act_parts)),
        out_specs=[vmem] * parts,
        scratch_shapes=[
            pltpu.VMEM((parts, 2 * pairs, width), jnp.float32),
            pltpu.VMEM((pairs * LANES, LANES), jnp.float32),
        ],
        compiler_params=pltpu.CompilerParams(vmem_limit_bytes=VMEM_BYTES),
        name="kron",
    )(act_parts[0], grads, *act_parts[1:])


def parcels_kernel(here, there, *parcels):
    count = here.shape[0]
    dp = len(parcels)
    width = parcels[0].shape[1]
    core, chip = lax.axis_index("seq"), lax.axis_index("tensor") * 2
    blocks = [chip + core, chip + 1 - core]
    for k, parcel in enumerate(parcels):
        for step, block in enumerate(blocks + [lax.axis_index("dp") ^ k]):
            lanes = pl.ds(pl.multiple_of(block * width, LANES), width)
            parcel[pl.ds(step * count, count), :] = here[:, lanes] + there[:, lanes]


def parcels_of(here, there, dp):
    count, width = here.shape
    vmem = pl.BlockSpec(memory_space=pltpu.VMEM)
    return pl.pallas_call(
        parcels_kernel,
        out_shape=[jax.ShapeDtypeStruct((3 * count, width // dp), jnp.float32)] * dp,
        in_specs=[vmem] * 2,
        out_specs=[vmem] * dp,
        compiler_params=pltpu.CompilerParams(vmem_limit_bytes=VMEM_BYTES),
        name="parcels",
    )(here, there)


def bundle_kernel(*refs):
    parcels, out = refs[:-1], refs[-1]
    rows = 2 * parcels[0].shape[0] // 3
    for k, parcel in enumerate(parcels):
        out[pl.ds(k * rows, rows), :] = parcel[pl.ds(rows // 2, rows), :]


def bundle_of(parcels):
    rows, width = parcels[0].shape
    vmem = pl.BlockSpec(memory_space=pltpu.VMEM)
    return pl.pallas_call(
        bundle_kernel,
        out_shape=jax.ShapeDtypeStruct((2 * rows // 3 * len(parcels), width), jnp.float32),
        in_specs=[vmem] * len(parcels),
        out_specs=vmem,
        compiler_params=pltpu.CompilerParams(vmem_limit_bytes=VMEM_BYTES),
        name="bundle",
    )(*parcels)


def fisher_kernel(scale, bundle, *refs):
    parcels, (mine, out, made, kept, left, right, sems) = refs[:-7], refs[-7:]
    rows = parcels[0].shape[0] // 3
    part = parcels[0].shape[1]
    core = lax.axis_index("seq")
    own = pl.ds(pl.multiple_of(core * part, LANES), part)
    others = pl.ds(pl.multiple_of((1 - core) * part, LANES), part)
    for k, parcel in enumerate(parcels):
        into = pl.ds(k * rows, rows)
        left[into, own] = parcel[pl.ds(0, rows), :]
        left[into, others] = bundle[pl.ds(2 * k * rows, rows), :]
        right[into, own] = parcel[pl.ds(2 * rows, rows), :]
        right[into, others] = bundle[pl.ds((2 * k + 1) * rows, rows), :]
    blocks, _, width = made.shape
    kept[...] = left[pl.ds(0, rows), :]
    copies = [pltpu.make_async_copy(kept, mine, sems.at[blocks])]
    copies[0].start()
    l1, l2, l3 = split3(left[...])
    r1, r2, r3 = split3(right[...] * scale)
    left_parts = jnp.concatenate([l1, l1, l2, l1, l3, l2, l2, l3], axis=0).T
    right_parts = jnp.concatenate([r1, r2, r1, r3, r1, r2, r3, r2], axis=0)
    for block in range(blocks):
        columns = slice(block * width, (block + 1) * width)
        made[block] = jnp.dot(left_parts, right_parts[:, columns], preferred_element_type=jnp.float32)
        copies.append(
            pltpu.make_async_copy(made.at[block], out.at[:, pl.ds(block * width, width)], sems.at[block])
        )
        copies[-1].start(priority=block % 2)
    for copy in copies:
        copy.wait()


def fisher_block(parcels, bundle):
    rows, part = parcels[0].shape
    rows //= 3
    width = 2 * part
    total = rows * len(parcels)
    blocks = 4
    hbm = pl.BlockSpec(memory_space=pltpu.HBM)
    return pl.pallas_call(
        functools.partial(fisher_kernel, 1.0 / total),
        out_shape=[
            jax.ShapeDtypeStruct((rows, width), jnp.float32),
            jax.ShapeDtypeStruct((width, width), jnp.float32),
        ],
        in_specs=[pl.BlockSpec(memory_space=pltpu.VMEM)] * (1 + len(parcels)),
        out_specs=[hbm] * 2,
        scratch_shapes=[
            pltpu.VMEM((blocks, width, width // blocks), jnp.float32),
            pltpu.VMEM((rows, width), jnp.float32),
            pltpu.VMEM((total, width), jnp.float32),
            pltpu.VMEM((total, width), jnp.float32),
            pltpu.SemaphoreType.DMA((blocks + 1,)),
        ],
        compiler_params=pltpu.CompilerParams(vmem_limit_bytes=VMEM_BYTES),
        name="fisher",
    )(bundle, *parcels)


def local(acts, grads, in_ids, in_signs, out_ids, out_signs, in_table, out_table):
    tensor, seq, dp = (lax.axis_size(name) for name in ("tensor", "seq", "dp"))
    shards = tensor * seq
    small = tensor == 2 and seq == 2 and dp == 4
    swap = [(0, 1), (1, 0)]

    act = project(acts, in_ids, in_signs, in_table, True, 512, "project_acts")
    if tensor == 2:
        act_parts = [act, lax.ppermute(act, "tensor", swap)]
    else:
        act_parts = [lax.psum(act, "tensor")]
    grad = project(grads, out_ids, out_signs, out_table, False, 1024, "project_grads")
    krons = kron_of(act_parts, grad, (shards, seq) if small else (1, 1))

    if not small:
        kron = lax.psum(krons[0], ("tensor", "seq"))
        width = kron.shape[1] // shards
        place = lax.axis_index("tensor") * seq + lax.axis_index("seq")
        mine = lax.dynamic_slice_in_dim(kron, place * width, width, 1)
        every = lax.all_gather(kron, "dp", axis=0, tiled=True)
        left = lax.dynamic_slice_in_dim(every, place * width, width, 1)
        columns = kron.shape[1] // dp
        right = lax.dynamic_slice_in_dim(every, lax.axis_index("dp") * columns, columns, 1)
        fisher = lax.dot_general(
            left, right, (((0,), (0,)), ((), ())), precision=lax.Precision.HIGHEST
        ) / left.shape[0]
        return mine, fisher

    part = krons[0] + lax.ppermute(krons[1], "seq", swap)
    parcels = list(parcels_of(part, lax.ppermute(part, "tensor", swap), dp))
    parcels = parcels[:1] + [
        lax.ppermute(parcels[k], "dp", [(d, d ^ k) for d in range(dp)]) for k in (2, 3, 1)
    ]
    mine, fisher = fisher_block(parcels, lax.ppermute(bundle_of(parcels), "seq", swap))
    return mine, fisher


def solution(mesh):
    in_specs = (
        P(("groups", "dp"), "seq", "tensor"),
        P(("groups", "dp"), "seq", "tensor"),
        P("tensor"),
        P("tensor"),
        P("tensor"),
        P("tensor"),
        P(),
        P(),
    )
    out_specs = (P(("groups", "dp"), ("tensor", "seq")), P(("groups", "tensor", "seq"), "dp"))
    return jax.shard_map(local, mesh=mesh, in_specs=in_specs, out_specs=out_specs, check_vma=False)
```

```python
import functools

import jax
import jax.numpy as jnp
from jax import lax
from jax.experimental import pallas as pl
from jax.experimental.pallas import tpu as pltpu
from jax.sharding import PartitionSpec as P

PROJ = 64
BLOCK = 64
LANES = 128
PLANE = ("tensor", "seq")
VMEM_BYTES = 48 * 1024 * 1024


def chunks_of(width, most):
    if width < 4 * most:
        most = LANES
    ends = most // 2 // LANES * LANES
    inner = width - 2 * ends
    chunk = most
    while inner % chunk:
        chunk -= LANES
    return [ends] * (ends > 0) + [chunk] * (inner // chunk) + [ends] * (ends > 0)


def split3(x):
    high = x.astype(jnp.bfloat16)
    rest = x - high.astype(jnp.float32)
    mid = rest.astype(jnp.bfloat16)
    low = (rest - mid.astype(jnp.float32)).astype(jnp.bfloat16)
    return high, mid, low


def spread_table(table, spread, signed):
    entries = table.shape[0]
    stride = spread.shape[0] // entries
    for row in range(0, BLOCK, 2):
        both = table[:, row * PROJ : row * PROJ + LANES].astype(jnp.float32)
        spread[pl.ds(row, entries, stride=stride), :] = both
        spread[pl.ds(row + 1, entries, stride=stride), :] = pltpu.roll(both, PROJ, 1)
    for entry in range(entries):
        block = spread[pl.ds(entry * stride, BLOCK), :].astype(jnp.bfloat16)
        signed[pl.ds((entries + entry) * BLOCK, BLOCK), :] = block
        signed[pl.ds(entry * BLOCK, BLOCK), :] = -block


def lay_blocks(ids, signs, entries, signed, matrix, first, last):
    for j in range(first, last):
        start = pl.multiple_of((signs[j] * entries + ids[j]) * BLOCK, BLOCK)
        matrix[pl.ds(j * BLOCK, BLOCK), :] = signed[pl.ds(start, BLOCK), :]


def project_kernel(widths, fetch, ids, signs, table, rows_ref, *refs):
    out, spread, signed, matrix, held, total, sems, *own = refs
    copies, starts, start = [], [], 0
    for c, width in enumerate(widths):
        columns = pl.ds(start, width)
        copies.append(pltpu.make_async_copy(rows_ref.at[:, columns], held.at[:, columns], sems.at[c]))
        starts.append(start)
        start += width
    if fetch:
        small = [
            pltpu.make_async_copy(source, kept, sems.at[len(widths) + k])
            for k, (source, kept) in enumerate(zip((table, ids, signs), own))
        ]
        for copy in small:
            copy.start()
        table, ids, signs = own
    for copy in copies:
        copy.start()
    if fetch:
        small[0].wait()
    spread_table(table, spread, signed)
    if fetch:
        small[1].wait()
        small[2].wait()
    lay = functools.partial(lay_blocks, ids, signs, table.shape[0], signed, matrix)
    lay(0, widths[0] // BLOCK)
    for c, copy in enumerate(copies):
        columns = pl.ds(starts[c], widths[c])
        copy.wait()
        if c + 1 < len(widths):
            lay(starts[c + 1] // BLOCK, (starts[c + 1] + widths[c + 1]) // BLOCK)
        part = lax.dot_general(
            matrix[columns, :PROJ],
            held[:, columns],
            (((0,), (1,)), ((), ())),
            preferred_element_type=jnp.float32,
        )
        if c == 0:
            total[...] = part
        else:
            total[...] += part
    pairs, _, tokens = out.shape
    for pair in range(pairs):
        for side in range(2):
            out[pair, pl.ds(side * PROJ, PROJ), :] = total[:, pl.ds((2 * pair + side) * tokens, tokens)]


def project(values, ids, signs, table, fetch, most, name):
    count, tokens, width = values.shape
    widths = chunks_of(width, most)
    rows = count * tokens
    entries = table.shape[0]
    smem = pl.BlockSpec(memory_space=pltpu.SMEM)
    vmem = pl.BlockSpec(memory_space=pltpu.VMEM)
    hbm = pl.BlockSpec(memory_space=pltpu.HBM)
    own = [
        pltpu.VMEM(table.shape, table.dtype),
        pltpu.SMEM(ids.shape, ids.dtype),
        pltpu.SMEM(signs.shape, signs.dtype),
    ]
    operands = [ids, signs, table, values.reshape(rows, width)]
    if fetch:
        operands = [pltpu.with_memory_space_constraint(each, pltpu.HBM) for each in operands]
    return pl.pallas_call(
        functools.partial(project_kernel, widths, fetch),
        out_shape=jax.ShapeDtypeStruct((count // 2, LANES, tokens), jnp.float32),
        in_specs=[hbm] * 4 if fetch else [smem, smem, vmem, hbm],
        out_specs=vmem,
        scratch_shapes=[
            pltpu.VMEM((entries * (BLOCK + 8), LANES), jnp.float32),
            pltpu.VMEM((2 * entries * BLOCK, LANES), jnp.bfloat16),
            pltpu.VMEM((width, LANES), jnp.bfloat16),
            pltpu.VMEM((rows, width), jnp.bfloat16),
            pltpu.VMEM((PROJ, rows), jnp.float32),
            pltpu.SemaphoreType.DMA((len(widths) + 3,)),
        ]
        + (own if fetch else []),
        compiler_params=pltpu.CompilerParams(vmem_limit_bytes=VMEM_BYTES),
        cost_estimate=pl.CostEstimate(
            flops=2 * rows * width * LANES, bytes_accessed=2 * rows * width, transcendentals=0
        ),
        name=name,
    )(*operands)


def kron_kernel(acts, grads, *refs):
    summands, out, products = refs[:-2], refs[-2], refs[-1]
    pairs = acts.shape[0]
    for pair in range(pairs):
        act = acts[pair]
        for other in summands:
            act = act + other[pair]
        a1, a2, a3 = split3(act)
        g1, g2, g3 = split3(grads[pair])
        left = jnp.concatenate([g1, g1, g2, g1, g3, g2], axis=1)
        right = jnp.concatenate([a1, a2, a1, a3, a1, a2], axis=1)
        products[pl.ds(pair * LANES, LANES), :] = lax.dot_general(
            left, right, (((1,), (1,)), ((), ())), preferred_element_type=jnp.float32
        )
    count = 2 * pairs
    lower = lax.broadcasted_iota(jnp.int32, (count, LANES), 1) < PROJ
    even = lax.broadcasted_iota(jnp.int32, (count, LANES), 0) % 2 == 0
    here = even == lower
    for tile in range(out.shape[1] // LANES):
        both = []
        for p in (2 * tile, 2 * tile + 1):
            v = products[pl.ds(p, count, stride=PROJ), :]
            both.append(jnp.where(here, v, pltpu.roll(v, PROJ, 1)))
        out[:, pl.ds(tile * LANES, LANES)] = jnp.where(lower, both[0], both[1])


def kron_of(act_parts, grads):
    pairs = grads.shape[0]
    vmem = pl.BlockSpec(memory_space=pltpu.VMEM)
    return pl.pallas_call(
        kron_kernel,
        out_shape=jax.ShapeDtypeStruct((2 * pairs, PROJ * PROJ), jnp.float32),
        in_specs=[vmem] * (1 + len(act_parts)),
        out_specs=vmem,
        scratch_shapes=[pltpu.VMEM((pairs * LANES, LANES), jnp.float32)],
        compiler_params=pltpu.CompilerParams(vmem_limit_bytes=VMEM_BYTES),
        name="kron",
    )(act_parts[0], grads, *act_parts[1:])


def parcels_kernel(here, there, *parcels):
    count = here.shape[0]
    width = parcels[0].shape[1]
    chip = lax.axis_index("tensor") * 2
    for k, parcel in enumerate(parcels):
        for step, block in enumerate((chip, chip + 1, lax.axis_index("dp") ^ k)):
            lanes = pl.ds(pl.multiple_of(block * width, LANES), width)
            parcel[pl.ds(step * count, count), :] = here[:, lanes] + there[:, lanes]


def parcels_of(here, there, dp):
    count, width = here.shape
    vmem = pl.BlockSpec(memory_space=pltpu.VMEM)
    return pl.pallas_call(
        parcels_kernel,
        out_shape=[jax.ShapeDtypeStruct((3 * count, width // dp), jnp.float32)] * dp,
        in_specs=[vmem] * 2,
        out_specs=[vmem] * dp,
        compiler_params=pltpu.CompilerParams(vmem_limit_bytes=VMEM_BYTES),
        name="parcels",
    )(here, there)


def bundle_kernel(*refs):
    parcels, out = refs[:-1], refs[-1]
    rows = parcels[0].shape[0] // 3
    for k, parcel in enumerate(parcels):
        out[pl.ds(2 * k * rows, rows), :] = parcel[pl.ds(0, rows), :]
        out[pl.ds((2 * k + 1) * rows, rows), :] = parcel[pl.ds(2 * rows, rows), :]


def bundle_of(parcels):
    rows, width = parcels[0].shape
    vmem = pl.BlockSpec(memory_space=pltpu.VMEM)
    return pl.pallas_call(
        bundle_kernel,
        out_shape=jax.ShapeDtypeStruct((2 * rows // 3 * len(parcels), width), jnp.float32),
        in_specs=[vmem] * len(parcels),
        out_specs=vmem,
        compiler_params=pltpu.CompilerParams(vmem_limit_bytes=VMEM_BYTES),
        name="bundle",
    )(*parcels)


def fisher_kernel(scale, bundle, *refs):
    parcels, (mine, out, made, kept, left, right, sems) = refs[:-7], refs[-7:]
    rows = kept.shape[0]

    @pl.when(lax.axis_index("seq") == 0)
    def _():
        for k in range(len(parcels)):
            left[pl.ds(k * rows, rows), :] = bundle[pl.ds(2 * k * rows, rows), :]
            right[pl.ds(k * rows, rows), :] = bundle[pl.ds((2 * k + 1) * rows, rows), :]

    @pl.when(lax.axis_index("seq") == 1)
    def _():
        for k, parcel in enumerate(parcels):
            left[pl.ds(k * rows, rows), :] = parcel[pl.ds(rows, rows), :]
            right[pl.ds(k * rows, rows), :] = parcel[pl.ds(2 * rows, rows), :]

    blocks, _, width = made.shape
    kept[...] = left[pl.ds(0, rows), :]
    copies = [pltpu.make_async_copy(kept, mine, sems.at[blocks])]
    copies[0].start()
    l1, l2, l3 = split3(left[...])
    r1, r2, r3 = split3(right[...] * scale)
    left_parts = jnp.concatenate([l1, l1, l2, l1, l3, l2, l2, l3], axis=0).T
    right_parts = jnp.concatenate([r1, r2, r1, r3, r1, r2, r3, r2], axis=0)
    for block in range(blocks):
        columns = slice(block * width, (block + 1) * width)
        made[block] = jnp.dot(left_parts, right_parts[:, columns], preferred_element_type=jnp.float32)
        copies.append(
            pltpu.make_async_copy(made.at[block], out.at[:, pl.ds(block * width, width)], sems.at[block])
        )
        copies[-1].start()
    for copy in copies:
        copy.wait()


def fisher_block(parcels, bundle):
    rows, width = parcels[0].shape
    rows //= 3
    total = rows * len(parcels)
    blocks = 4
    hbm = pl.BlockSpec(memory_space=pltpu.HBM)
    return pl.pallas_call(
        functools.partial(fisher_kernel, 1.0 / total),
        out_shape=[
            jax.ShapeDtypeStruct((rows, width), jnp.float32),
            jax.ShapeDtypeStruct((width, width), jnp.float32),
        ],
        in_specs=[pl.BlockSpec(memory_space=pltpu.VMEM)] * (1 + len(parcels)),
        out_specs=[hbm] * 2,
        scratch_shapes=[
            pltpu.VMEM((blocks, width, width // blocks), jnp.float32),
            pltpu.VMEM((rows, width), jnp.float32),
            pltpu.VMEM((total, width), jnp.float32),
            pltpu.VMEM((total, width), jnp.float32),
            pltpu.SemaphoreType.DMA((blocks + 1,)),
        ],
        compiler_params=pltpu.CompilerParams(vmem_limit_bytes=VMEM_BYTES),
        name="fisher",
    )(bundle, *parcels)


def local(acts, grads, in_ids, in_signs, out_ids, out_signs, in_table, out_table):
    tensor, seq, dp = (lax.axis_size(name) for name in ("tensor", "seq", "dp"))
    shards = tensor * seq
    small = tensor == 2 and seq == 2 and dp == 4

    act = project(acts, in_ids, in_signs, in_table, True, 512, "project_acts")
    if tensor == 2:
        act_parts = [act, lax.ppermute(act, "tensor", [(0, 1), (1, 0)])]
    else:
        act_parts = [lax.psum(act, "tensor")]
    grad = project(grads, out_ids, out_signs, out_table, False, 1024, "project_grads")
    kron = kron_of(act_parts, grad)

    if not small:
        kron = lax.psum(kron, PLANE)
        width = kron.shape[1] // shards
        place = lax.axis_index("tensor") * seq + lax.axis_index("seq")
        mine = lax.dynamic_slice_in_dim(kron, place * width, width, 1)
        every = lax.all_gather(kron, "dp", axis=0, tiled=True)
        left = lax.dynamic_slice_in_dim(every, place * width, width, 1)
        columns = kron.shape[1] // dp
        right = lax.dynamic_slice_in_dim(every, lax.axis_index("dp") * columns, columns, 1)
        fisher = lax.dot_general(
            left, right, (((0,), (0,)), ((), ())), precision=lax.Precision.HIGHEST
        ) / left.shape[0]
        return mine, fisher

    kron = kron + lax.ppermute(kron, PLANE, [(0, 1), (2, 3)])
    parcels = list(parcels_of(kron, lax.ppermute(kron, PLANE, [(1, 3), (3, 1)]), dp))
    parcels = parcels[:1] + [
        lax.ppermute(
            parcels[k],
            ("dp",) + PLANE,
            [(shards * d + place, shards * (d ^ k) + place) for d in range(dp) for place in (1, 3)],
        )
        for k in (2, 3, 1)
    ]
    bundle = lax.ppermute(bundle_of(parcels), PLANE, [(1, 0), (3, 2)])
    mine, fisher = fisher_block(parcels, bundle)
    return mine, fisher


def solution(mesh):
    in_specs = (
        P(("groups", "dp"), "seq", "tensor"),
        P(("groups", "dp"), "seq", "tensor"),
        P("tensor"),
        P("tensor"),
        P("tensor"),
        P("tensor"),
        P(),
        P(),
    )
    out_specs = (P(("groups", "dp"), ("tensor", "seq")), P(("groups", "tensor", "seq"), "dp"))
    return jax.shard_map(local, mesh=mesh, in_specs=in_specs, out_specs=out_specs, check_vma=False)
```

```python
import functools

import jax
import jax.numpy as jnp
from jax import lax
from jax.experimental import pallas as pl
from jax.experimental.pallas import tpu as pltpu
from jax.sharding import PartitionSpec as P

PROJ = 64
BLOCK = 64
LANES = 128
PLANE = ("tensor", "seq")
VMEM_BYTES = 48 * 1024 * 1024


def chunks_of(width, most):
    if width < 4 * most:
        most = LANES
    ends = most // 2 // LANES * LANES
    inner = width - 2 * ends
    chunk = most
    while inner % chunk:
        chunk -= LANES
    return [ends] * (ends > 0) + [chunk] * (inner // chunk) + [ends] * (ends > 0)


def split3(x):
    high = x.astype(jnp.bfloat16)
    rest = x - high.astype(jnp.float32)
    mid = rest.astype(jnp.bfloat16)
    low = (rest - mid.astype(jnp.float32)).astype(jnp.bfloat16)
    return high, mid, low


def spread_table(table, spread, signed):
    entries = table.shape[0]
    stride = spread.shape[0] // entries
    for row in range(0, BLOCK, 2):
        both = table[:, row * PROJ : row * PROJ + LANES].astype(jnp.float32)
        spread[pl.ds(row, entries, stride=stride), :] = both
        spread[pl.ds(row + 1, entries, stride=stride), :] = pltpu.roll(both, PROJ, 1)
    for entry in range(entries):
        block = spread[pl.ds(entry * stride, BLOCK), :].astype(jnp.bfloat16)
        signed[pl.ds((entries + entry) * BLOCK, BLOCK), :] = block
        signed[pl.ds(entry * BLOCK, BLOCK), :] = -block


def lay_blocks(ids, signs, entries, signed, matrix, first, last):
    for j in range(first, last):
        start = pl.multiple_of((signs[j] * entries + ids[j]) * BLOCK, BLOCK)
        matrix[pl.ds(j * BLOCK, BLOCK), :] = signed[pl.ds(start, BLOCK), :]


def project_kernel(widths, fetch, ids, signs, table, rows_ref, *refs):
    out, spread, signed, matrix, held, total, sems, *own = refs
    copies, starts, start = [], [], 0
    for c, width in enumerate(widths):
        columns = pl.ds(start, width)
        copies.append(pltpu.make_async_copy(rows_ref.at[:, columns], held.at[:, columns], sems.at[c]))
        starts.append(start)
        start += width
    if fetch:
        small = [
            pltpu.make_async_copy(source, kept, sems.at[len(widths) + k])
            for k, (source, kept) in enumerate(zip((table, ids, signs), own))
        ]
        for copy in small:
            copy.start()
        table, ids, signs = own
    for copy in copies:
        copy.start()
    if fetch:
        small[0].wait()
    spread_table(table, spread, signed)
    if fetch:
        small[1].wait()
        small[2].wait()
    lay = functools.partial(lay_blocks, ids, signs, table.shape[0], signed, matrix)
    lay(0, widths[0] // BLOCK)
    for c, copy in enumerate(copies):
        columns = pl.ds(starts[c], widths[c])
        copy.wait()
        if c + 1 < len(widths):
            lay(starts[c + 1] // BLOCK, (starts[c + 1] + widths[c + 1]) // BLOCK)
        part = lax.dot_general(
            matrix[columns, :PROJ],
            held[:, columns],
            (((0,), (1,)), ((), ())),
            preferred_element_type=jnp.float32,
        )
        if c == 0:
            total[...] = part
        else:
            total[...] += part
    pairs, _, tokens = out.shape
    for pair in range(pairs):
        for side in range(2):
            out[pair, pl.ds(side * PROJ, PROJ), :] = total[:, pl.ds((2 * pair + side) * tokens, tokens)]


def project(values, ids, signs, table, fetch, most, name):
    count, tokens, width = values.shape
    widths = chunks_of(width, most)
    rows = count * tokens
    entries = table.shape[0]
    smem = pl.BlockSpec(memory_space=pltpu.SMEM)
    vmem = pl.BlockSpec(memory_space=pltpu.VMEM)
    hbm = pl.BlockSpec(memory_space=pltpu.HBM)
    own = [
        pltpu.VMEM(table.shape, table.dtype),
        pltpu.SMEM(ids.shape, ids.dtype),
        pltpu.SMEM(signs.shape, signs.dtype),
    ]
    operands = [ids, signs, table, values.reshape(rows, width)]
    if fetch:
        operands = [pltpu.with_memory_space_constraint(each, pltpu.HBM) for each in operands]
    return pl.pallas_call(
        functools.partial(project_kernel, widths, fetch),
        out_shape=jax.ShapeDtypeStruct((count // 2, LANES, tokens), jnp.float32),
        in_specs=[hbm] * 4 if fetch else [smem, smem, vmem, hbm],
        out_specs=vmem,
        scratch_shapes=[
            pltpu.VMEM((entries * (BLOCK + 8), LANES), jnp.float32),
            pltpu.VMEM((2 * entries * BLOCK, LANES), jnp.bfloat16),
            pltpu.VMEM((width, LANES), jnp.bfloat16),
            pltpu.VMEM((rows, width), jnp.bfloat16),
            pltpu.VMEM((PROJ, rows), jnp.float32),
            pltpu.SemaphoreType.DMA((len(widths) + 3,)),
        ]
        + (own if fetch else []),
        compiler_params=pltpu.CompilerParams(vmem_limit_bytes=VMEM_BYTES),
        cost_estimate=pl.CostEstimate(
            flops=2 * rows * width * LANES, bytes_accessed=2 * rows * width, transcendentals=0
        ),
        name=name,
    )(*operands)


def kron_kernel(acts, grads, *refs):
    summands, out, products = refs[:-2], refs[-2], refs[-1]
    pairs = acts.shape[0]
    for pair in range(pairs):
        act = acts[pair]
        for other in summands:
            act = act + other[pair]
        a1, a2, a3 = split3(act)
        g1, g2, g3 = split3(grads[pair])
        left = jnp.concatenate([g1, g1, g2, g1, g3, g2], axis=1)
        right = jnp.concatenate([a1, a2, a1, a3, a1, a2], axis=1)
        products[pl.ds(pair * LANES, LANES), :] = lax.dot_general(
            left, right, (((1,), (1,)), ((), ())), preferred_element_type=jnp.float32
        )
    count = 2 * pairs
    lower = lax.broadcasted_iota(jnp.int32, (count, LANES), 1) < PROJ
    even = lax.broadcasted_iota(jnp.int32, (count, LANES), 0) % 2 == 0
    here = even == lower
    for tile in range(out.shape[1] // LANES):
        both = []
        for p in (2 * tile, 2 * tile + 1):
            v = products[pl.ds(p, count, stride=PROJ), :]
            both.append(jnp.where(here, v, pltpu.roll(v, PROJ, 1)))
        out[:, pl.ds(tile * LANES, LANES)] = jnp.where(lower, both[0], both[1])


def kron_of(act_parts, grads):
    pairs = grads.shape[0]
    vmem = pl.BlockSpec(memory_space=pltpu.VMEM)
    return pl.pallas_call(
        kron_kernel,
        out_shape=jax.ShapeDtypeStruct((2 * pairs, PROJ * PROJ), jnp.float32),
        in_specs=[vmem] * (1 + len(act_parts)),
        out_specs=vmem,
        scratch_shapes=[pltpu.VMEM((pairs * LANES, LANES), jnp.float32)],
        compiler_params=pltpu.CompilerParams(vmem_limit_bytes=VMEM_BYTES),
        name="kron",
    )(act_parts[0], grads, *act_parts[1:])


def parcels_kernel(here, there, *parcels):
    count = here.shape[0]
    width = parcels[0].shape[1]
    chip = lax.axis_index("tensor") * 2
    for k, parcel in enumerate(parcels):
        for step, block in enumerate((chip, chip + 1, lax.axis_index("dp") ^ k)):
            lanes = pl.ds(pl.multiple_of(block * width, LANES), width)
            parcel[pl.ds(step * count, count), :] = here[:, lanes] + there[:, lanes]


def parcels_of(here, there, dp):
    count, width = here.shape
    vmem = pl.BlockSpec(memory_space=pltpu.VMEM)
    return pl.pallas_call(
        parcels_kernel,
        out_shape=[jax.ShapeDtypeStruct((3 * count, width // dp), jnp.float32)] * dp,
        in_specs=[vmem] * 2,
        out_specs=[vmem] * dp,
        compiler_params=pltpu.CompilerParams(vmem_limit_bytes=VMEM_BYTES),
        name="parcels",
    )(here, there)


def bundle_kernel(*refs):
    parcels, out = refs[:-1], refs[-1]
    rows = parcels[0].shape[0] // 3
    for k, parcel in enumerate(parcels):
        out[pl.ds(2 * k * rows, rows), :] = parcel[pl.ds(0, rows), :]
        out[pl.ds((2 * k + 1) * rows, rows), :] = parcel[pl.ds(2 * rows, rows), :]


def bundle_of(parcels):
    rows, width = parcels[0].shape
    vmem = pl.BlockSpec(memory_space=pltpu.VMEM)
    return pl.pallas_call(
        bundle_kernel,
        out_shape=jax.ShapeDtypeStruct((2 * rows // 3 * len(parcels), width), jnp.float32),
        in_specs=[vmem] * len(parcels),
        out_specs=vmem,
        compiler_params=pltpu.CompilerParams(vmem_limit_bytes=VMEM_BYTES),
        name="bundle",
    )(*parcels)


def fisher_kernel(scale, bundle, *refs):
    parcels, (mine, out, made, kept, left, right, sems) = refs[:-7], refs[-7:]
    rows = kept.shape[0]

    @pl.when(lax.axis_index("seq") == 0)
    def _():
        for k in range(len(parcels)):
            left[pl.ds(k * rows, rows), :] = bundle[pl.ds(2 * k * rows, rows), :]
            right[pl.ds(k * rows, rows), :] = bundle[pl.ds((2 * k + 1) * rows, rows), :]

    @pl.when(lax.axis_index("seq") == 1)
    def _():
        for k, parcel in enumerate(parcels):
            left[pl.ds(k * rows, rows), :] = parcel[pl.ds(rows, rows), :]
            right[pl.ds(k * rows, rows), :] = parcel[pl.ds(2 * rows, rows), :]

    blocks, _, width = made.shape
    kept[...] = left[pl.ds(0, rows), :]
    copies = [pltpu.make_async_copy(kept, mine, sems.at[blocks])]
    copies[0].start()
    l1, l2, l3 = split3(left[...])
    r1, r2, r3 = split3(right[...] * scale)
    left_parts = jnp.concatenate([l1, l1, l2, l1, l3, l2, l2, l3], axis=0).T
    right_parts = jnp.concatenate([r1, r2, r1, r3, r1, r2, r3, r2], axis=0)
    for block in range(blocks):
        columns = slice(block * width, (block + 1) * width)
        made[block] = jnp.dot(left_parts, right_parts[:, columns], preferred_element_type=jnp.float32)
        copies.append(
            pltpu.make_async_copy(made.at[block], out.at[:, pl.ds(block * width, width)], sems.at[block])
        )
        copies[-1].start()
    for copy in copies:
        copy.wait()


def fisher_block(parcels, bundle):
    rows, width = parcels[0].shape
    rows //= 3
    total = rows * len(parcels)
    blocks = 4
    hbm = pl.BlockSpec(memory_space=pltpu.HBM)
    return pl.pallas_call(
        functools.partial(fisher_kernel, 1.0 / total),
        out_shape=[
            jax.ShapeDtypeStruct((rows, width), jnp.float32),
            jax.ShapeDtypeStruct((width, width), jnp.float32),
        ],
        in_specs=[pl.BlockSpec(memory_space=pltpu.VMEM)] * (1 + len(parcels)),
        out_specs=[hbm] * 2,
        scratch_shapes=[
            pltpu.VMEM((blocks, width, width // blocks), jnp.float32),
            pltpu.VMEM((rows, width), jnp.float32),
            pltpu.VMEM((total, width), jnp.float32),
            pltpu.VMEM((total, width), jnp.float32),
            pltpu.SemaphoreType.DMA((blocks + 1,)),
        ],
        compiler_params=pltpu.CompilerParams(vmem_limit_bytes=VMEM_BYTES),
        name="fisher",
    )(bundle, *parcels)


def local(acts, grads, in_ids, in_signs, out_ids, out_signs, in_table, out_table):
    tensor, seq, dp = (lax.axis_size(name) for name in ("tensor", "seq", "dp"))
    shards = tensor * seq
    small = tensor == 2 and seq == 2 and dp == 4

    act = project(acts, in_ids, in_signs, in_table, True, 512, "project_acts")
    if tensor == 2:
        act_parts = [act, lax.ppermute(act, "tensor", [(0, 1), (1, 0)])]
    else:
        act_parts = [lax.psum(act, "tensor")]
    grad = project(grads, out_ids, out_signs, out_table, False, 1024, "project_grads")
    kron = kron_of(act_parts, grad)

    if not small:
        kron = lax.psum(kron, PLANE)
        width = kron.shape[1] // shards
        place = lax.axis_index("tensor") * seq + lax.axis_index("seq")
        mine = lax.dynamic_slice_in_dim(kron, place * width, width, 1)
        every = lax.all_gather(kron, "dp", axis=0, tiled=True)
        left = lax.dynamic_slice_in_dim(every, place * width, width, 1)
        columns = kron.shape[1] // dp
        right = lax.dynamic_slice_in_dim(every, lax.axis_index("dp") * columns, columns, 1)
        fisher = lax.dot_general(
            left, right, (((0,), (0,)), ((), ())), precision=lax.Precision.HIGHEST
        ) / left.shape[0]
        return mine, fisher

    kron = kron + lax.ppermute(kron, PLANE, [(0, 1), (1, 0), (2, 3), (3, 2)])
    parcels = list(parcels_of(kron, lax.ppermute(kron, PLANE, [(0, 0), (1, 3), (2, 2), (3, 1)]), dp))
    parcels = parcels[:1] + [
        lax.ppermute(
            parcels[k],
            ("dp",) + PLANE,
            [
                (shards * d + place, shards * (d ^ k * (place % 2)) + place)
                for d in range(dp)
                for place in range(shards)
            ],
        )
        for k in (2, 3, 1)
    ]
    bundle = lax.ppermute(bundle_of(parcels), PLANE, [(0, 1), (1, 0), (2, 3), (3, 2)])
    mine, fisher = fisher_block(parcels, bundle)
    return mine, fisher


def solution(mesh):
    in_specs = (
        P(("groups", "dp"), "seq", "tensor"),
        P(("groups", "dp"), "seq", "tensor"),
        P("tensor"),
        P("tensor"),
        P("tensor"),
        P("tensor"),
        P(),
        P(),
    )
    out_specs = (P(("groups", "dp"), ("tensor", "seq")), P(("groups", "tensor", "seq"), "dp"))
    return jax.shard_map(local, mesh=mesh, in_specs=in_specs, out_specs=out_specs, check_vma=False)
```

```python
import functools

import jax
import jax.numpy as jnp
from jax import lax
from jax.experimental import pallas as pl
from jax.experimental.pallas import tpu as pltpu
from jax.sharding import PartitionSpec as P

PROJ = 64
BLOCK = 64
LANES = 128
VMEM_BYTES = 48 * 1024 * 1024


def chunks_of(width, most):
    if width >= 4 * most:
        inner = width - most
        ends = [most // 2] * 2
    else:
        inner, ends = width, []
    chunk = most
    while inner % chunk:
        chunk -= LANES
    return ends[:1] + [chunk] * (inner // chunk) + ends[1:]


def split3(x):
    high = x.astype(jnp.bfloat16)
    rest = x - high.astype(jnp.float32)
    mid = rest.astype(jnp.bfloat16)
    low = (rest - mid.astype(jnp.float32)).astype(jnp.bfloat16)
    return high, mid, low


def spread_table(table, spread, signed):
    entries = table.shape[0]
    stride = spread.shape[0] // entries
    for row in range(0, BLOCK, 2):
        both = table[:, row * PROJ : row * PROJ + LANES].astype(jnp.float32)
        spread[pl.ds(row, entries, stride=stride), :] = both
        spread[pl.ds(row + 1, entries, stride=stride), :] = pltpu.roll(both, PROJ, 1)
    for entry in range(entries):
        block = spread[pl.ds(entry * stride, BLOCK), :].astype(jnp.bfloat16)
        signed[pl.ds((entries + entry) * BLOCK, BLOCK), :] = block
        signed[pl.ds(entry * BLOCK, BLOCK), :] = -block


def lay_blocks(ids, signs, entries, signed, matrix, first, last):
    for j in range(first, last):
        start = pl.multiple_of((signs[j] * entries + ids[j]) * BLOCK, BLOCK)
        matrix[pl.ds(j * BLOCK, BLOCK), :] = signed[pl.ds(start, BLOCK), :]


def operand(x):
    x1, x2, x3 = split3(x)
    return jnp.concatenate([x1, x1, x2, x1, x3, x2], axis=1)


def products_with(left, act):
    a1, a2, a3 = split3(act)
    right = jnp.concatenate([a1, a2, a1, a3, a1, a2], axis=1)
    return lax.dot_general(left, right, (((1,), (1,)), ((), ())), preferred_element_type=jnp.float32)


def project_kernel(widths, fetch, ids, signs, table, rows_ref, *refs):
    if fetch:
        (out,), refs = refs[:1], refs[1:]
    else:
        (acts, lefts, products), refs = refs[:3], refs[3:]
    spread, signed, matrix, held, total, sems, *own = refs
    copies, starts, start = [], [], 0
    for c, width in enumerate(widths):
        columns = pl.ds(start, width)
        copies.append(pltpu.make_async_copy(rows_ref.at[:, columns], held.at[:, columns], sems.at[c]))
        starts.append(start)
        start += width
    if fetch:
        small = [
            pltpu.make_async_copy(source, kept, sems.at[len(widths) + k])
            for k, (source, kept) in enumerate(zip((table, ids, signs), own))
        ]
        for copy in small:
            copy.start()
        table, ids, signs = own
    for copy in copies:
        copy.start()
    if fetch:
        small[0].wait()
    spread_table(table, spread, signed)
    if fetch:
        small[1].wait()
        small[2].wait()
    lay = functools.partial(lay_blocks, ids, signs, table.shape[0], signed, matrix)
    lay(0, widths[0] // BLOCK)
    for c, copy in enumerate(copies):
        columns = pl.ds(starts[c], widths[c])
        copy.wait()
        if c + 1 < len(widths):
            lay(starts[c + 1] // BLOCK, (starts[c + 1] + widths[c + 1]) // BLOCK)
        part = lax.dot_general(
            matrix[columns, :PROJ],
            held[:, columns],
            (((0,), (1,)), ((), ())),
            preferred_element_type=jnp.float32,
        )
        if c == 0:
            total[...] = part
        else:
            total[...] += part
    pairs, _, tokens = out.shape if fetch else acts.shape
    for pair in range(pairs):
        sides = [total[:, pl.ds((2 * pair + side) * tokens, tokens)] for side in range(2)]
        if fetch:
            for side in range(2):
                out[pair, pl.ds(side * PROJ, PROJ), :] = sides[side]
        else:
            left = operand(jnp.concatenate(sides, axis=0))
            lefts[pair] = left
            products[pl.ds(pair * LANES, LANES), :] = products_with(left, acts[pair])


def project(values, ids, signs, table, acts, most, name):
    fetch = acts is None
    count, tokens, width = values.shape
    widths = chunks_of(width, most)
    rows = count * tokens
    entries = table.shape[0]
    smem = pl.BlockSpec(memory_space=pltpu.SMEM)
    vmem = pl.BlockSpec(memory_space=pltpu.VMEM)
    hbm = pl.BlockSpec(memory_space=pltpu.HBM)
    own = [
        pltpu.VMEM(table.shape, table.dtype),
        pltpu.SMEM(ids.shape, ids.dtype),
        pltpu.SMEM(signs.shape, signs.dtype),
    ]
    operands = [ids, signs, table, values.reshape(rows, width)]
    shapes = [jax.ShapeDtypeStruct((count // 2, LANES, tokens), jnp.float32)]
    if fetch:
        operands = [pltpu.with_memory_space_constraint(each, pltpu.HBM) for each in operands]
    else:
        operands.append(acts)
        shapes = [
            jax.ShapeDtypeStruct((count // 2, LANES, 6 * tokens), jnp.bfloat16),
            jax.ShapeDtypeStruct((count // 2 * LANES, LANES), jnp.float32),
        ]
    return pl.pallas_call(
        functools.partial(project_kernel, widths, fetch),
        out_shape=shapes,
        in_specs=[hbm] * 4 if fetch else [smem, smem, vmem, hbm, vmem],
        out_specs=[vmem] * len(shapes),
        scratch_shapes=[
            pltpu.VMEM((entries * (BLOCK + 8), LANES), jnp.float32),
            pltpu.VMEM((2 * entries * BLOCK, LANES), jnp.bfloat16),
            pltpu.VMEM((width, LANES), jnp.bfloat16),
            pltpu.VMEM((rows, width), jnp.bfloat16),
            pltpu.VMEM((PROJ, rows), jnp.float32),
            pltpu.SemaphoreType.DMA((len(widths) + 3,)),
        ]
        + (own if fetch else []),
        compiler_params=pltpu.CompilerParams(vmem_limit_bytes=VMEM_BYTES),
        cost_estimate=pl.CostEstimate(
            flops=2 * rows * width * LANES, bytes_accessed=2 * rows * width, transcendentals=0
        ),
        name=name,
    )(*operands)


def kron_kernel(cuts, lefts, own, act, *refs):
    parts = cuts[1]
    outs, rows, products = refs[:-2], refs[-2], refs[-1]
    pairs = act.shape[0]
    for pair in range(pairs):
        into = pl.ds(pair * LANES, LANES)
        products[into, :] = own[into, :] + products_with(lefts[pair], act[pair])
    count = 2 * pairs
    lower = lax.broadcasted_iota(jnp.int32, (count, LANES), 1) < PROJ
    even = lax.broadcasted_iota(jnp.int32, (count, LANES), 0) % 2 == 0
    here = even == lower
    tiles = rows.shape[2] // LANES // cuts[0]
    for tile in range(PROJ * PROJ // LANES):
        both = []
        for p in (2 * tile, 2 * tile + 1):
            v = products[pl.ds(p, count, stride=PROJ), :]
            both.append(jnp.where(here, v, pltpu.roll(v, PROJ, 1)))
        block, part, within = tile // tiles // parts, tile // tiles % parts, tile % tiles
        rows[part, :, pl.ds((block * tiles + within) * LANES, LANES)] = jnp.where(lower, both[0], both[1])
    for k, out in enumerate(outs):
        part = lax.rem(lax.axis_index("seq") + k, parts) if parts > 1 else 0
        out[...] = rows[part]


def kron_of(lefts, own, act, cuts):
    pairs = lefts.shape[0]
    parts = cuts[1]
    width = PROJ * PROJ // parts
    vmem = pl.BlockSpec(memory_space=pltpu.VMEM)
    return pl.pallas_call(
        functools.partial(kron_kernel, cuts),
        out_shape=[jax.ShapeDtypeStruct((2 * pairs, width), jnp.float32)] * parts,
        in_specs=[vmem] * 3,
        out_specs=[vmem] * parts,
        scratch_shapes=[
            pltpu.VMEM((parts, 2 * pairs, width), jnp.float32),
            pltpu.VMEM((pairs * LANES, LANES), jnp.float32),
        ],
        compiler_params=pltpu.CompilerParams(vmem_limit_bytes=VMEM_BYTES),
        name="kron",
    )(lefts, own, act)


def parcels_kernel(here, there, *parcels):
    count = here.shape[0]
    dp = len(parcels)
    width = parcels[0].shape[1]
    core, chip = lax.axis_index("seq"), lax.axis_index("tensor") * 2
    blocks = [chip + core, chip + 1 - core]
    for k, parcel in enumerate(parcels):
        for step, block in enumerate(blocks + [lax.rem(lax.axis_index("dp") + k, dp)]):
            lanes = pl.ds(pl.multiple_of(block * width, LANES), width)
            parcel[pl.ds(step * count, count), :] = here[:, lanes] + there[:, lanes]


def parcels_of(here, there, dp):
    count, width = here.shape
    vmem = pl.BlockSpec(memory_space=pltpu.VMEM)
    return pl.pallas_call(
        parcels_kernel,
        out_shape=[jax.ShapeDtypeStruct((3 * count, width // dp), jnp.float32)] * dp,
        in_specs=[vmem] * 2,
        out_specs=[vmem] * dp,
        compiler_params=pltpu.CompilerParams(vmem_limit_bytes=VMEM_BYTES),
        name="parcels",
    )(here, there)


def bundle_kernel(*refs):
    parcels, out = refs[:-1], refs[-1]
    rows = 2 * parcels[0].shape[0] // 3
    for k, parcel in enumerate(parcels):
        out[pl.ds(k * rows, rows), :] = parcel[pl.ds(rows // 2, rows), :]


def bundle_of(parcels):
    rows, width = parcels[0].shape
    vmem = pl.BlockSpec(memory_space=pltpu.VMEM)
    return pl.pallas_call(
        bundle_kernel,
        out_shape=jax.ShapeDtypeStruct((2 * rows // 3 * len(parcels), width), jnp.float32),
        in_specs=[vmem] * len(parcels),
        out_specs=vmem,
        compiler_params=pltpu.CompilerParams(vmem_limit_bytes=VMEM_BYTES),
        name="bundle",
    )(*parcels)


def left_operand(x):
    x1, x2, x3 = split3(x)
    return jnp.concatenate([x1, x1, x2, x1, x3, x2, x2, x3], axis=0).T


def right_operand(x):
    x1, x2, x3 = split3(x)
    return jnp.concatenate([x1, x2, x1, x3, x1, x2, x3, x2], axis=0)


def own_halves(parcels):
    rows = parcels[0].shape[0] // 3
    left = jnp.concatenate([parcel[pl.ds(0, rows), :] for parcel in parcels], axis=0)
    right = jnp.concatenate([parcel[pl.ds(2 * rows, rows), :] for parcel in parcels], axis=0)
    return left, right


def halves_at(part):
    core = lax.axis_index("seq")
    return [pl.ds(pl.multiple_of(place * part, part), part) for place in (core, 1 - core)]


TILE = 256


def quadrant_kernel(scale, *refs):
    parcels, (out, made, sems) = refs[:-3], refs[-3:]
    part = parcels[0].shape[1]
    left, right = own_halves(parcels)
    left, right = left_operand(left), right_operand(right * scale)
    here, _ = halves_at(part)
    copies = []
    for k in range(part // TILE):
        rows = slice(k * TILE, (k + 1) * TILE)
        made[rows, :] = jnp.dot(left[rows], right, preferred_element_type=jnp.float32)
        into = pl.ds(pl.multiple_of(lax.axis_index("seq") * part + k * TILE, TILE), TILE)
        copies.append(pltpu.make_async_copy(made.at[rows], out.at[into, here], sems.at[k]))
        copies[-1].start()
    for copy in copies:
        copy.wait()


def fisher_kernel(scale, begun, bundle, *refs):
    del begun
    parcels, (mine, out, made, kept, sems) = refs[:-5], refs[-5:]
    rows, part = parcels[0].shape[0] // 3, parcels[0].shape[1]
    here, there = halves_at(part)
    kept[:, here] = parcels[0][pl.ds(0, rows), :]
    kept[:, there] = bundle[pl.ds(0, rows), :]
    copies = [pltpu.make_async_copy(kept, mine, sems.at[0])]
    copies[0].start()
    left, right = own_halves(parcels)
    count = len(parcels)
    other_left = jnp.concatenate([bundle[pl.ds(2 * k * rows, rows), :] for k in range(count)], axis=0)
    other_right = jnp.concatenate([bundle[pl.ds((2 * k + 1) * rows, rows), :] for k in range(count)], axis=0)
    left, other_left = left_operand(left), left_operand(other_left)
    right, other_right = right_operand(right * scale), right_operand(other_right * scale)
    for k, (a, b, into) in enumerate(
        (
            (other_left, right, (there, here)),
            (other_left, other_right, (there, there)),
            (left, other_right, (here, there)),
        )
    ):
        made[k] = jnp.dot(a, b, preferred_element_type=jnp.float32)
        copies.append(pltpu.make_async_copy(made.at[k], out.at[into], sems.at[k + 1]))
        copies[-1].start()
    for copy in copies:
        copy.wait()


def quadrant_of(parcels):
    rows, part = parcels[0].shape
    total = rows // 3 * len(parcels)
    return pl.pallas_call(
        functools.partial(quadrant_kernel, 1.0 / total),
        out_shape=jax.ShapeDtypeStruct((2 * part, 2 * part), jnp.float32),
        in_specs=[pl.BlockSpec(memory_space=pltpu.VMEM)] * len(parcels),
        out_specs=pl.BlockSpec(memory_space=pltpu.HBM),
        scratch_shapes=[pltpu.VMEM((part, part), jnp.float32), pltpu.SemaphoreType.DMA((part // TILE,))],
        compiler_params=pltpu.CompilerParams(vmem_limit_bytes=VMEM_BYTES),
        cost_estimate=pl.CostEstimate(flops=2**28, bytes_accessed=4 * part * part, transcendentals=0),
        name="quadrant",
    )(*parcels)


def fisher_block(begun, parcels, bundle):
    rows, part = parcels[0].shape
    rows //= 3
    width = 2 * part
    hbm = pl.BlockSpec(memory_space=pltpu.HBM)
    vmem = pl.BlockSpec(memory_space=pltpu.VMEM)
    return pl.pallas_call(
        functools.partial(fisher_kernel, 1.0 / (rows * len(parcels))),
        out_shape=[
            jax.ShapeDtypeStruct((rows, width), jnp.float32),
            jax.ShapeDtypeStruct((width, width), jnp.float32),
        ],
        in_specs=[hbm] + [vmem] * (1 + len(parcels)),
        out_specs=[hbm] * 2,
        scratch_shapes=[
            pltpu.VMEM((3, part, part), jnp.float32),
            pltpu.VMEM((rows, width), jnp.float32),
            pltpu.SemaphoreType.DMA((4,)),
        ],
        input_output_aliases={0: 1},
        compiler_params=pltpu.CompilerParams(vmem_limit_bytes=VMEM_BYTES),
        name="fisher",
    )(begun, bundle, *parcels)


def local(acts, grads, in_ids, in_signs, out_ids, out_signs, in_table, out_table):
    tensor, seq, dp = (lax.axis_size(name) for name in ("tensor", "seq", "dp"))
    shards = tensor * seq
    small = tensor == 2 and seq == 2 and dp == 4
    swap = [(0, 1), (1, 0)]

    (act,) = project(acts, in_ids, in_signs, in_table, None, 512, "project_acts")
    if tensor == 2:
        other = lax.ppermute(act, "tensor", swap)
    else:
        act = lax.psum(act, "tensor")
        other = jnp.zeros_like(act)
    lefts, own = project(grads, out_ids, out_signs, out_table, act, 1024, "project_grads")
    krons = kron_of(lefts, own, other, (shards, seq) if small else (1, 1))

    if not small:
        kron = lax.psum(krons[0], ("tensor", "seq"))
        width = kron.shape[1] // shards
        place = lax.axis_index("tensor") * seq + lax.axis_index("seq")
        mine = lax.dynamic_slice_in_dim(kron, place * width, width, 1)
        every = lax.all_gather(kron, "dp", axis=0, tiled=True)
        left = lax.dynamic_slice_in_dim(every, place * width, width, 1)
        columns = kron.shape[1] // dp
        right = lax.dynamic_slice_in_dim(every, lax.axis_index("dp") * columns, columns, 1)
        fisher = lax.dot_general(
            left, right, (((0,), (0,)), ((), ())), precision=lax.Precision.HIGHEST
        ) / left.shape[0]
        return mine, fisher

    part = krons[0] + lax.ppermute(krons[1], "seq", swap)
    parcels = list(parcels_of(part, lax.ppermute(part, "tensor", swap), dp))
    for k in range(1, dp):
        parcels[k] = lax.ppermute(parcels[k], "dp", [(d, (d + k) % dp) for d in range(dp)])
    bundle = lax.ppermute(bundle_of(parcels), "seq", swap)
    mine, fisher = fisher_block(quadrant_of(parcels), parcels, bundle)
    return mine, fisher


def solution(mesh):
    in_specs = (
        P(("groups", "dp"), "seq", "tensor"),
        P(("groups", "dp"), "seq", "tensor"),
        P("tensor"),
        P("tensor"),
        P("tensor"),
        P("tensor"),
        P(),
        P(),
    )
    out_specs = (P(("groups", "dp"), ("tensor", "seq")), P(("groups", "tensor", "seq"), "dp"))
    return jax.shard_map(local, mesh=mesh, in_specs=in_specs, out_specs=out_specs, check_vma=False)
```

```python
import functools

import jax
import jax.numpy as jnp
from jax import lax
from jax.experimental import pallas as pl
from jax.experimental.pallas import tpu as pltpu
from jax.sharding import PartitionSpec as P

PROJ = 64
BLOCK = 64
LANES = 128
STRIDE = 72
VMEM_BYTES = 48 * 1024 * 1024


def chunks_of(width, most):
    if width >= 4 * most:
        inner = width - most
        ends = [most // 2] * 2
    else:
        inner, ends = width, []
    chunk = most
    while inner % chunk:
        chunk -= LANES
    return ends[:1] + [chunk] * (inner // chunk) + ends[1:]


def split3(x):
    high = x.astype(jnp.bfloat16)
    rest = x - high.astype(jnp.float32)
    mid = rest.astype(jnp.bfloat16)
    low = (rest - mid.astype(jnp.float32)).astype(jnp.bfloat16)
    return high, mid, low


def spread_table(table, spread):
    entries = table.shape[0]
    for row in range(0, BLOCK, 2):
        both = table[:, row * PROJ : row * PROJ + LANES].astype(jnp.float32)
        spread[pl.ds(row, entries, stride=STRIDE), :] = both
        spread[pl.ds(row + 1, entries, stride=STRIDE), :] = pltpu.roll(both, PROJ, 1)


def sign_table(spread, signed):
    entries = spread.shape[0] // STRIDE
    for entry in range(entries):
        block = spread[pl.ds(entry * STRIDE, BLOCK), :].astype(jnp.bfloat16)
        signed[pl.ds((entries + entry) * BLOCK, BLOCK), :] = block
        signed[pl.ds(entry * BLOCK, BLOCK), :] = -block


def lay_blocks(ids, signs, spread, signed, matrix, first, last):
    entries = spread.shape[0] // STRIDE
    for j in range(first, last):
        if signed is None:
            start = pl.multiple_of(ids[j] * STRIDE, 8)
            sign = (2 * signs[j] - 1).astype(jnp.float32)
            block = (spread[pl.ds(start, BLOCK), :] * sign).astype(jnp.bfloat16)
        else:
            start = pl.multiple_of((signs[j] * entries + ids[j]) * BLOCK, BLOCK)
            block = signed[pl.ds(start, BLOCK), :]
        matrix[pl.ds(j * BLOCK, BLOCK), :] = block


def operand(x):
    x1, x2, x3 = split3(x)
    return jnp.concatenate([x1, x1, x2, x1, x3, x2], axis=1)


def products_with(left, act):
    a1, a2, a3 = split3(act)
    right = jnp.concatenate([a1, a2, a1, a3, a1, a2], axis=1)
    return lax.dot_general(left, right, (((1,), (1,)), ((), ())), preferred_element_type=jnp.float32)


def project_kernel(widths, fetch, ids, signs, table, rows_ref, *refs):
    if fetch:
        (out,), refs = refs[:1], refs[1:]
    else:
        (acts, lefts, products), refs = refs[:3], refs[3:]
    spread, signed, matrix, held, total, sems, *own = refs
    copies, starts, start = [], [], 0
    for c, width in enumerate(widths):
        columns = pl.ds(start, width)
        copies.append(pltpu.make_async_copy(rows_ref.at[:, columns], held.at[:, columns], sems.at[c]))
        starts.append(start)
        start += width
    if fetch:
        small = [
            pltpu.make_async_copy(source, kept, sems.at[len(widths) + k])
            for k, (source, kept) in enumerate(zip((table, ids, signs), own))
        ]
        for copy in small:
            copy.start()
        table, ids, signs = own
    for copy in copies:
        copy.start()
    if fetch:
        small[0].wait()
    spread_table(table, spread)
    if fetch:
        signed = None
    else:
        sign_table(spread, signed)
    if fetch:
        small[1].wait()
        small[2].wait()
    lay = functools.partial(lay_blocks, ids, signs, spread, signed, matrix)
    lay(0, widths[0] // BLOCK)
    for c, copy in enumerate(copies):
        columns = pl.ds(starts[c], widths[c])
        copy.wait()
        if c + 1 < len(widths):
            lay(starts[c + 1] // BLOCK, (starts[c + 1] + widths[c + 1]) // BLOCK)
        part = lax.dot_general(
            matrix[columns, :PROJ],
            held[:, columns],
            (((0,), (1,)), ((), ())),
            preferred_element_type=jnp.float32,
        )
        if c == 0:
            total[...] = part
        else:
            total[...] += part
    pairs, _, tokens = out.shape if fetch else acts.shape
    for pair in range(pairs):
        sides = [total[:, pl.ds((2 * pair + side) * tokens, tokens)] for side in range(2)]
        if fetch:
            for side in range(2):
                out[pair, pl.ds(side * PROJ, PROJ), :] = sides[side]
        else:
            left = operand(jnp.concatenate(sides, axis=0))
            lefts[pair] = left
            products[pl.ds(pair * LANES, LANES), :] = products_with(left, acts[pair])


def project(values, ids, signs, table, acts, most, name):
    fetch = acts is None
    count, tokens, width = values.shape
    widths = chunks_of(width, most)
    rows = count * tokens
    entries = table.shape[0]
    smem = pl.BlockSpec(memory_space=pltpu.SMEM)
    vmem = pl.BlockSpec(memory_space=pltpu.VMEM)
    hbm = pl.BlockSpec(memory_space=pltpu.HBM)
    own = [
        pltpu.VMEM(table.shape, table.dtype),
        pltpu.SMEM(ids.shape, ids.dtype),
        pltpu.SMEM(signs.shape, signs.dtype),
    ]
    operands = [ids, signs, table, values.reshape(rows, width)]
    shapes = [jax.ShapeDtypeStruct((count // 2, LANES, tokens), jnp.float32)]
    if fetch:
        operands = [pltpu.with_memory_space_constraint(each, pltpu.HBM) for each in operands]
    else:
        operands.append(acts)
        shapes = [
            jax.ShapeDtypeStruct((count // 2, LANES, 6 * tokens), jnp.bfloat16),
            jax.ShapeDtypeStruct((count // 2 * LANES, LANES), jnp.float32),
        ]
    return pl.pallas_call(
        functools.partial(project_kernel, widths, fetch),
        out_shape=shapes,
        in_specs=[hbm] * 4 if fetch else [smem, smem, vmem, hbm, vmem],
        out_specs=[vmem] * len(shapes),
        scratch_shapes=[
            pltpu.VMEM((entries * STRIDE, LANES), jnp.float32),
            pltpu.VMEM((2 * entries * BLOCK, LANES), jnp.bfloat16),
            pltpu.VMEM((width, LANES), jnp.bfloat16),
            pltpu.VMEM((rows, width), jnp.bfloat16),
            pltpu.VMEM((PROJ, rows), jnp.float32),
            pltpu.SemaphoreType.DMA((len(widths) + 3,)),
        ]
        + (own if fetch else []),
        compiler_params=pltpu.CompilerParams(vmem_limit_bytes=VMEM_BYTES),
        cost_estimate=pl.CostEstimate(
            flops=2 * rows * width * LANES, bytes_accessed=2 * rows * width, transcendentals=0
        ),
        name=name,
    )(*operands)


def kron_kernel(cuts, lefts, own, act, *refs):
    parts = cuts[1]
    outs, rows, products = refs[:-2], refs[-2], refs[-1]
    pairs = act.shape[0]
    for pair in range(pairs):
        both = own[pl.ds(pair * LANES, LANES), :] + products_with(lefts[pair], act[pair])
        for side in range(2):
            products[pl.ds((2 * pair + side) * STRIDE, PROJ), :] = both[side * PROJ : (side + 1) * PROJ]
    count = 2 * pairs
    lower = lax.broadcasted_iota(jnp.int32, (count, LANES), 1) < PROJ
    even = lax.broadcasted_iota(jnp.int32, (count, LANES), 0) % 2 == 0
    here = even == lower
    tiles = rows.shape[2] // LANES // cuts[0]
    for tile in range(PROJ * PROJ // LANES):
        both = []
        for p in (2 * tile, 2 * tile + 1):
            v = products[pl.ds(p, count, stride=STRIDE), :]
            both.append(jnp.where(here, v, pltpu.roll(v, PROJ, 1)))
        block, part, within = tile // tiles // parts, tile // tiles % parts, tile % tiles
        rows[part, :, pl.ds((block * tiles + within) * LANES, LANES)] = jnp.where(lower, both[0], both[1])
    for k, out in enumerate(outs):
        part = lax.rem(lax.axis_index("seq") + k, parts) if parts > 1 else 0
        out[...] = rows[part]


def kron_of(lefts, own, act, cuts):
    pairs = lefts.shape[0]
    parts = cuts[1]
    width = PROJ * PROJ // parts
    vmem = pl.BlockSpec(memory_space=pltpu.VMEM)
    return pl.pallas_call(
        functools.partial(kron_kernel, cuts),
        out_shape=[jax.ShapeDtypeStruct((2 * pairs, width), jnp.float32)] * parts,
        in_specs=[vmem] * 3,
        out_specs=[vmem] * parts,
        scratch_shapes=[
            pltpu.VMEM((parts, 2 * pairs, width), jnp.float32),
            pltpu.VMEM((2 * pairs * STRIDE, LANES), jnp.float32),
        ],
        compiler_params=pltpu.CompilerParams(vmem_limit_bytes=VMEM_BYTES),
        name="kron",
    )(lefts, own, act)


def parcels_kernel(here, there, *parcels):
    count = here.shape[0]
    width = parcels[0].shape[1]
    core, chip = lax.axis_index("seq"), lax.axis_index("tensor") * 2
    blocks = [chip + core, chip + 1 - core]
    for k, parcel in enumerate(parcels):
        for step, block in enumerate(blocks + [lax.axis_index("dp") ^ k]):
            lanes = pl.ds(pl.multiple_of(block * width, LANES), width)
            parcel[pl.ds(step * count, count), :] = here[:, lanes] + there[:, lanes]


def parcels_of(here, there, dp):
    count, width = here.shape
    vmem = pl.BlockSpec(memory_space=pltpu.VMEM)
    return pl.pallas_call(
        parcels_kernel,
        out_shape=[jax.ShapeDtypeStruct((3 * count, width // dp), jnp.float32)] * dp,
        in_specs=[vmem] * 2,
        out_specs=[vmem] * dp,
        compiler_params=pltpu.CompilerParams(vmem_limit_bytes=VMEM_BYTES),
        name="parcels",
    )(here, there)


def bundle_kernel(*refs):
    parcels, out = refs[:-1], refs[-1]
    rows = 2 * parcels[0].shape[0] // 3
    for k, parcel in enumerate(parcels):
        out[pl.ds(k * rows, rows), :] = parcel[pl.ds(rows // 2, rows), :]


def bundle_of(parcels):
    rows, width = parcels[0].shape
    vmem = pl.BlockSpec(memory_space=pltpu.VMEM)
    return pl.pallas_call(
        bundle_kernel,
        out_shape=jax.ShapeDtypeStruct((2 * rows // 3 * len(parcels), width), jnp.float32),
        in_specs=[vmem] * len(parcels),
        out_specs=vmem,
        compiler_params=pltpu.CompilerParams(vmem_limit_bytes=VMEM_BYTES),
        name="bundle",
    )(*parcels)


def left_operand(x):
    x1, x2, x3 = split3(x)
    return jnp.concatenate([x1, x1, x2, x1, x3, x2, x2, x3], axis=0).T


def right_operand(x):
    x1, x2, x3 = split3(x)
    return jnp.concatenate([x1, x2, x1, x3, x1, x2, x3, x2], axis=0)


def own_halves(parcels):
    rows = parcels[0].shape[0] // 3
    left = jnp.concatenate([parcel[pl.ds(0, rows), :] for parcel in parcels], axis=0)
    right = jnp.concatenate([parcel[pl.ds(2 * rows, rows), :] for parcel in parcels], axis=0)
    return left, right


def halves_at(part):
    core = lax.axis_index("seq")
    return [pl.ds(pl.multiple_of(place * part, part), part) for place in (core, 1 - core)]


TILE = 256


def quadrant_kernel(scale, *refs):
    parcels, (out, left_ref, right_ref, made, sems) = refs[:-5], refs[-5:]
    part = parcels[0].shape[1]
    left, right = own_halves(parcels)
    left, right = left_operand(left), right_operand(right * scale)
    left_ref[...], right_ref[...] = left, right
    here, _ = halves_at(part)
    copies = []
    for k in range(part // TILE):
        rows = slice(k * TILE, (k + 1) * TILE)
        made[rows, :] = jnp.dot(left[rows], right, preferred_element_type=jnp.float32)
        into = pl.ds(pl.multiple_of(lax.axis_index("seq") * part + k * TILE, TILE), TILE)
        copies.append(pltpu.make_async_copy(made.at[rows], out.at[into, here], sems.at[k]))
        copies[-1].start()
    for copy in copies:
        copy.wait()


def fisher_kernel(scale, begun, left, right, bundle, *refs):
    del begun
    parcels, (mine, out, made, kept, sems) = refs[:-5], refs[-5:]
    rows, part = parcels[0].shape[0] // 3, parcels[0].shape[1]
    here, there = halves_at(part)
    kept[:, here] = parcels[0][pl.ds(0, rows), :]
    kept[:, there] = bundle[pl.ds(0, rows), :]
    copies = [pltpu.make_async_copy(kept, mine, sems.at[0])]
    copies[0].start()
    count = len(parcels)
    other_left = jnp.concatenate([bundle[pl.ds(2 * k * rows, rows), :] for k in range(count)], axis=0)
    other_right = jnp.concatenate([bundle[pl.ds((2 * k + 1) * rows, rows), :] for k in range(count)], axis=0)
    left, other_left = left[...], left_operand(other_left)
    right, other_right = right[...], right_operand(other_right * scale)
    for k, (a, b, into) in enumerate(
        (
            (other_left, right, (there, here)),
            (other_left, other_right, (there, there)),
            (left, other_right, (here, there)),
        )
    ):
        made[k] = jnp.dot(a, b, preferred_element_type=jnp.float32)
        copies.append(pltpu.make_async_copy(made.at[k], out.at[into], sems.at[k + 1]))
        copies[-1].start()
    for copy in copies:
        copy.wait()


def quadrant_of(parcels):
    rows, part = parcels[0].shape
    total = rows // 3 * len(parcels)
    vmem = pl.BlockSpec(memory_space=pltpu.VMEM)
    return pl.pallas_call(
        functools.partial(quadrant_kernel, 1.0 / total),
        out_shape=[
            jax.ShapeDtypeStruct((2 * part, 2 * part), jnp.float32),
            jax.ShapeDtypeStruct((part, 8 * total), jnp.bfloat16),
            jax.ShapeDtypeStruct((8 * total, part), jnp.bfloat16),
        ],
        in_specs=[vmem] * len(parcels),
        out_specs=[pl.BlockSpec(memory_space=pltpu.HBM), vmem, vmem],
        scratch_shapes=[pltpu.VMEM((part, part), jnp.float32), pltpu.SemaphoreType.DMA((part // TILE,))],
        compiler_params=pltpu.CompilerParams(vmem_limit_bytes=VMEM_BYTES),
        cost_estimate=pl.CostEstimate(flops=2**28, bytes_accessed=4 * part * part, transcendentals=0),
        name="quadrant",
    )(*parcels)


def fisher_block(begun, parcels, bundle):
    rows, part = parcels[0].shape
    rows //= 3
    width = 2 * part
    hbm = pl.BlockSpec(memory_space=pltpu.HBM)
    vmem = pl.BlockSpec(memory_space=pltpu.VMEM)
    return pl.pallas_call(
        functools.partial(fisher_kernel, 1.0 / (rows * len(parcels))),
        out_shape=[
            jax.ShapeDtypeStruct((rows, width), jnp.float32),
            jax.ShapeDtypeStruct((width, width), jnp.float32),
        ],
        in_specs=[hbm] + [vmem] * (3 + len(parcels)),
        out_specs=[hbm] * 2,
        scratch_shapes=[
            pltpu.VMEM((3, part, part), jnp.float32),
            pltpu.VMEM((rows, width), jnp.float32),
            pltpu.SemaphoreType.DMA((4,)),
        ],
        input_output_aliases={0: 1},
        compiler_params=pltpu.CompilerParams(vmem_limit_bytes=VMEM_BYTES),
        name="fisher",
    )(*begun, bundle, *parcels)


def local(acts, grads, in_ids, in_signs, out_ids, out_signs, in_table, out_table):
    tensor, seq, dp = (lax.axis_size(name) for name in ("tensor", "seq", "dp"))
    shards = tensor * seq
    small = tensor == 2 and seq == 2 and dp == 4
    swap = [(0, 1), (1, 0)]

    (act,) = project(acts, in_ids, in_signs, in_table, None, 512, "project_acts")
    if tensor == 2:
        other = lax.ppermute(act, "tensor", swap)
    else:
        act = lax.psum(act, "tensor")
        other = jnp.zeros_like(act)
    lefts, own = project(grads, out_ids, out_signs, out_table, act, 1024, "project_grads")
    krons = kron_of(lefts, own, other, (shards, seq) if small else (1, 1))

    if not small:
        kron = lax.psum(krons[0], ("tensor", "seq"))
        width = kron.shape[1] // shards
        place = lax.axis_index("tensor") * seq + lax.axis_index("seq")
        mine = lax.dynamic_slice_in_dim(kron, place * width, width, 1)
        every = lax.all_gather(kron, "dp", axis=0, tiled=True)
        left = lax.dynamic_slice_in_dim(every, place * width, width, 1)
        columns = kron.shape[1] // dp
        right = lax.dynamic_slice_in_dim(every, lax.axis_index("dp") * columns, columns, 1)
        fisher = lax.dot_general(
            left, right, (((0,), (0,)), ((), ())), precision=lax.Precision.HIGHEST
        ) / left.shape[0]
        return mine, fisher

    part = krons[0] + lax.ppermute(krons[1], "seq", swap)
    parcels = list(parcels_of(part, lax.ppermute(part, "tensor", swap), dp))
    for k in range(1, dp):
        parcels[k] = lax.ppermute(parcels[k], "dp", [(d, d ^ k) for d in range(dp)])
    bundle = lax.ppermute(bundle_of(parcels), "seq", swap)
    mine, fisher = fisher_block(quadrant_of(parcels), parcels, bundle)
    return mine, fisher


def solution(mesh):
    in_specs = (
        P(("groups", "dp"), "seq", "tensor"),
        P(("groups", "dp"), "seq", "tensor"),
        P("tensor"),
        P("tensor"),
        P("tensor"),
        P("tensor"),
        P(),
        P(),
    )
    out_specs = (P(("groups", "dp"), ("tensor", "seq")), P(("groups", "tensor", "seq"), "dp"))
    return jax.shard_map(local, mesh=mesh, in_specs=in_specs, out_specs=out_specs, check_vma=False)
```

```python
import functools

import jax
import jax.numpy as jnp
from jax import lax
from jax.experimental import pallas as pl
from jax.experimental.pallas import tpu as pltpu
from jax.sharding import PartitionSpec as P

PROJ = 64
BLOCK = 64
LANES = 128
STRIDE = 72
VMEM_BYTES = 48 * 1024 * 1024


def chunk_of(width, most):
    chunk = most
    while width % chunk:
        chunk -= LANES
    return chunk


def split3(x):
    high = x.astype(jnp.bfloat16)
    rest = x - high.astype(jnp.float32)
    mid = rest.astype(jnp.bfloat16)
    low = (rest - mid.astype(jnp.float32)).astype(jnp.bfloat16)
    return high, mid, low


def spread_table(table, spread):
    entries = table.shape[0]
    for row in range(0, BLOCK, 2):
        both = table[:, row * PROJ : row * PROJ + LANES].astype(jnp.float32)
        spread[pl.ds(row, entries, stride=STRIDE), :] = both
        spread[pl.ds(row + 1, entries, stride=STRIDE), :] = pltpu.roll(both, PROJ, 1)


def sign_table(spread, signed):
    entries = spread.shape[0] // STRIDE
    most = 4 if entries % 4 == 0 else 1

    def some(step, carry):
        for part in range(most):
            entry = step * most + part
            start = pl.multiple_of(entry * STRIDE, 8)
            block = spread[pl.ds(start, BLOCK), :].astype(jnp.bfloat16)
            signed[pl.ds(pl.multiple_of((entries + entry) * BLOCK, BLOCK), BLOCK), :] = block
            signed[pl.ds(pl.multiple_of(entry * BLOCK, BLOCK), BLOCK), :] = -block
        return carry

    lax.fori_loop(0, entries // most, some, 0)


def lay_blocks(ids, signs, spread, signed, matrix, first, count):
    entries = spread.shape[0] // STRIDE
    for part in range(count):
        j = first + part
        if signed is None:
            start = pl.multiple_of(ids[j] * STRIDE, 8)
            sign = (2 * signs[j] - 1).astype(jnp.float32)
            block = (spread[pl.ds(start, BLOCK), :] * sign).astype(jnp.bfloat16)
        else:
            start = pl.multiple_of((signs[j] * entries + ids[j]) * BLOCK, BLOCK)
            block = signed[pl.ds(start, BLOCK), :]
        matrix[pl.ds(part * BLOCK, BLOCK), :] = block


def operand(x):
    x1, x2, x3 = split3(x)
    return jnp.concatenate([x1, x1, x2, x1, x3, x2], axis=1)


def products_with(left, act):
    a1, a2, a3 = split3(act)
    right = jnp.concatenate([a1, a2, a1, a3, a1, a2], axis=1)
    return lax.dot_general(left, right, (((1,), (1,)), ((), ())), preferred_element_type=jnp.float32)


def project_kernel(fetch, ids, signs, table, rows_ref, *refs):
    if fetch:
        (out,), refs = refs[:1], refs[1:]
    else:
        (acts, lefts, products), refs = refs[:3], refs[3:]
    spread, signed, matrix, held, total, sems, *own = refs
    chunks, _, chunk = held.shape

    def copy_of(c):
        columns = pl.ds(pl.multiple_of(c * chunk, LANES), chunk)
        return pltpu.make_async_copy(rows_ref.at[:, columns], held.at[c], sems.at[c])

    if fetch:
        small = [
            pltpu.make_async_copy(source, kept, sems.at[chunks + k])
            for k, (source, kept) in enumerate(zip((table, ids, signs), own))
        ]
        for copy in small:
            copy.start()
        table, ids, signs = own
    for c in range(chunks):
        copy_of(c).start()
    if fetch:
        small[0].wait()
    spread_table(table, spread)
    if fetch:
        signed = None
    else:
        sign_table(spread, signed)
    if fetch:
        small[1].wait()
        small[2].wait()
    lay = functools.partial(lay_blocks, ids, signs, spread, signed)
    blocks = chunk // BLOCK
    total[...] = jnp.zeros_like(total)
    lay(matrix.at[0], 0, blocks)

    def some(c, carry):
        copy_of(c).wait()
        now = lax.rem(c, 2)
        part = lax.dot_general(
            matrix[now, :, :PROJ], held[c], (((0,), (1,)), ((), ())), preferred_element_type=jnp.float32
        )
        lay(matrix.at[1 - now], lax.min(c + 1, chunks - 1) * blocks, blocks)
        total[...] += part
        return carry

    lax.fori_loop(0, chunks, some, 0)
    pairs, _, tokens = out.shape if fetch else acts.shape
    for pair in range(pairs):
        sides = [total[:, pl.ds((2 * pair + side) * tokens, tokens)] for side in range(2)]
        if fetch:
            for side in range(2):
                out[pair, pl.ds(side * PROJ, PROJ), :] = sides[side]
        else:
            left = operand(jnp.concatenate(sides, axis=0))
            lefts[pair] = left
            products[pl.ds(pair * LANES, LANES), :] = products_with(left, acts[pair])


def project(values, ids, signs, table, acts, most, name):
    fetch = acts is None
    count, tokens, width = values.shape
    chunk = chunk_of(width, most)
    chunks = width // chunk
    rows = count * tokens
    entries = table.shape[0]
    smem = pl.BlockSpec(memory_space=pltpu.SMEM)
    vmem = pl.BlockSpec(memory_space=pltpu.VMEM)
    hbm = pl.BlockSpec(memory_space=pltpu.HBM)
    own = [
        pltpu.VMEM(table.shape, table.dtype),
        pltpu.SMEM(ids.shape, ids.dtype),
        pltpu.SMEM(signs.shape, signs.dtype),
    ]
    operands = [ids, signs, table, values.reshape(rows, width)]
    shapes = [jax.ShapeDtypeStruct((count // 2, LANES, tokens), jnp.float32)]
    if fetch:
        operands = [pltpu.with_memory_space_constraint(each, pltpu.HBM) for each in operands]
    else:
        operands.append(acts)
        shapes = [
            jax.ShapeDtypeStruct((count // 2, LANES, 6 * tokens), jnp.bfloat16),
            jax.ShapeDtypeStruct((count // 2 * LANES, LANES), jnp.float32),
        ]
    return pl.pallas_call(
        functools.partial(project_kernel, fetch),
        out_shape=shapes,
        in_specs=[hbm] * 4 if fetch else [smem, smem, vmem, hbm, vmem],
        out_specs=[vmem] * len(shapes),
        scratch_shapes=[
            pltpu.VMEM((entries * STRIDE, LANES), jnp.float32),
            pltpu.VMEM((2 * entries * BLOCK, LANES), jnp.bfloat16),
            pltpu.VMEM((2, chunk, LANES), jnp.bfloat16),
            pltpu.VMEM((chunks, rows, chunk), jnp.bfloat16),
            pltpu.VMEM((PROJ, rows), jnp.float32),
            pltpu.SemaphoreType.DMA((chunks + 3,)),
        ]
        + (own if fetch else []),
        compiler_params=pltpu.CompilerParams(vmem_limit_bytes=VMEM_BYTES),
        cost_estimate=pl.CostEstimate(
            flops=2 * rows * width * LANES, bytes_accessed=2 * rows * width, transcendentals=0
        ),
        name=name,
    )(*operands)


def kron_kernel(cuts, lefts, own, act, *refs):
    parts = cuts[1]
    outs, rows, products = refs[:-2], refs[-2], refs[-1]
    pairs = act.shape[0]
    for pair in range(pairs):
        both = own[pl.ds(pair * LANES, LANES), :] + products_with(lefts[pair], act[pair])
        for side in range(2):
            products[pl.ds((2 * pair + side) * STRIDE, PROJ), :] = both[side * PROJ : (side + 1) * PROJ]
    count = 2 * pairs
    lower = lax.broadcasted_iota(jnp.int32, (count, LANES), 1) < PROJ
    even = lax.broadcasted_iota(jnp.int32, (count, LANES), 0) % 2 == 0
    here = even == lower
    tiles = rows.shape[2] // LANES // cuts[0]
    for tile in range(PROJ * PROJ // LANES):
        both = []
        for p in (2 * tile, 2 * tile + 1):
            v = products[pl.ds(p, count, stride=STRIDE), :]
            both.append(jnp.where(here, v, pltpu.roll(v, PROJ, 1)))
        block, part, within = tile // tiles // parts, tile // tiles % parts, tile % tiles
        rows[part, :, pl.ds((block * tiles + within) * LANES, LANES)] = jnp.where(lower, both[0], both[1])
    for k, out in enumerate(outs):
        part = lax.rem(lax.axis_index("seq") + k, parts) if parts > 1 else 0
        out[...] = rows[part]


def kron_of(lefts, own, act, cuts):
    pairs = lefts.shape[0]
    parts = cuts[1]
    width = PROJ * PROJ // parts
    vmem = pl.BlockSpec(memory_space=pltpu.VMEM)
    return pl.pallas_call(
        functools.partial(kron_kernel, cuts),
        out_shape=[jax.ShapeDtypeStruct((2 * pairs, width), jnp.float32)] * parts,
        in_specs=[vmem] * 3,
        out_specs=[vmem] * parts,
        scratch_shapes=[
            pltpu.VMEM((parts, 2 * pairs, width), jnp.float32),
            pltpu.VMEM((2 * pairs * STRIDE, LANES), jnp.float32),
        ],
        compiler_params=pltpu.CompilerParams(vmem_limit_bytes=VMEM_BYTES),
        name="kron",
    )(lefts, own, act)


def parcels_kernel(here, there, *parcels):
    count = here.shape[0]
    dp = len(parcels)
    width = parcels[0].shape[1]
    core, chip = lax.axis_index("seq"), lax.axis_index("tensor") * 2
    blocks = [chip + core, chip + 1 - core]
    for k, parcel in enumerate(parcels):
        for step, block in enumerate(blocks + [lax.rem(lax.axis_index("dp") + k, dp)]):
            lanes = pl.ds(pl.multiple_of(block * width, LANES), width)
            parcel[pl.ds(step * count, count), :] = here[:, lanes] + there[:, lanes]


def parcels_of(here, there, dp):
    count, width = here.shape
    vmem = pl.BlockSpec(memory_space=pltpu.VMEM)
    return pl.pallas_call(
        parcels_kernel,
        out_shape=[jax.ShapeDtypeStruct((3 * count, width // dp), jnp.float32)] * dp,
        in_specs=[vmem] * 2,
        out_specs=[vmem] * dp,
        compiler_params=pltpu.CompilerParams(vmem_limit_bytes=VMEM_BYTES),
        name="parcels",
    )(here, there)


def bundle_kernel(*refs):
    parcels, out = refs[:-1], refs[-1]
    rows = 2 * parcels[0].shape[0] // 3
    for k, parcel in enumerate(parcels):
        out[pl.ds(k * rows, rows), :] = parcel[pl.ds(rows // 2, rows), :]


def bundle_of(parcels):
    rows, width = parcels[0].shape
    vmem = pl.BlockSpec(memory_space=pltpu.VMEM)
    return pl.pallas_call(
        bundle_kernel,
        out_shape=jax.ShapeDtypeStruct((2 * rows // 3 * len(parcels), width), jnp.float32),
        in_specs=[vmem] * len(parcels),
        out_specs=vmem,
        compiler_params=pltpu.CompilerParams(vmem_limit_bytes=VMEM_BYTES),
        name="bundle",
    )(*parcels)


def left_operand(x):
    x1, x2, x3 = split3(x)
    return jnp.concatenate([x1, x1, x2, x1, x3, x2, x2, x3], axis=0).T


def right_operand(x):
    x1, x2, x3 = split3(x)
    return jnp.concatenate([x1, x2, x1, x3, x1, x2, x3, x2], axis=0)


def own_halves(parcels):
    rows = parcels[0].shape[0] // 3
    left = jnp.concatenate([parcel[pl.ds(0, rows), :] for parcel in parcels], axis=0)
    right = jnp.concatenate([parcel[pl.ds(2 * rows, rows), :] for parcel in parcels], axis=0)
    return left, right


def halves_at(part):
    core = lax.axis_index("seq")
    return [pl.ds(pl.multiple_of(place * part, part), part) for place in (core, 1 - core)]


TILE = 256


def quadrant_kernel(scale, *refs):
    parcels, (out, left_ref, right_ref, made, sems) = refs[:-5], refs[-5:]
    part = parcels[0].shape[1]
    left, right = own_halves(parcels)
    left, right = left_operand(left), right_operand(right * scale)
    left_ref[...], right_ref[...] = left, right
    here, _ = halves_at(part)
    copies = []
    for k in range(part // TILE):
        rows = slice(k * TILE, (k + 1) * TILE)
        made[rows, :] = jnp.dot(left[rows], right, preferred_element_type=jnp.float32)
        into = pl.ds(pl.multiple_of(lax.axis_index("seq") * part + k * TILE, TILE), TILE)
        copies.append(pltpu.make_async_copy(made.at[rows], out.at[into, here], sems.at[k]))
        copies[-1].start()
    for copy in copies:
        copy.wait()


def fisher_kernel(scale, begun, left, right, bundle, *refs):
    del begun
    parcels, (mine, out, made, kept, sems) = refs[:-5], refs[-5:]
    rows, part = parcels[0].shape[0] // 3, parcels[0].shape[1]
    here, there = halves_at(part)
    kept[:, here] = parcels[0][pl.ds(0, rows), :]
    kept[:, there] = bundle[pl.ds(0, rows), :]
    copies = [pltpu.make_async_copy(kept, mine, sems.at[0])]
    copies[0].start()
    count = len(parcels)
    other_left = jnp.concatenate([bundle[pl.ds(2 * k * rows, rows), :] for k in range(count)], axis=0)
    other_right = jnp.concatenate([bundle[pl.ds((2 * k + 1) * rows, rows), :] for k in range(count)], axis=0)
    left, other_left = left[...], left_operand(other_left)
    right, other_right = right[...], right_operand(other_right * scale)
    for k, (a, b, into) in enumerate(
        (
            (other_left, right, (there, here)),
            (other_left, other_right, (there, there)),
            (left, other_right, (here, there)),
        )
    ):
        made[k] = jnp.dot(a, b, preferred_element_type=jnp.float32)
        copies.append(pltpu.make_async_copy(made.at[k], out.at[into], sems.at[k + 1]))
        copies[-1].start()
    for copy in copies:
        copy.wait()


def quadrant_of(parcels):
    rows, part = parcels[0].shape
    total = rows // 3 * len(parcels)
    vmem = pl.BlockSpec(memory_space=pltpu.VMEM)
    return pl.pallas_call(
        functools.partial(quadrant_kernel, 1.0 / total),
        out_shape=[
            jax.ShapeDtypeStruct((2 * part, 2 * part), jnp.float32),
            jax.ShapeDtypeStruct((part, 8 * total), jnp.bfloat16),
            jax.ShapeDtypeStruct((8 * total, part), jnp.bfloat16),
        ],
        in_specs=[vmem] * len(parcels),
        out_specs=[pl.BlockSpec(memory_space=pltpu.HBM), vmem, vmem],
        scratch_shapes=[pltpu.VMEM((part, part), jnp.float32), pltpu.SemaphoreType.DMA((part // TILE,))],
        compiler_params=pltpu.CompilerParams(vmem_limit_bytes=VMEM_BYTES),
        cost_estimate=pl.CostEstimate(flops=2**28, bytes_accessed=4 * part * part, transcendentals=0),
        name="quadrant",
    )(*parcels)


def fisher_block(begun, parcels, bundle):
    rows, part = parcels[0].shape
    rows //= 3
    width = 2 * part
    hbm = pl.BlockSpec(memory_space=pltpu.HBM)
    vmem = pl.BlockSpec(memory_space=pltpu.VMEM)
    return pl.pallas_call(
        functools.partial(fisher_kernel, 1.0 / (rows * len(parcels))),
        out_shape=[
            jax.ShapeDtypeStruct((rows, width), jnp.float32),
            jax.ShapeDtypeStruct((width, width), jnp.float32),
        ],
        in_specs=[hbm] + [vmem] * (3 + len(parcels)),
        out_specs=[hbm] * 2,
        scratch_shapes=[
            pltpu.VMEM((3, part, part), jnp.float32),
            pltpu.VMEM((rows, width), jnp.float32),
            pltpu.SemaphoreType.DMA((4,)),
        ],
        input_output_aliases={0: 1},
        compiler_params=pltpu.CompilerParams(vmem_limit_bytes=VMEM_BYTES),
        name="fisher",
    )(*begun, bundle, *parcels)


def local(acts, grads, in_ids, in_signs, out_ids, out_signs, in_table, out_table):
    tensor, seq, dp = (lax.axis_size(name) for name in ("tensor", "seq", "dp"))
    shards = tensor * seq
    small = tensor == 2 and seq == 2 and dp == 4
    swap = [(0, 1), (1, 0)]

    (act,) = project(acts, in_ids, in_signs, in_table, None, 512, "project_acts")
    if tensor == 2:
        other = lax.ppermute(act, "tensor", swap)
    else:
        act = lax.psum(act, "tensor")
        other = jnp.zeros_like(act)
    lefts, own = project(grads, out_ids, out_signs, out_table, act, 1024, "project_grads")
    krons = kron_of(lefts, own, other, (shards, seq) if small else (1, 1))

    if not small:
        kron = lax.psum(krons[0], ("tensor", "seq"))
        width = kron.shape[1] // shards
        place = lax.axis_index("tensor") * seq + lax.axis_index("seq")
        mine = lax.dynamic_slice_in_dim(kron, place * width, width, 1)
        every = lax.all_gather(kron, "dp", axis=0, tiled=True)
        left = lax.dynamic_slice_in_dim(every, place * width, width, 1)
        columns = kron.shape[1] // dp
        right = lax.dynamic_slice_in_dim(every, lax.axis_index("dp") * columns, columns, 1)
        fisher = lax.dot_general(
            left, right, (((0,), (0,)), ((), ())), precision=lax.Precision.HIGHEST
        ) / left.shape[0]
        return mine, fisher

    part = krons[0] + lax.ppermute(krons[1], "seq", swap)
    parcels = list(parcels_of(part, lax.ppermute(part, "tensor", swap), dp))
    for k in range(1, dp):
        parcels[k] = lax.ppermute(parcels[k], "dp", [(d, (d + k) % dp) for d in range(dp)])
    bundle = lax.ppermute(bundle_of(parcels), "seq", swap)
    mine, fisher = fisher_block(quadrant_of(parcels), parcels, bundle)
    return mine, fisher


def solution(mesh):
    in_specs = (
        P(("groups", "dp"), "seq", "tensor"),
        P(("groups", "dp"), "seq", "tensor"),
        P("tensor"),
        P("tensor"),
        P("tensor"),
        P("tensor"),
        P(),
        P(),
    )
    out_specs = (P(("groups", "dp"), ("tensor", "seq")), P(("groups", "tensor", "seq"), "dp"))
    return jax.shard_map(local, mesh=mesh, in_specs=in_specs, out_specs=out_specs, check_vma=False)
```

```python
import functools

import jax
import jax.numpy as jnp
from jax import lax
from jax.experimental import pallas as pl
from jax.experimental.pallas import tpu as pltpu
from jax.sharding import PartitionSpec as P

PROJ = 64
BLOCK = 64
LANES = 128
STRIDE = 72
VMEM_BYTES = 48 * 1024 * 1024


def chunks_of(width, most):
    if width >= 4 * most:
        inner = width - most
        ends = [most // 2] * 2
    else:
        inner, ends = width, []
    chunk = most
    while inner % chunk:
        chunk -= LANES
    return ends[:1] + [chunk] * (inner // chunk) + ends[1:]


def split3(x):
    high = x.astype(jnp.bfloat16)
    rest = x - high.astype(jnp.float32)
    mid = rest.astype(jnp.bfloat16)
    low = (rest - mid.astype(jnp.float32)).astype(jnp.bfloat16)
    return high, mid, low


def spread_table(table, spread):
    entries = table.shape[0]
    for row in range(0, BLOCK, 2):
        both = table[:, row * PROJ : row * PROJ + LANES].astype(jnp.float32)
        spread[pl.ds(row, entries, stride=STRIDE), :] = both
        spread[pl.ds(row + 1, entries, stride=STRIDE), :] = pltpu.roll(both, PROJ, 1)


def sign_table(spread, signed):
    entries = spread.shape[0] // STRIDE
    for entry in range(entries):
        block = spread[pl.ds(entry * STRIDE, BLOCK), :].astype(jnp.bfloat16)
        signed[pl.ds((entries + entry) * BLOCK, BLOCK), :] = block
        signed[pl.ds(entry * BLOCK, BLOCK), :] = -block


def lay_blocks(ids, signs, spread, signed, matrix, first, last):
    entries = spread.shape[0] // STRIDE
    for j in range(first, last):
        if signed is None:
            start = pl.multiple_of(ids[j] * STRIDE, 8)
            sign = (2 * signs[j] - 1).astype(jnp.float32)
            block = (spread[pl.ds(start, BLOCK), :] * sign).astype(jnp.bfloat16)
        else:
            start = pl.multiple_of((signs[j] * entries + ids[j]) * BLOCK, BLOCK)
            block = signed[pl.ds(start, BLOCK), :]
        matrix[pl.ds(j * BLOCK, BLOCK), :] = block


def operand(x):
    x1, x2, x3 = split3(x)
    return jnp.concatenate([x1, x1, x2, x1, x3, x2], axis=1)


def products_with(left, act):
    a1, a2, a3 = split3(act)
    right = jnp.concatenate([a1, a2, a1, a3, a1, a2], axis=1)
    return lax.dot_general(left, right, (((1,), (1,)), ((), ())), preferred_element_type=jnp.float32)


def project_kernel(widths, fetch, ids, signs, table, rows_ref, *refs):
    if fetch:
        (out,), refs = refs[:1], refs[1:]
    else:
        (acts, lefts, products), refs = refs[:3], refs[3:]
    spread, signed, matrix, held, total, sems, *own = refs
    copies, starts, start = [], [], 0
    for c, width in enumerate(widths):
        columns = pl.ds(start, width)
        copies.append(pltpu.make_async_copy(rows_ref.at[:, columns], held.at[:, columns], sems.at[c]))
        starts.append(start)
        start += width
    if fetch:
        small = [
            pltpu.make_async_copy(source, kept, sems.at[len(widths) + k])
            for k, (source, kept) in enumerate(zip((table, ids, signs), own))
        ]
        for copy in small:
            copy.start()
        table, ids, signs = own
    for copy in copies:
        copy.start()
    if fetch:
        small[0].wait()
    spread_table(table, spread)
    if fetch:
        signed = None
    else:
        sign_table(spread, signed)
    if fetch:
        small[1].wait()
        small[2].wait()
    lay = functools.partial(lay_blocks, ids, signs, spread, signed, matrix)
    lay(0, widths[0] // BLOCK)
    for c, copy in enumerate(copies):
        columns = pl.ds(starts[c], widths[c])
        copy.wait()
        if c + 1 < len(widths):
            lay(starts[c + 1] // BLOCK, (starts[c + 1] + widths[c + 1]) // BLOCK)
        part = lax.dot_general(
            matrix[columns, :PROJ],
            held[:, columns],
            (((0,), (1,)), ((), ())),
            preferred_element_type=jnp.float32,
        )
        if c == 0:
            total[...] = part
        else:
            total[...] += part
    pairs, _, tokens = out.shape if fetch else acts.shape
    for pair in range(pairs):
        sides = [total[:, pl.ds((2 * pair + side) * tokens, tokens)] for side in range(2)]
        if fetch:
            for side in range(2):
                out[pair, pl.ds(side * PROJ, PROJ), :] = sides[side]
        else:
            left = operand(jnp.concatenate(sides, axis=0))
            lefts[pair] = left
            products[pl.ds(pair * LANES, LANES), :] = products_with(left, acts[pair])


def project(values, ids, signs, table, acts, most, name):
    fetch = acts is None
    count, tokens, width = values.shape
    widths = chunks_of(width, most)
    rows = count * tokens
    entries = table.shape[0]
    smem = pl.BlockSpec(memory_space=pltpu.SMEM)
    vmem = pl.BlockSpec(memory_space=pltpu.VMEM)
    hbm = pl.BlockSpec(memory_space=pltpu.HBM)
    own = [
        pltpu.VMEM(table.shape, table.dtype),
        pltpu.SMEM(ids.shape, ids.dtype),
        pltpu.SMEM(signs.shape, signs.dtype),
    ]
    operands = [ids, signs, table, values.reshape(rows, width)]
    shapes = [jax.ShapeDtypeStruct((count // 2, LANES, tokens), jnp.float32)]
    if fetch:
        operands = [pltpu.with_memory_space_constraint(each, pltpu.HBM) for each in operands]
    else:
        operands.append(acts)
        shapes = [
            jax.ShapeDtypeStruct((count // 2, LANES, 6 * tokens), jnp.bfloat16),
            jax.ShapeDtypeStruct((count // 2 * LANES, LANES), jnp.float32),
        ]
    return pl.pallas_call(
        functools.partial(project_kernel, widths, fetch),
        out_shape=shapes,
        in_specs=[hbm] * 4 if fetch else [smem, smem, vmem, hbm, vmem],
        out_specs=[vmem] * len(shapes),
        scratch_shapes=[
            pltpu.VMEM((entries * STRIDE, LANES), jnp.float32),
            pltpu.VMEM((2 * entries * BLOCK, LANES), jnp.bfloat16),
            pltpu.VMEM((width, LANES), jnp.bfloat16),
            pltpu.VMEM((rows, width), jnp.bfloat16),
            pltpu.VMEM((PROJ, rows), jnp.float32),
            pltpu.SemaphoreType.DMA((len(widths) + 3,)),
        ]
        + (own if fetch else []),
        compiler_params=pltpu.CompilerParams(vmem_limit_bytes=VMEM_BYTES),
        cost_estimate=pl.CostEstimate(
            flops=2 * rows * width * LANES, bytes_accessed=2 * rows * width, transcendentals=0
        ),
        name=name,
    )(*operands)


def kron_kernel(cuts, lefts, own, act, *refs):
    parts = cuts[1]
    outs, rows, products = refs[:-2], refs[-2], refs[-1]
    pairs = act.shape[0]
    for pair in range(pairs):
        both = own[pl.ds(pair * LANES, LANES), :] + products_with(lefts[pair], act[pair])
        for side in range(2):
            products[pl.ds((2 * pair + side) * STRIDE, PROJ), :] = both[side * PROJ : (side + 1) * PROJ]
    count = 2 * pairs
    lower = lax.broadcasted_iota(jnp.int32, (count, LANES), 1) < PROJ
    even = lax.broadcasted_iota(jnp.int32, (count, LANES), 0) % 2 == 0
    here = even == lower
    tiles = rows.shape[2] // LANES // cuts[0]
    for tile in range(PROJ * PROJ // LANES):
        both = []
        for p in (2 * tile, 2 * tile + 1):
            v = products[pl.ds(p, count, stride=STRIDE), :]
            both.append(jnp.where(here, v, pltpu.roll(v, PROJ, 1)))
        block, part, within = tile // tiles // parts, tile // tiles % parts, tile % tiles
        rows[part, :, pl.ds((block * tiles + within) * LANES, LANES)] = jnp.where(lower, both[0], both[1])
    for k, out in enumerate(outs):
        part = lax.rem(lax.axis_index("seq") + k % 2, parts) if parts > 1 else 0
        out[...] = rows[part]


def kron_of(lefts, own, act, cuts):
    pairs = lefts.shape[0]
    parts = cuts[1]
    width = PROJ * PROJ // parts
    outs = 4 if parts > 1 else 1
    vmem = pl.BlockSpec(memory_space=pltpu.VMEM)
    return pl.pallas_call(
        functools.partial(kron_kernel, cuts),
        out_shape=[jax.ShapeDtypeStruct((2 * pairs, width), jnp.float32)] * outs,
        in_specs=[vmem] * 3,
        out_specs=[vmem] * outs,
        scratch_shapes=[
            pltpu.VMEM((parts, 2 * pairs, width), jnp.float32),
            pltpu.VMEM((2 * pairs * STRIDE, LANES), jnp.float32),
        ],
        compiler_params=pltpu.CompilerParams(vmem_limit_bytes=VMEM_BYTES),
        name="kron",
    )(lefts, own, act)


def parcels_kernel(parts, *refs):
    summands, parcels = refs[:parts], refs[parts:]
    count = summands[0].shape[0]
    dp = len(parcels)
    width = parcels[0].shape[1]
    core, chip = lax.axis_index("seq"), lax.axis_index("tensor") * 2
    blocks = [chip + core, chip + 1 - core]
    for k, parcel in enumerate(parcels):
        for step, block in enumerate(blocks + [lax.rem(lax.axis_index("dp") + k, dp)]):
            lanes = pl.ds(pl.multiple_of(block * width, LANES), width)
            row = summands[0][:, lanes]
            for other in summands[1:]:
                row = row + other[:, lanes]
            parcel[pl.ds(step * count, count), :] = row


def parcels_of(summands, dp):
    count, width = summands[0].shape
    vmem = pl.BlockSpec(memory_space=pltpu.VMEM)
    return pl.pallas_call(
        functools.partial(parcels_kernel, len(summands)),
        out_shape=[jax.ShapeDtypeStruct((3 * count, width // dp), jnp.float32)] * dp,
        in_specs=[vmem] * len(summands),
        out_specs=[vmem] * dp,
        compiler_params=pltpu.CompilerParams(vmem_limit_bytes=VMEM_BYTES),
        name="parcels",
    )(*summands)


def bundle_kernel(*refs):
    parcels, out = refs[:-1], refs[-1]
    rows = 2 * parcels[0].shape[0] // 3
    for k, parcel in enumerate(parcels):
        out[pl.ds(k * rows, rows), :] = parcel[pl.ds(rows // 2, rows), :]


def bundle_of(parcels):
    rows, width = parcels[0].shape
    vmem = pl.BlockSpec(memory_space=pltpu.VMEM)
    return pl.pallas_call(
        bundle_kernel,
        out_shape=jax.ShapeDtypeStruct((2 * rows // 3 * len(parcels), width), jnp.float32),
        in_specs=[vmem] * len(parcels),
        out_specs=vmem,
        compiler_params=pltpu.CompilerParams(vmem_limit_bytes=VMEM_BYTES),
        name="bundle",
    )(*parcels)


def left_operand(x):
    x1, x2, x3 = split3(x)
    return jnp.concatenate([x1, x1, x2, x1, x3, x2, x2, x3], axis=0).T


def right_operand(x):
    x1, x2, x3 = split3(x)
    return jnp.concatenate([x1, x2, x1, x3, x1, x2, x3, x2], axis=0)


def own_halves(parcels):
    rows = parcels[0].shape[0] // 3
    left = jnp.concatenate([parcel[pl.ds(0, rows), :] for parcel in parcels], axis=0)
    right = jnp.concatenate([parcel[pl.ds(2 * rows, rows), :] for parcel in parcels], axis=0)
    return left, right


def halves_at(part):
    core = lax.axis_index("seq")
    return [pl.ds(pl.multiple_of(place * part, part), part) for place in (core, 1 - core)]


TILE = 256


def quadrant_kernel(scale, *refs):
    parcels, (out, left_ref, right_ref, made, sems) = refs[:-5], refs[-5:]
    part = parcels[0].shape[1]
    left, right = own_halves(parcels)
    left, right = left_operand(left), right_operand(right * scale)
    left_ref[...], right_ref[...] = left, right
    here, _ = halves_at(part)
    copies = []
    for k in range(part // TILE):
        rows = slice(k * TILE, (k + 1) * TILE)
        made[rows, :] = jnp.dot(left[rows], right, preferred_element_type=jnp.float32)
        into = pl.ds(pl.multiple_of(lax.axis_index("seq") * part + k * TILE, TILE), TILE)
        copies.append(pltpu.make_async_copy(made.at[rows], out.at[into, here], sems.at[k]))
        copies[-1].start()
    for copy in copies:
        copy.wait()


def fisher_kernel(scale, begun, left, right, bundle, *refs):
    del begun
    parcels, (mine, out, made, kept, sems) = refs[:-5], refs[-5:]
    rows, part = parcels[0].shape[0] // 3, parcels[0].shape[1]
    here, there = halves_at(part)
    kept[:, here] = parcels[0][pl.ds(0, rows), :]
    kept[:, there] = bundle[pl.ds(0, rows), :]
    copies = [pltpu.make_async_copy(kept, mine, sems.at[0])]
    copies[0].start()
    count = len(parcels)
    other_left = jnp.concatenate([bundle[pl.ds(2 * k * rows, rows), :] for k in range(count)], axis=0)
    other_right = jnp.concatenate([bundle[pl.ds((2 * k + 1) * rows, rows), :] for k in range(count)], axis=0)
    left, other_left = left[...], left_operand(other_left)
    right, other_right = right[...], right_operand(other_right * scale)
    for k, (a, b, into) in enumerate(
        (
            (other_left, right, (there, here)),
            (other_left, other_right, (there, there)),
            (left, other_right, (here, there)),
        )
    ):
        made[k] = jnp.dot(a, b, preferred_element_type=jnp.float32)
        copies.append(pltpu.make_async_copy(made.at[k], out.at[into], sems.at[k + 1]))
        copies[-1].start()
    for copy in copies:
        copy.wait()


def quadrant_of(parcels):
    rows, part = parcels[0].shape
    total = rows // 3 * len(parcels)
    vmem = pl.BlockSpec(memory_space=pltpu.VMEM)
    return pl.pallas_call(
        functools.partial(quadrant_kernel, 1.0 / total),
        out_shape=[
            jax.ShapeDtypeStruct((2 * part, 2 * part), jnp.float32),
            jax.ShapeDtypeStruct((part, 8 * total), jnp.bfloat16),
            jax.ShapeDtypeStruct((8 * total, part), jnp.bfloat16),
        ],
        in_specs=[vmem] * len(parcels),
        out_specs=[pl.BlockSpec(memory_space=pltpu.HBM), vmem, vmem],
        scratch_shapes=[pltpu.VMEM((part, part), jnp.float32), pltpu.SemaphoreType.DMA((part // TILE,))],
        compiler_params=pltpu.CompilerParams(vmem_limit_bytes=VMEM_BYTES),
        cost_estimate=pl.CostEstimate(flops=2**28, bytes_accessed=4 * part * part, transcendentals=0),
        name="quadrant",
    )(*parcels)


def fisher_block(begun, parcels, bundle):
    rows, part = parcels[0].shape
    rows //= 3
    width = 2 * part
    hbm = pl.BlockSpec(memory_space=pltpu.HBM)
    vmem = pl.BlockSpec(memory_space=pltpu.VMEM)
    return pl.pallas_call(
        functools.partial(fisher_kernel, 1.0 / (rows * len(parcels))),
        out_shape=[
            jax.ShapeDtypeStruct((rows, width), jnp.float32),
            jax.ShapeDtypeStruct((width, width), jnp.float32),
        ],
        in_specs=[hbm] + [vmem] * (3 + len(parcels)),
        out_specs=[hbm] * 2,
        scratch_shapes=[
            pltpu.VMEM((3, part, part), jnp.float32),
            pltpu.VMEM((rows, width), jnp.float32),
            pltpu.SemaphoreType.DMA((4,)),
        ],
        input_output_aliases={0: 1},
        compiler_params=pltpu.CompilerParams(vmem_limit_bytes=VMEM_BYTES),
        name="fisher",
    )(*begun, bundle, *parcels)


def local(acts, grads, in_ids, in_signs, out_ids, out_signs, in_table, out_table):
    tensor, seq, dp = (lax.axis_size(name) for name in ("tensor", "seq", "dp"))
    shards = tensor * seq
    small = tensor == 2 and seq == 2 and dp == 4
    swap = [(0, 1), (1, 0)]

    (act,) = project(acts, in_ids, in_signs, in_table, None, 512, "project_acts")
    if tensor == 2:
        other = lax.ppermute(act, "tensor", swap)
    else:
        act = lax.psum(act, "tensor")
        other = jnp.zeros_like(act)
    lefts, own = project(grads, out_ids, out_signs, out_table, act, 1024, "project_grads")
    krons = kron_of(lefts, own, other, (shards, seq) if small else (1, 1))

    if not small:
        kron = lax.psum(krons[0], ("tensor", "seq"))
        width = kron.shape[1] // shards
        place = lax.axis_index("tensor") * seq + lax.axis_index("seq")
        mine = lax.dynamic_slice_in_dim(kron, place * width, width, 1)
        every = lax.all_gather(kron, "dp", axis=0, tiled=True)
        left = lax.dynamic_slice_in_dim(every, place * width, width, 1)
        columns = kron.shape[1] // dp
        right = lax.dynamic_slice_in_dim(every, lax.axis_index("dp") * columns, columns, 1)
        fisher = lax.dot_general(
            left, right, (((0,), (0,)), ((), ())), precision=lax.Precision.HIGHEST
        ) / left.shape[0]
        return mine, fisher

    across = lax.ppermute(krons[1], ("tensor", "seq"), [(p, 3 - p) for p in range(shards)])
    beside = lax.ppermute(krons[2], "tensor", swap)
    mate = lax.ppermute(krons[3], "seq", swap)
    parcels = list(parcels_of([across, beside, mate, krons[0]], dp))
    for k in range(1, dp):
        parcels[k] = lax.ppermute(parcels[k], "dp", [(d, (d + k) % dp) for d in range(dp)])
    bundle = lax.ppermute(bundle_of(parcels), "seq", swap)
    mine, fisher = fisher_block(quadrant_of(parcels), parcels, bundle)
    return mine, fisher


def solution(mesh):
    in_specs = (
        P(("groups", "dp"), "seq", "tensor"),
        P(("groups", "dp"), "seq", "tensor"),
        P("tensor"),
        P("tensor"),
        P("tensor"),
        P("tensor"),
        P(),
        P(),
    )
    out_specs = (P(("groups", "dp"), ("tensor", "seq")), P(("groups", "tensor", "seq"), "dp"))
    return jax.shard_map(local, mesh=mesh, in_specs=in_specs, out_specs=out_specs, check_vma=False)
```

```python
import functools

import jax
import jax.numpy as jnp
from jax import lax
from jax.experimental import pallas as pl
from jax.experimental.pallas import tpu as pltpu
from jax.sharding import PartitionSpec as P

PROJ = 64
BLOCK = 64
LANES = 128
STRIDE = 72
VMEM_BYTES = 48 * 1024 * 1024


def chunks_of(width, most):
    if width >= 4 * most:
        inner = width - most
        ends = [most // 2] * 2
    else:
        inner, ends = width, []
    chunk = most
    while inner % chunk:
        chunk -= LANES
    return ends[:1] + [chunk] * (inner // chunk) + ends[1:]


def split3(x):
    high = x.astype(jnp.bfloat16)
    rest = x - high.astype(jnp.float32)
    mid = rest.astype(jnp.bfloat16)
    low = (rest - mid.astype(jnp.float32)).astype(jnp.bfloat16)
    return high, mid, low


def spread_table(table, spread):
    entries = table.shape[0]
    for row in range(0, BLOCK, 2):
        both = table[:, row * PROJ : row * PROJ + LANES].astype(jnp.float32)
        spread[pl.ds(row, entries, stride=STRIDE), :] = both
        spread[pl.ds(row + 1, entries, stride=STRIDE), :] = pltpu.roll(both, PROJ, 1)


def sign_table(spread, signed):
    entries = spread.shape[0] // STRIDE
    for entry in range(entries):
        block = spread[pl.ds(entry * STRIDE, BLOCK), :].astype(jnp.bfloat16)
        signed[pl.ds((entries + entry) * BLOCK, BLOCK), :] = block
        signed[pl.ds(entry * BLOCK, BLOCK), :] = -block


def lay_blocks(ids, signs, spread, signed, matrix, first, last):
    entries = spread.shape[0] // STRIDE
    for j in range(first, last):
        if signed is None:
            start = pl.multiple_of(ids[j] * STRIDE, 8)
            sign = (2 * signs[j] - 1).astype(jnp.float32)
            block = (spread[pl.ds(start, BLOCK), :] * sign).astype(jnp.bfloat16)
        else:
            start = pl.multiple_of((signs[j] * entries + ids[j]) * BLOCK, BLOCK)
            block = signed[pl.ds(start, BLOCK), :]
        matrix[pl.ds(j * BLOCK, BLOCK), :] = block


def operand(x):
    x1, x2, x3 = split3(x)
    return jnp.concatenate([x1, x1, x2, x1, x3, x2], axis=1)


def products_with(left, act):
    a1, a2, a3 = split3(act)
    right = jnp.concatenate([a1, a2, a1, a3, a1, a2], axis=1)
    return lax.dot_general(left, right, (((1,), (1,)), ((), ())), preferred_element_type=jnp.float32)


def project_kernel(widths, fetch, ids, signs, table, rows_ref, *refs):
    out, spread, signed, matrix, held, total, sems, *own = refs
    copies, starts, start = [], [], 0
    for c, width in enumerate(widths):
        columns = pl.ds(start, width)
        copies.append(pltpu.make_async_copy(rows_ref.at[:, columns], held.at[:, columns], sems.at[c]))
        starts.append(start)
        start += width
    if fetch:
        small = [
            pltpu.make_async_copy(source, kept, sems.at[len(widths) + k])
            for k, (source, kept) in enumerate(zip((table, ids, signs), own))
        ]
        for copy in small:
            copy.start()
        table, ids, signs = own
    for copy in copies:
        copy.start()
    if fetch:
        small[0].wait()
    spread_table(table, spread)
    if fetch:
        signed = None
    else:
        sign_table(spread, signed)
    if fetch:
        small[1].wait()
        small[2].wait()
    lay = functools.partial(lay_blocks, ids, signs, spread, signed, matrix)
    lay(0, widths[0] // BLOCK)
    for c, copy in enumerate(copies):
        columns = pl.ds(starts[c], widths[c])
        copy.wait()
        if c + 1 < len(widths):
            lay(starts[c + 1] // BLOCK, (starts[c + 1] + widths[c + 1]) // BLOCK)
        part = lax.dot_general(
            matrix[columns, :PROJ],
            held[:, columns],
            (((0,), (1,)), ((), ())),
            preferred_element_type=jnp.float32,
        )
        if c == 0:
            total[...] = part
        else:
            total[...] += part
    pairs, _, tokens = out.shape
    for pair in range(pairs):
        for side in range(2):
            out[pair, pl.ds(side * PROJ, PROJ), :] = total[:, pl.ds((2 * pair + side) * tokens, tokens)]


def project(values, ids, signs, table, fetch, most, name):
    count, tokens, width = values.shape
    widths = chunks_of(width, most)
    rows = count * tokens
    entries = table.shape[0]
    smem = pl.BlockSpec(memory_space=pltpu.SMEM)
    vmem = pl.BlockSpec(memory_space=pltpu.VMEM)
    hbm = pl.BlockSpec(memory_space=pltpu.HBM)
    own = [
        pltpu.VMEM(table.shape, table.dtype),
        pltpu.SMEM(ids.shape, ids.dtype),
        pltpu.SMEM(signs.shape, signs.dtype),
    ]
    operands = [ids, signs, table, values.reshape(rows, width)]
    if fetch:
        operands = [pltpu.with_memory_space_constraint(each, pltpu.HBM) for each in operands]
    return pl.pallas_call(
        functools.partial(project_kernel, widths, fetch),
        out_shape=jax.ShapeDtypeStruct((count // 2, LANES, tokens), jnp.float32),
        in_specs=[hbm] * 4 if fetch else [smem, smem, vmem, hbm],
        out_specs=vmem,
        scratch_shapes=[
            pltpu.VMEM((entries * STRIDE, LANES), jnp.float32),
            pltpu.VMEM((2 * entries * BLOCK, LANES), jnp.bfloat16),
            pltpu.VMEM((width, LANES), jnp.bfloat16),
            pltpu.VMEM((rows, width), jnp.bfloat16),
            pltpu.VMEM((PROJ, rows), jnp.float32),
            pltpu.SemaphoreType.DMA((len(widths) + 3,)),
        ]
        + (own if fetch else []),
        compiler_params=pltpu.CompilerParams(vmem_limit_bytes=VMEM_BYTES),
        cost_estimate=pl.CostEstimate(
            flops=2 * rows * width * LANES, bytes_accessed=2 * rows * width, transcendentals=0
        ),
        name=name,
    )(*operands)


def kron_kernel(cuts, grads, own, act, *refs):
    parts = cuts[1]
    outs, rows, products = refs[:-2], refs[-2], refs[-1]
    pairs = act.shape[0]
    for pair in range(pairs):
        both = products_with(operand(grads[pair]), own[pair] + act[pair])
        for side in range(2):
            products[pl.ds((2 * pair + side) * STRIDE, PROJ), :] = both[side * PROJ : (side + 1) * PROJ]
    count = 2 * pairs
    lower = lax.broadcasted_iota(jnp.int32, (count, LANES), 1) < PROJ
    even = lax.broadcasted_iota(jnp.int32, (count, LANES), 0) % 2 == 0
    here = even == lower
    tiles = rows.shape[2] // LANES // cuts[0]
    for tile in range(PROJ * PROJ // LANES):
        both = []
        for p in (2 * tile, 2 * tile + 1):
            v = products[pl.ds(p, count, stride=STRIDE), :]
            both.append(jnp.where(here, v, pltpu.roll(v, PROJ, 1)))
        block, part, within = tile // tiles // parts, tile // tiles % parts, tile % tiles
        rows[part, :, pl.ds((block * tiles + within) * LANES, LANES)] = jnp.where(lower, both[0], both[1])
    for k, out in enumerate(outs):
        part = lax.rem(lax.axis_index("seq") + k % 2, parts) if parts > 1 else 0
        out[...] = rows[part]


def kron_of(grads, own, act, cuts):
    pairs = grads.shape[0]
    parts = cuts[1]
    width = PROJ * PROJ // parts
    outs = 4 if parts > 1 else 1
    vmem = pl.BlockSpec(memory_space=pltpu.VMEM)
    return pl.pallas_call(
        functools.partial(kron_kernel, cuts),
        out_shape=[jax.ShapeDtypeStruct((2 * pairs, width), jnp.float32)] * outs,
        in_specs=[vmem] * 3,
        out_specs=[vmem] * outs,
        scratch_shapes=[
            pltpu.VMEM((parts, 2 * pairs, width), jnp.float32),
            pltpu.VMEM((2 * pairs * STRIDE, LANES), jnp.float32),
        ],
        compiler_params=pltpu.CompilerParams(vmem_limit_bytes=VMEM_BYTES),
        name="kron",
    )(grads, own, act)


def parcels_kernel(parts, *refs):
    summands, parcels = refs[:parts], refs[parts:]
    count = summands[0].shape[0]
    dp = len(parcels)
    width = parcels[0].shape[1]
    core, chip = lax.axis_index("seq"), lax.axis_index("tensor") * 2
    blocks = [chip + core, chip + 1 - core]
    for k, parcel in enumerate(parcels):
        for step, block in enumerate(blocks + [lax.rem(lax.axis_index("dp") + k, dp)]):
            lanes = pl.ds(pl.multiple_of(block * width, LANES), width)
            row = summands[0][:, lanes]
            for other in summands[1:]:
                row = row + other[:, lanes]
            parcel[pl.ds(step * count, count), :] = row


def parcels_of(summands, dp):
    count, width = summands[0].shape
    vmem = pl.BlockSpec(memory_space=pltpu.VMEM)
    return pl.pallas_call(
        functools.partial(parcels_kernel, len(summands)),
        out_shape=[jax.ShapeDtypeStruct((3 * count, width // dp), jnp.float32)] * dp,
        in_specs=[vmem] * len(summands),
        out_specs=[vmem] * dp,
        compiler_params=pltpu.CompilerParams(vmem_limit_bytes=VMEM_BYTES),
        name="parcels",
    )(*summands)


def bundle_kernel(*refs):
    parcels, out = refs[:-1], refs[-1]
    rows = 2 * parcels[0].shape[0] // 3
    for k, parcel in enumerate(parcels):
        out[pl.ds(k * rows, rows), :] = parcel[pl.ds(rows // 2, rows), :]


def bundle_of(parcels):
    rows, width = parcels[0].shape
    vmem = pl.BlockSpec(memory_space=pltpu.VMEM)
    return pl.pallas_call(
        bundle_kernel,
        out_shape=jax.ShapeDtypeStruct((2 * rows // 3 * len(parcels), width), jnp.float32),
        in_specs=[vmem] * len(parcels),
        out_specs=vmem,
        compiler_params=pltpu.CompilerParams(vmem_limit_bytes=VMEM_BYTES),
        name="bundle",
    )(*parcels)


def left_operand(x):
    x1, x2, x3 = split3(x)
    return jnp.concatenate([x1, x1, x2, x1, x3, x2, x2, x3], axis=0).T


def right_operand(x):
    x1, x2, x3 = split3(x)
    return jnp.concatenate([x1, x2, x1, x3, x1, x2, x3, x2], axis=0)


def own_halves(parcels):
    rows = parcels[0].shape[0] // 3
    left = jnp.concatenate([parcel[pl.ds(0, rows), :] for parcel in parcels], axis=0)
    right = jnp.concatenate([parcel[pl.ds(2 * rows, rows), :] for parcel in parcels], axis=0)
    return left, right


def halves_at(part):
    core = lax.axis_index("seq")
    return [pl.ds(pl.multiple_of(place * part, part), part) for place in (core, 1 - core)]


TILE = 256


def quadrant_kernel(scale, *refs):
    parcels, (out, left_ref, right_ref, made, sems) = refs[:-5], refs[-5:]
    part = parcels[0].shape[1]
    left, right = own_halves(parcels)
    left, right = left_operand(left), right_operand(right * scale)
    left_ref[...], right_ref[...] = left, right
    here, _ = halves_at(part)
    copies = []
    for k in range(part // TILE):
        rows = slice(k * TILE, (k + 1) * TILE)
        made[rows, :] = jnp.dot(left[rows], right, preferred_element_type=jnp.float32)
        into = pl.ds(pl.multiple_of(lax.axis_index("seq") * part + k * TILE, TILE), TILE)
        copies.append(pltpu.make_async_copy(made.at[rows], out.at[into, here], sems.at[k]))
        copies[-1].start()
    for copy in copies:
        copy.wait()


def fisher_kernel(scale, begun, left, right, bundle, *refs):
    del begun
    parcels, (mine, out, made, kept, sems) = refs[:-5], refs[-5:]
    rows, part = parcels[0].shape[0] // 3, parcels[0].shape[1]
    here, there = halves_at(part)
    kept[:, here] = parcels[0][pl.ds(0, rows), :]
    kept[:, there] = bundle[pl.ds(0, rows), :]
    copies = [pltpu.make_async_copy(kept, mine, sems.at[0])]
    copies[0].start()
    count = len(parcels)
    other_left = jnp.concatenate([bundle[pl.ds(2 * k * rows, rows), :] for k in range(count)], axis=0)
    other_right = jnp.concatenate([bundle[pl.ds((2 * k + 1) * rows, rows), :] for k in range(count)], axis=0)
    right, other_right = right[...], right_operand(other_right * scale)
    for k in range(part // TILE):
        piece = slice(k * TILE, (k + 1) * TILE)
        made[0, piece, :] = jnp.dot(left[piece, :], other_right, preferred_element_type=jnp.float32)
        into = pl.ds(pl.multiple_of(lax.axis_index("seq") * part + k * TILE, TILE), TILE)
        copies.append(pltpu.make_async_copy(made.at[0, piece], out.at[into, there], sems.at[k + 1]))
        copies[-1].start()
    other_left = left_operand(other_left)
    for k, (operand_right, into) in enumerate(((other_right, there), (right, here))):
        made[k + 1] = jnp.dot(other_left, operand_right, preferred_element_type=jnp.float32)
        copies.append(pltpu.make_async_copy(made.at[k + 1], out.at[there, into], sems.at[part // TILE + k + 1]))
        copies[-1].start()
    for copy in copies:
        copy.wait()


def quadrant_of(parcels):
    rows, part = parcels[0].shape
    total = rows // 3 * len(parcels)
    vmem = pl.BlockSpec(memory_space=pltpu.VMEM)
    return pl.pallas_call(
        functools.partial(quadrant_kernel, 1.0 / total),
        out_shape=[
            jax.ShapeDtypeStruct((2 * part, 2 * part), jnp.float32),
            jax.ShapeDtypeStruct((part, 8 * total), jnp.bfloat16),
            jax.ShapeDtypeStruct((8 * total, part), jnp.bfloat16),
        ],
        in_specs=[vmem] * len(parcels),
        out_specs=[pl.BlockSpec(memory_space=pltpu.HBM), vmem, vmem],
        scratch_shapes=[pltpu.VMEM((part, part), jnp.float32), pltpu.SemaphoreType.DMA((part // TILE,))],
        compiler_params=pltpu.CompilerParams(vmem_limit_bytes=VMEM_BYTES),
        cost_estimate=pl.CostEstimate(flops=2**28, bytes_accessed=4 * part * part, transcendentals=0),
        name="quadrant",
    )(*parcels)


def fisher_block(begun, parcels, bundle):
    rows, part = parcels[0].shape
    rows //= 3
    width = 2 * part
    hbm = pl.BlockSpec(memory_space=pltpu.HBM)
    vmem = pl.BlockSpec(memory_space=pltpu.VMEM)
    return pl.pallas_call(
        functools.partial(fisher_kernel, 1.0 / (rows * len(parcels))),
        out_shape=[
            jax.ShapeDtypeStruct((rows, width), jnp.float32),
            jax.ShapeDtypeStruct((width, width), jnp.float32),
        ],
        in_specs=[hbm] + [vmem] * (3 + len(parcels)),
        out_specs=[hbm] * 2,
        scratch_shapes=[
            pltpu.VMEM((3, part, part), jnp.float32),
            pltpu.VMEM((rows, width), jnp.float32),
            pltpu.SemaphoreType.DMA((part // TILE + 3,)),
        ],
        input_output_aliases={0: 1},
        compiler_params=pltpu.CompilerParams(vmem_limit_bytes=VMEM_BYTES),
        name="fisher",
    )(*begun, bundle, *parcels)


def local(acts, grads, in_ids, in_signs, out_ids, out_signs, in_table, out_table):
    tensor, seq, dp = (lax.axis_size(name) for name in ("tensor", "seq", "dp"))
    shards = tensor * seq
    small = tensor == 2 and seq == 2 and dp == 4
    swap = [(0, 1), (1, 0)]

    act = project(acts, in_ids, in_signs, in_table, True, 512, "project_acts")
    if tensor == 2:
        other = lax.ppermute(act, "tensor", swap)
    else:
        act = lax.psum(act, "tensor")
        other = jnp.zeros_like(act)
    grad = project(grads, out_ids, out_signs, out_table, False, 1024, "project_grads")
    krons = kron_of(grad, act, other, (shards, seq) if small else (1, 1))

    if not small:
        kron = lax.psum(krons[0], ("tensor", "seq"))
        width = kron.shape[1] // shards
        place = lax.axis_index("tensor") * seq + lax.axis_index("seq")
        mine = lax.dynamic_slice_in_dim(kron, place * width, width, 1)
        every = lax.all_gather(kron, "dp", axis=0, tiled=True)
        left = lax.dynamic_slice_in_dim(every, place * width, width, 1)
        columns = kron.shape[1] // dp
        right = lax.dynamic_slice_in_dim(every, lax.axis_index("dp") * columns, columns, 1)
        fisher = lax.dot_general(
            left, right, (((0,), (0,)), ((), ())), precision=lax.Precision.HIGHEST
        ) / left.shape[0]
        return mine, fisher

    across = lax.ppermute(krons[1], ("tensor", "seq"), [(p, 3 - p) for p in range(shards)])
    beside = lax.ppermute(krons[2], "tensor", swap)
    mate = lax.ppermute(krons[3], "seq", swap)
    parcels = list(parcels_of([across, beside, mate, krons[0]], dp))
    for k in range(1, dp):
        parcels[k] = lax.ppermute(parcels[k], "dp", [(d, (d + k) % dp) for d in range(dp)])
    bundle = lax.ppermute(bundle_of(parcels), "seq", swap)
    mine, fisher = fisher_block(quadrant_of(parcels), parcels, bundle)
    return mine, fisher


def solution(mesh):
    in_specs = (
        P(("groups", "dp"), "seq", "tensor"),
        P(("groups", "dp"), "seq", "tensor"),
        P("tensor"),
        P("tensor"),
        P("tensor"),
        P("tensor"),
        P(),
        P(),
    )
    out_specs = (P(("groups", "dp"), ("tensor", "seq")), P(("groups", "tensor", "seq"), "dp"))
    return jax.shard_map(local, mesh=mesh, in_specs=in_specs, out_specs=out_specs, check_vma=False)
```

```python
import functools

import jax
import jax.numpy as jnp
from jax import lax
from jax.experimental import pallas as pl
from jax.experimental.pallas import tpu as pltpu
from jax.sharding import PartitionSpec as P

PROJ = 64
BLOCK = 64
LANES = 128
STRIDE = 72
VMEM_BYTES = 48 * 1024 * 1024


def chunks_of(width, most):
    if width < 4 * most or most % (4 * LANES):
        chunk = most
        while width % chunk:
            chunk -= LANES
        return [chunk] * (width // chunk)
    inner = width - most
    chunk = most
    while inner % chunk:
        chunk -= LANES
    return [most // 2] + [chunk] * (inner // chunk) + [most // 4] * 2


def split3(x):
    high = x.astype(jnp.bfloat16)
    rest = x - high.astype(jnp.float32)
    mid = rest.astype(jnp.bfloat16)
    low = (rest - mid.astype(jnp.float32)).astype(jnp.bfloat16)
    return high, mid, low


def spread_table(table, spread):
    entries = table.shape[0]
    for row in range(0, BLOCK, 2):
        both = table[:, row * PROJ : row * PROJ + LANES].astype(jnp.float32)
        spread[pl.ds(row, entries, stride=STRIDE), :] = both
        spread[pl.ds(row + 1, entries, stride=STRIDE), :] = pltpu.roll(both, PROJ, 1)


def sign_table(spread, signed):
    entries = spread.shape[0] // STRIDE
    for entry in range(entries):
        block = spread[pl.ds(entry * STRIDE, BLOCK), :].astype(jnp.bfloat16)
        signed[pl.ds((entries + entry) * BLOCK, BLOCK), :] = block
        signed[pl.ds(entry * BLOCK, BLOCK), :] = -block


def lay_blocks(ids, signs, spread, signed, matrix, first, last):
    entries = spread.shape[0] // STRIDE
    for j in range(first, last):
        if signed is None:
            start = pl.multiple_of(ids[j] * STRIDE, 8)
            sign = (2 * signs[j] - 1).astype(jnp.float32)
            block = (spread[pl.ds(start, BLOCK), :] * sign).astype(jnp.bfloat16)
        else:
            start = pl.multiple_of((signs[j] * entries + ids[j]) * BLOCK, BLOCK)
            block = signed[pl.ds(start, BLOCK), :]
        matrix[pl.ds(j * BLOCK, BLOCK), :] = block


def operand(x):
    x1, x2, x3 = split3(x)
    return jnp.concatenate([x1, x1, x2, x1, x3, x2], axis=1)


def products_with(left, act):
    a1, a2, a3 = split3(act)
    right = jnp.concatenate([a1, a2, a1, a3, a1, a2], axis=1)
    return lax.dot_general(left, right, (((1,), (1,)), ((), ())), preferred_element_type=jnp.float32)


def project_kernel(widths, ids, signs, table, rows_ref, out, *refs):
    spread, matrix, held, total, own_table, own_ids, own_signs, sems, *signed = refs
    signed = signed[0] if signed else None
    copies, starts, start = [], [], 0
    for c, width in enumerate(widths):
        columns = pl.ds(start, width)
        copies.append(pltpu.make_async_copy(rows_ref.at[:, columns], held.at[:, columns], sems.at[c]))
        starts.append(start)
        start += width
    small = [
        pltpu.make_async_copy(source, kept, sems.at[len(widths) + k])
        for k, (source, kept) in enumerate(((table, own_table), (ids, own_ids), (signs, own_signs)))
    ]
    for copy in small + copies:
        copy.start()
    small[0].wait()
    spread_table(own_table, spread)
    if signed is not None:
        sign_table(spread, signed)
    small[1].wait()
    small[2].wait()
    lay = functools.partial(lay_blocks, own_ids, own_signs, spread, signed, matrix)
    lay(0, widths[0] // BLOCK)
    for c, copy in enumerate(copies):
        columns = pl.ds(starts[c], widths[c])
        copy.wait()
        if c + 1 < len(widths):
            lay(starts[c + 1] // BLOCK, (starts[c + 1] + widths[c + 1]) // BLOCK)
        part = lax.dot_general(
            matrix[columns, :PROJ],
            held[:, columns],
            (((0,), (1,)), ((), ())),
            preferred_element_type=jnp.float32,
        )
        if c == 0:
            total[...] = part
        elif c + 1 < len(widths):
            total[...] += part
    part = total[...] + part if len(widths) > 1 else part
    pairs, _, tokens = out.shape
    for pair in range(pairs):
        for side in range(2):
            example = 2 * pair + side
            out[pair, pl.ds(side * PROJ, PROJ), :] = part[:, example * tokens : (example + 1) * tokens]


def project(values, ids, signs, table, most, name):
    count, tokens, width = values.shape
    widths = chunks_of(width, most)
    rows = count * tokens
    entries = table.shape[0]
    blocks = ids.shape[0]
    operands = [
        pltpu.with_memory_space_constraint(each, pltpu.HBM)
        for each in (ids, signs, table, values.reshape(rows, width))
    ]
    signed = [pltpu.VMEM((2 * entries * BLOCK, LANES), jnp.bfloat16)] if blocks > entries else []
    return pl.pallas_call(
        functools.partial(project_kernel, widths),
        out_shape=jax.ShapeDtypeStruct((count // 2, LANES, tokens), jnp.float32),
        in_specs=[pl.BlockSpec(memory_space=pltpu.HBM)] * 4,
        out_specs=pl.BlockSpec(memory_space=pltpu.VMEM),
        scratch_shapes=[
            pltpu.VMEM((entries * STRIDE, LANES), jnp.float32),
            pltpu.VMEM((width, LANES), jnp.bfloat16),
            pltpu.VMEM((rows, width), jnp.bfloat16),
            pltpu.VMEM((PROJ, rows), jnp.float32),
            pltpu.VMEM(table.shape, table.dtype),
            pltpu.SMEM(ids.shape, ids.dtype),
            pltpu.SMEM(signs.shape, signs.dtype),
            pltpu.SemaphoreType.DMA((len(widths) + 3,)),
        ]
        + signed,
        compiler_params=pltpu.CompilerParams(vmem_limit_bytes=VMEM_BYTES),
        cost_estimate=pl.CostEstimate(
            flops=2 * rows * width * LANES, bytes_accessed=2 * rows * width, transcendentals=0
        ),
        name=name,
    )(*operands)


def kron_kernel(cuts, grads, own, act, *refs):
    parts = cuts[1]
    outs, rows, products = refs[:-2], refs[-2], refs[-1]
    pairs = act.shape[0]
    for pair in range(pairs):
        both = products_with(operand(grads[pair]), own[pair] + act[pair])
        for side in range(2):
            products[pl.ds((2 * pair + side) * STRIDE, PROJ), :] = both[side * PROJ : (side + 1) * PROJ]
    count = 2 * pairs
    lower = lax.broadcasted_iota(jnp.int32, (count, LANES), 1) < PROJ
    even = lax.broadcasted_iota(jnp.int32, (count, LANES), 0) % 2 == 0
    here = even == lower
    tiles = rows.shape[2] // LANES // cuts[0]
    for tile in range(PROJ * PROJ // LANES):
        both = []
        for p in (2 * tile, 2 * tile + 1):
            v = products[pl.ds(p, count, stride=STRIDE), :]
            both.append(jnp.where(here, v, pltpu.roll(v, PROJ, 1)))
        block, part, within = tile // tiles // parts, tile // tiles % parts, tile % tiles
        rows[part, :, pl.ds((block * tiles + within) * LANES, LANES)] = jnp.where(lower, both[0], both[1])
    for k, out in enumerate(outs):
        part = lax.rem(lax.axis_index("seq") + k % 2, parts) if parts > 1 else 0
        out[...] = rows[part]


def kron_of(grads, own, act, cuts):
    pairs = grads.shape[0]
    parts = cuts[1]
    width = PROJ * PROJ // parts
    outs = 4 if parts > 1 else 1
    vmem = pl.BlockSpec(memory_space=pltpu.VMEM)
    return pl.pallas_call(
        functools.partial(kron_kernel, cuts),
        out_shape=[jax.ShapeDtypeStruct((2 * pairs, width), jnp.float32)] * outs,
        in_specs=[vmem] * 3,
        out_specs=[vmem] * outs,
        scratch_shapes=[
            pltpu.VMEM((parts, 2 * pairs, width), jnp.float32),
            pltpu.VMEM((2 * pairs * STRIDE, LANES), jnp.float32),
        ],
        compiler_params=pltpu.CompilerParams(vmem_limit_bytes=VMEM_BYTES),
        name="kron",
    )(grads, own, act)


def parcels_kernel(parts, *refs):
    summands, parcels = refs[:parts], refs[parts:]
    count = summands[0].shape[0]
    dp = len(parcels)
    width = parcels[0].shape[1]
    core, chip = lax.axis_index("seq"), lax.axis_index("tensor") * 2
    blocks = [chip + core, chip + 1 - core]
    for k, parcel in enumerate(parcels):
        for step, block in enumerate(blocks + [lax.rem(lax.axis_index("dp") + k, dp)]):
            lanes = pl.ds(pl.multiple_of(block * width, LANES), width)
            row = summands[0][:, lanes]
            for other in summands[1:]:
                row = row + other[:, lanes]
            parcel[pl.ds(step * count, count), :] = row


def parcels_of(summands, dp):
    count, width = summands[0].shape
    vmem = pl.BlockSpec(memory_space=pltpu.VMEM)
    return pl.pallas_call(
        functools.partial(parcels_kernel, len(summands)),
        out_shape=[jax.ShapeDtypeStruct((3 * count, width // dp), jnp.float32)] * dp,
        in_specs=[vmem] * len(summands),
        out_specs=[vmem] * dp,
        compiler_params=pltpu.CompilerParams(vmem_limit_bytes=VMEM_BYTES),
        name="parcels",
    )(*summands)


def bundle_kernel(*refs):
    parcels, out = refs[:-1], refs[-1]
    rows = 2 * parcels[0].shape[0] // 3
    for k, parcel in enumerate(parcels):
        out[pl.ds(k * rows, rows), :] = parcel[pl.ds(rows // 2, rows), :]


def bundle_of(parcels):
    rows, width = parcels[0].shape
    vmem = pl.BlockSpec(memory_space=pltpu.VMEM)
    return pl.pallas_call(
        bundle_kernel,
        out_shape=jax.ShapeDtypeStruct((2 * rows // 3 * len(parcels), width), jnp.float32),
        in_specs=[vmem] * len(parcels),
        out_specs=vmem,
        compiler_params=pltpu.CompilerParams(vmem_limit_bytes=VMEM_BYTES),
        name="bundle",
    )(*parcels)


def left_operand(x):
    x1, x2, x3 = split3(x)
    return jnp.concatenate([x1, x1, x2, x1, x3, x2, x2, x3], axis=0).T


def right_operand(x):
    x1, x2, x3 = split3(x)
    return jnp.concatenate([x1, x2, x1, x3, x1, x2, x3, x2], axis=0)


def own_halves(parcels):
    rows = parcels[0].shape[0] // 3
    left = jnp.concatenate([parcel[pl.ds(0, rows), :] for parcel in parcels], axis=0)
    right = jnp.concatenate([parcel[pl.ds(2 * rows, rows), :] for parcel in parcels], axis=0)
    return left, right


def halves_at(part):
    core = lax.axis_index("seq")
    return [pl.ds(pl.multiple_of(place * part, part), part) for place in (core, 1 - core)]


TILE = 256


def quadrant_kernel(scale, *refs):
    parcels, (out, left_ref, right_ref, made, sems) = refs[:-5], refs[-5:]
    part = parcels[0].shape[1]
    left, right = own_halves(parcels)
    left, right = left_operand(left), right_operand(right * scale)
    left_ref[...], right_ref[...] = left, right
    here, _ = halves_at(part)
    copies = []
    for k in range(part // TILE):
        rows = slice(k * TILE, (k + 1) * TILE)
        made[rows, :] = jnp.dot(left[rows], right, preferred_element_type=jnp.float32)
        into = pl.ds(pl.multiple_of(lax.axis_index("seq") * part + k * TILE, TILE), TILE)
        copies.append(pltpu.make_async_copy(made.at[rows], out.at[into, here], sems.at[k]))
        copies[-1].start()
    for copy in copies:
        copy.wait()


def fisher_kernel(scale, begun, left, right, bundle, *refs):
    del begun
    parcels, (mine, out, made, kept, sems) = refs[:-5], refs[-5:]
    rows, part = parcels[0].shape[0] // 3, parcels[0].shape[1]
    here, there = halves_at(part)
    kept[:, here] = parcels[0][pl.ds(0, rows), :]
    kept[:, there] = bundle[pl.ds(0, rows), :]
    copies = [pltpu.make_async_copy(kept, mine, sems.at[0])]
    copies[0].start()
    count = len(parcels)
    other_left = jnp.concatenate([bundle[pl.ds(2 * k * rows, rows), :] for k in range(count)], axis=0)
    other_right = jnp.concatenate([bundle[pl.ds((2 * k + 1) * rows, rows), :] for k in range(count)], axis=0)
    right, other_right = right[...], right_operand(other_right * scale)
    for k in range(part // TILE):
        piece = slice(k * TILE, (k + 1) * TILE)
        made[0, piece, :] = jnp.dot(left[piece, :], other_right, preferred_element_type=jnp.float32)
        into = pl.ds(pl.multiple_of(lax.axis_index("seq") * part + k * TILE, TILE), TILE)
        copies.append(pltpu.make_async_copy(made.at[0, piece], out.at[into, there], sems.at[k + 1]))
        copies[-1].start()
    other_left = left_operand(other_left)
    for k, (operand_right, into) in enumerate(((other_right, there), (right, here))):
        made[k + 1] = jnp.dot(other_left, operand_right, preferred_element_type=jnp.float32)
        copies.append(pltpu.make_async_copy(made.at[k + 1], out.at[there, into], sems.at[part // TILE + k + 1]))
        copies[-1].start()
    for copy in copies:
        copy.wait()


def quadrant_of(parcels):
    rows, part = parcels[0].shape
    total = rows // 3 * len(parcels)
    vmem = pl.BlockSpec(memory_space=pltpu.VMEM)
    return pl.pallas_call(
        functools.partial(quadrant_kernel, 1.0 / total),
        out_shape=[
            jax.ShapeDtypeStruct((2 * part, 2 * part), jnp.float32),
            jax.ShapeDtypeStruct((part, 8 * total), jnp.bfloat16),
            jax.ShapeDtypeStruct((8 * total, part), jnp.bfloat16),
        ],
        in_specs=[vmem] * len(parcels),
        out_specs=[pl.BlockSpec(memory_space=pltpu.HBM), vmem, vmem],
        scratch_shapes=[pltpu.VMEM((part, part), jnp.float32), pltpu.SemaphoreType.DMA((part // TILE,))],
        compiler_params=pltpu.CompilerParams(vmem_limit_bytes=VMEM_BYTES),
        cost_estimate=pl.CostEstimate(flops=2**28, bytes_accessed=4 * part * part, transcendentals=0),
        name="quadrant",
    )(*parcels)


def fisher_block(begun, parcels, bundle):
    rows, part = parcels[0].shape
    rows //= 3
    width = 2 * part
    hbm = pl.BlockSpec(memory_space=pltpu.HBM)
    vmem = pl.BlockSpec(memory_space=pltpu.VMEM)
    return pl.pallas_call(
        functools.partial(fisher_kernel, 1.0 / (rows * len(parcels))),
        out_shape=[
            jax.ShapeDtypeStruct((rows, width), jnp.float32),
            jax.ShapeDtypeStruct((width, width), jnp.float32),
        ],
        in_specs=[hbm] + [vmem] * (3 + len(parcels)),
        out_specs=[hbm] * 2,
        scratch_shapes=[
            pltpu.VMEM((3, part, part), jnp.float32),
            pltpu.VMEM((rows, width), jnp.float32),
            pltpu.SemaphoreType.DMA((part // TILE + 3,)),
        ],
        input_output_aliases={0: 1},
        compiler_params=pltpu.CompilerParams(vmem_limit_bytes=VMEM_BYTES),
        name="fisher",
    )(*begun, bundle, *parcels)


def local(acts, grads, in_ids, in_signs, out_ids, out_signs, in_table, out_table):
    tensor, seq, dp = (lax.axis_size(name) for name in ("tensor", "seq", "dp"))
    shards = tensor * seq
    small = tensor == 2 and seq == 2 and dp == 4
    swap = [(0, 1), (1, 0)]

    act = project(acts, in_ids, in_signs, in_table, 512, "project_acts")
    if tensor == 2:
        other = lax.ppermute(act, "tensor", swap)
    else:
        act = lax.psum(act, "tensor")
        other = jnp.zeros_like(act)
    grad = project(grads, out_ids, out_signs, out_table, 1024, "project_grads")
    krons = kron_of(grad, act, other, (shards, seq) if small else (1, 1))

    if not small:
        kron = lax.psum(krons[0], ("tensor", "seq"))
        width = kron.shape[1] // shards
        place = lax.axis_index("tensor") * seq + lax.axis_index("seq")
        mine = lax.dynamic_slice_in_dim(kron, place * width, width, 1)
        every = lax.all_gather(kron, "dp", axis=0, tiled=True)
        left = lax.dynamic_slice_in_dim(every, place * width, width, 1)
        columns = kron.shape[1] // dp
        right = lax.dynamic_slice_in_dim(every, lax.axis_index("dp") * columns, columns, 1)
        fisher = lax.dot_general(
            left, right, (((0,), (0,)), ((), ())), precision=lax.Precision.HIGHEST
        ) / left.shape[0]
        return mine, fisher

    across = lax.ppermute(krons[1], ("tensor", "seq"), [(p, 3 - p) for p in range(shards)])
    beside = lax.ppermute(krons[2], "tensor", swap)
    mate = lax.ppermute(krons[3], "seq", swap)
    parcels = list(parcels_of([across, beside, mate, krons[0]], dp))
    for k in range(1, dp):
        parcels[k] = lax.ppermute(parcels[k], "dp", [(d, (d + k) % dp) for d in range(dp)])
    bundle = lax.ppermute(bundle_of(parcels), "seq", swap)
    mine, fisher = fisher_block(quadrant_of(parcels), parcels, bundle)
    return mine, fisher


def solution(mesh):
    in_specs = (
        P(("groups", "dp"), "seq", "tensor"),
        P(("groups", "dp"), "seq", "tensor"),
        P("tensor"),
        P("tensor"),
        P("tensor"),
        P("tensor"),
        P(),
        P(),
    )
    out_specs = (P(("groups", "dp"), ("tensor", "seq")), P(("groups", "tensor", "seq"), "dp"))
    return jax.shard_map(local, mesh=mesh, in_specs=in_specs, out_specs=out_specs, check_vma=False)
```

```python
import functools

import jax
import jax.numpy as jnp
from jax import lax
from jax.experimental import pallas as pl
from jax.experimental.pallas import tpu as pltpu
from jax.sharding import PartitionSpec as P

PROJ = 64
BLOCK = 64
LANES = 128
STRIDE = 72
VMEM_BYTES = 48 * 1024 * 1024


def chunks_of(width, most):
    if width < 4 * most or most % (4 * LANES):
        chunk = most
        while width % chunk:
            chunk -= LANES
        return [chunk] * (width // chunk)
    inner = width - most
    chunk = most
    while inner % chunk:
        chunk -= LANES
    return [most // 2] + [chunk] * (inner // chunk) + [most // 4] * 2


def split3(x):
    high = x.astype(jnp.bfloat16)
    rest = x - high.astype(jnp.float32)
    mid = rest.astype(jnp.bfloat16)
    low = (rest - mid.astype(jnp.float32)).astype(jnp.bfloat16)
    return high, mid, low


def spread_table(table, spread):
    entries = table.shape[0]
    for row in range(0, BLOCK, 2):
        both = table[:, row * PROJ : row * PROJ + LANES].astype(jnp.float32)
        spread[pl.ds(row, entries, stride=STRIDE), :] = both
        spread[pl.ds(row + 1, entries, stride=STRIDE), :] = pltpu.roll(both, PROJ, 1)


def sign_table(spread, signed):
    entries = spread.shape[0] // STRIDE
    for entry in range(entries):
        block = spread[pl.ds(entry * STRIDE, BLOCK), :].astype(jnp.bfloat16)
        signed[pl.ds((entries + entry) * BLOCK, BLOCK), :] = block
        signed[pl.ds(entry * BLOCK, BLOCK), :] = -block


def lay_blocks(ids, signs, spread, signed, matrix, first, last):
    entries = spread.shape[0] // STRIDE
    for j in range(first, last):
        if signed is None:
            start = pl.multiple_of(ids[j] * STRIDE, 8)
            sign = (2 * signs[j] - 1).astype(jnp.float32)
            block = (spread[pl.ds(start, BLOCK), :] * sign).astype(jnp.bfloat16)
        else:
            start = pl.multiple_of((signs[j] * entries + ids[j]) * BLOCK, BLOCK)
            block = signed[pl.ds(start, BLOCK), :]
        matrix[pl.ds(j * BLOCK, BLOCK), :] = block


def operand(x):
    x1, x2, x3 = split3(x)
    return jnp.concatenate([x1, x1, x2, x1, x3, x2], axis=1)


def products_with(left, act):
    a1, a2, a3 = split3(act)
    right = jnp.concatenate([a1, a2, a1, a3, a1, a2], axis=1)
    return lax.dot_general(left, right, (((1,), (1,)), ((), ())), preferred_element_type=jnp.float32)


def project_kernel(widths, streamed, ids, signs, table, rows_ref, out, *refs):
    spread, matrix, held, total, own_table, own_ids, own_signs, sems, *signed = refs
    signed = signed[0] if signed else None
    half = held.shape[0] // 2
    copies, starts, start = [], [], 0
    for c, width in enumerate(widths):
        columns = pl.ds(start, width)
        copies.append(pltpu.make_async_copy(rows_ref.at[:, columns], held.at[:, columns], sems.at[c]))
        starts.append(start)
        start += width
    small = [
        pltpu.make_async_copy(source, kept, sems.at[len(widths) + k])
        for k, (source, kept) in enumerate(((table, own_table), (ids, own_ids), (signs, own_signs)))
    ]
    for copy in small + copies:
        copy.start()
    small[0].wait()
    spread_table(own_table, spread)
    if signed is not None:
        sign_table(spread, signed)
    small[1].wait()
    small[2].wait()
    lay = functools.partial(lay_blocks, own_ids, own_signs, spread, signed, matrix)
    lay(0, widths[0] // BLOCK)
    for c, copy in enumerate(copies):
        columns = pl.ds(starts[c], widths[c])
        copy.wait()
        if c + 1 < len(widths):
            lay(starts[c + 1] // BLOCK, (starts[c + 1] + widths[c + 1]) // BLOCK)
        if streamed:
            parts = [
                jnp.dot(held[pl.ds(k * half, half), columns], matrix[columns, :], preferred_element_type=jnp.float32)
                for k in range(2)
            ]
        else:
            parts = [
                lax.dot_general(
                    matrix[columns, :PROJ],
                    held[pl.ds(k * half, half), columns],
                    (((0,), (1,)), ((), ())),
                    preferred_element_type=jnp.float32,
                )
                for k in range(2)
            ]
        if c > 0:
            parts = [total[k] + part for k, part in enumerate(parts)]
        if c + 1 < len(widths):
            for k, part in enumerate(parts):
                total[k] = part
    pairs, _, tokens = out.shape
    for pair in range(pairs):
        for side in range(2):
            example = 2 * pair + side
            k, start = example * tokens // half, example * tokens % half
            if streamed:
                mine = parts[k][start : start + tokens, :].T[:PROJ, :]
            else:
                mine = parts[k][:, start : start + tokens]
            out[pair, pl.ds(side * PROJ, PROJ), :] = mine


def project(values, ids, signs, table, most, streamed, name):
    count, tokens, width = values.shape
    widths = chunks_of(width, most)
    rows = count * tokens
    entries = table.shape[0]
    blocks = ids.shape[0]
    operands = [
        pltpu.with_memory_space_constraint(each, pltpu.HBM)
        for each in (ids, signs, table, values.reshape(rows, width))
    ]
    signed = [pltpu.VMEM((2 * entries * BLOCK, LANES), jnp.bfloat16)] if blocks > entries else []
    return pl.pallas_call(
        functools.partial(project_kernel, widths, streamed),
        out_shape=jax.ShapeDtypeStruct((count // 2, LANES, tokens), jnp.float32),
        in_specs=[pl.BlockSpec(memory_space=pltpu.HBM)] * 4,
        out_specs=pl.BlockSpec(memory_space=pltpu.VMEM),
        scratch_shapes=[
            pltpu.VMEM((entries * STRIDE, LANES), jnp.float32),
            pltpu.VMEM((width, LANES), jnp.bfloat16),
            pltpu.VMEM((rows, width), jnp.bfloat16),
            pltpu.VMEM((2, rows // 2, LANES) if streamed else (2, PROJ, rows // 2), jnp.float32),
            pltpu.VMEM(table.shape, table.dtype),
            pltpu.SMEM(ids.shape, ids.dtype),
            pltpu.SMEM(signs.shape, signs.dtype),
            pltpu.SemaphoreType.DMA((len(widths) + 3,)),
        ]
        + signed,
        compiler_params=pltpu.CompilerParams(vmem_limit_bytes=VMEM_BYTES),
        cost_estimate=pl.CostEstimate(
            flops=2 * rows * width * LANES, bytes_accessed=2 * rows * width, transcendentals=0
        ),
        name=name,
    )(*operands)


def kron_kernel(cuts, grads, own, act, *refs):
    parts = cuts[1]
    outs, rows, products = refs[:-2], refs[-2], refs[-1]
    pairs = act.shape[0]
    for pair in range(pairs):
        both = products_with(operand(grads[pair]), own[pair] + act[pair])
        for side in range(2):
            products[pl.ds((2 * pair + side) * STRIDE, PROJ), :] = both[side * PROJ : (side + 1) * PROJ]
    count = 2 * pairs
    lower = lax.broadcasted_iota(jnp.int32, (count, LANES), 1) < PROJ
    even = lax.broadcasted_iota(jnp.int32, (count, LANES), 0) % 2 == 0
    here = even == lower
    tiles = rows.shape[2] // LANES // cuts[0]
    for tile in range(PROJ * PROJ // LANES):
        both = []
        for p in (2 * tile, 2 * tile + 1):
            v = products[pl.ds(p, count, stride=STRIDE), :]
            both.append(jnp.where(here, v, pltpu.roll(v, PROJ, 1)))
        block, part, within = tile // tiles // parts, tile // tiles % parts, tile % tiles
        rows[part, :, pl.ds((block * tiles + within) * LANES, LANES)] = jnp.where(lower, both[0], both[1])
    for k, out in enumerate(outs):
        part = lax.rem(lax.axis_index("seq") + k % 2, parts) if parts > 1 else 0
        out[...] = rows[part]


def kron_of(grads, own, act, cuts):
    pairs = grads.shape[0]
    parts = cuts[1]
    width = PROJ * PROJ // parts
    outs = 4 if parts > 1 else 1
    vmem = pl.BlockSpec(memory_space=pltpu.VMEM)
    return pl.pallas_call(
        functools.partial(kron_kernel, cuts),
        out_shape=[jax.ShapeDtypeStruct((2 * pairs, width), jnp.float32)] * outs,
        in_specs=[vmem] * 3,
        out_specs=[vmem] * outs,
        scratch_shapes=[
            pltpu.VMEM((parts, 2 * pairs, width), jnp.float32),
            pltpu.VMEM((2 * pairs * STRIDE, LANES), jnp.float32),
        ],
        compiler_params=pltpu.CompilerParams(vmem_limit_bytes=VMEM_BYTES),
        name="kron",
    )(grads, own, act)


def parcels_kernel(parts, *refs):
    summands, parcels = refs[:parts], refs[parts:]
    count = summands[0].shape[0]
    dp = len(parcels)
    width = parcels[0].shape[1]
    core, chip = lax.axis_index("seq"), lax.axis_index("tensor") * 2
    blocks = [chip + core, chip + 1 - core]
    for k, parcel in enumerate(parcels):
        for step, block in enumerate(blocks + [lax.rem(lax.axis_index("dp") + k, dp)]):
            lanes = pl.ds(pl.multiple_of(block * width, LANES), width)
            row = summands[0][:, lanes]
            for other in summands[1:]:
                row = row + other[:, lanes]
            parcel[pl.ds(step * count, count), :] = row


def parcels_of(summands, dp):
    count, width = summands[0].shape
    vmem = pl.BlockSpec(memory_space=pltpu.VMEM)
    return pl.pallas_call(
        functools.partial(parcels_kernel, len(summands)),
        out_shape=[jax.ShapeDtypeStruct((3 * count, width // dp), jnp.float32)] * dp,
        in_specs=[vmem] * len(summands),
        out_specs=[vmem] * dp,
        compiler_params=pltpu.CompilerParams(vmem_limit_bytes=VMEM_BYTES),
        name="parcels",
    )(*summands)


def bundle_kernel(*refs):
    parcels, out = refs[:-1], refs[-1]
    rows = 2 * parcels[0].shape[0] // 3
    for k, parcel in enumerate(parcels):
        out[pl.ds(k * rows, rows), :] = parcel[pl.ds(rows // 2, rows), :]


def bundle_of(parcels):
    rows, width = parcels[0].shape
    vmem = pl.BlockSpec(memory_space=pltpu.VMEM)
    return pl.pallas_call(
        bundle_kernel,
        out_shape=jax.ShapeDtypeStruct((2 * rows // 3 * len(parcels), width), jnp.float32),
        in_specs=[vmem] * len(parcels),
        out_specs=vmem,
        compiler_params=pltpu.CompilerParams(vmem_limit_bytes=VMEM_BYTES),
        name="bundle",
    )(*parcels)


def left_operand(x):
    x1, x2, x3 = split3(x)
    return jnp.concatenate([x1, x1, x2, x1, x3, x2, x2, x3], axis=0).T


def right_operand(x):
    x1, x2, x3 = split3(x)
    return jnp.concatenate([x1, x2, x1, x3, x1, x2, x3, x2], axis=0)


def own_halves(parcels):
    rows = parcels[0].shape[0] // 3
    left = jnp.concatenate([parcel[pl.ds(0, rows), :] for parcel in parcels], axis=0)
    right = jnp.concatenate([parcel[pl.ds(2 * rows, rows), :] for parcel in parcels], axis=0)
    return left, right


def halves_at(part):
    core = lax.axis_index("seq")
    return [pl.ds(pl.multiple_of(place * part, part), part) for place in (core, 1 - core)]


TILE = 256


def quadrant_kernel(scale, *refs):
    parcels, (out, left_ref, right_ref, made, sems) = refs[:-5], refs[-5:]
    part = parcels[0].shape[1]
    left, right = own_halves(parcels)
    left, right = left_operand(left), right_operand(right * scale)
    left_ref[...], right_ref[...] = left, right
    here, _ = halves_at(part)
    copies = []
    for k in range(part // TILE):
        rows = slice(k * TILE, (k + 1) * TILE)
        made[rows, :] = jnp.dot(left[rows], right, preferred_element_type=jnp.float32)
        into = pl.ds(pl.multiple_of(lax.axis_index("seq") * part + k * TILE, TILE), TILE)
        copies.append(pltpu.make_async_copy(made.at[rows], out.at[into, here], sems.at[k]))
        copies[-1].start()
    for copy in copies:
        copy.wait()


def fisher_kernel(scale, begun, left, right, bundle, *refs):
    del begun
    parcels, (mine, out, made, kept, sems) = refs[:-5], refs[-5:]
    rows, part = parcels[0].shape[0] // 3, parcels[0].shape[1]
    here, there = halves_at(part)
    kept[:, here] = parcels[0][pl.ds(0, rows), :]
    kept[:, there] = bundle[pl.ds(0, rows), :]
    copies = [pltpu.make_async_copy(kept, mine, sems.at[0])]
    copies[0].start()
    count = len(parcels)
    other_left = jnp.concatenate([bundle[pl.ds(2 * k * rows, rows), :] for k in range(count)], axis=0)
    other_right = jnp.concatenate([bundle[pl.ds((2 * k + 1) * rows, rows), :] for k in range(count)], axis=0)
    right, other_right = right[...], right_operand(other_right * scale)
    for k in range(part // TILE):
        piece = slice(k * TILE, (k + 1) * TILE)
        made[0, piece, :] = jnp.dot(left[piece, :], other_right, preferred_element_type=jnp.float32)
        into = pl.ds(pl.multiple_of(lax.axis_index("seq") * part + k * TILE, TILE), TILE)
        copies.append(pltpu.make_async_copy(made.at[0, piece], out.at[into, there], sems.at[k + 1]))
        copies[-1].start()
    other_left = left_operand(other_left)
    for k, (operand_right, into) in enumerate(((other_right, there), (right, here))):
        made[k + 1] = jnp.dot(other_left, operand_right, preferred_element_type=jnp.float32)
        copies.append(pltpu.make_async_copy(made.at[k + 1], out.at[there, into], sems.at[part // TILE + k + 1]))
        copies[-1].start()
    for copy in copies:
        copy.wait()


def quadrant_of(parcels):
    rows, part = parcels[0].shape
    total = rows // 3 * len(parcels)
    vmem = pl.BlockSpec(memory_space=pltpu.VMEM)
    return pl.pallas_call(
        functools.partial(quadrant_kernel, 1.0 / total),
        out_shape=[
            jax.ShapeDtypeStruct((2 * part, 2 * part), jnp.float32),
            jax.ShapeDtypeStruct((part, 8 * total), jnp.bfloat16),
            jax.ShapeDtypeStruct((8 * total, part), jnp.bfloat16),
        ],
        in_specs=[vmem] * len(parcels),
        out_specs=[pl.BlockSpec(memory_space=pltpu.HBM), vmem, vmem],
        scratch_shapes=[pltpu.VMEM((part, part), jnp.float32), pltpu.SemaphoreType.DMA((part // TILE,))],
        compiler_params=pltpu.CompilerParams(vmem_limit_bytes=VMEM_BYTES),
        cost_estimate=pl.CostEstimate(flops=2**28, bytes_accessed=4 * part * part, transcendentals=0),
        name="quadrant",
    )(*parcels)


def fisher_block(begun, parcels, bundle):
    rows, part = parcels[0].shape
    rows //= 3
    width = 2 * part
    hbm = pl.BlockSpec(memory_space=pltpu.HBM)
    vmem = pl.BlockSpec(memory_space=pltpu.VMEM)
    return pl.pallas_call(
        functools.partial(fisher_kernel, 1.0 / (rows * len(parcels))),
        out_shape=[
            jax.ShapeDtypeStruct((rows, width), jnp.float32),
            jax.ShapeDtypeStruct((width, width), jnp.float32),
        ],
        in_specs=[hbm] + [vmem] * (3 + len(parcels)),
        out_specs=[hbm] * 2,
        scratch_shapes=[
            pltpu.VMEM((3, part, part), jnp.float32),
            pltpu.VMEM((rows, width), jnp.float32),
            pltpu.SemaphoreType.DMA((part // TILE + 3,)),
        ],
        input_output_aliases={0: 1},
        compiler_params=pltpu.CompilerParams(vmem_limit_bytes=VMEM_BYTES),
        name="fisher",
    )(*begun, bundle, *parcels)


def local(acts, grads, in_ids, in_signs, out_ids, out_signs, in_table, out_table):
    tensor, seq, dp = (lax.axis_size(name) for name in ("tensor", "seq", "dp"))
    shards = tensor * seq
    small = tensor == 2 and seq == 2 and dp == 4
    swap = [(0, 1), (1, 0)]

    act = project(acts, in_ids, in_signs, in_table, 512, True, "project_acts")
    if tensor == 2:
        other = lax.ppermute(act, "tensor", swap)
    else:
        act = lax.psum(act, "tensor")
        other = jnp.zeros_like(act)
    grad = project(grads, out_ids, out_signs, out_table, 1024, False, "project_grads")
    krons = kron_of(grad, act, other, (shards, seq) if small else (1, 1))

    if not small:
        kron = lax.psum(krons[0], ("tensor", "seq"))
        width = kron.shape[1] // shards
        place = lax.axis_index("tensor") * seq + lax.axis_index("seq")
        mine = lax.dynamic_slice_in_dim(kron, place * width, width, 1)
        every = lax.all_gather(kron, "dp", axis=0, tiled=True)
        left = lax.dynamic_slice_in_dim(every, place * width, width, 1)
        columns = kron.shape[1] // dp
        right = lax.dynamic_slice_in_dim(every, lax.axis_index("dp") * columns, columns, 1)
        fisher = lax.dot_general(
            left, right, (((0,), (0,)), ((), ())), precision=lax.Precision.HIGHEST
        ) / left.shape[0]
        return mine, fisher

    across = lax.ppermute(krons[1], ("tensor", "seq"), [(p, 3 - p) for p in range(shards)])
    beside = lax.ppermute(krons[2], "tensor", swap)
    mate = lax.ppermute(krons[3], "seq", swap)
    parcels = list(parcels_of([across, beside, mate, krons[0]], dp))
    for k in range(1, dp):
        parcels[k] = lax.ppermute(parcels[k], "dp", [(d, (d + k) % dp) for d in range(dp)])
    bundle = lax.ppermute(bundle_of(parcels), "seq", swap)
    mine, fisher = fisher_block(quadrant_of(parcels), parcels, bundle)
    return mine, fisher


def solution(mesh):
    in_specs = (
        P(("groups", "dp"), "seq", "tensor"),
        P(("groups", "dp"), "seq", "tensor"),
        P("tensor"),
        P("tensor"),
        P("tensor"),
        P("tensor"),
        P(),
        P(),
    )
    out_specs = (P(("groups", "dp"), ("tensor", "seq")), P(("groups", "tensor", "seq"), "dp"))
    return jax.shard_map(local, mesh=mesh, in_specs=in_specs, out_specs=out_specs, check_vma=False)
```

```python
import functools

import jax
import jax.numpy as jnp
from jax import lax
from jax.experimental import pallas as pl
from jax.experimental.pallas import tpu as pltpu
from jax.sharding import PartitionSpec as P

PROJ = 64
BLOCK = 64
LANES = 128
STRIDE = 72
TABLE_COPIES = 4
VMEM_BYTES = 48 * 1024 * 1024


def chunks_of(width, most):
    if width < 4 * most or most % (4 * LANES):
        chunk = most
        while width % chunk:
            chunk -= LANES
        return [chunk] * (width // chunk)
    inner = width - most
    chunk = most
    while inner % chunk:
        chunk -= LANES
    return [most // 2] + [chunk] * (inner // chunk) + [most // 4] * 2


def split3(x):
    high = x.astype(jnp.bfloat16)
    rest = x - high.astype(jnp.float32)
    mid = rest.astype(jnp.bfloat16)
    low = (rest - mid.astype(jnp.float32)).astype(jnp.bfloat16)
    return high, mid, low


def spread_table(table, spread, first, last):
    entries = table.shape[0]
    for row in range(first, last, 2):
        both = table[:, row * PROJ : row * PROJ + LANES].astype(jnp.float32)
        spread[pl.ds(row, entries, stride=STRIDE), :] = both
        spread[pl.ds(row + 1, entries, stride=STRIDE), :] = pltpu.roll(both, PROJ, 1)


def sign_table(spread, signed):
    entries = spread.shape[0] // STRIDE
    for entry in range(entries):
        block = spread[pl.ds(entry * STRIDE, BLOCK), :].astype(jnp.bfloat16)
        signed[pl.ds((entries + entry) * BLOCK, BLOCK), :] = block
        signed[pl.ds(entry * BLOCK, BLOCK), :] = -block


def lay_blocks(ids, signs, spread, signed, matrix, first, last):
    entries = spread.shape[0] // STRIDE
    for j in range(first, last):
        if signed is None:
            start = pl.multiple_of(ids[j] * STRIDE, 8)
            sign = (2 * signs[j] - 1).astype(jnp.float32)
            block = (spread[pl.ds(start, BLOCK), :] * sign).astype(jnp.bfloat16)
        else:
            start = pl.multiple_of((signs[j] * entries + ids[j]) * BLOCK, BLOCK)
            block = signed[pl.ds(start, BLOCK), :]
        matrix[pl.ds(j * BLOCK, BLOCK), :] = block


def operand(x):
    x1, x2, x3 = split3(x)
    return jnp.concatenate([x1, x1, x2, x1, x3, x2], axis=1)


def products_with(left, act):
    a1, a2, a3 = split3(act)
    right = jnp.concatenate([a1, a2, a1, a3, a1, a2], axis=1)
    return lax.dot_general(left, right, (((1,), (1,)), ((), ())), preferred_element_type=jnp.float32)


def project_kernel(widths, ids, signs, table, rows_ref, out, *refs):
    spread, matrix, held, total, own_table, own_ids, own_signs, sems, *signed = refs
    signed = signed[0] if signed else None
    copies, starts, start = [], [], 0
    for c, width in enumerate(widths):
        columns = pl.ds(start, width)
        copies.append(pltpu.make_async_copy(rows_ref.at[:, columns], held.at[:, columns], sems.at[c]))
        starts.append(start)
        start += width
    quarter = BLOCK // TABLE_COPIES
    parts = [pl.ds(k * quarter * PROJ, quarter * PROJ) for k in range(TABLE_COPIES)]
    small = [(table.at[:, part], own_table.at[:, part]) for part in parts]
    small += [(ids, own_ids), (signs, own_signs)]
    small = [
        pltpu.make_async_copy(source, kept, sems.at[len(widths) + k]) for k, (source, kept) in enumerate(small)
    ]
    for copy in small + copies:
        copy.start()
    for k in range(TABLE_COPIES):
        small[k].wait()
        spread_table(own_table, spread, k * quarter, (k + 1) * quarter)
    if signed is not None:
        sign_table(spread, signed)
    for copy in small[TABLE_COPIES:]:
        copy.wait()
    lay = functools.partial(lay_blocks, own_ids, own_signs, spread, signed, matrix)
    lay(0, widths[0] // BLOCK)
    for c, copy in enumerate(copies):
        columns = pl.ds(starts[c], widths[c])
        copy.wait()
        if c + 1 < len(widths):
            lay(starts[c + 1] // BLOCK, (starts[c + 1] + widths[c + 1]) // BLOCK)
        part = lax.dot_general(
            matrix[columns, :PROJ],
            held[:, columns],
            (((0,), (1,)), ((), ())),
            preferred_element_type=jnp.float32,
        )
        if c == 0:
            total[...] = part
        elif c + 1 < len(widths):
            total[...] += part
    part = total[...] + part if len(widths) > 1 else part
    pairs, _, tokens = out.shape
    for pair in range(pairs):
        for side in range(2):
            example = 2 * pair + side
            out[pair, pl.ds(side * PROJ, PROJ), :] = part[:, example * tokens : (example + 1) * tokens]


def project(values, ids, signs, table, most, name):
    count, tokens, width = values.shape
    widths = chunks_of(width, most)
    rows = count * tokens
    entries = table.shape[0]
    blocks = ids.shape[0]
    operands = [
        pltpu.with_memory_space_constraint(each, pltpu.HBM)
        for each in (ids, signs, table, values.reshape(rows, width))
    ]
    signed = [pltpu.VMEM((2 * entries * BLOCK, LANES), jnp.bfloat16)] if blocks > entries else []
    return pl.pallas_call(
        functools.partial(project_kernel, widths),
        out_shape=jax.ShapeDtypeStruct((count // 2, LANES, tokens), jnp.float32),
        in_specs=[pl.BlockSpec(memory_space=pltpu.HBM)] * 4,
        out_specs=pl.BlockSpec(memory_space=pltpu.VMEM),
        scratch_shapes=[
            pltpu.VMEM((entries * STRIDE, LANES), jnp.float32),
            pltpu.VMEM((width, LANES), jnp.bfloat16),
            pltpu.VMEM((rows, width), jnp.bfloat16),
            pltpu.VMEM((PROJ, rows), jnp.float32),
            pltpu.VMEM(table.shape, table.dtype),
            pltpu.SMEM(ids.shape, ids.dtype),
            pltpu.SMEM(signs.shape, signs.dtype),
            pltpu.SemaphoreType.DMA((len(widths) + TABLE_COPIES + 2,)),
        ]
        + signed,
        compiler_params=pltpu.CompilerParams(vmem_limit_bytes=VMEM_BYTES),
        cost_estimate=pl.CostEstimate(
            flops=2 * rows * width * LANES, bytes_accessed=2 * rows * width, transcendentals=0
        ),
        name=name,
    )(*operands)


def kron_kernel(cuts, grads, own, act, *refs):
    parts = cuts[1]
    outs, rows, products = refs[:-2], refs[-2], refs[-1]
    pairs = act.shape[0]
    for pair in range(pairs):
        both = products_with(operand(grads[pair]), own[pair] + act[pair])
        for side in range(2):
            products[pl.ds((2 * pair + side) * STRIDE, PROJ), :] = both[side * PROJ : (side + 1) * PROJ]
    count = 2 * pairs
    lower = lax.broadcasted_iota(jnp.int32, (count, LANES), 1) < PROJ
    even = lax.broadcasted_iota(jnp.int32, (count, LANES), 0) % 2 == 0
    here = even == lower
    tiles = rows.shape[2] // LANES // cuts[0]
    for tile in range(PROJ * PROJ // LANES):
        both = []
        for p in (2 * tile, 2 * tile + 1):
            v = products[pl.ds(p, count, stride=STRIDE), :]
            both.append(jnp.where(here, v, pltpu.roll(v, PROJ, 1)))
        block, part, within = tile // tiles // parts, tile // tiles % parts, tile % tiles
        rows[part, :, pl.ds((block * tiles + within) * LANES, LANES)] = jnp.where(lower, both[0], both[1])
    for k, out in enumerate(outs):
        part = lax.rem(lax.axis_index("seq") + k % 2, parts) if parts > 1 else 0
        out[...] = rows[part]


def kron_of(grads, own, act, cuts):
    pairs = grads.shape[0]
    parts = cuts[1]
    width = PROJ * PROJ // parts
    outs = 4 if parts > 1 else 1
    vmem = pl.BlockSpec(memory_space=pltpu.VMEM)
    return pl.pallas_call(
        functools.partial(kron_kernel, cuts),
        out_shape=[jax.ShapeDtypeStruct((2 * pairs, width), jnp.float32)] * outs,
        in_specs=[vmem] * 3,
        out_specs=[vmem] * outs,
        scratch_shapes=[
            pltpu.VMEM((parts, 2 * pairs, width), jnp.float32),
            pltpu.VMEM((2 * pairs * STRIDE, LANES), jnp.float32),
        ],
        compiler_params=pltpu.CompilerParams(vmem_limit_bytes=VMEM_BYTES),
        name="kron",
    )(grads, own, act)


def parcels_kernel(parts, *refs):
    summands, parcels = refs[:parts], refs[parts:]
    count = summands[0].shape[0]
    dp = len(parcels)
    width = parcels[0].shape[1]
    core, chip = lax.axis_index("seq"), lax.axis_index("tensor") * 2
    blocks = [chip + core, chip + 1 - core]
    for k, parcel in enumerate(parcels):
        for step, block in enumerate(blocks + [lax.rem(lax.axis_index("dp") + k, dp)]):
            lanes = pl.ds(pl.multiple_of(block * width, LANES), width)
            row = summands[0][:, lanes]
            for other in summands[1:]:
                row = row + other[:, lanes]
            parcel[pl.ds(step * count, count), :] = row


def parcels_of(summands, dp):
    count, width = summands[0].shape
    vmem = pl.BlockSpec(memory_space=pltpu.VMEM)
    return pl.pallas_call(
        functools.partial(parcels_kernel, len(summands)),
        out_shape=[jax.ShapeDtypeStruct((3 * count, width // dp), jnp.float32)] * dp,
        in_specs=[vmem] * len(summands),
        out_specs=[vmem] * dp,
        compiler_params=pltpu.CompilerParams(vmem_limit_bytes=VMEM_BYTES),
        name="parcels",
    )(*summands)


def bundle_kernel(*refs):
    parcels, out = refs[:-1], refs[-1]
    rows = 2 * parcels[0].shape[0] // 3
    for k, parcel in enumerate(parcels):
        out[pl.ds(k * rows, rows), :] = parcel[pl.ds(rows // 2, rows), :]


def bundle_of(parcels):
    rows, width = parcels[0].shape
    vmem = pl.BlockSpec(memory_space=pltpu.VMEM)
    return pl.pallas_call(
        bundle_kernel,
        out_shape=jax.ShapeDtypeStruct((2 * rows // 3 * len(parcels), width), jnp.float32),
        in_specs=[vmem] * len(parcels),
        out_specs=vmem,
        compiler_params=pltpu.CompilerParams(vmem_limit_bytes=VMEM_BYTES),
        name="bundle",
    )(*parcels)


def left_operand(x):
    x1, x2, x3 = split3(x)
    return jnp.concatenate([x1, x1, x2, x1, x3, x2, x2, x3], axis=0).T


def right_operand(x):
    x1, x2, x3 = split3(x)
    return jnp.concatenate([x1, x2, x1, x3, x1, x2, x3, x2], axis=0)


def own_halves(parcels):
    rows = parcels[0].shape[0] // 3
    left = jnp.concatenate([parcel[pl.ds(0, rows), :] for parcel in parcels], axis=0)
    right = jnp.concatenate([parcel[pl.ds(2 * rows, rows), :] for parcel in parcels], axis=0)
    return left, right


def halves_at(part):
    core = lax.axis_index("seq")
    return [pl.ds(pl.multiple_of(place * part, part), part) for place in (core, 1 - core)]


TILE = 256


def quadrant_kernel(scale, *refs):
    parcels, (out, left_ref, right_ref, made, sems) = refs[:-5], refs[-5:]
    part = parcels[0].shape[1]
    left, right = own_halves(parcels)
    left, right = left_operand(left), right_operand(right * scale)
    left_ref[...], right_ref[...] = left, right
    here, _ = halves_at(part)
    copies = []
    for k in range(part // TILE):
        rows = slice(k * TILE, (k + 1) * TILE)
        made[rows, :] = jnp.dot(left[rows], right, preferred_element_type=jnp.float32)
        into = pl.ds(pl.multiple_of(lax.axis_index("seq") * part + k * TILE, TILE), TILE)
        copies.append(pltpu.make_async_copy(made.at[rows], out.at[into, here], sems.at[k]))
        copies[-1].start()
    for copy in copies:
        copy.wait()


def fisher_kernel(scale, begun, left, right, bundle, *refs):
    del begun
    parcels, (mine, out, made, kept, sems) = refs[:-5], refs[-5:]
    rows, part = parcels[0].shape[0] // 3, parcels[0].shape[1]
    here, there = halves_at(part)
    kept[:, here] = parcels[0][pl.ds(0, rows), :]
    kept[:, there] = bundle[pl.ds(0, rows), :]
    copies = [pltpu.make_async_copy(kept, mine, sems.at[0])]
    copies[0].start()
    count = len(parcels)
    other_left = jnp.concatenate([bundle[pl.ds(2 * k * rows, rows), :] for k in range(count)], axis=0)
    other_right = jnp.concatenate([bundle[pl.ds((2 * k + 1) * rows, rows), :] for k in range(count)], axis=0)
    right, other_right = right[...], right_operand(other_right * scale)
    for k in range(part // TILE):
        piece = slice(k * TILE, (k + 1) * TILE)
        made[0, piece, :] = jnp.dot(left[piece, :], other_right, preferred_element_type=jnp.float32)
        into = pl.ds(pl.multiple_of(lax.axis_index("seq") * part + k * TILE, TILE), TILE)
        copies.append(pltpu.make_async_copy(made.at[0, piece], out.at[into, there], sems.at[k + 1]))
        copies[-1].start()
    other_left = left_operand(other_left)
    for k, (operand_right, into) in enumerate(((other_right, there), (right, here))):
        made[k + 1] = jnp.dot(other_left, operand_right, preferred_element_type=jnp.float32)
        copies.append(pltpu.make_async_copy(made.at[k + 1], out.at[there, into], sems.at[part // TILE + k + 1]))
        copies[-1].start()
    for copy in copies:
        copy.wait()


def quadrant_of(parcels):
    rows, part = parcels[0].shape
    total = rows // 3 * len(parcels)
    vmem = pl.BlockSpec(memory_space=pltpu.VMEM)
    return pl.pallas_call(
        functools.partial(quadrant_kernel, 1.0 / total),
        out_shape=[
            jax.ShapeDtypeStruct((2 * part, 2 * part), jnp.float32),
            jax.ShapeDtypeStruct((part, 8 * total), jnp.bfloat16),
            jax.ShapeDtypeStruct((8 * total, part), jnp.bfloat16),
        ],
        in_specs=[vmem] * len(parcels),
        out_specs=[pl.BlockSpec(memory_space=pltpu.HBM), vmem, vmem],
        scratch_shapes=[pltpu.VMEM((part, part), jnp.float32), pltpu.SemaphoreType.DMA((part // TILE,))],
        compiler_params=pltpu.CompilerParams(vmem_limit_bytes=VMEM_BYTES),
        cost_estimate=pl.CostEstimate(flops=2**28, bytes_accessed=4 * part * part, transcendentals=0),
        name="quadrant",
    )(*parcels)


def fisher_block(begun, parcels, bundle):
    rows, part = parcels[0].shape
    rows //= 3
    width = 2 * part
    hbm = pl.BlockSpec(memory_space=pltpu.HBM)
    vmem = pl.BlockSpec(memory_space=pltpu.VMEM)
    return pl.pallas_call(
        functools.partial(fisher_kernel, 1.0 / (rows * len(parcels))),
        out_shape=[
            jax.ShapeDtypeStruct((rows, width), jnp.float32),
            jax.ShapeDtypeStruct((width, width), jnp.float32),
        ],
        in_specs=[hbm] + [vmem] * (3 + len(parcels)),
        out_specs=[hbm] * 2,
        scratch_shapes=[
            pltpu.VMEM((3, part, part), jnp.float32),
            pltpu.VMEM((rows, width), jnp.float32),
            pltpu.SemaphoreType.DMA((part // TILE + 3,)),
        ],
        input_output_aliases={0: 1},
        compiler_params=pltpu.CompilerParams(vmem_limit_bytes=VMEM_BYTES),
        name="fisher",
    )(*begun, bundle, *parcels)


def local(acts, grads, in_ids, in_signs, out_ids, out_signs, in_table, out_table):
    tensor, seq, dp = (lax.axis_size(name) for name in ("tensor", "seq", "dp"))
    shards = tensor * seq
    small = tensor == 2 and seq == 2 and dp == 4
    swap = [(0, 1), (1, 0)]

    act = project(acts, in_ids, in_signs, in_table, 512, "project_acts")
    if tensor == 2:
        other = lax.ppermute(act, "tensor", swap)
    else:
        act = lax.psum(act, "tensor")
        other = jnp.zeros_like(act)
    grad = project(grads, out_ids, out_signs, out_table, 1024, "project_grads")
    krons = kron_of(grad, act, other, (shards, seq) if small else (1, 1))

    if not small:
        kron = lax.psum(krons[0], ("tensor", "seq"))
        width = kron.shape[1] // shards
        place = lax.axis_index("tensor") * seq + lax.axis_index("seq")
        mine = lax.dynamic_slice_in_dim(kron, place * width, width, 1)
        every = lax.all_gather(kron, "dp", axis=0, tiled=True)
        left = lax.dynamic_slice_in_dim(every, place * width, width, 1)
        columns = kron.shape[1] // dp
        right = lax.dynamic_slice_in_dim(every, lax.axis_index("dp") * columns, columns, 1)
        fisher = lax.dot_general(
            left, right, (((0,), (0,)), ((), ())), precision=lax.Precision.HIGHEST
        ) / left.shape[0]
        return mine, fisher

    across = lax.ppermute(krons[1], ("tensor", "seq"), [(p, 3 - p) for p in range(shards)])
    beside = lax.ppermute(krons[2], "tensor", swap)
    mate = lax.ppermute(krons[3], "seq", swap)
    parcels = list(parcels_of([across, beside, mate, krons[0]], dp))
    for k in range(1, dp):
        parcels[k] = lax.ppermute(parcels[k], "dp", [(d, (d + k) % dp) for d in range(dp)])
    bundle = lax.ppermute(bundle_of(parcels), "seq", swap)
    mine, fisher = fisher_block(quadrant_of(parcels), parcels, bundle)
    return mine, fisher


def solution(mesh):
    in_specs = (
        P(("groups", "dp"), "seq", "tensor"),
        P(("groups", "dp"), "seq", "tensor"),
        P("tensor"),
        P("tensor"),
        P("tensor"),
        P("tensor"),
        P(),
        P(),
    )
    out_specs = (P(("groups", "dp"), ("tensor", "seq")), P(("groups", "tensor", "seq"), "dp"))
    return jax.shard_map(local, mesh=mesh, in_specs=in_specs, out_specs=out_specs, check_vma=False)
```

```python
import functools

import jax
import jax.numpy as jnp
from jax import lax
from jax.experimental import pallas as pl
from jax.experimental.pallas import tpu as pltpu
from jax.sharding import PartitionSpec as P

PROJ = 64
BLOCK = 64
LANES = 128
STRIDE = 72
VMEM_BYTES = 48 * 1024 * 1024


def chunks_of(width, most):
    if width < 4 * most or most % (4 * LANES):
        chunk = most
        while width % chunk:
            chunk -= LANES
        return [chunk] * (width // chunk)
    inner = width - most
    chunk = most
    while inner % chunk:
        chunk -= LANES
    return [most // 2] + [chunk] * (inner // chunk) + [most // 4] * 2


def split3(x):
    high = x.astype(jnp.bfloat16)
    rest = x - high.astype(jnp.float32)
    mid = rest.astype(jnp.bfloat16)
    low = (rest - mid.astype(jnp.float32)).astype(jnp.bfloat16)
    return high, mid, low


def gap(entries):
    return entries + 8


def spread_table(table, spread):
    entries = table.shape[0]
    for row in range(0, BLOCK, 2):
        both = table[:, row * PROJ : row * PROJ + LANES].astype(jnp.float32)
        spread[pl.ds(row * gap(entries), entries), :] = both
        spread[pl.ds((row + 1) * gap(entries), entries), :] = pltpu.roll(both, PROJ, 1)


def sign_table(entries, spread, signed):
    for entry in range(entries):
        block = spread[pl.ds(entry, BLOCK, stride=gap(entries)), :].astype(jnp.bfloat16)
        signed[pl.ds((entries + entry) * BLOCK, BLOCK), :] = block
        signed[pl.ds(entry * BLOCK, BLOCK), :] = -block


def lay_blocks(ids, signs, entries, spread, signed, matrix, first, last):
    for j in range(first, last):
        if signed is None:
            sign = (2 * signs[j] - 1).astype(jnp.float32)
            block = (spread[pl.ds(ids[j], BLOCK, stride=gap(entries)), :] * sign).astype(jnp.bfloat16)
        else:
            start = pl.multiple_of((signs[j] * entries + ids[j]) * BLOCK, BLOCK)
            block = signed[pl.ds(start, BLOCK), :]
        matrix[pl.ds(j * BLOCK, BLOCK), :] = block


def operand(x):
    x1, x2, x3 = split3(x)
    return jnp.concatenate([x1, x1, x2, x1, x3, x2], axis=1)


def products_with(left, act):
    a1, a2, a3 = split3(act)
    right = jnp.concatenate([a1, a2, a1, a3, a1, a2], axis=1)
    return lax.dot_general(left, right, (((1,), (1,)), ((), ())), preferred_element_type=jnp.float32)


def project_kernel(widths, ids, signs, table, rows_ref, out, *refs):
    spread, matrix, held, total, own_table, own_ids, own_signs, sems, *signed = refs
    signed = signed[0] if signed else None
    copies, starts, start = [], [], 0
    for c, width in enumerate(widths):
        columns = pl.ds(start, width)
        copies.append(pltpu.make_async_copy(rows_ref.at[:, columns], held.at[:, columns], sems.at[c]))
        starts.append(start)
        start += width
    small = [
        pltpu.make_async_copy(source, kept, sems.at[len(widths) + k])
        for k, (source, kept) in enumerate(((table, own_table), (ids, own_ids), (signs, own_signs)))
    ]
    for copy in small + copies:
        copy.start()
    small[0].wait()
    spread_table(own_table, spread)
    if signed is not None:
        sign_table(table.shape[0], spread, signed)
    small[1].wait()
    small[2].wait()
    lay = functools.partial(lay_blocks, own_ids, own_signs, table.shape[0], spread, signed, matrix)
    lay(0, widths[0] // BLOCK)
    for c, copy in enumerate(copies):
        columns = pl.ds(starts[c], widths[c])
        copy.wait()
        if c + 1 < len(widths):
            lay(starts[c + 1] // BLOCK, (starts[c + 1] + widths[c + 1]) // BLOCK)
        part = lax.dot_general(
            matrix[columns, :PROJ],
            held[:, columns],
            (((0,), (1,)), ((), ())),
            preferred_element_type=jnp.float32,
        )
        if c == 0:
            total[...] = part
        elif c + 1 < len(widths):
            total[...] += part
    part = total[...] + part if len(widths) > 1 else part
    pairs, _, tokens = out.shape
    for pair in range(pairs):
        for side in range(2):
            example = 2 * pair + side
            out[pair, pl.ds(side * PROJ, PROJ), :] = part[:, example * tokens : (example + 1) * tokens]


def project(values, ids, signs, table, most, name):
    count, tokens, width = values.shape
    widths = chunks_of(width, most)
    rows = count * tokens
    entries = table.shape[0]
    blocks = ids.shape[0]
    operands = [
        pltpu.with_memory_space_constraint(each, pltpu.HBM)
        for each in (ids, signs, table, values.reshape(rows, width))
    ]
    signed = [pltpu.VMEM((2 * entries * BLOCK, LANES), jnp.bfloat16)] if blocks > entries else []
    return pl.pallas_call(
        functools.partial(project_kernel, widths),
        out_shape=jax.ShapeDtypeStruct((count // 2, LANES, tokens), jnp.float32),
        in_specs=[pl.BlockSpec(memory_space=pltpu.HBM)] * 4,
        out_specs=pl.BlockSpec(memory_space=pltpu.VMEM),
        scratch_shapes=[
            pltpu.VMEM((BLOCK * gap(entries), LANES), jnp.float32),
            pltpu.VMEM((width, LANES), jnp.bfloat16),
            pltpu.VMEM((rows, width), jnp.bfloat16),
            pltpu.VMEM((PROJ, rows), jnp.float32),
            pltpu.VMEM(table.shape, table.dtype),
            pltpu.SMEM(ids.shape, ids.dtype),
            pltpu.SMEM(signs.shape, signs.dtype),
            pltpu.SemaphoreType.DMA((len(widths) + 3,)),
        ]
        + signed,
        compiler_params=pltpu.CompilerParams(vmem_limit_bytes=VMEM_BYTES),
        cost_estimate=pl.CostEstimate(
            flops=2 * rows * width * LANES, bytes_accessed=2 * rows * width, transcendentals=0
        ),
        name=name,
    )(*operands)


def kron_kernel(cuts, grads, own, act, *refs):
    parts = cuts[1]
    outs, rows, products = refs[:-2], refs[-2], refs[-1]
    pairs = act.shape[0]
    for pair in range(pairs):
        both = products_with(operand(grads[pair]), own[pair] + act[pair])
        for side in range(2):
            products[pl.ds((2 * pair + side) * STRIDE, PROJ), :] = both[side * PROJ : (side + 1) * PROJ]
    count = 2 * pairs
    lower = lax.broadcasted_iota(jnp.int32, (count, LANES), 1) < PROJ
    even = lax.broadcasted_iota(jnp.int32, (count, LANES), 0) % 2 == 0
    here = even == lower
    tiles = rows.shape[2] // LANES // cuts[0]
    for tile in range(PROJ * PROJ // LANES):
        both = []
        for p in (2 * tile, 2 * tile + 1):
            v = products[pl.ds(p, count, stride=STRIDE), :]
            both.append(jnp.where(here, v, pltpu.roll(v, PROJ, 1)))
        block, part, within = tile // tiles // parts, tile // tiles % parts, tile % tiles
        rows[part, :, pl.ds((block * tiles + within) * LANES, LANES)] = jnp.where(lower, both[0], both[1])
    for k, out in enumerate(outs):
        part = lax.rem(lax.axis_index("seq") + k % 2, parts) if parts > 1 else 0
        out[...] = rows[part]


def kron_of(grads, own, act, cuts):
    pairs = grads.shape[0]
    parts = cuts[1]
    width = PROJ * PROJ // parts
    outs = 4 if parts > 1 else 1
    vmem = pl.BlockSpec(memory_space=pltpu.VMEM)
    return pl.pallas_call(
        functools.partial(kron_kernel, cuts),
        out_shape=[jax.ShapeDtypeStruct((2 * pairs, width), jnp.float32)] * outs,
        in_specs=[vmem] * 3,
        out_specs=[vmem] * outs,
        scratch_shapes=[
            pltpu.VMEM((parts, 2 * pairs, width), jnp.float32),
            pltpu.VMEM((2 * pairs * STRIDE, LANES), jnp.float32),
        ],
        compiler_params=pltpu.CompilerParams(vmem_limit_bytes=VMEM_BYTES),
        name="kron",
    )(grads, own, act)


def parcels_kernel(parts, *refs):
    summands, parcels = refs[:parts], refs[parts:]
    count = summands[0].shape[0]
    dp = len(parcels)
    width = parcels[0].shape[1]
    core, chip = lax.axis_index("seq"), lax.axis_index("tensor") * 2
    blocks = [chip + core, chip + 1 - core]
    for k, parcel in enumerate(parcels):
        for step, block in enumerate(blocks + [lax.rem(lax.axis_index("dp") + k, dp)]):
            lanes = pl.ds(pl.multiple_of(block * width, LANES), width)
            row = summands[0][:, lanes]
            for other in summands[1:]:
                row = row + other[:, lanes]
            parcel[pl.ds(step * count, count), :] = row


def parcels_of(summands, dp):
    count, width = summands[0].shape
    vmem = pl.BlockSpec(memory_space=pltpu.VMEM)
    return pl.pallas_call(
        functools.partial(parcels_kernel, len(summands)),
        out_shape=[jax.ShapeDtypeStruct((3 * count, width // dp), jnp.float32)] * dp,
        in_specs=[vmem] * len(summands),
        out_specs=[vmem] * dp,
        compiler_params=pltpu.CompilerParams(vmem_limit_bytes=VMEM_BYTES),
        name="parcels",
    )(*summands)


def bundle_kernel(*refs):
    parcels, out = refs[:-1], refs[-1]
    rows = 2 * parcels[0].shape[0] // 3
    for k, parcel in enumerate(parcels):
        out[pl.ds(k * rows, rows), :] = parcel[pl.ds(rows // 2, rows), :]


def bundle_of(parcels):
    rows, width = parcels[0].shape
    vmem = pl.BlockSpec(memory_space=pltpu.VMEM)
    return pl.pallas_call(
        bundle_kernel,
        out_shape=jax.ShapeDtypeStruct((2 * rows // 3 * len(parcels), width), jnp.float32),
        in_specs=[vmem] * len(parcels),
        out_specs=vmem,
        compiler_params=pltpu.CompilerParams(vmem_limit_bytes=VMEM_BYTES),
        name="bundle",
    )(*parcels)


def left_operand(x):
    x1, x2, x3 = split3(x)
    return jnp.concatenate([x1, x1, x2, x1, x3, x2, x2, x3], axis=0).T


def right_operand(x):
    x1, x2, x3 = split3(x)
    return jnp.concatenate([x1, x2, x1, x3, x1, x2, x3, x2], axis=0)


def own_halves(parcels):
    rows = parcels[0].shape[0] // 3
    left = jnp.concatenate([parcel[pl.ds(0, rows), :] for parcel in parcels], axis=0)
    right = jnp.concatenate([parcel[pl.ds(2 * rows, rows), :] for parcel in parcels], axis=0)
    return left, right


def halves_at(part):
    core = lax.axis_index("seq")
    return [pl.ds(pl.multiple_of(place * part, part), part) for place in (core, 1 - core)]


TILE = 256


def quadrant_kernel(scale, *refs):
    parcels, (out, left_ref, right_ref, made, sems) = refs[:-5], refs[-5:]
    part = parcels[0].shape[1]
    left, right = own_halves(parcels)
    left, right = left_operand(left), right_operand(right * scale)
    left_ref[...], right_ref[...] = left, right
    here, _ = halves_at(part)
    copies = []
    for k in range(part // TILE):
        rows = slice(k * TILE, (k + 1) * TILE)
        made[rows, :] = jnp.dot(left[rows], right, preferred_element_type=jnp.float32)
        into = pl.ds(pl.multiple_of(lax.axis_index("seq") * part + k * TILE, TILE), TILE)
        copies.append(pltpu.make_async_copy(made.at[rows], out.at[into, here], sems.at[k]))
        copies[-1].start()
    for copy in copies:
        copy.wait()


def fisher_kernel(scale, begun, left, right, bundle, *refs):
    del begun
    parcels, (mine, out, made, kept, sems) = refs[:-5], refs[-5:]
    rows, part = parcels[0].shape[0] // 3, parcels[0].shape[1]
    here, there = halves_at(part)
    kept[:, here] = parcels[0][pl.ds(0, rows), :]
    kept[:, there] = bundle[pl.ds(0, rows), :]
    copies = [pltpu.make_async_copy(kept, mine, sems.at[0])]
    copies[0].start()
    count = len(parcels)
    other_left = jnp.concatenate([bundle[pl.ds(2 * k * rows, rows), :] for k in range(count)], axis=0)
    other_right = jnp.concatenate([bundle[pl.ds((2 * k + 1) * rows, rows), :] for k in range(count)], axis=0)
    right, other_right = right[...], right_operand(other_right * scale)
    for k in range(part // TILE):
        piece = slice(k * TILE, (k + 1) * TILE)
        made[0, piece, :] = jnp.dot(left[piece, :], other_right, preferred_element_type=jnp.float32)
        into = pl.ds(pl.multiple_of(lax.axis_index("seq") * part + k * TILE, TILE), TILE)
        copies.append(pltpu.make_async_copy(made.at[0, piece], out.at[into, there], sems.at[k + 1]))
        copies[-1].start()
    other_left = left_operand(other_left)
    for k, (operand_right, into) in enumerate(((other_right, there), (right, here))):
        made[k + 1] = jnp.dot(other_left, operand_right, preferred_element_type=jnp.float32)
        copies.append(pltpu.make_async_copy(made.at[k + 1], out.at[there, into], sems.at[part // TILE + k + 1]))
        copies[-1].start()
    for copy in copies:
        copy.wait()


def quadrant_of(parcels):
    rows, part = parcels[0].shape
    total = rows // 3 * len(parcels)
    vmem = pl.BlockSpec(memory_space=pltpu.VMEM)
    return pl.pallas_call(
        functools.partial(quadrant_kernel, 1.0 / total),
        out_shape=[
            jax.ShapeDtypeStruct((2 * part, 2 * part), jnp.float32),
            jax.ShapeDtypeStruct((part, 8 * total), jnp.bfloat16),
            jax.ShapeDtypeStruct((8 * total, part), jnp.bfloat16),
        ],
        in_specs=[vmem] * len(parcels),
        out_specs=[pl.BlockSpec(memory_space=pltpu.HBM), vmem, vmem],
        scratch_shapes=[pltpu.VMEM((part, part), jnp.float32), pltpu.SemaphoreType.DMA((part // TILE,))],
        compiler_params=pltpu.CompilerParams(vmem_limit_bytes=VMEM_BYTES),
        cost_estimate=pl.CostEstimate(flops=2**28, bytes_accessed=4 * part * part, transcendentals=0),
        name="quadrant",
    )(*parcels)


def fisher_block(begun, parcels, bundle):
    rows, part = parcels[0].shape
    rows //= 3
    width = 2 * part
    hbm = pl.BlockSpec(memory_space=pltpu.HBM)
    vmem = pl.BlockSpec(memory_space=pltpu.VMEM)
    return pl.pallas_call(
        functools.partial(fisher_kernel, 1.0 / (rows * len(parcels))),
        out_shape=[
            jax.ShapeDtypeStruct((rows, width), jnp.float32),
            jax.ShapeDtypeStruct((width, width), jnp.float32),
        ],
        in_specs=[hbm] + [vmem] * (3 + len(parcels)),
        out_specs=[hbm] * 2,
        scratch_shapes=[
            pltpu.VMEM((3, part, part), jnp.float32),
            pltpu.VMEM((rows, width), jnp.float32),
            pltpu.SemaphoreType.DMA((part // TILE + 3,)),
        ],
        input_output_aliases={0: 1},
        compiler_params=pltpu.CompilerParams(vmem_limit_bytes=VMEM_BYTES),
        name="fisher",
    )(*begun, bundle, *parcels)


def local(acts, grads, in_ids, in_signs, out_ids, out_signs, in_table, out_table):
    tensor, seq, dp = (lax.axis_size(name) for name in ("tensor", "seq", "dp"))
    shards = tensor * seq
    small = tensor == 2 and seq == 2 and dp == 4
    swap = [(0, 1), (1, 0)]

    act = project(acts, in_ids, in_signs, in_table, 512, "project_acts")
    if tensor == 2:
        other = lax.ppermute(act, "tensor", swap)
    else:
        act = lax.psum(act, "tensor")
        other = jnp.zeros_like(act)
    grad = project(grads, out_ids, out_signs, out_table, 1024, "project_grads")
    krons = kron_of(grad, act, other, (shards, seq) if small else (1, 1))

    if not small:
        kron = lax.psum(krons[0], ("tensor", "seq"))
        width = kron.shape[1] // shards
        place = lax.axis_index("tensor") * seq + lax.axis_index("seq")
        mine = lax.dynamic_slice_in_dim(kron, place * width, width, 1)
        every = lax.all_gather(kron, "dp", axis=0, tiled=True)
        left = lax.dynamic_slice_in_dim(every, place * width, width, 1)
        columns = kron.shape[1] // dp
        right = lax.dynamic_slice_in_dim(every, lax.axis_index("dp") * columns, columns, 1)
        fisher = lax.dot_general(
            left, right, (((0,), (0,)), ((), ())), precision=lax.Precision.HIGHEST
        ) / left.shape[0]
        return mine, fisher

    across = lax.ppermute(krons[1], ("tensor", "seq"), [(p, 3 - p) for p in range(shards)])
    beside = lax.ppermute(krons[2], "tensor", swap)
    mate = lax.ppermute(krons[3], "seq", swap)
    parcels = list(parcels_of([across, beside, mate, krons[0]], dp))
    for k in range(1, dp):
        parcels[k] = lax.ppermute(parcels[k], "dp", [(d, (d + k) % dp) for d in range(dp)])
    bundle = lax.ppermute(bundle_of(parcels), "seq", swap)
    mine, fisher = fisher_block(quadrant_of(parcels), parcels, bundle)
    return mine, fisher


def solution(mesh):
    in_specs = (
        P(("groups", "dp"), "seq", "tensor"),
        P(("groups", "dp"), "seq", "tensor"),
        P("tensor"),
        P("tensor"),
        P("tensor"),
        P("tensor"),
        P(),
        P(),
    )
    out_specs = (P(("groups", "dp"), ("tensor", "seq")), P(("groups", "tensor", "seq"), "dp"))
    return jax.shard_map(local, mesh=mesh, in_specs=in_specs, out_specs=out_specs, check_vma=False)
```

```python
import functools

import jax
import jax.numpy as jnp
from jax import lax
from jax.experimental import pallas as pl
from jax.experimental.pallas import tpu as pltpu
from jax.sharding import PartitionSpec as P

PROJ = 64
BLOCK = 64
LANES = 128
STRIDE = 72
VMEM_BYTES = 48 * 1024 * 1024


def chunks_of(width, most):
    if width < 4 * most or most % (4 * LANES):
        chunk = most
        while width % chunk:
            chunk -= LANES
        return [chunk] * (width // chunk)
    inner = width - most
    chunk = most
    while inner % chunk:
        chunk -= LANES
    return [most // 2] + [chunk] * (inner // chunk) + [most // 4] * 2


def split3(x):
    high = x.astype(jnp.bfloat16)
    rest = x - high.astype(jnp.float32)
    mid = rest.astype(jnp.bfloat16)
    low = (rest - mid.astype(jnp.float32)).astype(jnp.bfloat16)
    return high, mid, low


def spread_table(table, spread):
    entries = table.shape[0]
    for row in range(0, BLOCK, 2):
        both = table[:, row * PROJ : row * PROJ + LANES].astype(jnp.float32)
        spread[pl.ds(row, entries, stride=STRIDE), :] = both
        spread[pl.ds(row + 1, entries, stride=STRIDE), :] = pltpu.roll(both, PROJ, 1)


def sign_table(spread, signed):
    entries = spread.shape[0] // STRIDE
    for entry in range(entries):
        block = spread[pl.ds(entry * STRIDE, BLOCK), :].astype(jnp.bfloat16)
        signed[pl.ds((entries + entry) * BLOCK, BLOCK), :] = block
        signed[pl.ds(entry * BLOCK, BLOCK), :] = -block


def lay_blocks(ids, signs, spread, signed, matrix, first, last):
    entries = spread.shape[0] // STRIDE
    for j in range(first, last):
        if signed is None:
            start = pl.multiple_of(ids[j] * STRIDE, 8)
            sign = (2 * signs[j] - 1).astype(jnp.float32)
            block = (spread[pl.ds(start, BLOCK), :] * sign).astype(jnp.bfloat16)
        else:
            start = pl.multiple_of((signs[j] * entries + ids[j]) * BLOCK, BLOCK)
            block = signed[pl.ds(start, BLOCK), :]
        matrix[pl.ds(j * BLOCK, BLOCK), :] = block


def operand(x):
    x1, x2, x3 = split3(x)
    return jnp.concatenate([x1, x1, x2, x1, x3, x2], axis=1)


def products_with(left, act):
    a1, a2, a3 = split3(act)
    right = jnp.concatenate([a1, a2, a1, a3, a1, a2], axis=1)
    return lax.dot_general(left, right, (((1,), (1,)), ((), ())), preferred_element_type=jnp.float32)


def project_kernel(widths, ids, signs, table, rows_ref, out, *refs):
    spread, matrix, held, total, own_table, own_ids, own_signs, sems, *signed = refs
    signed = signed[0] if signed else None
    copies, starts, start = [], [], 0
    for c, width in enumerate(widths):
        columns = pl.ds(start, width)
        copies.append(pltpu.make_async_copy(rows_ref.at[:, columns], held.at[:, columns], sems.at[c]))
        starts.append(start)
        start += width
    small = [
        pltpu.make_async_copy(source, kept, sems.at[len(widths) + k])
        for k, (source, kept) in enumerate(((table, own_table), (ids, own_ids), (signs, own_signs)))
    ]
    for copy in small + copies:
        copy.start()
    small[0].wait()
    spread_table(own_table, spread)
    if signed is not None:
        sign_table(spread, signed)
    small[1].wait()
    small[2].wait()
    lay = functools.partial(lay_blocks, own_ids, own_signs, spread, signed, matrix)
    lay(0, widths[0] // BLOCK)
    for c, copy in enumerate(copies):
        columns = pl.ds(starts[c], widths[c])
        copy.wait()
        if c + 1 < len(widths):
            lay(starts[c + 1] // BLOCK, (starts[c + 1] + widths[c + 1]) // BLOCK)
        part = lax.dot_general(
            matrix[columns, :PROJ],
            held[:, columns],
            (((0,), (1,)), ((), ())),
            preferred_element_type=jnp.float32,
        )
        if c == 0:
            total[...] = part
        elif c + 1 < len(widths):
            total[...] += part
    part = total[...] + part if len(widths) > 1 else part
    pairs, _, tokens = out.shape
    for pair in range(pairs):
        for side in range(2):
            example = 2 * pair + side
            out[pair, pl.ds(side * PROJ, PROJ), :] = part[:, example * tokens : (example + 1) * tokens]


def project(values, ids, signs, table, most, name):
    count, tokens, width = values.shape
    widths = chunks_of(width, most)
    rows = count * tokens
    entries = table.shape[0]
    blocks = ids.shape[0]
    operands = [
        pltpu.with_memory_space_constraint(each, pltpu.HBM)
        for each in (ids, signs, table, values.reshape(rows, width))
    ]
    signed = [pltpu.VMEM((2 * entries * BLOCK, LANES), jnp.bfloat16)] if blocks > entries else []
    return pl.pallas_call(
        functools.partial(project_kernel, widths),
        out_shape=jax.ShapeDtypeStruct((count // 2, LANES, tokens), jnp.float32),
        in_specs=[pl.BlockSpec(memory_space=pltpu.HBM)] * 4,
        out_specs=pl.BlockSpec(memory_space=pltpu.VMEM),
        scratch_shapes=[
            pltpu.VMEM((entries * STRIDE, LANES), jnp.float32),
            pltpu.VMEM((width, LANES), jnp.bfloat16),
            pltpu.VMEM((rows, width), jnp.bfloat16),
            pltpu.VMEM((PROJ, rows), jnp.float32),
            pltpu.VMEM(table.shape, table.dtype),
            pltpu.SMEM(ids.shape, ids.dtype),
            pltpu.SMEM(signs.shape, signs.dtype),
            pltpu.SemaphoreType.DMA((len(widths) + 3,)),
        ]
        + signed,
        compiler_params=pltpu.CompilerParams(vmem_limit_bytes=VMEM_BYTES),
        cost_estimate=pl.CostEstimate(
            flops=2 * rows * width * LANES, bytes_accessed=2 * rows * width, transcendentals=0
        ),
        name=name,
    )(*operands)


def kron_kernel(cuts, grads, own, act, *refs):
    parts = cuts[1]
    outs, rows, products = refs[:-2], refs[-2], refs[-1]
    pairs = act.shape[0]
    for pair in range(pairs):
        both = products_with(operand(grads[pair]), own[pair] + act[pair])
        for side in range(2):
            products[pl.ds((2 * pair + side) * STRIDE, PROJ), :] = both[side * PROJ : (side + 1) * PROJ]
    count = 2 * pairs
    lower = lax.broadcasted_iota(jnp.int32, (count, LANES), 1) < PROJ
    even = lax.broadcasted_iota(jnp.int32, (count, LANES), 0) % 2 == 0
    here = even == lower
    tiles = rows.shape[2] // LANES // cuts[0]
    for tile in range(PROJ * PROJ // LANES):
        both = []
        for p in (2 * tile, 2 * tile + 1):
            v = products[pl.ds(p, count, stride=STRIDE), :]
            both.append(jnp.where(here, v, pltpu.roll(v, PROJ, 1)))
        block, part, within = tile // tiles // parts, tile // tiles % parts, tile % tiles
        rows[part, :, pl.ds((block * tiles + within) * LANES, LANES)] = jnp.where(lower, both[0], both[1])
    for k, out in enumerate(outs):
        part = lax.rem(lax.axis_index("seq") + k % 2, parts) if parts > 1 else 0
        out[...] = rows[part]


def kron_of(grads, own, act, cuts):
    pairs = grads.shape[0]
    parts = cuts[1]
    width = PROJ * PROJ // parts
    outs = 4 if parts > 1 else 1
    vmem = pl.BlockSpec(memory_space=pltpu.VMEM)
    return pl.pallas_call(
        functools.partial(kron_kernel, cuts),
        out_shape=[jax.ShapeDtypeStruct((2 * pairs, width), jnp.float32)] * outs,
        in_specs=[vmem] * 3,
        out_specs=[vmem] * outs,
        scratch_shapes=[
            pltpu.VMEM((parts, 2 * pairs, width), jnp.float32),
            pltpu.VMEM((2 * pairs * STRIDE, LANES), jnp.float32),
        ],
        compiler_params=pltpu.CompilerParams(vmem_limit_bytes=VMEM_BYTES),
        name="kron",
    )(grads, own, act)


def parcels_kernel(parts, *refs):
    summands, parcels = refs[:parts], refs[parts:]
    count = summands[0].shape[0]
    dp = len(parcels)
    width = parcels[0].shape[1]
    core, chip = lax.axis_index("seq"), lax.axis_index("tensor") * 2
    blocks = [chip + core, chip + 1 - core]
    for k, parcel in enumerate(parcels):
        for step, block in enumerate(blocks + [lax.rem(lax.axis_index("dp") + k, dp)]):
            lanes = pl.ds(pl.multiple_of(block * width, LANES), width)
            row = summands[0][:, lanes]
            for other in summands[1:]:
                row = row + other[:, lanes]
            parcel[pl.ds(step * count, count), :] = row


def parcels_of(summands, dp):
    count, width = summands[0].shape
    vmem = pl.BlockSpec(memory_space=pltpu.VMEM)
    return pl.pallas_call(
        functools.partial(parcels_kernel, len(summands)),
        out_shape=[jax.ShapeDtypeStruct((3 * count, width // dp), jnp.float32)] * dp,
        in_specs=[vmem] * len(summands),
        out_specs=[vmem] * dp,
        compiler_params=pltpu.CompilerParams(vmem_limit_bytes=VMEM_BYTES),
        name="parcels",
    )(*summands)


def bundle_kernel(*refs):
    parcels, out = refs[:-1], refs[-1]
    rows = 2 * parcels[0].shape[0] // 3
    for k, parcel in enumerate(parcels):
        out[pl.ds(k * rows, rows), :] = parcel[pl.ds(rows // 2, rows), :]


def bundle_of(parcels):
    rows, width = parcels[0].shape
    vmem = pl.BlockSpec(memory_space=pltpu.VMEM)
    return pl.pallas_call(
        bundle_kernel,
        out_shape=jax.ShapeDtypeStruct((2 * rows // 3 * len(parcels), width), jnp.float32),
        in_specs=[vmem] * len(parcels),
        out_specs=vmem,
        compiler_params=pltpu.CompilerParams(vmem_limit_bytes=VMEM_BYTES),
        name="bundle",
    )(*parcels)


def left_operand(x):
    x1, x2, x3 = split3(x)
    return jnp.concatenate([x1, x1, x2, x1, x3, x2, x2, x3], axis=0).T


def right_operand(x):
    x1, x2, x3 = split3(x)
    return jnp.concatenate([x1, x2, x1, x3, x1, x2, x3, x2], axis=0)


def own_halves(parcels):
    rows = parcels[0].shape[0] // 3
    left = jnp.concatenate([parcel[pl.ds(0, rows), :] for parcel in parcels], axis=0)
    right = jnp.concatenate([parcel[pl.ds(2 * rows, rows), :] for parcel in parcels], axis=0)
    return left, right


def halves_at(part):
    core = lax.axis_index("seq")
    return [pl.ds(pl.multiple_of(place * part, part), part) for place in (core, 1 - core)]


def quadrant_kernel(scale, *refs):
    parcels, (quadrant, left, right) = refs[:-3], refs[-3:]
    own_left, own_right = own_halves(parcels)
    left[...], right[...] = left_operand(own_left), right_operand(own_right * scale)
    quadrant[...] = jnp.dot(left[...], right[...], preferred_element_type=jnp.float32)


def fisher_kernel(scale, quadrant, left, right, bundle, *refs):
    parcels, (mine, out, made, kept, sems) = refs[:-5], refs[-5:]
    rows, part = parcels[0].shape[0] // 3, parcels[0].shape[1]
    here, there = halves_at(part)
    kept[:, here] = parcels[0][pl.ds(0, rows), :]
    kept[:, there] = bundle[pl.ds(0, rows), :]
    copies = [
        pltpu.make_async_copy(quadrant, out.at[here, here], sems.at[0]),
        pltpu.make_async_copy(kept, mine, sems.at[1]),
    ]
    for copy in copies:
        copy.start()
    count = len(parcels)
    other_left = jnp.concatenate([bundle[pl.ds(2 * k * rows, rows), :] for k in range(count)], axis=0)
    other_right = jnp.concatenate([bundle[pl.ds((2 * k + 1) * rows, rows), :] for k in range(count)], axis=0)
    other_right = right_operand(other_right * scale)
    made[0] = jnp.dot(left[...], other_right, preferred_element_type=jnp.float32)
    copies.append(pltpu.make_async_copy(made.at[0], out.at[here, there], sems.at[2]))
    copies[-1].start()
    other_left = left_operand(other_left)
    for k, (operand_right, into) in enumerate(((other_right, there), (right[...], here))):
        made[k + 1] = jnp.dot(other_left, operand_right, preferred_element_type=jnp.float32)
        copies.append(pltpu.make_async_copy(made.at[k + 1], out.at[there, into], sems.at[k + 3]))
        copies[-1].start()
    for copy in copies:
        copy.wait()


def quadrant_of(parcels):
    rows, part = parcels[0].shape
    total = rows // 3 * len(parcels)
    vmem = pl.BlockSpec(memory_space=pltpu.VMEM)
    return pl.pallas_call(
        functools.partial(quadrant_kernel, 1.0 / total),
        out_shape=[
            jax.ShapeDtypeStruct((part, part), jnp.float32),
            jax.ShapeDtypeStruct((part, 8 * total), jnp.bfloat16),
            jax.ShapeDtypeStruct((8 * total, part), jnp.bfloat16),
        ],
        in_specs=[vmem] * len(parcels),
        out_specs=[vmem] * 3,
        compiler_params=pltpu.CompilerParams(vmem_limit_bytes=VMEM_BYTES),
        cost_estimate=pl.CostEstimate(flops=2**28, bytes_accessed=4 * part * part, transcendentals=0),
        name="quadrant",
    )(*parcels)


def fisher_block(begun, parcels, bundle):
    rows, part = parcels[0].shape
    rows //= 3
    width = 2 * part
    hbm = pl.BlockSpec(memory_space=pltpu.HBM)
    vmem = pl.BlockSpec(memory_space=pltpu.VMEM)
    return pl.pallas_call(
        functools.partial(fisher_kernel, 1.0 / (rows * len(parcels))),
        out_shape=[
            jax.ShapeDtypeStruct((rows, width), jnp.float32),
            jax.ShapeDtypeStruct((width, width), jnp.float32),
        ],
        in_specs=[vmem] * (4 + len(parcels)),
        out_specs=[hbm] * 2,
        scratch_shapes=[
            pltpu.VMEM((3, part, part), jnp.float32),
            pltpu.VMEM((rows, width), jnp.float32),
            pltpu.SemaphoreType.DMA((5,)),
        ],
        compiler_params=pltpu.CompilerParams(vmem_limit_bytes=VMEM_BYTES),
        name="fisher",
    )(*begun, bundle, *parcels)


def local(acts, grads, in_ids, in_signs, out_ids, out_signs, in_table, out_table):
    tensor, seq, dp = (lax.axis_size(name) for name in ("tensor", "seq", "dp"))
    shards = tensor * seq
    small = tensor == 2 and seq == 2 and dp == 4
    swap = [(0, 1), (1, 0)]

    act = project(acts, in_ids, in_signs, in_table, 512, "project_acts")
    if tensor == 2:
        other = lax.ppermute(act, "tensor", swap)
    else:
        act = lax.psum(act, "tensor")
        other = jnp.zeros_like(act)
    grad = project(grads, out_ids, out_signs, out_table, 1024, "project_grads")
    krons = kron_of(grad, act, other, (shards, seq) if small else (1, 1))

    if not small:
        kron = lax.psum(krons[0], ("tensor", "seq"))
        width = kron.shape[1] // shards
        place = lax.axis_index("tensor") * seq + lax.axis_index("seq")
        mine = lax.dynamic_slice_in_dim(kron, place * width, width, 1)
        every = lax.all_gather(kron, "dp", axis=0, tiled=True)
        left = lax.dynamic_slice_in_dim(every, place * width, width, 1)
        columns = kron.shape[1] // dp
        right = lax.dynamic_slice_in_dim(every, lax.axis_index("dp") * columns, columns, 1)
        fisher = lax.dot_general(
            left, right, (((0,), (0,)), ((), ())), precision=lax.Precision.HIGHEST
        ) / left.shape[0]
        return mine, fisher

    across = lax.ppermute(krons[1], ("tensor", "seq"), [(p, 3 - p) for p in range(shards)])
    beside = lax.ppermute(krons[2], "tensor", swap)
    mate = lax.ppermute(krons[3], "seq", swap)
    parcels = list(parcels_of([across, beside, mate, krons[0]], dp))
    for k in range(1, dp):
        parcels[k] = lax.ppermute(parcels[k], "dp", [(d, (d + k) % dp) for d in range(dp)])
    bundle = lax.ppermute(bundle_of(parcels), "seq", swap)
    mine, fisher = fisher_block(quadrant_of(parcels), parcels, bundle)
    return mine, fisher


def solution(mesh):
    in_specs = (
        P(("groups", "dp"), "seq", "tensor"),
        P(("groups", "dp"), "seq", "tensor"),
        P("tensor"),
        P("tensor"),
        P("tensor"),
        P("tensor"),
        P(),
        P(),
    )
    out_specs = (P(("groups", "dp"), ("tensor", "seq")), P(("groups", "tensor", "seq"), "dp"))
    return jax.shard_map(local, mesh=mesh, in_specs=in_specs, out_specs=out_specs, check_vma=False)
```

```python
import functools

import jax
import jax.numpy as jnp
from jax import lax
from jax.experimental import pallas as pl
from jax.experimental.pallas import tpu as pltpu
from jax.sharding import PartitionSpec as P

PROJ = 64
BLOCK = 64
LANES = 128
STRIDE = 72
VMEM_BYTES = 48 * 1024 * 1024


def chunks_of(width, most):
    if width < 4 * most or most % (4 * LANES):
        chunk = most
        while width % chunk:
            chunk -= LANES
        return [chunk] * (width // chunk)
    inner = width - most
    chunk = most
    while inner % chunk:
        chunk -= LANES
    return [most // 2] + [chunk] * (inner // chunk) + [most // 4] * 2


def split3(x):
    high = x.astype(jnp.bfloat16)
    rest = x - high.astype(jnp.float32)
    mid = rest.astype(jnp.bfloat16)
    low = (rest - mid.astype(jnp.float32)).astype(jnp.bfloat16)
    return high, mid, low


def spread_table(table, spread):
    entries = table.shape[0]
    for row in range(0, BLOCK, 2):
        both = table[:, row * PROJ : row * PROJ + LANES].astype(jnp.float32)
        spread[pl.ds(row, entries, stride=STRIDE), :] = both
        spread[pl.ds(row + 1, entries, stride=STRIDE), :] = pltpu.roll(both, PROJ, 1)


def sign_table(spread, signed):
    entries = spread.shape[0] // STRIDE
    for entry in range(entries):
        block = spread[pl.ds(entry * STRIDE, BLOCK), :].astype(jnp.bfloat16)
        signed[pl.ds((entries + entry) * BLOCK, BLOCK), :] = block
        signed[pl.ds(entry * BLOCK, BLOCK), :] = -block


def lay_blocks(ids, signs, spread, signed, matrix, first, last):
    entries = spread.shape[0] // STRIDE
    for j in range(first, last):
        if signed is None:
            start = pl.multiple_of(ids[j] * STRIDE, 8)
            sign = (2 * signs[j] - 1).astype(jnp.float32)
            block = (spread[pl.ds(start, BLOCK), :] * sign).astype(jnp.bfloat16)
        else:
            start = pl.multiple_of((signs[j] * entries + ids[j]) * BLOCK, BLOCK)
            block = signed[pl.ds(start, BLOCK), :]
        matrix[pl.ds(j * BLOCK, BLOCK), :] = block


def operand(x):
    x1, x2, x3 = split3(x)
    return jnp.concatenate([x1, x1, x2, x1, x3, x2], axis=1)


def products_with(left, act):
    a1, a2, a3 = split3(act)
    right = jnp.concatenate([a1, a2, a1, a3, a1, a2], axis=1)
    return lax.dot_general(left, right, (((1,), (1,)), ((), ())), preferred_element_type=jnp.float32)


def project_kernel(widths, ids, signs, table, rows_ref, out, *refs):
    spread, matrix, across, held, total, own_table, own_ids, own_signs, sems, *signed = refs
    signed = signed[0] if signed else None
    copies, starts, start = [], [], 0
    for c, width in enumerate(widths):
        columns = pl.ds(start, width)
        copies.append(pltpu.make_async_copy(rows_ref.at[:, columns], held.at[:, columns], sems.at[c]))
        starts.append(start)
        start += width
    small = [
        pltpu.make_async_copy(source, kept, sems.at[len(widths) + k])
        for k, (source, kept) in enumerate(((table, own_table), (ids, own_ids), (signs, own_signs)))
    ]
    for copy in small + copies:
        copy.start()
    small[0].wait()
    spread_table(own_table, spread)
    if signed is not None:
        sign_table(spread, signed)
    small[1].wait()
    small[2].wait()

    def lay(c):
        lay_blocks(
            own_ids, own_signs, spread, signed, matrix, starts[c] // BLOCK, (starts[c] + widths[c]) // BLOCK
        )
        rows = pl.ds(starts[c], widths[c])
        across[:, rows] = matrix[rows, :].T[:PROJ, :]

    lay(0)
    for c, copy in enumerate(copies):
        columns = pl.ds(starts[c], widths[c])
        copy.wait()
        if c + 1 < len(widths):
            lay(c + 1)
        part = lax.dot_general(
            across[:, columns], held[:, columns], (((1,), (1,)), ((), ())), preferred_element_type=jnp.float32
        )
        if c == 0:
            total[...] = part
        elif c + 1 < len(widths):
            total[...] += part
    part = total[...] + part if len(widths) > 1 else part
    pairs, _, tokens = out.shape
    for pair in range(pairs):
        for side in range(2):
            example = 2 * pair + side
            out[pair, pl.ds(side * PROJ, PROJ), :] = part[:, example * tokens : (example + 1) * tokens]


def project(values, ids, signs, table, most, name):
    count, tokens, width = values.shape
    widths = chunks_of(width, most)
    rows = count * tokens
    entries = table.shape[0]
    blocks = ids.shape[0]
    operands = [
        pltpu.with_memory_space_constraint(each, pltpu.HBM)
        for each in (ids, signs, table, values.reshape(rows, width))
    ]
    signed = [pltpu.VMEM((2 * entries * BLOCK, LANES), jnp.bfloat16)] if blocks > entries else []
    return pl.pallas_call(
        functools.partial(project_kernel, widths),
        out_shape=jax.ShapeDtypeStruct((count // 2, LANES, tokens), jnp.float32),
        in_specs=[pl.BlockSpec(memory_space=pltpu.HBM)] * 4,
        out_specs=pl.BlockSpec(memory_space=pltpu.VMEM),
        scratch_shapes=[
            pltpu.VMEM((entries * STRIDE, LANES), jnp.float32),
            pltpu.VMEM((width, LANES), jnp.bfloat16),
            pltpu.VMEM((PROJ, width), jnp.bfloat16),
            pltpu.VMEM((rows, width), jnp.bfloat16),
            pltpu.VMEM((PROJ, rows), jnp.float32),
            pltpu.VMEM(table.shape, table.dtype),
            pltpu.SMEM(ids.shape, ids.dtype),
            pltpu.SMEM(signs.shape, signs.dtype),
            pltpu.SemaphoreType.DMA((len(widths) + 3,)),
        ]
        + signed,
        compiler_params=pltpu.CompilerParams(vmem_limit_bytes=VMEM_BYTES),
        cost_estimate=pl.CostEstimate(
            flops=2 * rows * width * LANES, bytes_accessed=2 * rows * width, transcendentals=0
        ),
        name=name,
    )(*operands)


def kron_kernel(cuts, grads, own, act, *refs):
    parts = cuts[1]
    outs, rows, products = refs[:-2], refs[-2], refs[-1]
    pairs = act.shape[0]
    for pair in range(pairs):
        both = products_with(operand(grads[pair]), own[pair] + act[pair])
        for side in range(2):
            products[pl.ds((2 * pair + side) * STRIDE, PROJ), :] = both[side * PROJ : (side + 1) * PROJ]
    count = 2 * pairs
    lower = lax.broadcasted_iota(jnp.int32, (count, LANES), 1) < PROJ
    even = lax.broadcasted_iota(jnp.int32, (count, LANES), 0) % 2 == 0
    here = even == lower
    tiles = rows.shape[2] // LANES // cuts[0]
    for tile in range(PROJ * PROJ // LANES):
        both = []
        for p in (2 * tile, 2 * tile + 1):
            v = products[pl.ds(p, count, stride=STRIDE), :]
            both.append(jnp.where(here, v, pltpu.roll(v, PROJ, 1)))
        block, part, within = tile // tiles // parts, tile // tiles % parts, tile % tiles
        rows[part, :, pl.ds((block * tiles + within) * LANES, LANES)] = jnp.where(lower, both[0], both[1])
    for k, out in enumerate(outs):
        part = lax.rem(lax.axis_index("seq") + k % 2, parts) if parts > 1 else 0
        out[...] = rows[part]


def kron_of(grads, own, act, cuts):
    pairs = grads.shape[0]
    parts = cuts[1]
    width = PROJ * PROJ // parts
    outs = 4 if parts > 1 else 1
    vmem = pl.BlockSpec(memory_space=pltpu.VMEM)
    return pl.pallas_call(
        functools.partial(kron_kernel, cuts),
        out_shape=[jax.ShapeDtypeStruct((2 * pairs, width), jnp.float32)] * outs,
        in_specs=[vmem] * 3,
        out_specs=[vmem] * outs,
        scratch_shapes=[
            pltpu.VMEM((parts, 2 * pairs, width), jnp.float32),
            pltpu.VMEM((2 * pairs * STRIDE, LANES), jnp.float32),
        ],
        compiler_params=pltpu.CompilerParams(vmem_limit_bytes=VMEM_BYTES),
        name="kron",
    )(grads, own, act)


def parcels_kernel(parts, *refs):
    summands, parcels = refs[:parts], refs[parts:]
    count = summands[0].shape[0]
    dp = len(parcels)
    width = parcels[0].shape[1]
    core, chip = lax.axis_index("seq"), lax.axis_index("tensor") * 2
    blocks = [chip + core, chip + 1 - core]
    for k, parcel in enumerate(parcels):
        for step, block in enumerate(blocks + [lax.rem(lax.axis_index("dp") + k, dp)]):
            lanes = pl.ds(pl.multiple_of(block * width, LANES), width)
            row = summands[0][:, lanes]
            for other in summands[1:]:
                row = row + other[:, lanes]
            parcel[pl.ds(step * count, count), :] = row


def parcels_of(summands, dp):
    count, width = summands[0].shape
    vmem = pl.BlockSpec(memory_space=pltpu.VMEM)
    return pl.pallas_call(
        functools.partial(parcels_kernel, len(summands)),
        out_shape=[jax.ShapeDtypeStruct((3 * count, width // dp), jnp.float32)] * dp,
        in_specs=[vmem] * len(summands),
        out_specs=[vmem] * dp,
        compiler_params=pltpu.CompilerParams(vmem_limit_bytes=VMEM_BYTES),
        name="parcels",
    )(*summands)


def bundle_kernel(*refs):
    parcels, out = refs[:-1], refs[-1]
    rows = 2 * parcels[0].shape[0] // 3
    for k, parcel in enumerate(parcels):
        out[pl.ds(k * rows, rows), :] = parcel[pl.ds(rows // 2, rows), :]


def bundle_of(parcels):
    rows, width = parcels[0].shape
    vmem = pl.BlockSpec(memory_space=pltpu.VMEM)
    return pl.pallas_call(
        bundle_kernel,
        out_shape=jax.ShapeDtypeStruct((2 * rows // 3 * len(parcels), width), jnp.float32),
        in_specs=[vmem] * len(parcels),
        out_specs=vmem,
        compiler_params=pltpu.CompilerParams(vmem_limit_bytes=VMEM_BYTES),
        name="bundle",
    )(*parcels)


def left_operand(x):
    x1, x2, x3 = split3(x)
    return jnp.concatenate([x1, x1, x2, x1, x3, x2, x2, x3], axis=0).T


def right_operand(x):
    x1, x2, x3 = split3(x)
    return jnp.concatenate([x1, x2, x1, x3, x1, x2, x3, x2], axis=0)


def own_halves(parcels):
    rows = parcels[0].shape[0] // 3
    left = jnp.concatenate([parcel[pl.ds(0, rows), :] for parcel in parcels], axis=0)
    right = jnp.concatenate([parcel[pl.ds(2 * rows, rows), :] for parcel in parcels], axis=0)
    return left, right


def halves_at(part):
    core = lax.axis_index("seq")
    return [pl.ds(pl.multiple_of(place * part, part), part) for place in (core, 1 - core)]


TILE = 256


def quadrant_kernel(scale, *refs):
    parcels, (out, left_ref, right_ref, made, sems) = refs[:-5], refs[-5:]
    part = parcels[0].shape[1]
    left, right = own_halves(parcels)
    left, right = left_operand(left), right_operand(right * scale)
    left_ref[...], right_ref[...] = left, right
    here, _ = halves_at(part)
    copies = []
    for k in range(part // TILE):
        rows = slice(k * TILE, (k + 1) * TILE)
        made[rows, :] = jnp.dot(left[rows], right, preferred_element_type=jnp.float32)
        into = pl.ds(pl.multiple_of(lax.axis_index("seq") * part + k * TILE, TILE), TILE)
        copies.append(pltpu.make_async_copy(made.at[rows], out.at[into, here], sems.at[k]))
        copies[-1].start()
    for copy in copies:
        copy.wait()


def fisher_kernel(scale, begun, left, right, bundle, *refs):
    del begun
    parcels, (mine, out, made, kept, sems) = refs[:-5], refs[-5:]
    rows, part = parcels[0].shape[0] // 3, parcels[0].shape[1]
    here, there = halves_at(part)
    kept[:, here] = parcels[0][pl.ds(0, rows), :]
    kept[:, there] = bundle[pl.ds(0, rows), :]
    copies = [pltpu.make_async_copy(kept, mine, sems.at[0])]
    copies[0].start()
    count = len(parcels)
    other_left = jnp.concatenate([bundle[pl.ds(2 * k * rows, rows), :] for k in range(count)], axis=0)
    other_right = jnp.concatenate([bundle[pl.ds((2 * k + 1) * rows, rows), :] for k in range(count)], axis=0)
    right, other_right = right[...], right_operand(other_right * scale)
    for k in range(part // TILE):
        piece = slice(k * TILE, (k + 1) * TILE)
        made[0, piece, :] = jnp.dot(left[piece, :], other_right, preferred_element_type=jnp.float32)
        into = pl.ds(pl.multiple_of(lax.axis_index("seq") * part + k * TILE, TILE), TILE)
        copies.append(pltpu.make_async_copy(made.at[0, piece], out.at[into, there], sems.at[k + 1]))
        copies[-1].start()
    other_left = left_operand(other_left)
    for k, (operand_right, into) in enumerate(((other_right, there), (right, here))):
        made[k + 1] = jnp.dot(other_left, operand_right, preferred_element_type=jnp.float32)
        copies.append(pltpu.make_async_copy(made.at[k + 1], out.at[there, into], sems.at[part // TILE + k + 1]))
        copies[-1].start()
    for copy in copies:
        copy.wait()


def quadrant_of(parcels):
    rows, part = parcels[0].shape
    total = rows // 3 * len(parcels)
    vmem = pl.BlockSpec(memory_space=pltpu.VMEM)
    return pl.pallas_call(
        functools.partial(quadrant_kernel, 1.0 / total),
        out_shape=[
            jax.ShapeDtypeStruct((2 * part, 2 * part), jnp.float32),
            jax.ShapeDtypeStruct((part, 8 * total), jnp.bfloat16),
            jax.ShapeDtypeStruct((8 * total, part), jnp.bfloat16),
        ],
        in_specs=[vmem] * len(parcels),
        out_specs=[pl.BlockSpec(memory_space=pltpu.HBM), vmem, vmem],
        scratch_shapes=[pltpu.VMEM((part, part), jnp.float32), pltpu.SemaphoreType.DMA((part // TILE,))],
        compiler_params=pltpu.CompilerParams(vmem_limit_bytes=VMEM_BYTES),
        cost_estimate=pl.CostEstimate(flops=2**28, bytes_accessed=4 * part * part, transcendentals=0),
        name="quadrant",
    )(*parcels)


def fisher_block(begun, parcels, bundle):
    rows, part = parcels[0].shape
    rows //= 3
    width = 2 * part
    hbm = pl.BlockSpec(memory_space=pltpu.HBM)
    vmem = pl.BlockSpec(memory_space=pltpu.VMEM)
    return pl.pallas_call(
        functools.partial(fisher_kernel, 1.0 / (rows * len(parcels))),
        out_shape=[
            jax.ShapeDtypeStruct((rows, width), jnp.float32),
            jax.ShapeDtypeStruct((width, width), jnp.float32),
        ],
        in_specs=[hbm] + [vmem] * (3 + len(parcels)),
        out_specs=[hbm] * 2,
        scratch_shapes=[
            pltpu.VMEM((3, part, part), jnp.float32),
            pltpu.VMEM((rows, width), jnp.float32),
            pltpu.SemaphoreType.DMA((part // TILE + 3,)),
        ],
        input_output_aliases={0: 1},
        compiler_params=pltpu.CompilerParams(vmem_limit_bytes=VMEM_BYTES),
        name="fisher",
    )(*begun, bundle, *parcels)


def local(acts, grads, in_ids, in_signs, out_ids, out_signs, in_table, out_table):
    tensor, seq, dp = (lax.axis_size(name) for name in ("tensor", "seq", "dp"))
    shards = tensor * seq
    small = tensor == 2 and seq == 2 and dp == 4
    swap = [(0, 1), (1, 0)]

    act = project(acts, in_ids, in_signs, in_table, 512, "project_acts")
    if tensor == 2:
        other = lax.ppermute(act, "tensor", swap)
    else:
        act = lax.psum(act, "tensor")
        other = jnp.zeros_like(act)
    grad = project(grads, out_ids, out_signs, out_table, 1024, "project_grads")
    krons = kron_of(grad, act, other, (shards, seq) if small else (1, 1))

    if not small:
        kron = lax.psum(krons[0], ("tensor", "seq"))
        width = kron.shape[1] // shards
        place = lax.axis_index("tensor") * seq + lax.axis_index("seq")
        mine = lax.dynamic_slice_in_dim(kron, place * width, width, 1)
        every = lax.all_gather(kron, "dp", axis=0, tiled=True)
        left = lax.dynamic_slice_in_dim(every, place * width, width, 1)
        columns = kron.shape[1] // dp
        right = lax.dynamic_slice_in_dim(every, lax.axis_index("dp") * columns, columns, 1)
        fisher = lax.dot_general(
            left, right, (((0,), (0,)), ((), ())), precision=lax.Precision.HIGHEST
        ) / left.shape[0]
        return mine, fisher

    across = lax.ppermute(krons[1], ("tensor", "seq"), [(p, 3 - p) for p in range(shards)])
    beside = lax.ppermute(krons[2], "tensor", swap)
    mate = lax.ppermute(krons[3], "seq", swap)
    parcels = list(parcels_of([across, beside, mate, krons[0]], dp))
    for k in range(1, dp):
        parcels[k] = lax.ppermute(parcels[k], "dp", [(d, (d + k) % dp) for d in range(dp)])
    bundle = lax.ppermute(bundle_of(parcels), "seq", swap)
    mine, fisher = fisher_block(quadrant_of(parcels), parcels, bundle)
    return mine, fisher


def solution(mesh):
    in_specs = (
        P(("groups", "dp"), "seq", "tensor"),
        P(("groups", "dp"), "seq", "tensor"),
        P("tensor"),
        P("tensor"),
        P("tensor"),
        P("tensor"),
        P(),
        P(),
    )
    out_specs = (P(("groups", "dp"), ("tensor", "seq")), P(("groups", "tensor", "seq"), "dp"))
    return jax.shard_map(local, mesh=mesh, in_specs=in_specs, out_specs=out_specs, check_vma=False)
```

```python
import functools

import jax
import jax.numpy as jnp
from jax import lax
from jax.experimental import pallas as pl
from jax.experimental.pallas import tpu as pltpu
from jax.sharding import PartitionSpec as P

PROJ = 64
BLOCK = 64
LANES = 128
STRIDE = 72
VMEM_BYTES = 48 * 1024 * 1024


def chunks_of(width, shares):
    unit = width // sum(shares)
    if unit * sum(shares) == width and unit % LANES == 0:
        return [share * unit for share in shares]
    chunk = 8 * LANES
    while width % chunk:
        chunk -= LANES
    return [chunk] * (width // chunk)


def split3(x):
    high = x.astype(jnp.bfloat16)
    rest = x - high.astype(jnp.float32)
    mid = rest.astype(jnp.bfloat16)
    low = (rest - mid.astype(jnp.float32)).astype(jnp.bfloat16)
    return high, mid, low


def spread_table(table, spread):
    entries = table.shape[0]
    for row in range(0, BLOCK, 2):
        both = table[:, row * PROJ : row * PROJ + LANES].astype(jnp.float32)
        spread[pl.ds(row, entries, stride=STRIDE), :] = both
        spread[pl.ds(row + 1, entries, stride=STRIDE), :] = pltpu.roll(both, PROJ, 1)


def sign_table(spread, signed):
    entries = spread.shape[0] // STRIDE
    for entry in range(entries):
        block = spread[pl.ds(entry * STRIDE, BLOCK), :].astype(jnp.bfloat16)
        signed[pl.ds((entries + entry) * BLOCK, BLOCK), :] = block
        signed[pl.ds(entry * BLOCK, BLOCK), :] = -block


def lay_blocks(ids, signs, spread, signed, matrix, first, last):
    entries = spread.shape[0] // STRIDE
    for j in range(first, last):
        if signed is None:
            start = pl.multiple_of(ids[j] * STRIDE, 8)
            sign = (2 * signs[j] - 1).astype(jnp.float32)
            block = (spread[pl.ds(start, BLOCK), :] * sign).astype(jnp.bfloat16)
        else:
            start = pl.multiple_of((signs[j] * entries + ids[j]) * BLOCK, BLOCK)
            block = signed[pl.ds(start, BLOCK), :]
        matrix[pl.ds(j * BLOCK, BLOCK), :] = block


def operand(x):
    x1, x2, x3 = split3(x)
    return jnp.concatenate([x1, x1, x2, x1, x3, x2], axis=1)


def products_with(left, act):
    a1, a2, a3 = split3(act)
    right = jnp.concatenate([a1, a2, a1, a3, a1, a2], axis=1)
    return lax.dot_general(left, right, (((1,), (1,)), ((), ())), preferred_element_type=jnp.float32)


def project_kernel(widths, ids, signs, table, rows_ref, out, *refs):
    spread, matrix, across, held, total, own_table, own_ids, own_signs, sems, *signed = refs
    signed = signed[0] if signed else None
    copies, starts, start = [], [], 0
    for c, width in enumerate(widths):
        columns = pl.ds(start, width)
        copies.append(pltpu.make_async_copy(rows_ref.at[:, columns], held.at[:, columns], sems.at[c]))
        starts.append(start)
        start += width
    small = [
        pltpu.make_async_copy(source, kept, sems.at[len(widths) + k])
        for k, (source, kept) in enumerate(((table, own_table), (ids, own_ids), (signs, own_signs)))
    ]
    for copy in small + copies:
        copy.start()
    small[0].wait()
    spread_table(own_table, spread)
    if signed is not None:
        sign_table(spread, signed)
    small[1].wait()
    small[2].wait()

    def lay(c):
        lay_blocks(
            own_ids, own_signs, spread, signed, matrix, starts[c] // BLOCK, (starts[c] + widths[c]) // BLOCK
        )
        rows = pl.ds(starts[c], widths[c])
        across[:, rows] = matrix[rows, :].T[:PROJ, :]

    lay(0)
    for c, copy in enumerate(copies):
        columns = pl.ds(starts[c], widths[c])
        copy.wait()
        if c + 1 < len(widths):
            lay(c + 1)
        part = lax.dot_general(
            across[:, columns], held[:, columns], (((1,), (1,)), ((), ())), preferred_element_type=jnp.float32
        )
        if c == 0:
            total[...] = part
        elif c + 1 < len(widths):
            total[...] += part
    part = total[...] + part if len(widths) > 1 else part
    pairs, _, tokens = out.shape
    for pair in range(pairs):
        for side in range(2):
            example = 2 * pair + side
            out[pair, pl.ds(side * PROJ, PROJ), :] = part[:, example * tokens : (example + 1) * tokens]


def project(values, ids, signs, table, shares, name):
    count, tokens, width = values.shape
    widths = chunks_of(width, shares)
    rows = count * tokens
    entries = table.shape[0]
    blocks = ids.shape[0]
    operands = [
        pltpu.with_memory_space_constraint(each, pltpu.HBM)
        for each in (ids, signs, table, values.reshape(rows, width))
    ]
    signed = [pltpu.VMEM((2 * entries * BLOCK, LANES), jnp.bfloat16)] if blocks > entries else []
    return pl.pallas_call(
        functools.partial(project_kernel, widths),
        out_shape=jax.ShapeDtypeStruct((count // 2, LANES, tokens), jnp.float32),
        in_specs=[pl.BlockSpec(memory_space=pltpu.HBM)] * 4,
        out_specs=pl.BlockSpec(memory_space=pltpu.VMEM),
        scratch_shapes=[
            pltpu.VMEM((entries * STRIDE, LANES), jnp.float32),
            pltpu.VMEM((width, LANES), jnp.bfloat16),
            pltpu.VMEM((PROJ, width), jnp.bfloat16),
            pltpu.VMEM((rows, width), jnp.bfloat16),
            pltpu.VMEM((PROJ, rows), jnp.float32),
            pltpu.VMEM(table.shape, table.dtype),
            pltpu.SMEM(ids.shape, ids.dtype),
            pltpu.SMEM(signs.shape, signs.dtype),
            pltpu.SemaphoreType.DMA((len(widths) + 3,)),
        ]
        + signed,
        compiler_params=pltpu.CompilerParams(vmem_limit_bytes=VMEM_BYTES),
        cost_estimate=pl.CostEstimate(
            flops=2 * rows * width * LANES, bytes_accessed=2 * rows * width, transcendentals=0
        ),
        name=name,
    )(*operands)


def kron_kernel(cuts, grads, own, act, *refs):
    parts = cuts[1]
    outs, products = refs[:-1], refs[-1]
    pairs = act.shape[0]
    for pair in range(pairs):
        both = products_with(operand(grads[pair]), own[pair] + act[pair])
        for side in range(2):
            products[pl.ds((2 * pair + side) * STRIDE, PROJ), :] = both[side * PROJ : (side + 1) * PROJ]
    count = 2 * pairs
    lower = lax.broadcasted_iota(jnp.int32, (count, LANES), 1) < PROJ
    even = lax.broadcasted_iota(jnp.int32, (count, LANES), 0) % 2 == 0
    here = even == lower
    tiles = outs[0].shape[1] // LANES // cuts[0]
    made = []
    for tile in range(PROJ * PROJ // LANES):
        both = []
        for p in (2 * tile, 2 * tile + 1):
            v = products[pl.ds(p, count, stride=STRIDE), :]
            both.append(jnp.where(here, v, pltpu.roll(v, PROJ, 1)))
        made.append(jnp.where(lower, both[0], both[1]))

    def store(shift):
        for tile, value in enumerate(made):
            block, part, within = tile // tiles // parts, tile // tiles % parts, tile % tiles
            into = pl.ds((block * tiles + within) * LANES, LANES)
            for out in outs[(part - shift) % parts :: parts]:
                out[:, into] = value

    if parts == 1:
        store(0)
    else:
        for core in range(parts):
            pl.when(lax.axis_index("seq") == core)(functools.partial(store, core))


def kron_of(grads, own, act, cuts):
    pairs = grads.shape[0]
    parts = cuts[1]
    width = PROJ * PROJ // parts
    outs = 4 if parts > 1 else 1
    vmem = pl.BlockSpec(memory_space=pltpu.VMEM)
    return pl.pallas_call(
        functools.partial(kron_kernel, cuts),
        out_shape=[jax.ShapeDtypeStruct((2 * pairs, width), jnp.float32)] * outs,
        in_specs=[vmem] * 3,
        out_specs=[vmem] * outs,
        scratch_shapes=[
            pltpu.VMEM((2 * pairs * STRIDE, LANES), jnp.float32),
        ],
        compiler_params=pltpu.CompilerParams(vmem_limit_bytes=VMEM_BYTES),
        name="kron",
    )(grads, own, act)


def parcels_kernel(parts, *refs):
    summands, parcels = refs[:parts], refs[parts:]
    count = summands[0].shape[0]
    dp = len(parcels)
    width = parcels[0].shape[1]
    core, chip = lax.axis_index("seq"), lax.axis_index("tensor") * 2
    blocks = [chip + core, chip + 1 - core]
    for k, parcel in enumerate(parcels):
        for step, block in enumerate(blocks + [lax.rem(lax.axis_index("dp") + k, dp)]):
            lanes = pl.ds(pl.multiple_of(block * width, LANES), width)
            row = summands[0][:, lanes]
            for other in summands[1:]:
                row = row + other[:, lanes]
            parcel[pl.ds(step * count, count), :] = row


def parcels_of(summands, dp):
    count, width = summands[0].shape
    vmem = pl.BlockSpec(memory_space=pltpu.VMEM)
    return pl.pallas_call(
        functools.partial(parcels_kernel, len(summands)),
        out_shape=[jax.ShapeDtypeStruct((3 * count, width // dp), jnp.float32)] * dp,
        in_specs=[vmem] * len(summands),
        out_specs=[vmem] * dp,
        compiler_params=pltpu.CompilerParams(vmem_limit_bytes=VMEM_BYTES),
        name="parcels",
    )(*summands)


def bundle_kernel(*refs):
    parcels, out = refs[:-1], refs[-1]
    rows = 2 * parcels[0].shape[0] // 3
    for k, parcel in enumerate(parcels):
        out[pl.ds(k * rows, rows), :] = parcel[pl.ds(rows // 2, rows), :]


def bundle_of(parcels):
    rows, width = parcels[0].shape
    vmem = pl.BlockSpec(memory_space=pltpu.VMEM)
    return pl.pallas_call(
        bundle_kernel,
        out_shape=jax.ShapeDtypeStruct((2 * rows // 3 * len(parcels), width), jnp.float32),
        in_specs=[vmem] * len(parcels),
        out_specs=vmem,
        compiler_params=pltpu.CompilerParams(vmem_limit_bytes=VMEM_BYTES),
        name="bundle",
    )(*parcels)


def left_operand(x):
    x1, x2, x3 = split3(x)
    return jnp.concatenate([x1, x1, x2, x1, x3, x2, x2, x3], axis=0).T


def right_operand(x):
    x1, x2, x3 = split3(x)
    return jnp.concatenate([x1, x2, x1, x3, x1, x2, x3, x2], axis=0)


def own_halves(parcels):
    rows = parcels[0].shape[0] // 3
    left = jnp.concatenate([parcel[pl.ds(0, rows), :] for parcel in parcels], axis=0)
    right = jnp.concatenate([parcel[pl.ds(2 * rows, rows), :] for parcel in parcels], axis=0)
    return left, right


def halves_at(part):
    core = lax.axis_index("seq")
    return [pl.ds(pl.multiple_of(place * part, part), part) for place in (core, 1 - core)]


TILE = 256


def quadrant_kernel(scale, *refs):
    parcels, (out, left_ref, right_ref, made, sems) = refs[:-5], refs[-5:]
    part = parcels[0].shape[1]
    left, right = own_halves(parcels)
    left, right = left_operand(left), right_operand(right * scale)
    left_ref[...], right_ref[...] = left, right
    here, _ = halves_at(part)
    copies = []
    for k in range(part // TILE):
        rows = slice(k * TILE, (k + 1) * TILE)
        made[rows, :] = jnp.dot(left[rows], right, preferred_element_type=jnp.float32)
        into = pl.ds(pl.multiple_of(lax.axis_index("seq") * part + k * TILE, TILE), TILE)
        copies.append(pltpu.make_async_copy(made.at[rows], out.at[into, here], sems.at[k]))
        copies[-1].start()
    for copy in copies:
        copy.wait()


def fisher_kernel(scale, begun, left, right, bundle, *refs):
    del begun
    parcels, (mine, out, made, kept, sems) = refs[:-5], refs[-5:]
    rows, part = parcels[0].shape[0] // 3, parcels[0].shape[1]
    here, there = halves_at(part)
    kept[:, here] = parcels[0][pl.ds(0, rows), :]
    kept[:, there] = bundle[pl.ds(0, rows), :]
    copies = [pltpu.make_async_copy(kept, mine, sems.at[0])]
    copies[0].start()
    count = len(parcels)
    other_left = jnp.concatenate([bundle[pl.ds(2 * k * rows, rows), :] for k in range(count)], axis=0)
    other_right = jnp.concatenate([bundle[pl.ds((2 * k + 1) * rows, rows), :] for k in range(count)], axis=0)
    right, other_right = right[...], right_operand(other_right * scale)
    for k in range(part // TILE):
        piece = slice(k * TILE, (k + 1) * TILE)
        made[0, piece, :] = jnp.dot(left[piece, :], other_right, preferred_element_type=jnp.float32)
        into = pl.ds(pl.multiple_of(lax.axis_index("seq") * part + k * TILE, TILE), TILE)
        copies.append(pltpu.make_async_copy(made.at[0, piece], out.at[into, there], sems.at[k + 1]))
        copies[-1].start()
    other_left = left_operand(other_left)
    for k, (operand_right, into) in enumerate(((other_right, there), (right, here))):
        made[k + 1] = jnp.dot(other_left, operand_right, preferred_element_type=jnp.float32)
        copies.append(pltpu.make_async_copy(made.at[k + 1], out.at[there, into], sems.at[part // TILE + k + 1]))
        copies[-1].start()
    for copy in copies:
        copy.wait()


def quadrant_of(parcels):
    rows, part = parcels[0].shape
    total = rows // 3 * len(parcels)
    vmem = pl.BlockSpec(memory_space=pltpu.VMEM)
    return pl.pallas_call(
        functools.partial(quadrant_kernel, 1.0 / total),
        out_shape=[
            jax.ShapeDtypeStruct((2 * part, 2 * part), jnp.float32),
            jax.ShapeDtypeStruct((part, 8 * total), jnp.bfloat16),
            jax.ShapeDtypeStruct((8 * total, part), jnp.bfloat16),
        ],
        in_specs=[vmem] * len(parcels),
        out_specs=[pl.BlockSpec(memory_space=pltpu.HBM), vmem, vmem],
        scratch_shapes=[pltpu.VMEM((part, part), jnp.float32), pltpu.SemaphoreType.DMA((part // TILE,))],
        compiler_params=pltpu.CompilerParams(vmem_limit_bytes=VMEM_BYTES),
        cost_estimate=pl.CostEstimate(flops=2**28, bytes_accessed=4 * part * part, transcendentals=0),
        name="quadrant",
    )(*parcels)


def fisher_block(begun, parcels, bundle):
    rows, part = parcels[0].shape
    rows //= 3
    width = 2 * part
    hbm = pl.BlockSpec(memory_space=pltpu.HBM)
    vmem = pl.BlockSpec(memory_space=pltpu.VMEM)
    return pl.pallas_call(
        functools.partial(fisher_kernel, 1.0 / (rows * len(parcels))),
        out_shape=[
            jax.ShapeDtypeStruct((rows, width), jnp.float32),
            jax.ShapeDtypeStruct((width, width), jnp.float32),
        ],
        in_specs=[hbm] + [vmem] * (3 + len(parcels)),
        out_specs=[hbm] * 2,
        scratch_shapes=[
            pltpu.VMEM((3, part, part), jnp.float32),
            pltpu.VMEM((rows, width), jnp.float32),
            pltpu.SemaphoreType.DMA((part // TILE + 3,)),
        ],
        input_output_aliases={0: 1},
        compiler_params=pltpu.CompilerParams(vmem_limit_bytes=VMEM_BYTES),
        name="fisher",
    )(*begun, bundle, *parcels)


def local(acts, grads, in_ids, in_signs, out_ids, out_signs, in_table, out_table):
    tensor, seq, dp = (lax.axis_size(name) for name in ("tensor", "seq", "dp"))
    shards = tensor * seq
    small = tensor == 2 and seq == 2 and dp == 4
    swap = [(0, 1), (1, 0)]

    act = project(acts, in_ids, in_signs, in_table, (2, 3, 2, 1), "project_acts")
    if tensor == 2:
        other = lax.ppermute(act, "tensor", swap)
    else:
        act = lax.psum(act, "tensor")
        other = jnp.zeros_like(act)
    grad = project(grads, out_ids, out_signs, out_table, (2, 4, 4, 4, 4, 4, 4, 1, 1), "project_grads")
    krons = kron_of(grad, act, other, (shards, seq) if small else (1, 1))

    if not small:
        kron = lax.psum(krons[0], ("tensor", "seq"))
        width = kron.shape[1] // shards
        place = lax.axis_index("tensor") * seq + lax.axis_index("seq")
        mine = lax.dynamic_slice_in_dim(kron, place * width, width, 1)
        every = lax.all_gather(kron, "dp", axis=0, tiled=True)
        left = lax.dynamic_slice_in_dim(every, place * width, width, 1)
        columns = kron.shape[1] // dp
        right = lax.dynamic_slice_in_dim(every, lax.axis_index("dp") * columns, columns, 1)
        fisher = lax.dot_general(
            left, right, (((0,), (0,)), ((), ())), precision=lax.Precision.HIGHEST
        ) / left.shape[0]
        return mine, fisher

    across = lax.ppermute(krons[1], ("tensor", "seq"), [(p, 3 - p) for p in range(shards)])
    beside = lax.ppermute(krons[2], "tensor", swap)
    mate = lax.ppermute(krons[3], "seq", swap)
    parcels = list(parcels_of([across, beside, mate, krons[0]], dp))
    for k in range(1, dp):
        parcels[k] = lax.ppermute(parcels[k], "dp", [(d, (d + k) % dp) for d in range(dp)])
    bundle = lax.ppermute(bundle_of(parcels), "seq", swap)
    mine, fisher = fisher_block(quadrant_of(parcels), parcels, bundle)
    return mine, fisher


def solution(mesh):
    in_specs = (
        P(("groups", "dp"), "seq", "tensor"),
        P(("groups", "dp"), "seq", "tensor"),
        P("tensor"),
        P("tensor"),
        P("tensor"),
        P("tensor"),
        P(),
        P(),
    )
    out_specs = (P(("groups", "dp"), ("tensor", "seq")), P(("groups", "tensor", "seq"), "dp"))
    return jax.shard_map(local, mesh=mesh, in_specs=in_specs, out_specs=out_specs, check_vma=False)
```

```python
import functools

import jax
import jax.numpy as jnp
from jax import lax
from jax.experimental import pallas as pl
from jax.experimental.pallas import tpu as pltpu
from jax.sharding import PartitionSpec as P

PROJ = 64
BLOCK = 64
LANES = 128
STRIDE = 72
VMEM_BYTES = 48 * 1024 * 1024


def chunks_of(width, most):
    if width < 4 * most or most % (4 * LANES):
        chunk = most
        while width % chunk:
            chunk -= LANES
        return [chunk] * (width // chunk)
    inner = width - most
    chunk = most
    while inner % chunk:
        chunk -= LANES
    return [most // 2] + [chunk] * (inner // chunk) + [most // 4] * 2


def split3(x):
    high = x.astype(jnp.bfloat16)
    rest = x - high.astype(jnp.float32)
    mid = rest.astype(jnp.bfloat16)
    low = (rest - mid.astype(jnp.float32)).astype(jnp.bfloat16)
    return high, mid, low


def spread_table(table, spread):
    entries = table.shape[0]
    for row in range(0, BLOCK, 2):
        both = table[:, row * PROJ : row * PROJ + LANES].astype(jnp.float32)
        spread[pl.ds(row, entries, stride=STRIDE), :] = both
        spread[pl.ds(row + 1, entries, stride=STRIDE), :] = pltpu.roll(both, PROJ, 1)


def sign_table(spread, signed):
    entries = spread.shape[0] // STRIDE
    for entry in range(entries):
        block = spread[pl.ds(entry * STRIDE, BLOCK), :].astype(jnp.bfloat16)
        signed[pl.ds((entries + entry) * BLOCK, BLOCK), :] = block
        signed[pl.ds(entry * BLOCK, BLOCK), :] = -block


def lay_blocks(ids, signs, spread, signed, matrix, first, last):
    entries = spread.shape[0] // STRIDE
    for j in range(first, last):
        if signed is None:
            start = pl.multiple_of(ids[j] * STRIDE, 8)
            sign = (2 * signs[j] - 1).astype(jnp.float32)
            block = (spread[pl.ds(start, BLOCK), :] * sign).astype(jnp.bfloat16)
        else:
            start = pl.multiple_of((signs[j] * entries + ids[j]) * BLOCK, BLOCK)
            block = signed[pl.ds(start, BLOCK), :]
        matrix[pl.ds(j * BLOCK, BLOCK), :] = block


def operand(x):
    x1, x2, x3 = split3(x)
    return jnp.concatenate([x1, x1, x2, x1, x3, x2], axis=1)


def products_with(left, act):
    a1, a2, a3 = split3(act)
    right = jnp.concatenate([a1, a2, a1, a3, a1, a2], axis=1)
    return lax.dot_general(left, right, (((1,), (1,)), ((), ())), preferred_element_type=jnp.float32)


def project_kernel(widths, ids, signs, table, rows_ref, out, *refs):
    spread, matrix, held, total, own_table, own_ids, own_signs, sems, *signed = refs
    signed = signed[0] if signed else None
    copies, starts, start = [], [], 0
    for c, width in enumerate(widths):
        columns = pl.ds(start, width)
        copies.append(pltpu.make_async_copy(rows_ref.at[:, columns], held.at[:, columns], sems.at[c]))
        starts.append(start)
        start += width
    small = [
        pltpu.make_async_copy(source, kept, sems.at[len(widths) + k])
        for k, (source, kept) in enumerate(((table, own_table), (ids, own_ids), (signs, own_signs)))
    ]
    for copy in small + copies:
        copy.start()
    small[0].wait()
    spread_table(own_table, spread)
    if signed is not None:
        sign_table(spread, signed)
    small[1].wait()
    small[2].wait()
    lay = functools.partial(lay_blocks, own_ids, own_signs, spread, signed, matrix)
    lay(0, widths[0] // BLOCK)
    for c, copy in enumerate(copies):
        columns = pl.ds(starts[c], widths[c])
        copy.wait()
        if c + 1 < len(widths):
            lay(starts[c + 1] // BLOCK, (starts[c + 1] + widths[c + 1]) // BLOCK)
        part = lax.dot_general(
            matrix[columns, :PROJ],
            held[:, columns],
            (((0,), (1,)), ((), ())),
            preferred_element_type=jnp.float32,
        )
        if c == 0:
            total[...] = part
        elif c + 1 < len(widths):
            total[...] += part
    part = total[...] + part if len(widths) > 1 else part
    pairs, _, tokens = out.shape
    for pair in range(pairs):
        for side in range(2):
            example = 2 * pair + side
            out[pair, pl.ds(side * PROJ, PROJ), :] = part[:, example * tokens : (example + 1) * tokens]


def project(values, ids, signs, table, most, name):
    count, tokens, width = values.shape
    widths = chunks_of(width, most)
    rows = count * tokens
    entries = table.shape[0]
    blocks = ids.shape[0]
    operands = [
        pltpu.with_memory_space_constraint(each, pltpu.HBM)
        for each in (ids, signs, table, values.reshape(rows, width))
    ]
    signed = [pltpu.VMEM((2 * entries * BLOCK, LANES), jnp.bfloat16)] if blocks > entries else []
    return pl.pallas_call(
        functools.partial(project_kernel, widths),
        out_shape=jax.ShapeDtypeStruct((count // 2, LANES, tokens), jnp.float32),
        in_specs=[pl.BlockSpec(memory_space=pltpu.HBM)] * 4,
        out_specs=pl.BlockSpec(memory_space=pltpu.VMEM),
        scratch_shapes=[
            pltpu.VMEM((entries * STRIDE, LANES), jnp.float32),
            pltpu.VMEM((width, LANES), jnp.bfloat16),
            pltpu.VMEM((rows, width), jnp.bfloat16),
            pltpu.VMEM((PROJ, rows), jnp.float32),
            pltpu.VMEM(table.shape, table.dtype),
            pltpu.SMEM(ids.shape, ids.dtype),
            pltpu.SMEM(signs.shape, signs.dtype),
            pltpu.SemaphoreType.DMA((len(widths) + 3,)),
        ]
        + signed,
        compiler_params=pltpu.CompilerParams(vmem_limit_bytes=VMEM_BYTES),
        cost_estimate=pl.CostEstimate(
            flops=2 * rows * width * LANES, bytes_accessed=2 * rows * width, transcendentals=0
        ),
        name=name,
    )(*operands)


def kron_kernel(cuts, grads, own, act, *refs):
    parts = cuts[1]
    outs, rows, products = refs[:-2], refs[-2], refs[-1]
    pairs = act.shape[0]
    for pair in range(pairs):
        both = products_with(operand(grads[pair]), own[pair] + act[pair])
        for side in range(2):
            products[pl.ds((2 * pair + side) * STRIDE, PROJ), :] = both[side * PROJ : (side + 1) * PROJ]
    count = 2 * pairs
    lower = lax.broadcasted_iota(jnp.int32, (count, LANES), 1) < PROJ
    even = lax.broadcasted_iota(jnp.int32, (count, LANES), 0) % 2 == 0
    here = even == lower
    tiles = rows.shape[2] // LANES // cuts[0]
    for tile in range(PROJ * PROJ // LANES):
        both = []
        for p in (2 * tile, 2 * tile + 1):
            v = products[pl.ds(p, count, stride=STRIDE), :]
            both.append(jnp.where(here, v, pltpu.roll(v, PROJ, 1)))
        block, part, within = tile // tiles // parts, tile // tiles % parts, tile % tiles
        rows[part, :, pl.ds((block * tiles + within) * LANES, LANES)] = jnp.where(lower, both[0], both[1])
    for k, out in enumerate(outs):
        part = lax.rem(lax.axis_index("seq") + k % 2, parts) if parts > 1 else 0
        out[...] = rows[part]


def kron_of(grads, own, act, cuts):
    pairs = grads.shape[0]
    parts = cuts[1]
    width = PROJ * PROJ // parts
    outs = 4 if parts > 1 else 1
    vmem = pl.BlockSpec(memory_space=pltpu.VMEM)
    return pl.pallas_call(
        functools.partial(kron_kernel, cuts),
        out_shape=[jax.ShapeDtypeStruct((2 * pairs, width), jnp.float32)] * outs,
        in_specs=[vmem] * 3,
        out_specs=[vmem] * outs,
        scratch_shapes=[
            pltpu.VMEM((parts, 2 * pairs, width), jnp.float32),
            pltpu.VMEM((2 * pairs * STRIDE, LANES), jnp.float32),
        ],
        compiler_params=pltpu.CompilerParams(vmem_limit_bytes=VMEM_BYTES),
        name="kron",
    )(grads, own, act)


def parcels_kernel(parts, *refs):
    summands, parcels = refs[:parts], refs[parts:]
    count = summands[0].shape[0]
    dp = len(parcels)
    width = parcels[0].shape[1]
    core, chip = lax.axis_index("seq"), lax.axis_index("tensor") * 2
    blocks = [chip + core, chip + 1 - core]
    for k, parcel in enumerate(parcels):
        for step, block in enumerate(blocks + [lax.rem(lax.axis_index("dp") + k, dp)]):
            lanes = pl.ds(pl.multiple_of(block * width, LANES), width)
            row = summands[0][:, lanes]
            for other in summands[1:]:
                row = row + other[:, lanes]
            parcel[pl.ds(step * count, count), :] = row


def parcels_of(summands, dp):
    count, width = summands[0].shape
    vmem = pl.BlockSpec(memory_space=pltpu.VMEM)
    return pl.pallas_call(
        functools.partial(parcels_kernel, len(summands)),
        out_shape=[jax.ShapeDtypeStruct((3 * count, width // dp), jnp.float32)] * dp,
        in_specs=[vmem] * len(summands),
        out_specs=[vmem] * dp,
        compiler_params=pltpu.CompilerParams(vmem_limit_bytes=VMEM_BYTES),
        name="parcels",
    )(*summands)


def bundle_kernel(*refs):
    parcels, out = refs[:-1], refs[-1]
    rows = 2 * parcels[0].shape[0] // 3
    for k, parcel in enumerate(parcels):
        out[pl.ds(k * rows, rows), :] = parcel[pl.ds(rows // 2, rows), :]


def bundle_of(parcels):
    rows, width = parcels[0].shape
    vmem = pl.BlockSpec(memory_space=pltpu.VMEM)
    return pl.pallas_call(
        bundle_kernel,
        out_shape=jax.ShapeDtypeStruct((2 * rows // 3 * len(parcels), width), jnp.float32),
        in_specs=[vmem] * len(parcels),
        out_specs=vmem,
        compiler_params=pltpu.CompilerParams(vmem_limit_bytes=VMEM_BYTES),
        name="bundle",
    )(*parcels)


def left_operand(x):
    x1, x2, x3 = split3(x)
    return jnp.concatenate([x1, x1, x2, x1, x3, x2, x2, x3], axis=0).T


def right_operand(x):
    x1, x2, x3 = split3(x)
    return jnp.concatenate([x1, x2, x1, x3, x1, x2, x3, x2], axis=0)


def own_halves(parcels):
    rows = parcels[0].shape[0] // 3
    left = jnp.concatenate([parcel[pl.ds(0, rows), :] for parcel in parcels], axis=0)
    right = jnp.concatenate([parcel[pl.ds(2 * rows, rows), :] for parcel in parcels], axis=0)
    return left, right


def halves_at(part):
    core = lax.axis_index("seq")
    return [pl.ds(pl.multiple_of(place * part, part), part) for place in (core, 1 - core)]


TILE = 256


def quadrant_kernel(scale, *refs):
    parcels, (out, left_ref, right_ref, made, sems) = refs[:-5], refs[-5:]
    part = parcels[0].shape[1]
    left, right = own_halves(parcels)
    left, right = left_operand(left), right_operand(right * scale)
    left_ref[...], right_ref[...] = left, right
    here, _ = halves_at(part)
    copies = []
    for k in range(part // TILE):
        rows = slice(k * TILE, (k + 1) * TILE)
        made[rows, :] = jnp.dot(left[rows], right, preferred_element_type=jnp.float32)
        into = pl.ds(pl.multiple_of(lax.axis_index("seq") * part + k * TILE, TILE), TILE)
        copies.append(pltpu.make_async_copy(made.at[rows], out.at[into, here], sems.at[k]))
        copies[-1].start()
    for copy in copies:
        copy.wait()


def fisher_kernel(scale, begun, left, right, bundle, *refs):
    del begun
    parcels, (mine, out, made, kept, sems) = refs[:-5], refs[-5:]
    rows, part = parcels[0].shape[0] // 3, parcels[0].shape[1]
    here, there = halves_at(part)
    kept[:, here] = parcels[0][pl.ds(0, rows), :]
    kept[:, there] = bundle[pl.ds(0, rows), :]
    copies = [pltpu.make_async_copy(kept, mine, sems.at[0])]
    copies[0].start()
    count = len(parcels)
    other_left = jnp.concatenate([bundle[pl.ds(2 * k * rows, rows), :] for k in range(count)], axis=0)
    other_right = jnp.concatenate([bundle[pl.ds((2 * k + 1) * rows, rows), :] for k in range(count)], axis=0)
    right, other_right = right[...], right_operand(other_right * scale)
    for k in range(part // TILE):
        piece = slice(k * TILE, (k + 1) * TILE)
        made[0, piece, :] = jnp.dot(left[piece, :], other_right, preferred_element_type=jnp.float32)
        into = pl.ds(pl.multiple_of(lax.axis_index("seq") * part + k * TILE, TILE), TILE)
        copies.append(pltpu.make_async_copy(made.at[0, piece], out.at[into, there], sems.at[k + 1]))
        copies[-1].start()
    other_left = left_operand(other_left)
    for k, (operand_right, into) in enumerate(((other_right, there), (right, here))):
        made[k + 1] = jnp.dot(other_left, operand_right, preferred_element_type=jnp.float32)
        copies.append(pltpu.make_async_copy(made.at[k + 1], out.at[there, into], sems.at[part // TILE + k + 1]))
        copies[-1].start()
    for copy in copies:
        copy.wait()


def quadrant_of(parcels):
    rows, part = parcels[0].shape
    total = rows // 3 * len(parcels)
    vmem = pl.BlockSpec(memory_space=pltpu.VMEM)
    return pl.pallas_call(
        functools.partial(quadrant_kernel, 1.0 / total),
        out_shape=[
            jax.ShapeDtypeStruct((2 * part, 2 * part), jnp.float32),
            jax.ShapeDtypeStruct((part, 8 * total), jnp.bfloat16),
            jax.ShapeDtypeStruct((8 * total, part), jnp.bfloat16),
        ],
        in_specs=[vmem] * len(parcels),
        out_specs=[pl.BlockSpec(memory_space=pltpu.HBM), vmem, vmem],
        scratch_shapes=[pltpu.VMEM((part, part), jnp.float32), pltpu.SemaphoreType.DMA((part // TILE,))],
        compiler_params=pltpu.CompilerParams(vmem_limit_bytes=VMEM_BYTES),
        cost_estimate=pl.CostEstimate(flops=2**28, bytes_accessed=4 * part * part, transcendentals=0),
        name="quadrant",
    )(*parcels)


def fisher_block(begun, parcels, bundle):
    rows, part = parcels[0].shape
    rows //= 3
    width = 2 * part
    hbm = pl.BlockSpec(memory_space=pltpu.HBM)
    vmem = pl.BlockSpec(memory_space=pltpu.VMEM)
    return pl.pallas_call(
        functools.partial(fisher_kernel, 1.0 / (rows * len(parcels))),
        out_shape=[
            jax.ShapeDtypeStruct((rows, width), jnp.float32),
            jax.ShapeDtypeStruct((width, width), jnp.float32),
        ],
        in_specs=[hbm] + [vmem] * (3 + len(parcels)),
        out_specs=[hbm] * 2,
        scratch_shapes=[
            pltpu.VMEM((3, part, part), jnp.float32),
            pltpu.VMEM((rows, width), jnp.float32),
            pltpu.SemaphoreType.DMA((part // TILE + 3,)),
        ],
        input_output_aliases={0: 1},
        compiler_params=pltpu.CompilerParams(vmem_limit_bytes=VMEM_BYTES),
        name="fisher",
    )(*begun, bundle, *parcels)


def local(acts, grads, in_ids, in_signs, out_ids, out_signs, in_table, out_table):
    tensor, seq, dp = (lax.axis_size(name) for name in ("tensor", "seq", "dp"))
    shards = tensor * seq
    small = tensor == 2 and seq == 2 and dp == 4
    swap = [(0, 1), (1, 0)]

    act = project(acts, in_ids, in_signs, in_table, 512, "project_acts")
    if tensor == 2:
        other = lax.ppermute(act, "tensor", swap)
    else:
        act = lax.psum(act, "tensor")
        other = jnp.zeros_like(act)
    grad = project(grads, out_ids, out_signs, out_table, 1024, "project_grads")
    krons = kron_of(grad, act, other, (shards, seq) if small else (1, 1))

    if not small:
        kron = lax.psum(krons[0], ("tensor", "seq"))
        width = kron.shape[1] // shards
        place = lax.axis_index("tensor") * seq + lax.axis_index("seq")
        mine = lax.dynamic_slice_in_dim(kron, place * width, width, 1)
        every = lax.all_gather(kron, "dp", axis=0, tiled=True)
        left = lax.dynamic_slice_in_dim(every, place * width, width, 1)
        columns = kron.shape[1] // dp
        right = lax.dynamic_slice_in_dim(every, lax.axis_index("dp") * columns, columns, 1)
        fisher = lax.dot_general(
            left, right, (((0,), (0,)), ((), ())), precision=lax.Precision.HIGHEST
        ) / left.shape[0]
        return mine, fisher

    across = lax.ppermute(krons[1], ("tensor", "seq"), [(p, 3 - p) for p in range(shards)])
    beside = lax.ppermute(krons[2], "tensor", swap)
    mate = lax.ppermute(krons[3], "seq", swap)
    parcels = list(parcels_of([beside, across, mate, krons[0]], dp))
    for k in range(1, dp):
        parcels[k] = lax.ppermute(parcels[k], "dp", [(d, (d + k) % dp) for d in range(dp)])
    bundle = lax.ppermute(bundle_of(parcels), "seq", swap)
    mine, fisher = fisher_block(quadrant_of(parcels), parcels, bundle)
    return mine, fisher


def solution(mesh):
    in_specs = (
        P(("groups", "dp"), "seq", "tensor"),
        P(("groups", "dp"), "seq", "tensor"),
        P("tensor"),
        P("tensor"),
        P("tensor"),
        P("tensor"),
        P(),
        P(),
    )
    out_specs = (P(("groups", "dp"), ("tensor", "seq")), P(("groups", "tensor", "seq"), "dp"))
    return jax.shard_map(local, mesh=mesh, in_specs=in_specs, out_specs=out_specs, check_vma=False)
```

```python
import functools

import jax
import jax.numpy as jnp
from jax import lax
from jax.experimental import pallas as pl
from jax.experimental.pallas import tpu as pltpu
from jax.sharding import PartitionSpec as P

PROJ = 64
BLOCK = 64
LANES = 128
STRIDE = 72
VMEM_BYTES = 48 * 1024 * 1024


def chunks_of(width, most):
    if width < 4 * most or most % (4 * LANES):
        chunk = most
        while width % chunk:
            chunk -= LANES
        return [chunk] * (width // chunk)
    inner = width - most
    chunk = most
    while inner % chunk:
        chunk -= LANES
    return [most // 2] + [chunk] * (inner // chunk) + [most // 4] * 2


def split3(x):
    high = x.astype(jnp.bfloat16)
    rest = x - high.astype(jnp.float32)
    mid = rest.astype(jnp.bfloat16)
    low = (rest - mid.astype(jnp.float32)).astype(jnp.bfloat16)
    return high, mid, low


def spread_table(table, spread):
    entries = table.shape[0]
    for row in range(0, BLOCK, 2):
        both = table[:, row * PROJ : row * PROJ + LANES].astype(jnp.float32)
        spread[pl.ds(row, entries, stride=STRIDE), :] = both
        spread[pl.ds(row + 1, entries, stride=STRIDE), :] = pltpu.roll(both, PROJ, 1)


def sign_table(spread, signed):
    entries = spread.shape[0] // STRIDE
    for entry in range(entries):
        block = spread[pl.ds(entry * STRIDE, BLOCK), :].astype(jnp.bfloat16)
        signed[pl.ds((entries + entry) * BLOCK, BLOCK), :] = block
        signed[pl.ds(entry * BLOCK, BLOCK), :] = -block


def lay_blocks(ids, signs, spread, signed, matrix, first, last):
    entries = spread.shape[0] // STRIDE
    for j in range(first, last):
        if signed is None:
            start = pl.multiple_of(ids[j] * STRIDE, 8)
            sign = (2 * signs[j] - 1).astype(jnp.float32)
            block = (spread[pl.ds(start, BLOCK), :] * sign).astype(jnp.bfloat16)
        else:
            start = pl.multiple_of((signs[j] * entries + ids[j]) * BLOCK, BLOCK)
            block = signed[pl.ds(start, BLOCK), :]
        matrix[pl.ds(j * BLOCK, BLOCK), :] = block


def operand(x):
    x1, x2, x3 = split3(x)
    return jnp.concatenate([x1, x1, x2, x1, x3, x2], axis=1)


def products_with(left, act):
    a1, a2, a3 = split3(act)
    right = jnp.concatenate([a1, a2, a1, a3, a1, a2], axis=1)
    return lax.dot_general(left, right, (((1,), (1,)), ((), ())), preferred_element_type=jnp.float32)


def project_kernel(widths, ids, signs, table, rows_ref, out, *refs):
    spread, matrix, held, total, own_table, own_ids, own_signs, sems, *signed = refs
    signed = signed[0] if signed else None
    copies, starts, start = [], [], 0
    for c, width in enumerate(widths):
        columns = pl.ds(start, width)
        copies.append(pltpu.make_async_copy(rows_ref.at[:, columns], held.at[:, columns], sems.at[c]))
        starts.append(start)
        start += width
    small = [
        pltpu.make_async_copy(source, kept, sems.at[len(widths) + k])
        for k, (source, kept) in enumerate(((table, own_table), (ids, own_ids), (signs, own_signs)))
    ]
    for copy in small + copies:
        copy.start()
    small[0].wait()
    spread_table(own_table, spread)
    if signed is not None:
        sign_table(spread, signed)
    small[1].wait()
    small[2].wait()
    lay = functools.partial(lay_blocks, own_ids, own_signs, spread, signed, matrix)
    lay(0, widths[0] // BLOCK)
    for c, copy in enumerate(copies):
        columns = pl.ds(starts[c], widths[c])
        copy.wait()
        if c + 1 < len(widths):
            lay(starts[c + 1] // BLOCK, (starts[c + 1] + widths[c + 1]) // BLOCK)
        part = lax.dot_general(
            matrix[columns, :PROJ],
            held[:, columns],
            (((0,), (1,)), ((), ())),
            preferred_element_type=jnp.float32,
        )
        if c == 0:
            total[...] = part
        elif c + 1 < len(widths):
            total[...] += part
    part = total[...] + part if len(widths) > 1 else part
    pairs, _, tokens = out.shape
    for pair in range(pairs):
        for side in range(2):
            example = 2 * pair + side
            out[pair, pl.ds(side * PROJ, PROJ), :] = part[:, example * tokens : (example + 1) * tokens]


def project(values, ids, signs, table, most, name):
    count, tokens, width = values.shape
    widths = chunks_of(width, most)
    rows = count * tokens
    entries = table.shape[0]
    blocks = ids.shape[0]
    operands = [
        pltpu.with_memory_space_constraint(each, pltpu.HBM)
        for each in (ids, signs, table, values.reshape(rows, width))
    ]
    signed = [pltpu.VMEM((2 * entries * BLOCK, LANES), jnp.bfloat16)] if blocks > entries else []
    return pl.pallas_call(
        functools.partial(project_kernel, widths),
        out_shape=jax.ShapeDtypeStruct((count // 2, LANES, tokens), jnp.float32),
        in_specs=[pl.BlockSpec(memory_space=pltpu.HBM)] * 4,
        out_specs=pl.BlockSpec(memory_space=pltpu.VMEM),
        scratch_shapes=[
            pltpu.VMEM((entries * STRIDE, LANES), jnp.float32),
            pltpu.VMEM((width, LANES), jnp.bfloat16),
            pltpu.VMEM((rows, width), jnp.bfloat16),
            pltpu.VMEM((PROJ, rows), jnp.float32),
            pltpu.VMEM(table.shape, table.dtype),
            pltpu.SMEM(ids.shape, ids.dtype),
            pltpu.SMEM(signs.shape, signs.dtype),
            pltpu.SemaphoreType.DMA((len(widths) + 3,)),
        ]
        + signed,
        compiler_params=pltpu.CompilerParams(vmem_limit_bytes=VMEM_BYTES),
        cost_estimate=pl.CostEstimate(
            flops=2 * rows * width * LANES, bytes_accessed=2 * rows * width, transcendentals=0
        ),
        name=name,
    )(*operands)


def kron_kernel(cuts, grads, own, act, *refs):
    parts = cuts[1]
    outs, rows, products = refs[:-2], refs[-2], refs[-1]
    pairs = act.shape[0]
    for pair in range(pairs):
        both = products_with(operand(grads[pair]), own[pair] + act[pair])
        for side in range(2):
            products[pl.ds((2 * pair + side) * STRIDE, PROJ), :] = both[side * PROJ : (side + 1) * PROJ]
    count = 2 * pairs
    lower = lax.broadcasted_iota(jnp.int32, (count, LANES), 1) < PROJ
    even = lax.broadcasted_iota(jnp.int32, (count, LANES), 0) % 2 == 0
    here = even == lower
    tiles = rows.shape[2] // LANES // cuts[0]
    for tile in range(PROJ * PROJ // LANES):
        both = []
        for p in (2 * tile, 2 * tile + 1):
            v = products[pl.ds(p, count, stride=STRIDE), :]
            both.append(jnp.where(here, v, pltpu.roll(v, PROJ, 1)))
        block, part, within = tile // tiles // parts, tile // tiles % parts, tile % tiles
        rows[part, :, pl.ds((block * tiles + within) * LANES, LANES)] = jnp.where(lower, both[0], both[1])
    for k, out in enumerate(outs):
        part = lax.rem(lax.axis_index("seq") + k % 2, parts) if parts > 1 else 0
        out[...] = rows[part]


def kron_of(grads, own, act, cuts):
    pairs = grads.shape[0]
    parts = cuts[1]
    width = PROJ * PROJ // parts
    outs = 4 if parts > 1 else 1
    vmem = pl.BlockSpec(memory_space=pltpu.VMEM)
    return pl.pallas_call(
        functools.partial(kron_kernel, cuts),
        out_shape=[jax.ShapeDtypeStruct((2 * pairs, width), jnp.float32)] * outs,
        in_specs=[vmem] * 3,
        out_specs=[vmem] * outs,
        scratch_shapes=[
            pltpu.VMEM((parts, 2 * pairs, width), jnp.float32),
            pltpu.VMEM((2 * pairs * STRIDE, LANES), jnp.float32),
        ],
        compiler_params=pltpu.CompilerParams(vmem_limit_bytes=VMEM_BYTES),
        name="kron",
    )(grads, own, act)


def parcels_kernel(parts, *refs):
    summands, parcels = refs[:parts], refs[parts:]
    count = summands[0].shape[0]
    dp = len(parcels)
    width = parcels[0].shape[1]
    core, chip = lax.axis_index("seq"), lax.axis_index("tensor") * 2
    blocks = [chip + core, chip + 1 - core]
    for k, parcel in enumerate(parcels):
        for step, block in enumerate(blocks + [lax.rem(lax.axis_index("dp") + k, dp)]):
            lanes = pl.ds(pl.multiple_of(block * width, LANES), width)
            row = summands[0][:, lanes]
            for other in summands[1:]:
                row = row + other[:, lanes]
            parcel[pl.ds(step * count, count), :] = row


def parcels_of(summands, dp):
    count, width = summands[0].shape
    vmem = pl.BlockSpec(memory_space=pltpu.VMEM)
    return pl.pallas_call(
        functools.partial(parcels_kernel, len(summands)),
        out_shape=[jax.ShapeDtypeStruct((3 * count, width // dp), jnp.float32)] * dp,
        in_specs=[vmem] * len(summands),
        out_specs=[vmem] * dp,
        compiler_params=pltpu.CompilerParams(vmem_limit_bytes=VMEM_BYTES),
        name="parcels",
    )(*summands)


def bundle_kernel(*refs):
    parcels, out = refs[:-1], refs[-1]
    rows = 2 * parcels[0].shape[0] // 3
    for k, parcel in enumerate(parcels):
        out[pl.ds(k * rows, rows), :] = parcel[pl.ds(rows // 2, rows), :]


def bundle_of(parcels):
    rows, width = parcels[0].shape
    vmem = pl.BlockSpec(memory_space=pltpu.VMEM)
    return pl.pallas_call(
        bundle_kernel,
        out_shape=jax.ShapeDtypeStruct((2 * rows // 3 * len(parcels), width), jnp.float32),
        in_specs=[vmem] * len(parcels),
        out_specs=vmem,
        compiler_params=pltpu.CompilerParams(vmem_limit_bytes=VMEM_BYTES),
        name="bundle",
    )(*parcels)


def left_operand(x):
    x1, x2, x3 = split3(x)
    return jnp.concatenate([x1, x1, x2, x1, x3, x2, x2, x3], axis=0).T


def right_operand(x):
    x1, x2, x3 = split3(x)
    return jnp.concatenate([x1, x2, x1, x3, x1, x2, x3, x2], axis=0)


def own_halves(parcels):
    rows = parcels[0].shape[0] // 3
    left = jnp.concatenate([parcel[pl.ds(0, rows), :] for parcel in parcels], axis=0)
    right = jnp.concatenate([parcel[pl.ds(2 * rows, rows), :] for parcel in parcels], axis=0)
    return left, right


def halves_at(part):
    core = lax.axis_index("seq")
    return [pl.ds(pl.multiple_of(place * part, part), part) for place in (core, 1 - core)]


TILE = 128


def quadrant_kernel(scale, *refs):
    parcels, (out, left_ref, right_ref, made, sems) = refs[:-5], refs[-5:]
    part = parcels[0].shape[1]
    left, right = own_halves(parcels)
    left, right = left_operand(left), right_operand(right * scale)
    left_ref[...], right_ref[...] = left, right
    here, _ = halves_at(part)
    copies = []
    for k in range(part // TILE):
        rows = slice(k * TILE, (k + 1) * TILE)
        made[rows, :] = jnp.dot(left[rows], right, preferred_element_type=jnp.float32)
        into = pl.ds(pl.multiple_of(lax.axis_index("seq") * part + k * TILE, TILE), TILE)
        copies.append(pltpu.make_async_copy(made.at[rows], out.at[into, here], sems.at[k]))
        copies[-1].start()
    for copy in copies:
        copy.wait()


def fisher_kernel(scale, begun, left, right, bundle, *refs):
    del begun
    parcels, (mine, out, made, kept, sems) = refs[:-5], refs[-5:]
    rows, part = parcels[0].shape[0] // 3, parcels[0].shape[1]
    here, there = halves_at(part)
    kept[:, here] = parcels[0][pl.ds(0, rows), :]
    kept[:, there] = bundle[pl.ds(0, rows), :]
    copies = [pltpu.make_async_copy(kept, mine, sems.at[0])]
    copies[0].start()
    count = len(parcels)
    other_left = jnp.concatenate([bundle[pl.ds(2 * k * rows, rows), :] for k in range(count)], axis=0)
    other_right = jnp.concatenate([bundle[pl.ds((2 * k + 1) * rows, rows), :] for k in range(count)], axis=0)
    right, other_right = right[...], right_operand(other_right * scale)
    for k in range(part // TILE):
        piece = slice(k * TILE, (k + 1) * TILE)
        made[0, piece, :] = jnp.dot(left[piece, :], other_right, preferred_element_type=jnp.float32)
        into = pl.ds(pl.multiple_of(lax.axis_index("seq") * part + k * TILE, TILE), TILE)
        copies.append(pltpu.make_async_copy(made.at[0, piece], out.at[into, there], sems.at[k + 1]))
        copies[-1].start()
    other_left = left_operand(other_left)
    for k, (operand_right, into) in enumerate(((other_right, there), (right, here))):
        made[k + 1] = jnp.dot(other_left, operand_right, preferred_element_type=jnp.float32)
        copies.append(pltpu.make_async_copy(made.at[k + 1], out.at[there, into], sems.at[part // TILE + k + 1]))
        copies[-1].start()
    for copy in copies:
        copy.wait()


def quadrant_of(parcels):
    rows, part = parcels[0].shape
    total = rows // 3 * len(parcels)
    vmem = pl.BlockSpec(memory_space=pltpu.VMEM)
    return pl.pallas_call(
        functools.partial(quadrant_kernel, 1.0 / total),
        out_shape=[
            jax.ShapeDtypeStruct((2 * part, 2 * part), jnp.float32),
            jax.ShapeDtypeStruct((part, 8 * total), jnp.bfloat16),
            jax.ShapeDtypeStruct((8 * total, part), jnp.bfloat16),
        ],
        in_specs=[vmem] * len(parcels),
        out_specs=[pl.BlockSpec(memory_space=pltpu.HBM), vmem, vmem],
        scratch_shapes=[pltpu.VMEM((part, part), jnp.float32), pltpu.SemaphoreType.DMA((part // TILE,))],
        compiler_params=pltpu.CompilerParams(vmem_limit_bytes=VMEM_BYTES),
        cost_estimate=pl.CostEstimate(flops=2**28, bytes_accessed=4 * part * part, transcendentals=0),
        name="quadrant",
    )(*parcels)


def fisher_block(begun, parcels, bundle):
    rows, part = parcels[0].shape
    rows //= 3
    width = 2 * part
    hbm = pl.BlockSpec(memory_space=pltpu.HBM)
    vmem = pl.BlockSpec(memory_space=pltpu.VMEM)
    return pl.pallas_call(
        functools.partial(fisher_kernel, 1.0 / (rows * len(parcels))),
        out_shape=[
            jax.ShapeDtypeStruct((rows, width), jnp.float32),
            jax.ShapeDtypeStruct((width, width), jnp.float32),
        ],
        in_specs=[hbm] + [vmem] * (3 + len(parcels)),
        out_specs=[hbm] * 2,
        scratch_shapes=[
            pltpu.VMEM((3, part, part), jnp.float32),
            pltpu.VMEM((rows, width), jnp.float32),
            pltpu.SemaphoreType.DMA((part // TILE + 3,)),
        ],
        input_output_aliases={0: 1},
        compiler_params=pltpu.CompilerParams(vmem_limit_bytes=VMEM_BYTES),
        name="fisher",
    )(*begun, bundle, *parcels)


def local(acts, grads, in_ids, in_signs, out_ids, out_signs, in_table, out_table):
    tensor, seq, dp = (lax.axis_size(name) for name in ("tensor", "seq", "dp"))
    shards = tensor * seq
    small = tensor == 2 and seq == 2 and dp == 4
    swap = [(0, 1), (1, 0)]

    act = project(acts, in_ids, in_signs, in_table, 512, "project_acts")
    if tensor == 2:
        other = lax.ppermute(act, "tensor", swap)
    else:
        act = lax.psum(act, "tensor")
        other = jnp.zeros_like(act)
    grad = project(grads, out_ids, out_signs, out_table, 1024, "project_grads")
    krons = kron_of(grad, act, other, (shards, seq) if small else (1, 1))

    if not small:
        kron = lax.psum(krons[0], ("tensor", "seq"))
        width = kron.shape[1] // shards
        place = lax.axis_index("tensor") * seq + lax.axis_index("seq")
        mine = lax.dynamic_slice_in_dim(kron, place * width, width, 1)
        every = lax.all_gather(kron, "dp", axis=0, tiled=True)
        left = lax.dynamic_slice_in_dim(every, place * width, width, 1)
        columns = kron.shape[1] // dp
        right = lax.dynamic_slice_in_dim(every, lax.axis_index("dp") * columns, columns, 1)
        fisher = lax.dot_general(
            left, right, (((0,), (0,)), ((), ())), precision=lax.Precision.HIGHEST
        ) / left.shape[0]
        return mine, fisher

    across = lax.ppermute(krons[1], ("tensor", "seq"), [(p, 3 - p) for p in range(shards)])
    beside = lax.ppermute(krons[2], "tensor", swap)
    mate = lax.ppermute(krons[3], "seq", swap)
    parcels = list(parcels_of([across, beside, mate, krons[0]], dp))
    for k in range(1, dp):
        parcels[k] = lax.ppermute(parcels[k], "dp", [(d, (d + k) % dp) for d in range(dp)])
    bundle = lax.ppermute(bundle_of(parcels), "seq", swap)
    mine, fisher = fisher_block(quadrant_of(parcels), parcels, bundle)
    return mine, fisher


def solution(mesh):
    in_specs = (
        P(("groups", "dp"), "seq", "tensor"),
        P(("groups", "dp"), "seq", "tensor"),
        P("tensor"),
        P("tensor"),
        P("tensor"),
        P("tensor"),
        P(),
        P(),
    )
    out_specs = (P(("groups", "dp"), ("tensor", "seq")), P(("groups", "tensor", "seq"), "dp"))
    return jax.shard_map(local, mesh=mesh, in_specs=in_specs, out_specs=out_specs, check_vma=False)
```

```python
import functools

import jax
import jax.numpy as jnp
from jax import lax
from jax.experimental import pallas as pl
from jax.experimental.pallas import tpu as pltpu
from jax.sharding import PartitionSpec as P

PROJ = 64
BLOCK = 64
LANES = 128
STRIDE = 72
ROUTES = ((0, 1, 2, 3), (1, 3, 0, 2), (3, 2, 1, 0), (2, 0, 3, 1))
VMEM_BYTES = 48 * 1024 * 1024


def chunks_of(width, most):
    if width < 4 * most or most % (4 * LANES):
        chunk = most
        while width % chunk:
            chunk -= LANES
        return [chunk] * (width // chunk)
    inner = width - most
    chunk = most
    while inner % chunk:
        chunk -= LANES
    return [most // 2] + [chunk] * (inner // chunk) + [most // 4] * 2


def split3(x):
    high = x.astype(jnp.bfloat16)
    rest = x - high.astype(jnp.float32)
    mid = rest.astype(jnp.bfloat16)
    low = (rest - mid.astype(jnp.float32)).astype(jnp.bfloat16)
    return high, mid, low


def spread_table(table, spread):
    entries = table.shape[0]
    for row in range(0, BLOCK, 2):
        both = table[:, row * PROJ : row * PROJ + LANES].astype(jnp.float32)
        spread[pl.ds(row, entries, stride=STRIDE), :] = both
        spread[pl.ds(row + 1, entries, stride=STRIDE), :] = pltpu.roll(both, PROJ, 1)


def sign_table(spread, signed):
    entries = spread.shape[0] // STRIDE
    for entry in range(entries):
        block = spread[pl.ds(entry * STRIDE, BLOCK), :].astype(jnp.bfloat16)
        signed[pl.ds((entries + entry) * BLOCK, BLOCK), :] = block
        signed[pl.ds(entry * BLOCK, BLOCK), :] = -block


def lay_blocks(ids, signs, spread, signed, matrix, first, last):
    entries = spread.shape[0] // STRIDE
    for j in range(first, last):
        if signed is None:
            start = pl.multiple_of(ids[j] * STRIDE, 8)
            sign = (2 * signs[j] - 1).astype(jnp.float32)
            block = (spread[pl.ds(start, BLOCK), :] * sign).astype(jnp.bfloat16)
        else:
            start = pl.multiple_of((signs[j] * entries + ids[j]) * BLOCK, BLOCK)
            block = signed[pl.ds(start, BLOCK), :]
        matrix[pl.ds(j * BLOCK, BLOCK), :] = block


def operand(x):
    x1, x2, x3 = split3(x)
    return jnp.concatenate([x1, x1, x2, x1, x3, x2], axis=1)


def products_with(left, act):
    a1, a2, a3 = split3(act)
    right = jnp.concatenate([a1, a2, a1, a3, a1, a2], axis=1)
    return lax.dot_general(left, right, (((1,), (1,)), ((), ())), preferred_element_type=jnp.float32)


def project_kernel(widths, ids, signs, table, rows_ref, out, *refs):
    spread, matrix, held, total, own_table, own_ids, own_signs, sems, *signed = refs
    signed = signed[0] if signed else None
    copies, starts, start = [], [], 0
    for c, width in enumerate(widths):
        columns = pl.ds(start, width)
        copies.append(pltpu.make_async_copy(rows_ref.at[:, columns], held.at[:, columns], sems.at[c]))
        starts.append(start)
        start += width
    small = [
        pltpu.make_async_copy(source, kept, sems.at[len(widths) + k])
        for k, (source, kept) in enumerate(((table, own_table), (ids, own_ids), (signs, own_signs)))
    ]
    for copy in small + copies:
        copy.start()
    small[0].wait()
    spread_table(own_table, spread)
    if signed is not None:
        sign_table(spread, signed)
    small[1].wait()
    small[2].wait()
    lay = functools.partial(lay_blocks, own_ids, own_signs, spread, signed, matrix)
    lay(0, widths[0] // BLOCK)
    for c, copy in enumerate(copies):
        columns = pl.ds(starts[c], widths[c])
        copy.wait()
        if c + 1 < len(widths):
            lay(starts[c + 1] // BLOCK, (starts[c + 1] + widths[c + 1]) // BLOCK)
        part = lax.dot_general(
            matrix[columns, :PROJ],
            held[:, columns],
            (((0,), (1,)), ((), ())),
            preferred_element_type=jnp.float32,
        )
        if c == 0:
            total[...] = part
        elif c + 1 < len(widths):
            total[...] += part
    part = total[...] + part if len(widths) > 1 else part
    pairs, _, tokens = out.shape
    for pair in range(pairs):
        for side in range(2):
            example = 2 * pair + side
            out[pair, pl.ds(side * PROJ, PROJ), :] = part[:, example * tokens : (example + 1) * tokens]


def project(values, ids, signs, table, most, name):
    count, tokens, width = values.shape
    widths = chunks_of(width, most)
    rows = count * tokens
    entries = table.shape[0]
    blocks = ids.shape[0]
    operands = [
        pltpu.with_memory_space_constraint(each, pltpu.HBM)
        for each in (ids, signs, table, values.reshape(rows, width))
    ]
    signed = [pltpu.VMEM((2 * entries * BLOCK, LANES), jnp.bfloat16)] if blocks > entries else []
    return pl.pallas_call(
        functools.partial(project_kernel, widths),
        out_shape=jax.ShapeDtypeStruct((count // 2, LANES, tokens), jnp.float32),
        in_specs=[pl.BlockSpec(memory_space=pltpu.HBM)] * 4,
        out_specs=pl.BlockSpec(memory_space=pltpu.VMEM),
        scratch_shapes=[
            pltpu.VMEM((entries * STRIDE, LANES), jnp.float32),
            pltpu.VMEM((width, LANES), jnp.bfloat16),
            pltpu.VMEM((rows, width), jnp.bfloat16),
            pltpu.VMEM((PROJ, rows), jnp.float32),
            pltpu.VMEM(table.shape, table.dtype),
            pltpu.SMEM(ids.shape, ids.dtype),
            pltpu.SMEM(signs.shape, signs.dtype),
            pltpu.SemaphoreType.DMA((len(widths) + 3,)),
        ]
        + signed,
        compiler_params=pltpu.CompilerParams(vmem_limit_bytes=VMEM_BYTES),
        cost_estimate=pl.CostEstimate(
            flops=2 * rows * width * LANES, bytes_accessed=2 * rows * width, transcendentals=0
        ),
        name=name,
    )(*operands)


def kron_kernel(cuts, grads, own, act, *refs):
    parts = cuts[1]
    outs, rows, products = refs[:-2], refs[-2], refs[-1]
    pairs = act.shape[0]
    for pair in range(pairs):
        both = products_with(operand(grads[pair]), own[pair] + act[pair])
        for side in range(2):
            products[pl.ds((2 * pair + side) * STRIDE, PROJ), :] = both[side * PROJ : (side + 1) * PROJ]
    count = 2 * pairs
    lower = lax.broadcasted_iota(jnp.int32, (count, LANES), 1) < PROJ
    even = lax.broadcasted_iota(jnp.int32, (count, LANES), 0) % 2 == 0
    here = even == lower
    tiles = rows.shape[2] // LANES // cuts[0]
    for tile in range(PROJ * PROJ // LANES):
        both = []
        for p in (2 * tile, 2 * tile + 1):
            v = products[pl.ds(p, count, stride=STRIDE), :]
            both.append(jnp.where(here, v, pltpu.roll(v, PROJ, 1)))
        block, part, within = tile // tiles // parts, tile // tiles % parts, tile % tiles
        rows[part, :, pl.ds((block * tiles + within) * LANES, LANES)] = jnp.where(lower, both[0], both[1])
    for k, out in enumerate(outs):
        part = lax.rem(lax.axis_index("seq") + k % 2, parts) if parts > 1 else 0
        out[...] = rows[part]


def kron_of(grads, own, act, cuts):
    pairs = grads.shape[0]
    parts = cuts[1]
    width = PROJ * PROJ // parts
    outs = 4 if parts > 1 else 1
    vmem = pl.BlockSpec(memory_space=pltpu.VMEM)
    return pl.pallas_call(
        functools.partial(kron_kernel, cuts),
        out_shape=[jax.ShapeDtypeStruct((2 * pairs, width), jnp.float32)] * outs,
        in_specs=[vmem] * 3,
        out_specs=[vmem] * outs,
        scratch_shapes=[
            pltpu.VMEM((parts, 2 * pairs, width), jnp.float32),
            pltpu.VMEM((2 * pairs * STRIDE, LANES), jnp.float32),
        ],
        compiler_params=pltpu.CompilerParams(vmem_limit_bytes=VMEM_BYTES),
        name="kron",
    )(grads, own, act)


def parcels_kernel(parts, *refs):
    summands, parcels = refs[:parts], refs[parts:]
    count = summands[0].shape[0]
    dp = len(parcels)
    width = parcels[0].shape[1]
    core, chip = lax.axis_index("seq"), lax.axis_index("tensor") * 2
    blocks = [chip + core, chip + 1 - core]
    for k, parcel in enumerate(parcels):
        need = ROUTES[k][0]
        for d in range(1, dp):
            need = jnp.where(lax.axis_index("dp") == d, ROUTES[k][d], need)
        for step, block in enumerate(blocks + [need]):
            lanes = pl.ds(pl.multiple_of(block * width, LANES), width)
            row = summands[0][:, lanes]
            for other in summands[1:]:
                row = row + other[:, lanes]
            parcel[pl.ds(step * count, count), :] = row


def parcels_of(summands, dp):
    count, width = summands[0].shape
    vmem = pl.BlockSpec(memory_space=pltpu.VMEM)
    return pl.pallas_call(
        functools.partial(parcels_kernel, len(summands)),
        out_shape=[jax.ShapeDtypeStruct((3 * count, width // dp), jnp.float32)] * dp,
        in_specs=[vmem] * len(summands),
        out_specs=[vmem] * dp,
        compiler_params=pltpu.CompilerParams(vmem_limit_bytes=VMEM_BYTES),
        name="parcels",
    )(*summands)


def bundle_kernel(*refs):
    parcels, out = refs[:-1], refs[-1]
    rows = 2 * parcels[0].shape[0] // 3
    for k, parcel in enumerate(parcels):
        out[pl.ds(k * rows, rows), :] = parcel[pl.ds(rows // 2, rows), :]


def bundle_of(parcels):
    rows, width = parcels[0].shape
    vmem = pl.BlockSpec(memory_space=pltpu.VMEM)
    return pl.pallas_call(
        bundle_kernel,
        out_shape=jax.ShapeDtypeStruct((2 * rows // 3 * len(parcels), width), jnp.float32),
        in_specs=[vmem] * len(parcels),
        out_specs=vmem,
        compiler_params=pltpu.CompilerParams(vmem_limit_bytes=VMEM_BYTES),
        name="bundle",
    )(*parcels)


def left_operand(x):
    x1, x2, x3 = split3(x)
    return jnp.concatenate([x1, x1, x2, x1, x3, x2, x2, x3], axis=0).T


def right_operand(x):
    x1, x2, x3 = split3(x)
    return jnp.concatenate([x1, x2, x1, x3, x1, x2, x3, x2], axis=0)


def own_halves(parcels):
    rows = parcels[0].shape[0] // 3
    left = jnp.concatenate([parcel[pl.ds(0, rows), :] for parcel in parcels], axis=0)
    right = jnp.concatenate([parcel[pl.ds(2 * rows, rows), :] for parcel in parcels], axis=0)
    return left, right


def halves_at(part):
    core = lax.axis_index("seq")
    return [pl.ds(pl.multiple_of(place * part, part), part) for place in (core, 1 - core)]


TILE = 256


def quadrant_kernel(scale, *refs):
    parcels, (out, left_ref, right_ref, made, sems) = refs[:-5], refs[-5:]
    part = parcels[0].shape[1]
    left, right = own_halves(parcels)
    left, right = left_operand(left), right_operand(right * scale)
    left_ref[...], right_ref[...] = left, right
    here, _ = halves_at(part)
    copies = []
    for k in range(part // TILE):
        rows = slice(k * TILE, (k + 1) * TILE)
        made[rows, :] = jnp.dot(left[rows], right, preferred_element_type=jnp.float32)
        into = pl.ds(pl.multiple_of(lax.axis_index("seq") * part + k * TILE, TILE), TILE)
        copies.append(pltpu.make_async_copy(made.at[rows], out.at[into, here], sems.at[k]))
        copies[-1].start()
    for copy in copies:
        copy.wait()


def fisher_kernel(scale, begun, left, right, bundle, *refs):
    del begun
    parcels, (mine, out, made, kept, sems) = refs[:-5], refs[-5:]
    rows, part = parcels[0].shape[0] // 3, parcels[0].shape[1]
    here, there = halves_at(part)
    kept[:, here] = parcels[0][pl.ds(0, rows), :]
    kept[:, there] = bundle[pl.ds(0, rows), :]
    copies = [pltpu.make_async_copy(kept, mine, sems.at[0])]
    copies[0].start()
    count = len(parcels)
    other_left = jnp.concatenate([bundle[pl.ds(2 * k * rows, rows), :] for k in range(count)], axis=0)
    other_right = jnp.concatenate([bundle[pl.ds((2 * k + 1) * rows, rows), :] for k in range(count)], axis=0)
    right, other_right = right[...], right_operand(other_right * scale)
    for k in range(part // TILE):
        piece = slice(k * TILE, (k + 1) * TILE)
        made[0, piece, :] = jnp.dot(left[piece, :], other_right, preferred_element_type=jnp.float32)
        into = pl.ds(pl.multiple_of(lax.axis_index("seq") * part + k * TILE, TILE), TILE)
        copies.append(pltpu.make_async_copy(made.at[0, piece], out.at[into, there], sems.at[k + 1]))
        copies[-1].start()
    other_left = left_operand(other_left)
    for k, (operand_right, into) in enumerate(((other_right, there), (right, here))):
        made[k + 1] = jnp.dot(other_left, operand_right, preferred_element_type=jnp.float32)
        copies.append(pltpu.make_async_copy(made.at[k + 1], out.at[there, into], sems.at[part // TILE + k + 1]))
        copies[-1].start()
    for copy in copies:
        copy.wait()


def quadrant_of(parcels):
    rows, part = parcels[0].shape
    total = rows // 3 * len(parcels)
    vmem = pl.BlockSpec(memory_space=pltpu.VMEM)
    return pl.pallas_call(
        functools.partial(quadrant_kernel, 1.0 / total),
        out_shape=[
            jax.ShapeDtypeStruct((2 * part, 2 * part), jnp.float32),
            jax.ShapeDtypeStruct((part, 8 * total), jnp.bfloat16),
            jax.ShapeDtypeStruct((8 * total, part), jnp.bfloat16),
        ],
        in_specs=[vmem] * len(parcels),
        out_specs=[pl.BlockSpec(memory_space=pltpu.HBM), vmem, vmem],
        scratch_shapes=[pltpu.VMEM((part, part), jnp.float32), pltpu.SemaphoreType.DMA((part // TILE,))],
        compiler_params=pltpu.CompilerParams(vmem_limit_bytes=VMEM_BYTES),
        cost_estimate=pl.CostEstimate(flops=2**28, bytes_accessed=4 * part * part, transcendentals=0),
        name="quadrant",
    )(*parcels)


def fisher_block(begun, parcels, bundle):
    rows, part = parcels[0].shape
    rows //= 3
    width = 2 * part
    hbm = pl.BlockSpec(memory_space=pltpu.HBM)
    vmem = pl.BlockSpec(memory_space=pltpu.VMEM)
    return pl.pallas_call(
        functools.partial(fisher_kernel, 1.0 / (rows * len(parcels))),
        out_shape=[
            jax.ShapeDtypeStruct((rows, width), jnp.float32),
            jax.ShapeDtypeStruct((width, width), jnp.float32),
        ],
        in_specs=[hbm] + [vmem] * (3 + len(parcels)),
        out_specs=[hbm] * 2,
        scratch_shapes=[
            pltpu.VMEM((3, part, part), jnp.float32),
            pltpu.VMEM((rows, width), jnp.float32),
            pltpu.SemaphoreType.DMA((part // TILE + 3,)),
        ],
        input_output_aliases={0: 1},
        compiler_params=pltpu.CompilerParams(vmem_limit_bytes=VMEM_BYTES),
        name="fisher",
    )(*begun, bundle, *parcels)


def local(acts, grads, in_ids, in_signs, out_ids, out_signs, in_table, out_table):
    tensor, seq, dp = (lax.axis_size(name) for name in ("tensor", "seq", "dp"))
    shards = tensor * seq
    small = tensor == 2 and seq == 2 and dp == 4
    swap = [(0, 1), (1, 0)]

    act = project(acts, in_ids, in_signs, in_table, 512, "project_acts")
    if tensor == 2:
        other = lax.ppermute(act, "tensor", swap)
    else:
        act = lax.psum(act, "tensor")
        other = jnp.zeros_like(act)
    grad = project(grads, out_ids, out_signs, out_table, 1024, "project_grads")
    krons = kron_of(grad, act, other, (shards, seq) if small else (1, 1))

    if not small:
        kron = lax.psum(krons[0], ("tensor", "seq"))
        width = kron.shape[1] // shards
        place = lax.axis_index("tensor") * seq + lax.axis_index("seq")
        mine = lax.dynamic_slice_in_dim(kron, place * width, width, 1)
        every = lax.all_gather(kron, "dp", axis=0, tiled=True)
        left = lax.dynamic_slice_in_dim(every, place * width, width, 1)
        columns = kron.shape[1] // dp
        right = lax.dynamic_slice_in_dim(every, lax.axis_index("dp") * columns, columns, 1)
        fisher = lax.dot_general(
            left, right, (((0,), (0,)), ((), ())), precision=lax.Precision.HIGHEST
        ) / left.shape[0]
        return mine, fisher

    across = lax.ppermute(krons[1], ("tensor", "seq"), [(p, 3 - p) for p in range(shards)])
    beside = lax.ppermute(krons[2], "tensor", swap)
    mate = lax.ppermute(krons[3], "seq", swap)
    parcels = list(parcels_of([beside, across, mate, krons[0]], dp))
    for k in range(1, dp):
        parcels[k] = lax.ppermute(parcels[k], "dp", list(enumerate(ROUTES[k])))
    bundle = lax.ppermute(bundle_of(parcels), "seq", swap)
    mine, fisher = fisher_block(quadrant_of(parcels), parcels, bundle)
    return mine, fisher


def solution(mesh):
    in_specs = (
        P(("groups", "dp"), "seq", "tensor"),
        P(("groups", "dp"), "seq", "tensor"),
        P("tensor"),
        P("tensor"),
        P("tensor"),
        P("tensor"),
        P(),
        P(),
    )
    out_specs = (P(("groups", "dp"), ("tensor", "seq")), P(("groups", "tensor", "seq"), "dp"))
    return jax.shard_map(local, mesh=mesh, in_specs=in_specs, out_specs=out_specs, check_vma=False)
```

```python
import functools

import jax
import jax.numpy as jnp
from jax import lax
from jax.experimental import pallas as pl
from jax.experimental.pallas import tpu as pltpu
from jax.sharding import PartitionSpec as P

PROJ = 64
BLOCK = 64
LANES = 128
STRIDE = 72
ROUTES = ((0, 1, 2, 3), (1, 3, 0, 2), (3, 2, 1, 0), (2, 0, 3, 1))
VMEM_BYTES = 48 * 1024 * 1024


def chunks_of(width, most):
    if width < 4 * most or most % (4 * LANES):
        chunk = most
        while width % chunk:
            chunk -= LANES
        return [chunk] * (width // chunk)
    inner = width - most
    chunk = most
    while inner % chunk:
        chunk -= LANES
    return [most // 2] + [chunk] * (inner // chunk) + [most // 4] * 2


def split3(x):
    high = x.astype(jnp.bfloat16)
    rest = x - high.astype(jnp.float32)
    mid = rest.astype(jnp.bfloat16)
    low = (rest - mid.astype(jnp.float32)).astype(jnp.bfloat16)
    return high, mid, low


def spread_table(table, spread):
    entries = table.shape[0]
    for row in range(0, BLOCK, 2):
        both = table[:, row * PROJ : row * PROJ + LANES].astype(jnp.float32)
        spread[pl.ds(row, entries, stride=STRIDE), :] = both
        spread[pl.ds(row + 1, entries, stride=STRIDE), :] = pltpu.roll(both, PROJ, 1)


def sign_table(spread, signed):
    entries = spread.shape[0] // STRIDE
    for entry in range(entries):
        block = spread[pl.ds(entry * STRIDE, BLOCK), :].astype(jnp.bfloat16)
        signed[pl.ds((entries + entry) * BLOCK, BLOCK), :] = block
        signed[pl.ds(entry * BLOCK, BLOCK), :] = -block


def lay_blocks(ids, signs, spread, signed, matrix, first, last):
    entries = spread.shape[0] // STRIDE
    for j in range(first, last):
        if signed is None:
            start = pl.multiple_of(ids[j] * STRIDE, 8)
            sign = (2 * signs[j] - 1).astype(jnp.float32)
            block = (spread[pl.ds(start, BLOCK), :] * sign).astype(jnp.bfloat16)
        else:
            start = pl.multiple_of((signs[j] * entries + ids[j]) * BLOCK, BLOCK)
            block = signed[pl.ds(start, BLOCK), :]
        matrix[pl.ds(j * BLOCK, BLOCK), :] = block


def operand(x):
    x1, x2, x3 = split3(x)
    return jnp.concatenate([x1, x1, x2, x1, x3, x2], axis=1)


def products_with(left, act):
    a1, a2, a3 = split3(act)
    right = jnp.concatenate([a1, a2, a1, a3, a1, a2], axis=1)
    return lax.dot_general(left, right, (((1,), (1,)), ((), ())), preferred_element_type=jnp.float32)


def project_kernel(widths, ids, signs, table, rows_ref, out, *refs):
    spread, matrix, held, total, own_table, own_ids, own_signs, sems, *signed = refs
    signed = signed[0] if signed else None
    copies, starts, start = [], [], 0
    for c, width in enumerate(widths):
        columns = pl.ds(start, width)
        copies.append(pltpu.make_async_copy(rows_ref.at[:, columns], held.at[:, columns], sems.at[c]))
        starts.append(start)
        start += width
    small = [
        pltpu.make_async_copy(source, kept, sems.at[len(widths) + k])
        for k, (source, kept) in enumerate(((table, own_table), (ids, own_ids), (signs, own_signs)))
    ]
    for copy in small + copies:
        copy.start()
    small[0].wait()
    spread_table(own_table, spread)
    if signed is not None:
        sign_table(spread, signed)
    small[1].wait()
    small[2].wait()
    lay = functools.partial(lay_blocks, own_ids, own_signs, spread, signed, matrix)
    lay(0, widths[0] // BLOCK)
    for c, copy in enumerate(copies):
        columns = pl.ds(starts[c], widths[c])
        copy.wait()
        if c + 1 < len(widths):
            lay(starts[c + 1] // BLOCK, (starts[c + 1] + widths[c + 1]) // BLOCK)
        part = lax.dot_general(
            matrix[columns, :PROJ],
            held[:, columns],
            (((0,), (1,)), ((), ())),
            preferred_element_type=jnp.float32,
        )
        if c == 0:
            total[...] = part
        elif c + 1 < len(widths):
            total[...] += part
    part = total[...] + part if len(widths) > 1 else part
    pairs, _, tokens = out.shape
    for pair in range(pairs):
        for side in range(2):
            example = 2 * pair + side
            out[pair, pl.ds(side * PROJ, PROJ), :] = part[:, example * tokens : (example + 1) * tokens]


def project(values, ids, signs, table, most, name):
    count, tokens, width = values.shape
    widths = chunks_of(width, most)
    rows = count * tokens
    entries = table.shape[0]
    blocks = ids.shape[0]
    operands = [
        pltpu.with_memory_space_constraint(each, pltpu.HBM)
        for each in (ids, signs, table, values.reshape(rows, width))
    ]
    signed = [pltpu.VMEM((2 * entries * BLOCK, LANES), jnp.bfloat16)] if blocks > entries else []
    return pl.pallas_call(
        functools.partial(project_kernel, widths),
        out_shape=jax.ShapeDtypeStruct((count // 2, LANES, tokens), jnp.float32),
        in_specs=[pl.BlockSpec(memory_space=pltpu.HBM)] * 4,
        out_specs=pl.BlockSpec(memory_space=pltpu.VMEM),
        scratch_shapes=[
            pltpu.VMEM((entries * STRIDE, LANES), jnp.float32),
            pltpu.VMEM((width, LANES), jnp.bfloat16),
            pltpu.VMEM((rows, width), jnp.bfloat16),
            pltpu.VMEM((PROJ, rows), jnp.float32),
            pltpu.VMEM(table.shape, table.dtype),
            pltpu.SMEM(ids.shape, ids.dtype),
            pltpu.SMEM(signs.shape, signs.dtype),
            pltpu.SemaphoreType.DMA((len(widths) + 3,)),
        ]
        + signed,
        compiler_params=pltpu.CompilerParams(vmem_limit_bytes=VMEM_BYTES),
        cost_estimate=pl.CostEstimate(
            flops=2 * rows * width * LANES, bytes_accessed=2 * rows * width, transcendentals=0
        ),
        name=name,
    )(*operands)


def kron_kernel(cuts, grads, own, act, *refs):
    parts = cuts[1]
    outs, rows, products = refs[:-2], refs[-2], refs[-1]
    pairs = act.shape[0]
    for pair in range(pairs):
        both = products_with(operand(grads[pair]), own[pair] + act[pair])
        for side in range(2):
            products[pl.ds((2 * pair + side) * STRIDE, PROJ), :] = both[side * PROJ : (side + 1) * PROJ]
    count = 2 * pairs
    lower = lax.broadcasted_iota(jnp.int32, (count, LANES), 1) < PROJ
    even = lax.broadcasted_iota(jnp.int32, (count, LANES), 0) % 2 == 0
    here = even == lower
    tiles = rows.shape[2] // LANES // cuts[0]
    for tile in range(PROJ * PROJ // LANES):
        both = []
        for p in (2 * tile, 2 * tile + 1):
            v = products[pl.ds(p, count, stride=STRIDE), :]
            both.append(jnp.where(here, v, pltpu.roll(v, PROJ, 1)))
        block, part, within = tile // tiles // parts, tile // tiles % parts, tile % tiles
        rows[part, :, pl.ds((block * tiles + within) * LANES, LANES)] = jnp.where(lower, both[0], both[1])
    for k, out in enumerate(outs):
        part = lax.rem(lax.axis_index("seq") + k % 2, parts) if parts > 1 else 0
        out[...] = rows[part]


def kron_of(grads, own, act, cuts):
    pairs = grads.shape[0]
    parts = cuts[1]
    width = PROJ * PROJ // parts
    outs = 4 if parts > 1 else 1
    vmem = pl.BlockSpec(memory_space=pltpu.VMEM)
    return pl.pallas_call(
        functools.partial(kron_kernel, cuts),
        out_shape=[jax.ShapeDtypeStruct((2 * pairs, width), jnp.float32)] * outs,
        in_specs=[vmem] * 3,
        out_specs=[vmem] * outs,
        scratch_shapes=[
            pltpu.VMEM((parts, 2 * pairs, width), jnp.float32),
            pltpu.VMEM((2 * pairs * STRIDE, LANES), jnp.float32),
        ],
        compiler_params=pltpu.CompilerParams(vmem_limit_bytes=VMEM_BYTES),
        name="kron",
    )(grads, own, act)


def parcels_kernel(parts, *refs):
    summands, parcels = refs[:parts], refs[parts:]
    count = summands[0].shape[0]
    dp = len(parcels)
    width = parcels[0].shape[1]
    core, chip = lax.axis_index("seq"), lax.axis_index("tensor") * 2
    blocks = [chip + core, chip + 1 - core]
    for k, parcel in enumerate(parcels):
        need = ROUTES[k][0]
        for d in range(1, dp):
            need = jnp.where(lax.axis_index("dp") == d, ROUTES[k][d], need)
        for step, block in enumerate(blocks + [need]):
            lanes = pl.ds(pl.multiple_of(block * width, LANES), width)
            row = summands[0][:, lanes]
            for other in summands[1:]:
                row = row + other[:, lanes]
            parcel[pl.ds(step * count, count), :] = row


def parcels_of(summands, dp):
    count, width = summands[0].shape
    vmem = pl.BlockSpec(memory_space=pltpu.VMEM)
    return pl.pallas_call(
        functools.partial(parcels_kernel, len(summands)),
        out_shape=[jax.ShapeDtypeStruct((3 * count, width // dp), jnp.float32)] * dp,
        in_specs=[vmem] * len(summands),
        out_specs=[vmem] * dp,
        compiler_params=pltpu.CompilerParams(vmem_limit_bytes=VMEM_BYTES),
        name="parcels",
    )(*summands)


def bundle_kernel(*refs):
    parcels, out = refs[:-1], refs[-1]
    rows = 2 * parcels[0].shape[0] // 3
    for k, parcel in enumerate(parcels):
        out[pl.ds(k * rows, rows), :] = parcel[pl.ds(rows // 2, rows), :]


def bundle_of(parcels):
    rows, width = parcels[0].shape
    vmem = pl.BlockSpec(memory_space=pltpu.VMEM)
    return pl.pallas_call(
        bundle_kernel,
        out_shape=jax.ShapeDtypeStruct((2 * rows // 3 * len(parcels), width), jnp.float32),
        in_specs=[vmem] * len(parcels),
        out_specs=vmem,
        compiler_params=pltpu.CompilerParams(vmem_limit_bytes=VMEM_BYTES),
        name="bundle",
    )(*parcels)


def left_operand(x):
    x1, x2, x3 = split3(x)
    return jnp.concatenate([x1, x1, x2, x1, x3, x2, x2, x3], axis=0).T


def right_operand(x):
    x1, x2, x3 = split3(x)
    return jnp.concatenate([x1, x2, x1, x3, x1, x2, x3, x2], axis=0)


def own_halves(parcels):
    rows = parcels[0].shape[0] // 3
    left = jnp.concatenate([parcel[pl.ds(0, rows), :] for parcel in parcels], axis=0)
    right = jnp.concatenate([parcel[pl.ds(2 * rows, rows), :] for parcel in parcels], axis=0)
    return left, right


def halves_at(part):
    core = lax.axis_index("seq")
    return [pl.ds(pl.multiple_of(place * part, part), part) for place in (core, 1 - core)]


TILE = 256


def quadrant_kernel(scale, *refs):
    parcels, (out, left_ref, right_ref, made, sems) = refs[:-5], refs[-5:]
    part = parcels[0].shape[1]
    left, right = own_halves(parcels)
    left, right = left_operand(left), right_operand(right * scale)
    left_ref[...], right_ref[...] = left, right
    here, _ = halves_at(part)
    copies = []
    for k in range(part // TILE):
        rows = slice(k * TILE, (k + 1) * TILE)
        made[rows, :] = jnp.dot(left[rows], right, preferred_element_type=jnp.float32)
        into = pl.ds(pl.multiple_of(lax.axis_index("seq") * part + k * TILE, TILE), TILE)
        copies.append(pltpu.make_async_copy(made.at[rows], out.at[into, here], sems.at[k]))
        copies[-1].start()
    for copy in copies:
        copy.wait()


def fisher_kernel(scale, begun, left, right, bundle, *refs):
    del begun
    parcels, (mine, out, made, kept, sems) = refs[:-5], refs[-5:]
    rows, part = parcels[0].shape[0] // 3, parcels[0].shape[1]
    here, there = halves_at(part)
    kept[:, here] = parcels[0][pl.ds(0, rows), :]
    kept[:, there] = bundle[pl.ds(0, rows), :]
    copies = [pltpu.make_async_copy(kept, mine, sems.at[0])]
    copies[0].start()
    count = len(parcels)
    other_left = jnp.concatenate([bundle[pl.ds(2 * k * rows, rows), :] for k in range(count)], axis=0)
    other_right = jnp.concatenate([bundle[pl.ds((2 * k + 1) * rows, rows), :] for k in range(count)], axis=0)
    right, other_right = right[...], right_operand(other_right * scale)
    for k in range(part // TILE):
        piece = slice(k * TILE, (k + 1) * TILE)
        made[0, piece, :] = jnp.dot(left[piece, :], other_right, preferred_element_type=jnp.float32)
        into = pl.ds(pl.multiple_of(lax.axis_index("seq") * part + k * TILE, TILE), TILE)
        copies.append(pltpu.make_async_copy(made.at[0, piece], out.at[into, there], sems.at[k + 1]))
        copies[-1].start()
    other_left = left_operand(other_left)
    for k, (operand_right, into) in enumerate(((other_right, there), (right, here))):
        made[k + 1] = jnp.dot(other_left, operand_right, preferred_element_type=jnp.float32)
        copies.append(pltpu.make_async_copy(made.at[k + 1], out.at[there, into], sems.at[part // TILE + k + 1]))
        copies[-1].start()
    for copy in copies:
        copy.wait()


def quadrant_of(parcels):
    rows, part = parcels[0].shape
    total = rows // 3 * len(parcels)
    vmem = pl.BlockSpec(memory_space=pltpu.VMEM)
    return pl.pallas_call(
        functools.partial(quadrant_kernel, 1.0 / total),
        out_shape=[
            jax.ShapeDtypeStruct((2 * part, 2 * part), jnp.float32),
            jax.ShapeDtypeStruct((part, 8 * total), jnp.bfloat16),
            jax.ShapeDtypeStruct((8 * total, part), jnp.bfloat16),
        ],
        in_specs=[vmem] * len(parcels),
        out_specs=[pl.BlockSpec(memory_space=pltpu.HBM), vmem, vmem],
        scratch_shapes=[pltpu.VMEM((part, part), jnp.float32), pltpu.SemaphoreType.DMA((part // TILE,))],
        compiler_params=pltpu.CompilerParams(vmem_limit_bytes=VMEM_BYTES),
        cost_estimate=pl.CostEstimate(flops=2**28, bytes_accessed=4 * part * part, transcendentals=0),
        name="quadrant",
    )(*parcels)


def fisher_block(begun, parcels, bundle):
    rows, part = parcels[0].shape
    rows //= 3
    width = 2 * part
    hbm = pl.BlockSpec(memory_space=pltpu.HBM)
    vmem = pl.BlockSpec(memory_space=pltpu.VMEM)
    return pl.pallas_call(
        functools.partial(fisher_kernel, 1.0 / (rows * len(parcels))),
        out_shape=[
            jax.ShapeDtypeStruct((rows, width), jnp.float32),
            jax.ShapeDtypeStruct((width, width), jnp.float32),
        ],
        in_specs=[hbm] + [vmem] * (3 + len(parcels)),
        out_specs=[hbm] * 2,
        scratch_shapes=[
            pltpu.VMEM((3, part, part), jnp.float32),
            pltpu.VMEM((rows, width), jnp.float32),
            pltpu.SemaphoreType.DMA((part // TILE + 3,)),
        ],
        input_output_aliases={0: 1},
        compiler_params=pltpu.CompilerParams(vmem_limit_bytes=VMEM_BYTES),
        name="fisher",
    )(*begun, bundle, *parcels)


def local(acts, grads, in_ids, in_signs, out_ids, out_signs, in_table, out_table):
    tensor, seq, dp = (lax.axis_size(name) for name in ("tensor", "seq", "dp"))
    shards = tensor * seq
    small = tensor == 2 and seq == 2 and dp == 4
    swap = [(0, 1), (1, 0)]

    act = project(acts, in_ids, in_signs, in_table, 512, "project_acts")
    if tensor == 2:
        other = lax.ppermute(act, "tensor", swap)
    else:
        act = lax.psum(act, "tensor")
        other = jnp.zeros_like(act)
    grad = project(grads, out_ids, out_signs, out_table, 1024, "project_grads")
    krons = kron_of(grad, act, other, (shards, seq) if small else (1, 1))

    if not small:
        kron = lax.psum(krons[0], ("tensor", "seq"))
        width = kron.shape[1] // shards
        place = lax.axis_index("tensor") * seq + lax.axis_index("seq")
        mine = lax.dynamic_slice_in_dim(kron, place * width, width, 1)
        every = lax.all_gather(kron, "dp", axis=0, tiled=True)
        left = lax.dynamic_slice_in_dim(every, place * width, width, 1)
        columns = kron.shape[1] // dp
        right = lax.dynamic_slice_in_dim(every, lax.axis_index("dp") * columns, columns, 1)
        fisher = lax.dot_general(
            left, right, (((0,), (0,)), ((), ())), precision=lax.Precision.HIGHEST
        ) / left.shape[0]
        return mine, fisher

    across = lax.ppermute(krons[1], ("tensor", "seq"), [(p, 3 - p) for p in range(shards)])
    beside = lax.ppermute(krons[2], "tensor", swap)
    mate = lax.ppermute(krons[3], "seq", swap)
    parcels = list(parcels_of([across, beside, mate, krons[0]], dp))
    for k in range(1, dp):
        parcels[k] = lax.ppermute(parcels[k], "dp", list(enumerate(ROUTES[k])))
    bundle = lax.ppermute(bundle_of(parcels), "seq", swap)
    mine, fisher = fisher_block(quadrant_of(parcels), parcels, bundle)
    return mine, fisher


def solution(mesh):
    in_specs = (
        P(("groups", "dp"), "seq", "tensor"),
        P(("groups", "dp"), "seq", "tensor"),
        P("tensor"),
        P("tensor"),
        P("tensor"),
        P("tensor"),
        P(),
        P(),
    )
    out_specs = (P(("groups", "dp"), ("tensor", "seq")), P(("groups", "tensor", "seq"), "dp"))
    return jax.shard_map(local, mesh=mesh, in_specs=in_specs, out_specs=out_specs, check_vma=False)
```

```python
import functools

import jax
import jax.numpy as jnp
from jax import lax
from jax.experimental import pallas as pl
from jax.experimental.pallas import tpu as pltpu
from jax.sharding import PartitionSpec as P

PROJ = 64
BLOCK = 64
LANES = 128
STRIDE = 72
ROUTES = ((0, 1, 2, 3), (1, 3, 0, 2), (3, 2, 1, 0), (2, 0, 3, 1))
VMEM_BYTES = 48 * 1024 * 1024


def chunks_of(width, most):
    if width < 4 * most or most % (4 * LANES):
        chunk = most
        while width % chunk:
            chunk -= LANES
        return [chunk] * (width // chunk)
    inner = width - most
    chunk = most
    while inner % chunk:
        chunk -= LANES
    return [most // 2] + [chunk] * (inner // chunk) + [most // 2]


def split3(x):
    high = x.astype(jnp.bfloat16)
    rest = x - high.astype(jnp.float32)
    mid = rest.astype(jnp.bfloat16)
    low = (rest - mid.astype(jnp.float32)).astype(jnp.bfloat16)
    return high, mid, low


def spread_table(table, spread):
    entries = table.shape[0]
    for row in range(0, BLOCK, 2):
        both = table[:, row * PROJ : row * PROJ + LANES].astype(jnp.float32)
        spread[pl.ds(row, entries, stride=STRIDE), :] = both
        spread[pl.ds(row + 1, entries, stride=STRIDE), :] = pltpu.roll(both, PROJ, 1)


def sign_table(spread, signed):
    entries = spread.shape[0] // STRIDE
    for entry in range(entries):
        block = spread[pl.ds(entry * STRIDE, BLOCK), :].astype(jnp.bfloat16)
        signed[pl.ds((entries + entry) * BLOCK, BLOCK), :] = block
        signed[pl.ds(entry * BLOCK, BLOCK), :] = -block


def lay_blocks(ids, signs, spread, signed, matrix, first, last):
    entries = spread.shape[0] // STRIDE
    for j in range(first, last):
        if signed is None:
            start = pl.multiple_of(ids[j] * STRIDE, 8)
            sign = (2 * signs[j] - 1).astype(jnp.float32)
            block = (spread[pl.ds(start, BLOCK), :] * sign).astype(jnp.bfloat16)
        else:
            start = pl.multiple_of((signs[j] * entries + ids[j]) * BLOCK, BLOCK)
            block = signed[pl.ds(start, BLOCK), :]
        matrix[pl.ds(j * BLOCK, BLOCK), :] = block


def operand(x):
    x1, x2, x3 = split3(x)
    return jnp.concatenate([x1, x1, x2, x1, x3, x2], axis=1)


def products_with(left, act):
    a1, a2, a3 = split3(act)
    right = jnp.concatenate([a1, a2, a1, a3, a1, a2], axis=1)
    return lax.dot_general(left, right, (((1,), (1,)), ((), ())), preferred_element_type=jnp.float32)


def project_kernel(widths, ids, signs, table, rows_ref, out, *refs):
    spread, matrix, held, total, own_table, own_ids, own_signs, sems, *signed = refs
    signed = signed[0] if signed else None
    copies, starts, start = [], [], 0
    for c, width in enumerate(widths):
        columns = pl.ds(start, width)
        copies.append(pltpu.make_async_copy(rows_ref.at[:, columns], held.at[:, columns], sems.at[c]))
        starts.append(start)
        start += width
    small = [
        pltpu.make_async_copy(source, kept, sems.at[len(widths) + k])
        for k, (source, kept) in enumerate(((table, own_table), (ids, own_ids), (signs, own_signs)))
    ]
    for copy in small + copies:
        copy.start()
    small[0].wait()
    spread_table(own_table, spread)
    if signed is not None:
        sign_table(spread, signed)
    small[1].wait()
    small[2].wait()
    lay = functools.partial(lay_blocks, own_ids, own_signs, spread, signed, matrix)
    lay(0, widths[0] // BLOCK)
    for c, copy in enumerate(copies):
        columns = pl.ds(starts[c], widths[c])
        copy.wait()
        if c + 1 < len(widths):
            lay(starts[c + 1] // BLOCK, (starts[c + 1] + widths[c + 1]) // BLOCK)
        part = lax.dot_general(
            matrix[columns, :PROJ],
            held[:, columns],
            (((0,), (1,)), ((), ())),
            preferred_element_type=jnp.float32,
        )
        if c == 0:
            total[...] = part
        elif c + 1 < len(widths):
            total[...] += part
    part = total[...] + part if len(widths) > 1 else part
    pairs, _, tokens = out.shape
    for pair in range(pairs):
        for side in range(2):
            example = 2 * pair + side
            out[pair, pl.ds(side * PROJ, PROJ), :] = part[:, example * tokens : (example + 1) * tokens]


def project(values, ids, signs, table, most, name):
    count, tokens, width = values.shape
    widths = chunks_of(width, most)
    rows = count * tokens
    entries = table.shape[0]
    blocks = ids.shape[0]
    operands = [
        pltpu.with_memory_space_constraint(each, pltpu.HBM)
        for each in (ids, signs, table, values.reshape(rows, width))
    ]
    signed = [pltpu.VMEM((2 * entries * BLOCK, LANES), jnp.bfloat16)] if blocks > entries else []
    return pl.pallas_call(
        functools.partial(project_kernel, widths),
        out_shape=jax.ShapeDtypeStruct((count // 2, LANES, tokens), jnp.float32),
        in_specs=[pl.BlockSpec(memory_space=pltpu.HBM)] * 4,
        out_specs=pl.BlockSpec(memory_space=pltpu.VMEM),
        scratch_shapes=[
            pltpu.VMEM((entries * STRIDE, LANES), jnp.float32),
            pltpu.VMEM((width, LANES), jnp.bfloat16),
            pltpu.VMEM((rows, width), jnp.bfloat16),
            pltpu.VMEM((PROJ, rows), jnp.float32),
            pltpu.VMEM(table.shape, table.dtype),
            pltpu.SMEM(ids.shape, ids.dtype),
            pltpu.SMEM(signs.shape, signs.dtype),
            pltpu.SemaphoreType.DMA((len(widths) + 3,)),
        ]
        + signed,
        compiler_params=pltpu.CompilerParams(vmem_limit_bytes=VMEM_BYTES),
        cost_estimate=pl.CostEstimate(
            flops=2 * rows * width * LANES, bytes_accessed=2 * rows * width, transcendentals=0
        ),
        name=name,
    )(*operands)


def kron_kernel(cuts, grads, own, act, *refs):
    parts = cuts[1]
    outs, rows, products = refs[:-2], refs[-2], refs[-1]
    pairs = act.shape[0]
    for pair in range(pairs):
        both = products_with(operand(grads[pair]), own[pair] + act[pair])
        for side in range(2):
            products[pl.ds((2 * pair + side) * STRIDE, PROJ), :] = both[side * PROJ : (side + 1) * PROJ]
    count = 2 * pairs
    lower = lax.broadcasted_iota(jnp.int32, (count, LANES), 1) < PROJ
    even = lax.broadcasted_iota(jnp.int32, (count, LANES), 0) % 2 == 0
    here = even == lower
    tiles = rows.shape[2] // LANES // cuts[0]
    for tile in range(PROJ * PROJ // LANES):
        both = []
        for p in (2 * tile, 2 * tile + 1):
            v = products[pl.ds(p, count, stride=STRIDE), :]
            both.append(jnp.where(here, v, pltpu.roll(v, PROJ, 1)))
        block, part, within = tile // tiles // parts, tile // tiles % parts, tile % tiles
        rows[part, :, pl.ds((block * tiles + within) * LANES, LANES)] = jnp.where(lower, both[0], both[1])
    for k, out in enumerate(outs):
        part = lax.rem(lax.axis_index("seq") + k % 2, parts) if parts > 1 else 0
        out[...] = rows[part]


def kron_of(grads, own, act, cuts):
    pairs = grads.shape[0]
    parts = cuts[1]
    width = PROJ * PROJ // parts
    outs = 4 if parts > 1 else 1
    vmem = pl.BlockSpec(memory_space=pltpu.VMEM)
    return pl.pallas_call(
        functools.partial(kron_kernel, cuts),
        out_shape=[jax.ShapeDtypeStruct((2 * pairs, width), jnp.float32)] * outs,
        in_specs=[vmem] * 3,
        out_specs=[vmem] * outs,
        scratch_shapes=[
            pltpu.VMEM((parts, 2 * pairs, width), jnp.float32),
            pltpu.VMEM((2 * pairs * STRIDE, LANES), jnp.float32),
        ],
        compiler_params=pltpu.CompilerParams(vmem_limit_bytes=VMEM_BYTES),
        name="kron",
    )(grads, own, act)


def parcels_kernel(parts, *refs):
    summands, parcels = refs[:parts], refs[parts:]
    count = summands[0].shape[0]
    dp = len(parcels)
    width = parcels[0].shape[1]
    core, chip = lax.axis_index("seq"), lax.axis_index("tensor") * 2
    blocks = [chip + core, chip + 1 - core]
    for k, parcel in enumerate(parcels):
        need = ROUTES[k][0]
        for d in range(1, dp):
            need = jnp.where(lax.axis_index("dp") == d, ROUTES[k][d], need)
        for step, block in enumerate(blocks + [need]):
            lanes = pl.ds(pl.multiple_of(block * width, LANES), width)
            row = summands[0][:, lanes]
            for other in summands[1:]:
                row = row + other[:, lanes]
            parcel[pl.ds(step * count, count), :] = row


def parcels_of(summands, dp):
    count, width = summands[0].shape
    vmem = pl.BlockSpec(memory_space=pltpu.VMEM)
    return pl.pallas_call(
        functools.partial(parcels_kernel, len(summands)),
        out_shape=[jax.ShapeDtypeStruct((3 * count, width // dp), jnp.float32)] * dp,
        in_specs=[vmem] * len(summands),
        out_specs=[vmem] * dp,
        compiler_params=pltpu.CompilerParams(vmem_limit_bytes=VMEM_BYTES),
        name="parcels",
    )(*summands)


def bundle_kernel(*refs):
    parcels, out = refs[:-1], refs[-1]
    rows = 2 * parcels[0].shape[0] // 3
    for k, parcel in enumerate(parcels):
        out[pl.ds(k * rows, rows), :] = parcel[pl.ds(rows // 2, rows), :]


def bundle_of(parcels):
    rows, width = parcels[0].shape
    vmem = pl.BlockSpec(memory_space=pltpu.VMEM)
    return pl.pallas_call(
        bundle_kernel,
        out_shape=jax.ShapeDtypeStruct((2 * rows // 3 * len(parcels), width), jnp.float32),
        in_specs=[vmem] * len(parcels),
        out_specs=vmem,
        compiler_params=pltpu.CompilerParams(vmem_limit_bytes=VMEM_BYTES),
        name="bundle",
    )(*parcels)


def left_operand(x):
    x1, x2, x3 = split3(x)
    return jnp.concatenate([x1, x1, x2, x1, x3, x2, x2, x3], axis=0).T


def right_operand(x):
    x1, x2, x3 = split3(x)
    return jnp.concatenate([x1, x2, x1, x3, x1, x2, x3, x2], axis=0)


def own_halves(parcels):
    rows = parcels[0].shape[0] // 3
    left = jnp.concatenate([parcel[pl.ds(0, rows), :] for parcel in parcels], axis=0)
    right = jnp.concatenate([parcel[pl.ds(2 * rows, rows), :] for parcel in parcels], axis=0)
    return left, right


def halves_at(part):
    core = lax.axis_index("seq")
    return [pl.ds(pl.multiple_of(place * part, part), part) for place in (core, 1 - core)]


TILE = 256


def quadrant_kernel(scale, *refs):
    parcels, (out, left_ref, right_ref, made, sems) = refs[:-5], refs[-5:]
    part = parcels[0].shape[1]
    left, right = own_halves(parcels)
    left, right = left_operand(left), right_operand(right * scale)
    left_ref[...], right_ref[...] = left, right
    here, _ = halves_at(part)
    copies = []
    for k in range(part // TILE):
        rows = slice(k * TILE, (k + 1) * TILE)
        made[rows, :] = jnp.dot(left[rows], right, preferred_element_type=jnp.float32)
        into = pl.ds(pl.multiple_of(lax.axis_index("seq") * part + k * TILE, TILE), TILE)
        copies.append(pltpu.make_async_copy(made.at[rows], out.at[into, here], sems.at[k]))
        copies[-1].start()
    for copy in copies:
        copy.wait()


def fisher_kernel(scale, begun, left, right, bundle, *refs):
    del begun
    parcels, (mine, out, made, kept, sems) = refs[:-5], refs[-5:]
    rows, part = parcels[0].shape[0] // 3, parcels[0].shape[1]
    here, there = halves_at(part)
    kept[:, here] = parcels[0][pl.ds(0, rows), :]
    kept[:, there] = bundle[pl.ds(0, rows), :]
    copies = [pltpu.make_async_copy(kept, mine, sems.at[0])]
    copies[0].start()
    count = len(parcels)
    other_left = jnp.concatenate([bundle[pl.ds(2 * k * rows, rows), :] for k in range(count)], axis=0)
    other_right = jnp.concatenate([bundle[pl.ds((2 * k + 1) * rows, rows), :] for k in range(count)], axis=0)
    right, other_right = right[...], right_operand(other_right * scale)
    for k in range(part // TILE):
        piece = slice(k * TILE, (k + 1) * TILE)
        made[0, piece, :] = jnp.dot(left[piece, :], other_right, preferred_element_type=jnp.float32)
        into = pl.ds(pl.multiple_of(lax.axis_index("seq") * part + k * TILE, TILE), TILE)
        copies.append(pltpu.make_async_copy(made.at[0, piece], out.at[into, there], sems.at[k + 1]))
        copies[-1].start()
    other_left = left_operand(other_left)
    for k, (operand_right, into) in enumerate(((other_right, there), (right, here))):
        made[k + 1] = jnp.dot(other_left, operand_right, preferred_element_type=jnp.float32)
        copies.append(pltpu.make_async_copy(made.at[k + 1], out.at[there, into], sems.at[part // TILE + k + 1]))
        copies[-1].start()
    for copy in copies:
        copy.wait()


def quadrant_of(parcels):
    rows, part = parcels[0].shape
    total = rows // 3 * len(parcels)
    vmem = pl.BlockSpec(memory_space=pltpu.VMEM)
    return pl.pallas_call(
        functools.partial(quadrant_kernel, 1.0 / total),
        out_shape=[
            jax.ShapeDtypeStruct((2 * part, 2 * part), jnp.float32),
            jax.ShapeDtypeStruct((part, 8 * total), jnp.bfloat16),
            jax.ShapeDtypeStruct((8 * total, part), jnp.bfloat16),
        ],
        in_specs=[vmem] * len(parcels),
        out_specs=[pl.BlockSpec(memory_space=pltpu.HBM), vmem, vmem],
        scratch_shapes=[pltpu.VMEM((part, part), jnp.float32), pltpu.SemaphoreType.DMA((part // TILE,))],
        compiler_params=pltpu.CompilerParams(vmem_limit_bytes=VMEM_BYTES),
        cost_estimate=pl.CostEstimate(flops=2**28, bytes_accessed=4 * part * part, transcendentals=0),
        name="quadrant",
    )(*parcels)


def fisher_block(begun, parcels, bundle):
    rows, part = parcels[0].shape
    rows //= 3
    width = 2 * part
    hbm = pl.BlockSpec(memory_space=pltpu.HBM)
    vmem = pl.BlockSpec(memory_space=pltpu.VMEM)
    return pl.pallas_call(
        functools.partial(fisher_kernel, 1.0 / (rows * len(parcels))),
        out_shape=[
            jax.ShapeDtypeStruct((rows, width), jnp.float32),
            jax.ShapeDtypeStruct((width, width), jnp.float32),
        ],
        in_specs=[hbm] + [vmem] * (3 + len(parcels)),
        out_specs=[hbm] * 2,
        scratch_shapes=[
            pltpu.VMEM((3, part, part), jnp.float32),
            pltpu.VMEM((rows, width), jnp.float32),
            pltpu.SemaphoreType.DMA((part // TILE + 3,)),
        ],
        input_output_aliases={0: 1},
        compiler_params=pltpu.CompilerParams(vmem_limit_bytes=VMEM_BYTES),
        name="fisher",
    )(*begun, bundle, *parcels)


def local(acts, grads, in_ids, in_signs, out_ids, out_signs, in_table, out_table):
    tensor, seq, dp = (lax.axis_size(name) for name in ("tensor", "seq", "dp"))
    shards = tensor * seq
    small = tensor == 2 and seq == 2 and dp == 4
    swap = [(0, 1), (1, 0)]

    act = project(acts, in_ids, in_signs, in_table, 512, "project_acts")
    if tensor == 2:
        other = lax.ppermute(act, "tensor", swap)
    else:
        act = lax.psum(act, "tensor")
        other = jnp.zeros_like(act)
    grad = project(grads, out_ids, out_signs, out_table, 1024, "project_grads")
    krons = kron_of(grad, act, other, (shards, seq) if small else (1, 1))

    if not small:
        kron = lax.psum(krons[0], ("tensor", "seq"))
        width = kron.shape[1] // shards
        place = lax.axis_index("tensor") * seq + lax.axis_index("seq")
        mine = lax.dynamic_slice_in_dim(kron, place * width, width, 1)
        every = lax.all_gather(kron, "dp", axis=0, tiled=True)
        left = lax.dynamic_slice_in_dim(every, place * width, width, 1)
        columns = kron.shape[1] // dp
        right = lax.dynamic_slice_in_dim(every, lax.axis_index("dp") * columns, columns, 1)
        fisher = lax.dot_general(
            left, right, (((0,), (0,)), ((), ())), precision=lax.Precision.HIGHEST
        ) / left.shape[0]
        return mine, fisher

    across = lax.ppermute(krons[1], ("tensor", "seq"), [(p, 3 - p) for p in range(shards)])
    beside = lax.ppermute(krons[2], "tensor", swap)
    mate = lax.ppermute(krons[3], "seq", swap)
    parcels = list(parcels_of([beside, across, mate, krons[0]], dp))
    for k in range(1, dp):
        parcels[k] = lax.ppermute(parcels[k], "dp", list(enumerate(ROUTES[k])))
    bundle = lax.ppermute(bundle_of(parcels), "seq", swap)
    mine, fisher = fisher_block(quadrant_of(parcels), parcels, bundle)
    return mine, fisher


def solution(mesh):
    in_specs = (
        P(("groups", "dp"), "seq", "tensor"),
        P(("groups", "dp"), "seq", "tensor"),
        P("tensor"),
        P("tensor"),
        P("tensor"),
        P("tensor"),
        P(),
        P(),
    )
    out_specs = (P(("groups", "dp"), ("tensor", "seq")), P(("groups", "tensor", "seq"), "dp"))
    return jax.shard_map(local, mesh=mesh, in_specs=in_specs, out_specs=out_specs, check_vma=False)
```
